128 devices in a mesh: ch: 4 (over y), rows: 32 (over x, z, core).
Axes of the slice: x: 4, y: 4, z: 4, core: 2. Of those that a mesh axis runs over, the one named last changes fastest.
Arguments:
- features: bfloat16 [2, 32, 512, 512], P(None, 'rows', None, 'ch'), may hold values from -6 to 6
- lengths: int32 [2, 32], P(None, 'rows'), may hold values from 128 to 512, as said below
- input_gain: bfloat16 [512], P(('ch', 'rows')), may hold values from 0.5 to 1.5
- input_bias: bfloat16 [512], P(('ch', 'rows')), may hold values from -1.25 to 1.25
- proj_weight: bfloat16 [512, 768], P(('ch', 'rows')), may hold values from -0.25 to 0.25
- proj_bias: bfloat16 [768], P(('ch', 'rows')), may hold values from -1.25 to 1.25
- conv_weight: bfloat16 [768, 48, 128], P(('ch', 'rows')), may hold values from -0.078125 to 0.078125
- conv_bias: bfloat16 [768], P(('ch', 'rows')), may hold values from -1.25 to 1.25
- encoder_gain: bfloat16 [768], P(('ch', 'rows')), may hold values from 0.5 to 1.5
- encoder_bias: bfloat16 [768], P(('ch', 'rows')), may hold values from -1.25 to 1.25
- attend_weight: bfloat16 [768, 2304], P(('ch', 'rows')), may hold values from -0.3125 to 0.3125
- query_bias: bfloat16 [768], P(('ch', 'rows')), may hold values from -1.25 to 1.25
- value_bias: bfloat16 [768], P(('ch', 'rows')), may hold values from -1.25 to 1.25
- output_weight: bfloat16 [768, 768], P(('ch', 'rows')), may hold values from -1.75 to 1.75
- output_bias: bfloat16 [768], P(('ch', 'rows')), may hold values from -3.5 to 3.5
- attend_gain: bfloat16 [768], P(('ch', 'rows')), may hold values from 0.5 to 1.5
- attend_bias: bfloat16 [768], P(('ch', 'rows')), may hold values from -1.25 to 1.25
- hidden_weight: bfloat16 [768, 3072], P(('ch', 'rows')), may hold values from -0.21875 to 0.21875
- hidden_bias: bfloat16 [3072], P(('ch', 'rows')), may hold values from -1.25 to 1.25
- return_weight: bfloat16 [3072, 768], P(('ch', 'rows')), may hold values from -0.109375 to 0.109375
- return_bias: bfloat16 [768], P(('ch', 'rows')), may hold values from -1.25 to 1.25
- final_gain: bfloat16 [768], P(('ch', 'rows')), may hold values from 0.5 to 1.5
- final_bias: bfloat16 [768], P(('ch', 'rows')), may hold values from -1.25 to 1.25
- out_grad: bfloat16 [2, 32, 512, 768], P(None, 'rows', 'ch'), may hold values from -6 to 6
Outputs:
- output: bfloat16 [2, 32, 512, 768], P(None, 'rows', 'ch')
- features_grad: float32 [2, 32, 512, 512], P(None, 'rows', None, 'ch')
- input_gain_grad: float32 [512], P(('ch', 'rows'))
- input_bias_grad: float32 [512], P(('ch', 'rows'))
- proj_weight_grad: float32 [512, 768], P(('ch', 'rows'))
- proj_bias_grad: float32 [768], P(('ch', 'rows'))
- conv_weight_grad: float32 [768, 48, 128], P(('ch', 'rows'))
- conv_bias_grad: float32 [768], P(('ch', 'rows'))
- encoder_gain_grad: float32 [768], P(('ch', 'rows'))
- encoder_bias_grad: float32 [768], P(('ch', 'rows'))
- attend_weight_grad: float32 [768, 2304], P(('ch', 'rows'))
- query_bias_grad: float32 [768], P(('ch', 'rows'))
- value_bias_grad: float32 [768], P(('ch', 'rows'))
- output_weight_grad: float32 [768, 768], P(('ch', 'rows'))
- output_bias_grad: float32 [768], P(('ch', 'rows'))
- attend_gain_grad: float32 [768], P(('ch', 'rows'))
- attend_bias_grad: float32 [768], P(('ch', 'rows'))
- hidden_weight_grad: float32 [768, 3072], P(('ch', 'rows'))
- hidden_bias_grad: float32 [3072], P(('ch', 'rows'))
- return_weight_grad: float32 [3072, 768], P(('ch', 'rows'))
- return_bias_grad: float32 [768], P(('ch', 'rows'))
- final_gain_grad: float32 [768], P(('ch', 'rows'))
- final_bias_grad: float32 [768], P(('ch', 'rows'))
The draws below stay inside these ranges and needn't reach their ends.
Inputs may be any that keep to these rules, and one draw needn't show every extreme that they name: `lengths`: each entry is the number of valid frames at the start of one utterance slot of 512 frames; in every column one of the 2 entries exceeds 3 * 128.
All inputs are finite; a program needn't handle non-finite values.
Results may differ from the reference program's by a relative error of at most 0.033.
Values may be sent and summed in bfloat16 or wider, within the bound.
A program may use at most 192 MiB of HBM per device.

```python
import jax
import jax.numpy as jnp
from jax import lax

C = 512
D = 768
HEADS = 12
HEAD_DIM = 64
FF = 3072
K = 128
GROUPS = 16
MICRO = 2
TOK_DEV = 128
GROUP = 512
UTTS = 32
GW = 48


def draw_lengths(key, part):
    key = jax.random.fold_in(key, 11)
    first, second, third, fourth = jax.random.split(key, 4)
    common = jax.random.randint(first, (MICRO, UTTS), GROUP // 4, GROUP + 1)
    longest = jax.random.randint(second, (MICRO, UTTS), 3 * TOK_DEV + 1, GROUP + 1)
    chosen = jax.random.randint(third, (UTTS,), 0, MICRO)
    marked = jnp.arange(MICRO)[:, None] == chosen[None, :]
    lengths = jnp.where(marked, longest, common)
    column = jax.random.randint(fourth, (), 0, UTTS)
    filled = marked & (jnp.arange(UTTS)[None, :] == column)
    return jnp.where(filled, GROUP, lengths).astype(jnp.int32)


def level_of(stream_key, dims, pieces, low, largest):
    def one(dim, parts):
        heights = jax.random.uniform(jax.random.fold_in(jax.random.fold_in(stream_key, 6), dim), (parts,), jnp.float32, low / len(pieces), largest / len(pieces))
        return jnp.repeat(jnp.exp(heights), dims[dim] // parts).reshape((-1,) + (1,) * (len(dims) - dim - 1))

    level = one(*pieces[0])
    for cut in pieces[1:]:
        level = level * one(*cut)
    return level


def normal_values(rng, dims, scale, most, shards=(), held_as=jnp.bfloat16):
    drawn = scale * jax.random.normal(rng, dims, jnp.float32)
    if shards:
        drawn = drawn * level_of(rng, dims, shards, -0.22, 0.18)
    return jnp.clip(drawn, -most, most).astype(held_as)


def setup_inputs(seed: int = 0) -> dict:
    key_list = jax.random.split(jax.random.key(seed), 25)
    return {
        "features": normal_values(key_list[0], (MICRO, UTTS, GROUP, C), 1.0, 6.0, ((1, 32), (3, 4))),
        "lengths": draw_lengths(jax.random.fold_in(key_list[24], 71), 0),
        "input_gain": jnp.clip(1.0 + 0.1 * jax.random.normal(key_list[2], (C,), jnp.float32), 0.5, 1.5).astype(jnp.bfloat16),
        "input_bias": normal_values(key_list[3], (C,), 0.2, 1.25, ((0, 128),)),
        "proj_weight": normal_values(key_list[4], (C, D), C ** -0.5, 0.25, ((0, 128),)),
        "proj_bias": normal_values(key_list[5], (D,), 0.2, 1.25, ((0, 128),)),
        "conv_weight": normal_values(key_list[6], (D, GW, K), (GW * K) ** -0.5, 0.078125, ((0, 128),)),
        "conv_bias": normal_values(key_list[7], (D,), 0.2, 1.25, ((0, 128),)),
        "encoder_gain": jnp.clip(1.0 + 0.1 * jax.random.normal(key_list[8], (D,), jnp.float32), 0.5, 1.5).astype(jnp.bfloat16),
        "encoder_bias": normal_values(key_list[9], (D,), 0.2, 1.25, ((0, 128),)),
        "attend_weight": normal_values(key_list[10], (D, 3 * D), (D // 2) ** -0.5, 0.3125, ((0, 128),)),
        "query_bias": normal_values(key_list[11], (D,), 0.2, 1.25, ((0, 128),)),
        "value_bias": normal_values(key_list[12], (D,), 0.2, 1.25, ((0, 128),)),
        "output_weight": normal_values(key_list[13], (D, D), (D // 64) ** -0.5, 1.75, ((0, 128),)),
        "output_bias": normal_values(key_list[14], (D,), 0.6, 3.5, ((0, 128),)),
        "attend_gain": jnp.clip(1.0 + 0.1 * jax.random.normal(key_list[15], (D,), jnp.float32), 0.5, 1.5).astype(jnp.bfloat16),
        "attend_bias": normal_values(key_list[16], (D,), 0.2, 1.25, ((0, 128),)),
        "hidden_weight": normal_values(key_list[17], (D, FF), D ** -0.5, 0.21875, ((0, 128),)),
        "hidden_bias": normal_values(key_list[18], (FF,), 0.2, 1.25, ((0, 128),)),
        "return_weight": normal_values(key_list[19], (FF, D), FF ** -0.5, 0.109375, ((0, 128),)),
        "return_bias": normal_values(key_list[20], (D,), 0.2, 1.25, ((0, 128),)),
        "final_gain": jnp.clip(1.0 + 0.1 * jax.random.normal(key_list[21], (D,), jnp.float32), 0.5, 1.5).astype(jnp.bfloat16),
        "final_bias": normal_values(key_list[22], (D,), 0.2, 1.25, ((0, 128),)),
        "out_grad": normal_values(key_list[23], (MICRO, UTTS, GROUP, D), 1.0, 6.0, ((1, 32), (2, 4))),
    }


@jax.custom_vjp
def low(v):
    return lax.optimization_barrier(v.astype(jnp.bfloat16)).astype(jnp.float32)

@jax.custom_vjp
def low_back(v):
    return v

def low_keep(v):
    return (low(v), None)

def low_pass(kept, grad):
    return (grad,)

def back_keep(v):
    return (v, None)

def back_low(kept, grad):
    return (low(grad),)
low.defvjp(low_keep, low_pass)
low_back.defvjp(back_keep, back_low)
EPS = 1e-05
HIGH = lax.Precision.HIGHEST

def norm_rows(values, gain, shift):
    mean = lax.optimization_barrier(jnp.mean(values, axis=-1, keepdims=True))
    centred = values - mean
    spread = lax.optimization_barrier(jnp.mean(centred * centred, axis=-1, keepdims=True))
    return centred * lax.rsqrt(spread + EPS) * gain + shift

def matmul(left, right):
    return jnp.dot(left, right, precision=HIGH, preferred_element_type=jnp.float32)

def smooth(values):
    return jax.nn.gelu(values, approximate=False)

def utterance(weights, frames, length):
    input_gain, input_bias, proj_weight, proj_bias, conv_weight, conv_bias, encoder_gain, encoder_bias, attend_weight, query_bias, value_bias, output_weight, output_bias, attend_gain, attend_bias, hidden_weight, hidden_bias, return_weight, return_bias, final_gain, final_bias = weights
    valid = jnp.arange(GROUP, dtype=jnp.int32) < length
    keep = valid.astype(jnp.float32)
    normed_in = norm_rows(frames, input_gain, input_bias)
    projected = low_back((matmul(low(normed_in), proj_weight) + proj_bias) * keep[:, None])
    kernel = jnp.transpose(conv_weight, (2, 1, 0))
    conv = lax.conv_general_dilated(low(projected)[None], kernel, (1,), [(K // 2, K // 2 - 1)], dimension_numbers=('NWC', 'WIO', 'NWC'), feature_group_count=GROUPS, precision=HIGH)[0]
    before = low_back(conv + conv_bias)
    summed_pos = projected + smooth(before)
    encoded = norm_rows(summed_pos, encoder_gain, encoder_bias)
    joint = matmul(low(encoded), attend_weight)
    query = low(low_back(joint[:, :D] + query_bias)).reshape(GROUP, HEADS, HEAD_DIM)
    key_rows = low(low_back(joint[:, D:2 * D])).reshape(GROUP, HEADS, HEAD_DIM)
    value_rows = low(low_back(joint[:, 2 * D:] + value_bias)).reshape(GROUP, HEADS, HEAD_DIM)
    raw = jnp.einsum('thd,shd->hts', query, key_rows, precision=HIGH) * HEAD_DIM ** (-0.5)
    scores = low_back(jnp.where(valid[None, None, :], raw, -1000000000.0))
    top = lax.optimization_barrier(jnp.max(scores, axis=-1, keepdims=True))
    expo = jnp.exp(scores - top)
    probs = expo / lax.optimization_barrier(jnp.sum(expo, axis=-1, keepdims=True))
    mixed = jnp.einsum('hts,shd->thd', low(probs), value_rows, precision=HIGH).reshape(GROUP, D)
    context = low(low_back(mixed))
    attended = low_back(matmul(context, output_weight) + output_bias)
    attn_norm = norm_rows(encoded + attended, attend_gain, attend_bias)
    pre_hidden = low_back(matmul(low(attn_norm), hidden_weight) + hidden_bias)
    outer = low_back(matmul(low(smooth(pre_hidden)), return_weight) + return_bias)
    return norm_rows(attn_norm + outer, final_gain, final_bias)

def reference(features, lengths, input_gain, input_bias, proj_weight, proj_bias, conv_weight, conv_bias, encoder_gain, encoder_bias, attend_weight, query_bias, value_bias, output_weight, output_bias, attend_gain, attend_bias, hidden_weight, hidden_bias, return_weight, return_bias, final_gain, final_bias, out_grad):
    weights = tuple((item.astype(jnp.float32) for item in (input_gain, input_bias, proj_weight, proj_bias, conv_weight, conv_bias, encoder_gain, encoder_bias, attend_weight, query_bias, value_bias, output_weight, output_bias, attend_gain, attend_bias, hidden_weight, hidden_bias, return_weight, return_bias, final_gain, final_bias)))
    frames = features.astype(jnp.float32).reshape(MICRO * UTTS, GROUP, C)
    counts = lengths.reshape(MICRO * UTTS).astype(jnp.int32)

    def forward(params, inputs):

        def single(item):
            return jax.checkpoint(utterance)(params, item[0], item[1])
        return lax.map(single, (inputs, counts))
    result, pullback = jax.vjp(forward, weights, frames)
    grads, frame_grad = pullback(out_grad.astype(jnp.float32).reshape(MICRO * UTTS, GROUP, D))
    return (result.reshape(MICRO, UTTS, GROUP, D).astype(jnp.bfloat16), frame_grad.reshape(MICRO, UTTS, GROUP, C), grads[0], grads[1], grads[2], grads[3], grads[4], grads[5], grads[6], grads[7], grads[8], grads[9], grads[10], grads[11], grads[12], grads[13], grads[14], grads[15], grads[16], grads[17], grads[18], grads[19], grads[20])
```

```python
import jax
import jax.numpy as jnp
from jax import lax
from jax.sharding import PartitionSpec as P

HEAD_DIM = 64
EPS = 1e-05
NEGATIVE = -1000000000.0
FOLD = 16
ALL = ("ch", "rows")
LOW = jnp.bfloat16


def widen(values):
    return values.astype(jnp.float32)


def dot(left, right):
    return jnp.dot(left, right, preferred_element_type=jnp.float32)


def contract(spec, left, right):
    return jnp.einsum(spec, left, right, preferred_element_type=jnp.float32)


def smooth(values):
    return 0.5 * values * (1.0 + lax.erf(values * 0.7071067811865476))


def smooth_slope(values):
    return 0.5 * (1.0 + lax.erf(values * 0.7071067811865476)) + values * 0.3989422804014327 * jnp.exp(
        -0.5 * values * values
    )


def norm(values):
    mean = jnp.mean(values, axis=-1, keepdims=True)
    centred = values - mean
    scale = lax.rsqrt(jnp.mean(centred * centred, axis=-1, keepdims=True) + EPS)
    return centred * scale, scale


def norm_back(incoming, normal, scale, gain):
    scaled = incoming * gain
    first = jnp.mean(scaled, axis=-1, keepdims=True)
    second = jnp.mean(scaled * normal, axis=-1, keepdims=True)
    return scale * (scaled - first - normal * second)


def total(values):
    return jnp.sum(values.reshape(-1, values.shape[-1]), axis=0)


def fold_taps(turned, width, begin):
    span = turned.shape[-1] + width
    padded = jnp.pad(turned, [(0, 0)] * (turned.ndim - 1) + [(begin, width + FOLD - begin)])
    return jnp.stack([padded[..., j : j + span] for j in range(FOLD)], axis=2)


def per_device(
    features, lengths, input_gain, input_bias, proj_weight, proj_bias, conv_weight, conv_bias,
    encoder_gain, encoder_bias, attend_weight, query_bias, value_bias, output_weight, output_bias,
    attend_gain, attend_bias, hidden_weight, hidden_bias, return_weight, return_bias, final_gain,
    final_bias, out_grad,
):
    parts = lax.axis_size("ch")
    ranks = lax.axis_size("rows")
    here = lax.axis_index("ch")
    micros, _, frames, narrow = features.shape
    own = proj_bias.shape[0]
    width = proj_weight.shape[1]
    quarter = width // parts
    inner, taps = conv_weight.shape[1:]
    blocks = taps // FOLD
    groups = quarter // inner
    heads = quarter // HEAD_DIM
    hidden = hidden_weight.shape[1]
    deep = hidden // parts
    wide_in = narrow * parts
    own_in = input_gain.shape[0]
    own_hid = hidden_bias.shape[0]
    seg = out_grad.shape[2]

    small = jnp.stack(
        [proj_bias, conv_bias, encoder_gain, encoder_bias, query_bias, value_bias, output_bias,
         attend_gain, attend_bias, return_bias, final_gain, final_bias]
    )
    packed = jnp.concatenate([small.reshape(-1), input_gain, input_bias, hidden_bias])
    vectors = widen(lax.all_gather(packed, ALL, axis=0, tiled=False))
    count = small.shape[0]
    table = vectors[:, : count * own].reshape(-1, count, own).transpose(1, 0, 2).reshape(count, width)
    edge = count * own
    gain_in = vectors[:, edge : edge + own_in].reshape(-1)
    bias_in = vectors[:, edge + own_in : edge + 2 * own_in].reshape(-1)
    bias_hid = vectors[:, edge + 2 * own_in :].reshape(-1)
    mine = lax.dynamic_slice_in_dim(table, here * quarter, quarter, 1)
    proj_full = lax.all_gather(proj_weight, ALL, axis=0, tiled=True)
    folded = conv_weight.reshape(own, inner, blocks, FOLD).transpose(0, 2, 3, 1)
    folded = folded.reshape(own * blocks, FOLD * inner)
    conv_all = lax.all_gather(folded, "rows", axis=0, tiled=True)
    conv_all = conv_all.reshape(groups, inner, blocks, FOLD * inner).transpose(0, 2, 1, 3)
    conv_all = conv_all.reshape(groups, blocks * inner, FOLD * inner)
    mixed = jnp.concatenate(
        [
            attend_weight.reshape(own, 3, parts, quarter).transpose(2, 0, 1, 3).reshape(parts, own, 3 * quarter),
            output_weight.reshape(own, parts, quarter).transpose(1, 0, 2),
            hidden_weight.reshape(own, parts, deep).transpose(1, 0, 2),
        ],
        axis=2,
    )
    mixed = lax.all_to_all(mixed, "ch", split_axis=0, concat_axis=0, tiled=True)
    mixed = mixed.reshape(parts * own, -1)
    attend_all = lax.all_gather(mixed[:, : 3 * quarter], "rows", axis=0, tiled=True)
    attend_all = attend_all.reshape(ranks, parts, own, 3 * quarter).transpose(1, 0, 2, 3)
    attend_all = attend_all.reshape(width, 3 * quarter)
    mid = lax.all_gather(mixed[:, 3 * quarter :], ALL, axis=0, tiled=True)
    mid = mid.reshape(parts, ranks, parts, own, quarter + deep).transpose(2, 1, 3, 0, 4)
    mid = mid.reshape(width, parts, quarter + deep)
    output_full = mid[:, :, :quarter].reshape(width, width)
    hidden_full = mid[:, :, quarter:].reshape(width, hidden)
    return_full = lax.all_gather(return_weight, ALL, axis=0, tiled=True)

    live = jnp.arange(frames, dtype=jnp.int32)[None, :] < lengths
    keep = widen(live)[:, :, None]
    source = lax.all_gather(features[:, 0], "ch", axis=2, tiled=True)
    normal_in, scale_in = norm(widen(source))
    normed_low = (normal_in * gain_in + bias_in).astype(LOW)
    proj_mine = lax.dynamic_slice_in_dim(proj_full, here * quarter, quarter, 1)
    projected = (dot(normed_low, proj_mine) + mine[0]) * keep
    turned = projected.astype(LOW).transpose(0, 2, 1).reshape(micros, groups, inner, frames)
    spread = fold_taps(turned, taps, taps // 2)
    span = spread.shape[-1]
    spread = spread.reshape(micros, groups, FOLD * inner, span)
    sums = contract("gpk,mgku->mgpu", conv_all, spread)
    sums = sums.reshape(micros, groups, blocks, inner, span)
    conv = sum(sums[:, :, b, :, FOLD * b : FOLD * b + frames] for b in range(blocks))
    before = conv.reshape(micros, quarter, frames).transpose(0, 2, 1) + mine[1]
    summed = (projected + smooth(before)).astype(LOW)
    summed = lax.all_gather(summed, "ch", axis=2, tiled=True)

    normal_enc, scale_enc = norm(widen(summed))
    encoded = normal_enc * table[2] + table[3]
    encoded_low = encoded.astype(LOW)
    joint = dot(encoded_low, attend_all).reshape(micros, frames, 3, quarter)
    shape = (micros, frames, heads, HEAD_DIM)
    query = (joint[:, :, 0] + mine[4]).astype(LOW).reshape(shape)
    keys = joint[:, :, 1].astype(LOW).reshape(shape)
    value = (joint[:, :, 2] + mine[5]).astype(LOW).reshape(shape)
    ratio = HEAD_DIM ** (-0.5)
    scores = contract("mthd,mshd->mhts", query, keys) * ratio
    scores = jnp.where(live[:, None, None, :], scores, NEGATIVE)
    expo = jnp.exp(scores - jnp.max(scores, axis=-1, keepdims=True))
    probs = expo / jnp.sum(expo, axis=-1, keepdims=True)
    probs_low = probs.astype(LOW)
    context = contract("mhts,mshd->mthd", probs_low, value).astype(LOW)
    context = context.reshape(micros, frames, quarter)
    context = lax.all_to_all(context, "ch", split_axis=1, concat_axis=2, tiled=True)

    def mine_rows(values):
        return lax.dynamic_slice_in_dim(values, here * seg, seg, 1)

    attn_sum = mine_rows(encoded) + dot(context, output_full) + table[6]
    normal_att, scale_att = norm(attn_sum)
    attn_norm = normal_att * table[7] + table[8]
    attn_low = attn_norm.astype(LOW)
    pre_hidden = dot(attn_low, hidden_full) + bias_hid
    activated = smooth(pre_hidden).astype(LOW)
    ffn_sum = attn_norm + dot(activated, return_full) + table[9]
    normal_fin, scale_fin = norm(ffn_sum)
    output = (normal_fin * table[10] + table[11]).astype(LOW)
    upstream = widen(out_grad[:, 0])
    grad_ffn = norm_back(upstream, normal_fin, scale_fin, table[10])
    slope_outer = grad_ffn.astype(LOW)
    return_grad = contract("mtf,mtd->fd", activated, slope_outer)
    grad_act = contract("mtd,fd->mtf", slope_outer, return_full)
    slope_inner = (grad_act * smooth_slope(pre_hidden)).astype(LOW)
    hidden_grad = contract("mtc,mtf->cf", attn_low, slope_inner)
    grad_norm2 = grad_ffn + contract("mtf,cf->mtc", slope_inner, hidden_full)
    grad_attn = norm_back(grad_norm2, normal_att, scale_att, table[7])
    slope_att = grad_attn.astype(LOW)
    output_grad = contract("mtc,mtd->cd", context, slope_att)
    grad_context = contract("mtd,cd->mtc", slope_att, output_full).astype(LOW)

    return_share = lax.psum_scatter(return_grad.astype(LOW), ALL, scatter_dimension=0, tiled=True)
    middle = jnp.concatenate(
        [output_grad.reshape(width, parts, quarter), hidden_grad.reshape(width, parts, deep)], axis=2
    ).astype(LOW)
    middle = middle.reshape(parts, ranks, own, parts, quarter + deep).transpose(3, 1, 0, 2, 4)
    middle = middle.reshape(-1, quarter + deep)
    middle_share = lax.psum_scatter(middle, ALL, scatter_dimension=0, tiled=True)

    grad_context = lax.all_to_all(grad_context, "ch", split_axis=2, concat_axis=1, tiled=True)
    grad_context = grad_context.reshape(shape)
    grad_probs = contract("mthd,mshd->mhts", grad_context, value)
    grad_value = contract("mhts,mthd->mshd", probs_low, grad_context).astype(LOW)
    centre = jnp.sum(probs * grad_probs, axis=-1, keepdims=True)
    slope_scores = (probs * (grad_probs - centre)).astype(LOW)
    grad_query = (contract("mhts,mshd->mthd", slope_scores, keys) * ratio).astype(LOW)
    grad_key = (contract("mhts,mthd->mshd", slope_scores, query) * ratio).astype(LOW)
    flat = (micros, frames, quarter)
    slope_joint = jnp.concatenate(
        [grad_query.reshape(flat), grad_key.reshape(flat), grad_value.reshape(flat)], axis=2
    )
    attend_grad = contract("mtc,mtk->ck", encoded_low, slope_joint).astype(LOW)
    attend_grad = attend_grad.reshape(parts, ranks, own, 3 * quarter).transpose(1, 0, 2, 3)
    attend_share = lax.psum_scatter(
        attend_grad.reshape(-1, 3 * quarter), "rows", scatter_dimension=0, tiled=True
    )
    terms = contract("mtk,ck->mtc", slope_joint, attend_all).astype(LOW)
    terms = lax.psum_scatter(terms, "ch", scatter_dimension=1, tiled=True)
    grad_encoded = grad_attn + widen(terms)
    normal_own = mine_rows(normal_enc)
    grad_pos = norm_back(grad_encoded, normal_own, mine_rows(scale_enc), table[2])
    grad_pos = lax.all_to_all(grad_pos.astype(LOW), "ch", split_axis=2, concat_axis=1, tiled=True)

    grad_pos = widen(grad_pos)
    slope_conv = (grad_pos * smooth_slope(before)).astype(LOW)
    slope_turned = slope_conv.transpose(0, 2, 1).reshape(micros, groups, inner, frames)
    shifted = jnp.stack(
        [
            jnp.pad(slope_turned, ((0, 0), (0, 0), (0, 0), (FOLD * b, taps - FOLD * b)))
            for b in range(blocks)
        ],
        axis=2,
    ).reshape(micros, groups, blocks * inner, span)
    conv_grad = contract("mgpu,mgku->gpk", shifted, spread).astype(LOW)
    conv_grad = conv_grad.reshape(groups, blocks, inner, FOLD * inner).transpose(0, 2, 1, 3)
    conv_share = lax.psum_scatter(
        conv_grad.reshape(-1, FOLD * inner), "rows", scatter_dimension=0, tiled=True
    )
    back = contract("gpk,mgpu->mgku", conv_all, shifted)
    back = back.reshape(micros, groups, FOLD, inner, span)
    half = taps // 2
    conv_in = sum(back[:, :, j, :, half - j : half - j + frames] for j in range(FOLD))
    conv_in = conv_in.reshape(micros, quarter, frames).transpose(0, 2, 1)
    slope_proj = jnp.where(live[:, :, None], grad_pos + conv_in, 0.0).astype(LOW)
    slope_all = lax.all_gather(slope_proj, "ch", axis=2, tiled=True)
    grad_normed = contract("mtd,cd->mtc", slope_all, proj_full)
    source_grad = norm_back(grad_normed, normal_in, scale_in, gain_in)

    def mine_channels(values):
        return lax.dynamic_slice_in_dim(values, here * narrow, narrow, 2)

    features_grad = mine_channels(source_grad)
    proj_grad = contract("mtc,mtd->cd", mine_channels(normed_low), slope_all).astype(LOW)
    proj_share = lax.psum_scatter(proj_grad, "rows", scatter_dimension=0, tiled=True)

    whole = jnp.stack(
        [
            total(grad_encoded * normal_own), total(grad_encoded), total(widen(slope_att)),
            total(grad_norm2 * normal_att), total(grad_norm2), total(widen(slope_outer)),
            total(upstream * normal_fin), total(upstream),
        ]
    )
    whole = whole.reshape(8, -1, own).transpose(1, 0, 2).reshape(-1, 8 * own)
    whole = jnp.concatenate([whole, total(widen(slope_inner)).reshape(-1, own_hid)], axis=1)
    whole = lax.psum_scatter(whole, ALL, scatter_dimension=0, tiled=False)
    local = jnp.stack(
        [total(widen(slope_proj)), total(widen(slope_conv)), total(widen(grad_query).reshape(flat)),
         total(widen(grad_value).reshape(flat))]
    ).reshape(4, -1, own).transpose(1, 0, 2).reshape(-1, 4 * own)
    edges = mine_channels(grad_normed)
    local = jnp.concatenate(
        [
            local,
            total(edges * mine_channels(normal_in)).reshape(-1, own_in),
            total(edges).reshape(-1, own_in),
        ],
        axis=1,
    )
    local = lax.psum_scatter(local, "rows", scatter_dimension=0, tiled=False)

    share = jnp.concatenate([attend_share, middle_share], axis=1).reshape(parts, own, -1)
    share = lax.all_to_all(share, "ch", split_axis=0, concat_axis=0, tiled=True)
    share = widen(share)
    attend_share = share[:, :, : 3 * quarter].reshape(parts, own, 3, quarter).transpose(1, 2, 0, 3)
    output_share = share[:, :, 3 * quarter : 4 * quarter].transpose(1, 0, 2)
    hidden_share = share[:, :, 4 * quarter :].transpose(1, 0, 2)
    conv_share = widen(conv_share).reshape(own, blocks, FOLD, inner).transpose(0, 3, 1, 2)
    local_parts = [local[i * own : (i + 1) * own] for i in range(4)]
    whole_parts = [whole[i * own : (i + 1) * own] for i in range(8)]
    return (
        output[:, None],
        features_grad[:, None],
        local[4 * own : 4 * own + own_in],
        local[4 * own + own_in :],
        widen(proj_share),
        local_parts[0],
        conv_share.reshape(conv_weight.shape),
        local_parts[1],
        whole_parts[0],
        whole_parts[1],
        attend_share.reshape(attend_weight.shape),
        local_parts[2],
        local_parts[3],
        output_share.reshape(output_weight.shape),
        whole_parts[2],
        whole_parts[3],
        whole_parts[4],
        hidden_share.reshape(hidden_weight.shape),
        whole[8 * own :],
        widen(return_share),
        whole_parts[5],
        whole_parts[6],
        whole_parts[7],
    )


def solution(mesh):
    vector, matrix, cube = P(ALL), P(ALL, None), P(ALL, None, None)
    weights = (
        vector, vector, matrix, vector, cube, vector, vector, vector, matrix, vector, vector,
        matrix, vector, vector, vector, matrix, vector, matrix, vector, vector, vector,
    )
    by_channel = P(None, "rows", None, "ch")
    by_frame = P(None, "rows", "ch", None)
    return jax.shard_map(
        per_device,
        mesh=mesh,
        in_specs=(by_channel, P(None, "rows")) + weights + (by_frame,),
        out_specs=(by_frame, by_channel) + weights,
        check_vma=False,
    )
```

```python
import functools
import math

import jax
import jax.numpy as jnp
from jax import lax
from jax.experimental import pallas as pl
from jax.experimental.pallas import tpu as pltpu
from jax.sharding import PartitionSpec as P

HEAD_DIM = 64
EPS = 1e-05
NEGATIVE = -1000000000.0
FOLD = 16
ALL = ("ch", "rows")
LOW = jnp.bfloat16
MESH = pl.DeviceIdType.MESH
ROOM = 60 * 1024 * 1024


def widen(values):
    return values.astype(jnp.float32)


def dot(left, right):
    return jnp.dot(left, right, preferred_element_type=jnp.float32)


def contract(spec, left, right):
    return jnp.einsum(spec, left, right, preferred_element_type=jnp.float32)


def place(side):
    rank = lax.axis_index("rows")
    return {
        "y": lax.axis_index("ch"),
        "x": rank // (2 * side),
        "z": (rank // 2) % side,
        "k": rank % 2,
    }


def peer(spot, axis, step, sizes):
    moved = dict(spot)
    moved[axis] = (spot[axis] + step) % sizes[axis]
    return moved, (moved["y"], (moved["x"] * sizes["z"] + moved["z"]) * 2 + moved["k"])


def greet(targets):
    barrier = pltpu.get_barrier_semaphore()
    for target in targets:
        pl.semaphore_signal(barrier, inc=1, device_id=target, device_id_type=MESH)
    pl.semaphore_wait(barrier, len(targets))


def send(source, target, send_sem, recv_sem, device):
    copy = pltpu.make_async_remote_copy(
        src_ref=source, dst_ref=target, send_sem=send_sem, recv_sem=recv_sem,
        device_id=device, device_id_type=MESH,
    )
    copy.start()
    return copy


def whole(count):
    return [pl.BlockSpec(memory_space=pltpu.VMEM)] * count


def call_remote(kernel, shapes, ins, outs, scratch, ident, *values):
    return pl.pallas_call(
        kernel,
        out_shape=shapes,
        in_specs=ins,
        out_specs=outs,
        scratch_shapes=scratch,
        compiler_params=pltpu.CompilerParams(
            collective_id=ident, has_side_effects=True, vmem_limit_bytes=ROOM
        ),
    )(*values)


def over_ch(values, ident, mode, parts):
    block = values.shape if mode == "gather" else values.shape[1:]

    def kernel(in_ref, out_ref, held, send_sems, recv_sems):
        here = lax.axis_index("ch")
        others = [(here + step) % parts for step in range(1, parts)]
        rank = lax.axis_index("rows")
        greet([(other, rank) for other in others])
        copies = []
        for step, other in enumerate(others):
            source = in_ref if mode == "gather" else in_ref.at[other]
            target = held.at[step] if mode == "add" else out_ref.at[here]
            copies.append(
                send(source, target, send_sems.at[step], recv_sems.at[step], (other, rank))
            )
        if mode == "gather":
            out_ref[here] = in_ref[...]
        elif mode == "swap":
            out_ref[here] = in_ref[here]
        for copy in copies:
            copy.wait()
        if mode == "add":
            result = widen(in_ref[here])
            for step in range(parts - 1):
                result = result + widen(held[step])
            out_ref[...] = result

    shape = jax.ShapeDtypeStruct(
        block if mode == "add" else (parts,) + block,
        jnp.float32 if mode == "add" else values.dtype,
    )
    slots = (parts - 1,) + block if mode == "add" else (1, 16, 128)
    return call_remote(
        kernel, shape, whole(1), whole(1)[0],
        [
            pltpu.VMEM(slots, values.dtype),
            pltpu.SemaphoreType.DMA((parts - 1,)),
            pltpu.SemaphoreType.DMA((parts - 1,)),
        ],
        ident, values,
    )


def over_eight(blocks, pair, ident, parts):
    count = 2 * parts

    def kernel(block_ref, pair_ref, block_out, pair_out, send_sems, recv_sems):
        here, rank = lax.axis_index("ch"), lax.axis_index("rows")
        core = rank % 2
        mine = here * 2 + core
        base = rank - core
        steps = range(1, count)
        others = [(mine + step) % count for step in steps]
        devices = [(other // 2, base + other % 2) for other in others]
        greet(devices)
        copies = []
        for index, (other, device) in enumerate(zip(others, devices)):
            copies.append(
                send(block_ref.at[other], block_out.at[mine], send_sems.at[index],
                     recv_sems.at[index], device)
            )
        copies.append(
            send(pair_ref.at[1 - core], pair_out.at[core], send_sems.at[count - 1],
                 recv_sems.at[count - 1], (here, base + 1 - core))
        )
        block_out[mine] = block_ref[mine]
        pair_out[core] = pair_ref[core]
        for copy in copies:
            copy.wait()

    shapes = [jax.ShapeDtypeStruct(v.shape, v.dtype) for v in (blocks, pair)]
    return call_remote(
        kernel, shapes, whole(2), whole(2),
        [pltpu.SemaphoreType.DMA((count,)), pltpu.SemaphoreType.DMA((count,))],
        ident, blocks, pair,
    )


def job_copies(jobs, sizes):
    return sum(
        len(cuts) + sum(sizes[a] - 1 for order in orders for a in order)
        for _, cuts, orders in jobs
    )


def neighbours(jobs, spot, sizes):
    found = [peer(spot, "k", 1, sizes)[1]]
    for axis in ("y", "x", "z"):
        if any(axis in axes for axes, _, _ in jobs):
            found += [peer(spot, axis, step, sizes)[1] for step in range(1, sizes[axis])]
    return found


def window(axes, fixed, cut):
    lead = tuple(fixed.get(axis, slice(None)) for axis in axes)
    return lead + (pl.ds(cut[0], cut[1]), pl.ds(cut[2], cut[3]))


def gather_jobs(values, jobs, ident, sizes):
    total = job_copies(jobs, sizes)

    def kernel(*refs):
        count = len(jobs)
        ins, outs = refs[:count], refs[count : 2 * count]
        local, send_sems, recv_sems = refs[2 * count :]
        spot = place(sizes["z"])
        core = spot["k"]
        for number, (axes, _, _) in enumerate(jobs):
            pltpu.make_async_copy(
                ins[number],
                outs[number].at[(core,) + tuple(spot[a] for a in axes)],
                local.at[number],
            ).start()
        greet(neighbours(jobs, spot, sizes))
        for number, (axes, _, _) in enumerate(jobs):
            pltpu.make_async_copy(
                ins[number],
                outs[number].at[(core,) + tuple(spot[a] for a in axes)],
                local.at[number],
            ).wait()
        used = 0
        pending = []
        finished = []
        depth = max(len(axes) for axes, _, _ in jobs)
        waiting = {}
        for stage in range(depth + 1):
            for number, (axes, cuts, orders) in enumerate(jobs):
                for piece, (cut, order) in enumerate(zip(cuts, orders)):
                    if stage > len(order):
                        continue
                    for copy in waiting.pop((number, piece), []):
                        copy.wait_recv()
                    copies = []
                    if stage < len(order):
                        axis = order[stage]
                        fixed = {a: spot[a] for a in order[stage:]}
                        steps = range(1, sizes[axis])
                    else:
                        axis, fixed, steps = "k", {}, (1,)
                    view = outs[number].at[(core,) + window(axes, fixed, cut)]
                    for step in steps:
                        device = peer(spot, axis, step, sizes)[1]
                        copies.append(
                            send(view, view, send_sems.at[used], recv_sems.at[used], device)
                        )
                        used += 1
                    waiting[(number, piece)] = copies
                    finished += copies
        for copies in waiting.values():
            for copy in copies:
                copy.wait_recv()
        for copy in finished:
            copy.wait_send()

    shapes = [
        jax.ShapeDtypeStruct((2,) + tuple(sizes[a] for a in axes) + value.shape, value.dtype)
        for value, (axes, _, _) in zip(values, jobs)
    ]
    count = len(values)
    return call_remote(
        kernel, shapes, whole(count), whole(count),
        [
            pltpu.SemaphoreType.DMA((count,)),
            pltpu.SemaphoreType.DMA((total,)),
            pltpu.SemaphoreType.DMA((total,)),
        ],
        ident, *values,
    )


def loop_blocks(dims, body):
    count = math.prod(dims)
    if count == 1:
        body((0,) * len(dims))
        return

    def step(flat, carry):
        index = []
        rest = flat
        for size in reversed(dims):
            index.append(rest % size)
            rest = rest // size
        body(tuple(reversed(index)))
        return carry

    lax.fori_loop(0, count, step, 0)


def reduce_jobs(values, jobs, ident, sizes):
    total = job_copies(jobs, sizes)
    scratch = []
    layout = []
    for value, (axes, cuts, orders) in zip(values, jobs):
        for cut, order in zip(cuts, orders):
            block = (cut[1], cut[3])
            dims = tuple(sizes[a] for a in axes)
            entry = {"start": len(scratch)}
            scratch += [pltpu.VMEM(dims + block, LOW), pltpu.VMEM(dims + block, LOW)]
            left = list(axes)
            for axis in order:
                left.remove(axis)
                dims = tuple(sizes[a] for a in left)
                scratch.append(pltpu.VMEM((max(sizes[axis] - 1, 1),) + dims + block, LOW))
                if left:
                    scratch.append(pltpu.VMEM(dims + block, LOW))
            layout.append(entry)

    def kernel(*refs):
        count = len(jobs)
        ins, outs = refs[:count], refs[count : 2 * count]
        held = refs[2 * count : 2 * count + len(scratch)]
        local, send_sems, recv_sems = refs[2 * count + len(scratch) :]
        spot = place(sizes["z"])
        core = spot["k"]
        greet(neighbours(jobs, spot, sizes))
        used = 0
        finished = []
        states = []
        for number, (axes, cuts, orders) in enumerate(jobs):
            for cut, order in zip(cuts, orders):
                begin = layout[len(states)]["start"]
                arrived, summed = held[begin], held[begin + 1]
                cut_at = window(axes, {}, cut)
                copy = send(
                    ins[number].at[(1 - core,) + cut_at], arrived, send_sems.at[used],
                    recv_sems.at[used], peer(spot, "k", 1, sizes)[1],
                )
                mine = pltpu.make_async_copy(
                    ins[number].at[(core,) + cut_at], summed, local.at[len(states)]
                )
                mine.start()
                used += 1
                finished.append(copy)
                states.append(
                    {
                        "number": number, "axes": axes, "cut": cut, "order": order,
                        "next": begin + 2, "left": list(axes), "held": summed,
                        "arrived": arrived, "copies": [copy], "mine": mine,
                    }
                )
        depth = max(len(axes) for axes, _, _ in jobs)
        for stage in range(depth + 1):
            for state in states:
                order, left = state["order"], state["left"]
                if stage > len(order):
                    continue
                for copy in state["copies"]:
                    copy.wait_recv()
                cut = state["cut"]
                if stage == 0:
                    state["mine"].wait()
                    summed, arrived = state["held"], state["arrived"]

                    def pair(index, summed=summed, arrived=arrived):
                        summed[index] = summed[index] + arrived[index]

                    loop_blocks(tuple(sizes[a] for a in left), pair)
                else:
                    axis = order[stage - 1]
                    before, arrived = state["held"], state["arrived"]
                    spot_at = left.index(axis)
                    left.remove(axis)
                    rest = tuple(sizes[a] for a in left)
                    if left:
                        target = held[state["next"]]
                        state["next"] += 1
                    else:
                        target = None

                    def merge(
                        index, before=before, arrived=arrived, spot_at=spot_at, axis=axis,
                        target=target, cut=cut, number=state["number"], left=tuple(left),
                    ):
                        own = index[:spot_at] + (spot[axis],) + index[spot_at:] if left else (spot[axis],)
                        result = widen(before[own])
                        for step in range(sizes[axis] - 1):
                            result = result + widen(arrived[(step,) + (index if left else ())])
                        if target is None:
                            outs[number][cut[0] : cut[0] + cut[1], cut[2] : cut[2] + cut[3]] = result
                        else:
                            target[index] = result.astype(LOW)

                    loop_blocks(rest if left else (1,), merge)
                    state["held"] = target
                if stage < len(order):
                    axis = order[stage]
                    arrived = held[state["next"]]
                    state["next"] += 1
                    copies = []
                    for step in range(1, sizes[axis]):
                        moved, device = peer(spot, axis, step, sizes)
                        lead = tuple(
                            moved[axis] if a == axis else slice(None) for a in left
                        )
                        copies.append(
                            send(
                                state["held"].at[lead], arrived.at[step - 1],
                                send_sems.at[used], recv_sems.at[used], device,
                            )
                        )
                        used += 1
                    state["copies"] = copies
                    state["arrived"] = arrived
                    finished += copies
        for copy in finished:
            copy.wait_send()

    shapes = [jax.ShapeDtypeStruct(value.shape[-2:], jnp.float32) for value in values]
    count = len(values)
    pieces = len(layout)
    return call_remote(
        kernel, shapes, [pl.BlockSpec(memory_space=pl.ANY)] * count, whole(count),
        scratch
        + [
            pltpu.SemaphoreType.DMA((pieces,)),
            pltpu.SemaphoreType.DMA((total,)),
            pltpu.SemaphoreType.DMA((total,)),
        ],
        ident, *values,
    )


def smooth(values):
    return 0.5 * values * (1.0 + lax.erf(values * 0.7071067811865476))


def smooth_slope(values):
    return 0.5 * (1.0 + lax.erf(values * 0.7071067811865476)) + values * 0.3989422804014327 * jnp.exp(
        -0.5 * values * values
    )


def norm(values):
    mean = jnp.mean(values, axis=-1, keepdims=True)
    centred = values - mean
    scale = lax.rsqrt(jnp.mean(centred * centred, axis=-1, keepdims=True) + EPS)
    return centred * scale, scale


def norm_back(incoming, normal, scale, gain):
    scaled = incoming * gain
    first = jnp.mean(scaled, axis=-1, keepdims=True)
    second = jnp.mean(scaled * normal, axis=-1, keepdims=True)
    return scale * (scaled - first - normal * second)


def total(values):
    return jnp.sum(values.reshape(-1, values.shape[-1]), axis=0)


def fold_taps(turned, width, begin):
    span = turned.shape[-1] + width
    padded = jnp.pad(turned, [(0, 0)] * (turned.ndim - 1) + [(begin, width + FOLD - begin)])
    return jnp.stack([padded[..., j : j + span] for j in range(FOLD)], axis=2)


def unslab(count, parts, side):
    cells = jnp.arange(count, dtype=jnp.int32).reshape(parts, side * side, 2, -1)
    cells = cells.transpose(1, 0, 2, 3).reshape(1, count)
    return (jnp.arange(count, dtype=jnp.int32)[:, None] == cells).astype(LOW)


def ffn_grads(activated, slope_outer, inputs, slope_inner, context, slope_att, parts, slabs, tall):
    deep, frames = activated.shape[0] // parts, activated.shape[1]
    width = inputs.shape[0]
    half, eighth, thin = slope_outer.shape[1] // 2, deep // 2, width // (2 * parts)
    lanes = half + eighth + 128 * (-(-thin // 128))

    def kernel(act_ref, outer_ref, in_ref, inner_ref, ctx_ref, att_ref, out_ref):
        def put(left, right, begin, size):
            block = dot(left, right).astype(LOW)
            out_ref[0, 0, :, :, begin : begin + size] = block.reshape(slabs, tall, size)

        put(act_ref[...], outer_ref[...], 0, half)
        put(in_ref[...], inner_ref[...], half, eighth)
        put(ctx_ref[...], att_ref[0], half + eighth, lanes - half - eighth)

    return pl.pallas_call(
        kernel,
        grid=(2, parts),
        out_shape=jax.ShapeDtypeStruct((2, parts, slabs, tall, lanes), LOW),
        in_specs=[
            pl.BlockSpec((deep, frames), lambda k, c: (c, 0)),
            pl.BlockSpec((frames, half), lambda k, c: (0, k)),
            pl.BlockSpec((width, frames), lambda k, c: (0, 0)),
            pl.BlockSpec((frames, eighth), lambda k, c: (0, 2 * c + k)),
            pl.BlockSpec((width, frames), lambda k, c: (0, 0)),
            pl.BlockSpec((1, frames, lanes - half - eighth), lambda k, c: (2 * c + k, 0, 0)),
        ],
        out_specs=pl.BlockSpec((1, 1, slabs, tall, lanes), lambda k, c: (k, c, 0, 0, 0)),
        compiler_params=pltpu.CompilerParams(vmem_limit_bytes=ROOM),
    )(activated, slope_outer, inputs, slope_inner, context, slope_att)


def per_device(
    features, lengths, input_gain, input_bias, proj_weight, proj_bias, conv_weight, conv_bias,
    encoder_gain, encoder_bias, attend_weight, query_bias, value_bias, output_weight, output_bias,
    attend_gain, attend_bias, hidden_weight, hidden_bias, return_weight, return_bias, final_gain,
    final_bias, out_grad,
):
    parts = lax.axis_size("ch")
    ranks = lax.axis_size("rows")
    side = math.isqrt(ranks // 2)
    sizes = {"y": parts, "x": side, "z": side, "k": 2}
    here = lax.axis_index("ch")
    micros, _, frames, narrow = features.shape
    own = proj_bias.shape[0]
    width = proj_weight.shape[1]
    quarter = width // parts
    inner, taps = conv_weight.shape[1:]
    blocks = taps // FOLD
    groups = quarter // inner
    heads = quarter // HEAD_DIM
    hidden = hidden_weight.shape[1]
    wide_in = narrow * parts
    own_in = input_gain.shape[0]
    own_hid = hidden_bias.shape[0]
    seg = out_grad.shape[2]
    eight = 2 * parts
    squares = side * side
    tall = eight * own
    deep, thin, att = hidden // eight, width // eight, 3 * quarter // 2
    half = width // 2

    cut = jnp.concatenate(
        [
            hidden_weight.reshape(own, eight, deep),
            output_weight.reshape(own, eight, thin),
            attend_weight.reshape(own, 3, parts, quarter).transpose(0, 2, 1, 3).reshape(own, eight, att),
        ],
        axis=2,
    ).transpose(1, 0, 2)
    cut = jnp.pad(cut, ((0, 0), (0, -own % 16), (0, 0)))
    first = proj_weight.reshape(own_in, eight, thin).transpose(1, 0, 2).reshape(eight, 1, -1)
    lanes_cut = cut.shape[2]
    first = jnp.pad(first, ((0, 0), (0, 0), (0, -first.shape[2] % lanes_cut)))
    first = first.reshape(eight, -1, lanes_cut)
    first = jnp.pad(first, ((0, 0), (0, -first.shape[1] % 16), (0, 0)))
    cut = jnp.concatenate([cut, first], axis=1)
    tall_cut = own + -own % 16
    pair = return_weight.reshape(-1, 2, half).transpose(1, 0, 2)
    own_ret = pair.shape[1]
    pair = jnp.pad(pair, ((0, 0), (0, -own_ret % 16), (0, 0)))
    cut, pair = over_eight(cut, pair, 0, parts)
    first = cut[:, tall_cut:].reshape(eight, -1)[:, : own_in * thin].reshape(eight * own_in, thin)
    cut = cut[:, :own].reshape(tall, lanes_cut)
    pair = pair[:, :own_ret].reshape(2 * own_ret, half)
    slab = jnp.concatenate(
        [pair, cut[:, :deep], jnp.pad(cut[:, deep : deep + thin], ((0, 0), (0, -thin % 128)))], axis=1
    )
    everything = lax.all_gather(slab, ALL, axis=0, tiled=False)
    everything = everything.reshape(parts, squares, 2, tall, -1)

    small = jnp.stack(
        [proj_bias, conv_bias, encoder_gain, encoder_bias, query_bias, value_bias, output_bias,
         attend_gain, attend_bias, return_bias, final_gain, final_bias]
    )
    packed = jnp.concatenate([small.reshape(-1), input_gain, input_bias, hidden_bias])
    spare = 128 - thin
    vector_rows = -(-packed.shape[0] // spare)
    packed = jnp.pad(packed, (0, vector_rows * spare - packed.shape[0])).reshape(vector_rows, spare)
    packed = jnp.pad(packed, ((0, first.shape[0] - vector_rows), (0, 0)))
    early = jnp.concatenate([first, packed], axis=1)
    folded = conv_weight.reshape(own, inner, blocks, FOLD).transpose(0, 2, 3, 1)
    folded = folded.reshape(own * blocks, FOLD * inner)
    own_att = cut[:, deep + thin :]
    second = jnp.concatenate([folded, jnp.pad(own_att, ((0, 0), (0, -att % 128)))], axis=1)
    lanes_b = second.shape[1]
    split_b = lanes_b // 256 * 128
    cuts_b = [(0, tall, 0, split_b), (0, tall, split_b, lanes_b - split_b)]
    orders_b = [("z", "x"), ("x", "z")]
    early, second = gather_jobs(
        [early, second],
        [
            (("y", "x", "z"), [(0, early.shape[0], 0, 128)], [("z", "x", "y")]),
            (("x", "z"), cuts_b, orders_b),
        ],
        1, sizes,
    )
    early = early.reshape(2, parts, squares, -1, 128)
    vectors = early[:, :, :, :vector_rows, thin:].transpose(1, 2, 0, 3, 4)
    vectors = widen(vectors.reshape(parts * ranks, -1))
    count = small.shape[0]
    table = vectors[:, : count * own].reshape(-1, count, own).transpose(1, 0, 2).reshape(count, width)
    edge = count * own
    gain_in = vectors[:, edge : edge + own_in].reshape(-1)
    bias_in = vectors[:, edge + own_in : edge + 2 * own_in].reshape(-1)
    bias_hid = vectors[:, edge + 2 * own_in : edge + 2 * own_in + own_hid].reshape(-1)
    mine = lax.dynamic_slice_in_dim(table, here * quarter, quarter, 1)
    proj_full = early[..., :thin].transpose(2, 3, 1, 0, 4).reshape(wide_in, width)
    proj_full = dot(unslab(wide_in, parts, side), proj_full).astype(LOW)
    natural = unslab(width, parts, side)
    attend_all = second[..., FOLD * inner : FOLD * inner + att].reshape(2, width, att)
    attend_all = dot(natural, attend_all.transpose(1, 0, 2).reshape(width, 2 * att)).astype(LOW)
    conv_all = second[..., : FOLD * inner].reshape(2, squares, own, blocks, FOLD * inner)
    conv_all = conv_all.transpose(1, 0, 2, 3, 4).reshape(groups, inner, blocks, FOLD * inner)
    conv_all = conv_all.transpose(0, 2, 1, 3).reshape(groups, blocks * inner, FOLD * inner)

    live = jnp.arange(frames, dtype=jnp.int32)[None, :] < lengths
    keep = widen(live)[:, :, None]
    rows = micros * frames

    def join(gathered):
        return gathered.transpose(1, 0, 2).reshape(micros, frames, -1)

    source = join(over_ch(features.reshape(rows, narrow), 2, "gather", parts))
    normal_in, scale_in = norm(widen(source))
    normed_low = (normal_in * gain_in + bias_in).astype(LOW)
    proj_mine = lax.dynamic_slice_in_dim(proj_full, here * quarter, quarter, 1)
    projected = (dot(normed_low, proj_mine) + mine[0]) * keep
    turned = projected.astype(LOW).transpose(0, 2, 1).reshape(micros, groups, inner, frames)
    spread = fold_taps(turned, taps, taps // 2)
    span = spread.shape[-1]
    spread = spread.reshape(micros, groups, FOLD * inner, span)
    sums = contract("gpk,mgku->mgpu", conv_all, spread)
    sums = sums.reshape(micros, groups, blocks, inner, span)
    conv = sum(sums[:, :, b, :, FOLD * b : FOLD * b + frames] for b in range(blocks))
    before = conv.reshape(micros, quarter, frames).transpose(0, 2, 1) + mine[1]
    summed = (projected + smooth(before)).astype(LOW)
    summed = join(over_ch(summed.reshape(rows, quarter), 3, "gather", parts))

    normal_enc, scale_enc = norm(widen(summed))
    encoded = normal_enc * table[2] + table[3]
    encoded_low = encoded.astype(LOW)
    joint = dot(encoded_low, attend_all).reshape(micros, frames, 3, quarter)
    shape = (micros, frames, heads, HEAD_DIM)
    query = (joint[:, :, 0] + mine[4]).astype(LOW).reshape(shape)
    keys = joint[:, :, 1].astype(LOW).reshape(shape)
    value = (joint[:, :, 2] + mine[5]).astype(LOW).reshape(shape)
    ratio = HEAD_DIM ** (-0.5)
    scores = contract("mthd,mshd->mhts", query, keys) * ratio
    scores = jnp.where(live[:, None, None, :], scores, NEGATIVE)
    expo = jnp.exp(scores - jnp.max(scores, axis=-1, keepdims=True))
    probs = expo / jnp.sum(expo, axis=-1, keepdims=True)
    probs_low = probs.astype(LOW)
    context = contract("mhts,mshd->mthd", probs_low, value).astype(LOW)

    def to_frames(values):
        blocks_out = values.reshape(micros, parts, seg, quarter).transpose(1, 0, 2, 3)
        return blocks_out.reshape(parts, micros * seg, quarter)

    def to_channels(values):
        blocks_out = values.reshape(micros * seg, parts, quarter)
        return blocks_out.transpose(1, 0, 2)

    def from_frames(values):
        back = values.reshape(parts, micros, seg, quarter)
        return back.transpose(1, 0, 2, 3).reshape(micros, frames, quarter)

    context = over_ch(to_frames(context.reshape(micros, frames, quarter)), 4, "swap", parts)
    context = context.transpose(1, 0, 2).reshape(micros * seg, width)

    def mine_rows(values):
        picked = lax.dynamic_slice_in_dim(values, here * seg, seg, 1)
        return picked.reshape(micros * seg, values.shape[2])

    return_full = everything[..., :half].transpose(0, 1, 3, 2, 4).reshape(hidden, width)
    hidden_full = everything[..., half : half + deep].transpose(1, 3, 0, 2, 4).reshape(width, hidden)
    output_full = everything[..., half + deep : half + deep + thin].transpose(1, 3, 0, 2, 4)
    output_full = dot(natural, output_full.reshape(width, width)).astype(LOW)

    attn_sum = mine_rows(encoded) + dot(context, output_full) + table[6]
    normal_att, scale_att = norm(attn_sum)
    attn_norm = normal_att * table[7] + table[8]
    attn_low = dot(attn_norm.astype(LOW), natural).astype(LOW)
    pre_hidden = dot(attn_low, hidden_full) + bias_hid
    activated = smooth(pre_hidden).astype(LOW)
    ffn_sum = attn_norm + dot(activated, return_full) + table[9]
    normal_fin, scale_fin = norm(ffn_sum)
    output = (normal_fin * table[10] + table[11]).astype(LOW)
    upstream = widen(out_grad).reshape(micros * seg, width)
    grad_ffn = norm_back(upstream, normal_fin, scale_fin, table[10])
    slope_outer = grad_ffn.astype(LOW)
    grad_act = contract("td,fd->tf", slope_outer, return_full)
    slope_inner = (grad_act * smooth_slope(pre_hidden)).astype(LOW)
    hidden_nat = dot(natural, hidden_full).astype(LOW)
    grad_norm2 = grad_ffn + contract("tf,cf->tc", slope_inner, hidden_nat)
    grad_attn = norm_back(grad_norm2, normal_att, scale_att, table[7])
    slope_att = grad_attn.astype(LOW)
    grad_context = contract("td,cd->tc", slope_att, output_full).astype(LOW)
    att_cut = slope_att.reshape(micros * seg, eight, thin).transpose(1, 0, 2)
    att_cut = jnp.pad(att_cut, ((0, 0), (0, 0), (0, -thin % 128)))
    context_slab = contract("tc,cp->pt", context, natural).astype(LOW)
    ffn = ffn_grads(
        activated.T, slope_outer, attn_low.T, slope_inner, context_slab, att_cut, parts, squares, tall
    ).reshape(2, parts, side, side, tall, -1)

    grad_context = from_frames(over_ch(to_channels(grad_context), 5, "swap", parts)).reshape(shape)
    grad_probs = contract("mthd,mshd->mhts", grad_context, value)
    grad_value = contract("mhts,mthd->mshd", probs_low, grad_context).astype(LOW)
    centre = jnp.sum(probs * grad_probs, axis=-1, keepdims=True)
    slope_scores = (probs * (grad_probs - centre)).astype(LOW)
    grad_query = (contract("mhts,mshd->mthd", slope_scores, keys) * ratio).astype(LOW)
    grad_key = (contract("mhts,mthd->mshd", slope_scores, query) * ratio).astype(LOW)
    flat = (rows, quarter)
    slope_joint = jnp.concatenate(
        [grad_query.reshape(flat), grad_key.reshape(flat), grad_value.reshape(flat)], axis=1
    )
    encoded_slab = dot(encoded_low.reshape(rows, width), natural).astype(LOW)
    attend_grad = contract("tc,tk->ck", encoded_slab, slope_joint).astype(LOW)
    terms = contract("tk,ck->tc", slope_joint, attend_all).astype(LOW)
    terms = terms.reshape(micros, parts, seg, width).transpose(1, 0, 2, 3)
    terms = over_ch(terms.reshape(parts, micros * seg, width), 6, "add", parts)
    grad_encoded = grad_attn + terms
    normal_own = mine_rows(normal_enc)
    grad_pos = norm_back(grad_encoded, normal_own, mine_rows(scale_enc), table[2])
    grad_pos = widen(from_frames(over_ch(to_channels(grad_pos.astype(LOW)), 7, "swap", parts)))

    slope_conv = (grad_pos * smooth_slope(before)).astype(LOW)
    slope_turned = slope_conv.transpose(0, 2, 1).reshape(micros, groups, inner, frames)
    shifted = jnp.stack(
        [
            jnp.pad(slope_turned, ((0, 0), (0, 0), (0, 0), (FOLD * b, taps - FOLD * b)))
            for b in range(blocks)
        ],
        axis=2,
    ).reshape(micros, groups, blocks * inner, span)
    conv_grad = contract("mgpu,mgku->gpk", shifted, spread).astype(LOW)
    conv_grad = conv_grad.reshape(groups, blocks, inner, FOLD * inner).transpose(0, 2, 1, 3)
    conv_grad = conv_grad.reshape(squares, 2, tall, FOLD * inner).transpose(1, 0, 2, 3)
    back = contract("gpk,mgpu->mgku", conv_all, shifted)
    back = back.reshape(micros, groups, FOLD, inner, span)
    offset = taps // 2
    conv_in = sum(back[:, :, j, :, offset - j : offset - j + frames] for j in range(FOLD))
    conv_in = conv_in.reshape(micros, quarter, frames).transpose(0, 2, 1)
    slope_proj = jnp.where(live[:, :, None], grad_pos + conv_in, 0.0).astype(LOW)
    slope_all = join(over_ch(slope_proj.reshape(flat), 8, "gather", parts))
    grad_normed = contract("mtd,cd->mtc", slope_all, proj_full)
    source_grad = norm_back(grad_normed, normal_in, scale_in, gain_in)

    def mine_channels(values):
        return lax.dynamic_slice_in_dim(values, here * narrow, narrow, 2)

    features_grad = mine_channels(source_grad)
    proj_grad = contract("mtc,mtd->cd", mine_channels(normed_low), slope_all)

    full = jnp.stack(
        [
            total(grad_encoded * normal_own), total(grad_encoded), total(widen(slope_att)),
            total(grad_norm2 * normal_att), total(grad_norm2), total(widen(slope_outer)),
            total(upstream * normal_fin), total(upstream),
        ]
    )
    full = full.reshape(8, -1, own).transpose(1, 0, 2).reshape(-1, 8 * own)
    full = jnp.concatenate([full, total(widen(slope_inner)).reshape(-1, own_hid)], axis=1)
    full_count = full.shape[1]
    full = full.reshape(parts, squares, 2, 1, full_count).transpose(2, 0, 1, 3, 4).astype(LOW)
    full = jnp.pad(full, ((0, 0), (0, 0), (0, 0), (0, 15), (0, -full_count % 128)))
    full = full.reshape(2, parts, side, side, 16, -1)
    local = jnp.stack(
        [total(widen(slope_proj)), total(widen(slope_conv)), total(widen(grad_query).reshape(flat)),
         total(widen(grad_value).reshape(flat))]
    ).reshape(4, -1, own).transpose(1, 0, 2).reshape(-1, 4 * own)
    edges = mine_channels(grad_normed)
    local = jnp.concatenate(
        [
            local,
            total(edges * mine_channels(normal_in)).reshape(-1, own_in),
            total(edges).reshape(-1, own_in),
        ],
        axis=1,
    )
    local_count = local.shape[1]
    local = jnp.pad(local, ((0, 0), (0, width - local_count))).reshape(ranks, 1, width)
    local = jnp.concatenate([proj_grad.reshape(ranks, own_in, width), local], axis=1).astype(LOW)
    local = jnp.pad(local, ((0, 0), (0, -(own_in + 1) % 16), (0, 0)))
    local = local.reshape(squares, 2, -1, width).transpose(1, 0, 2, 3)
    local = local.reshape(2, side, side, -1, width)
    attend_grad = attend_grad.reshape(squares, tall, 2, att).transpose(2, 0, 1, 3)
    attend_grad = jnp.pad(attend_grad, ((0, 0), (0, 0), (0, 0), (0, -att % 128)))
    second_grad = jnp.concatenate([conv_grad, attend_grad], axis=3)
    second_grad = second_grad.reshape(2, side, side, tall, lanes_b)
    third = tall // 3
    lanes_a = ffn.shape[-1]
    ffn, full, second_grad, local = reduce_jobs(
        [ffn, full, second_grad, local],
        [
            (
                ("y", "x", "z"),
                [(i * third, third, 0, lanes_a) for i in range(3)],
                [("x", "z", "y"), ("z", "y", "x"), ("y", "x", "z")],
            ),
            (("y", "x", "z"), [(0, 16, 0, full.shape[-1])], [("y", "x", "z")]),
            (("x", "z"), cuts_b, orders_b),
            (("x", "z"), [(0, local.shape[-2], 0, width)], [("x", "z")]),
        ],
        9, sizes,
    )

    cut = jnp.concatenate(
        [ffn[:, half : half + deep], ffn[:, half + deep : half + deep + thin],
         second_grad[:, FOLD * inner : FOLD * inner + att]], axis=1
    ).reshape(eight, own, -1)
    cut = jnp.pad(cut, ((0, 0), (0, -own % 8), (0, 0)))
    cut, pair = over_eight(cut, ffn[:, :half].reshape(2, own_ret, half), 10, parts)
    cut = cut[:, :own].transpose(1, 0, 2)
    hidden_share = cut[:, :, :deep].reshape(hidden_weight.shape)
    output_share = cut[:, :, deep : deep + thin].reshape(output_weight.shape)
    attend_share = cut[:, :, deep + thin :].reshape(own, parts, 3, quarter).transpose(0, 2, 1, 3)
    return_share = pair.transpose(1, 0, 2).reshape(return_weight.shape)
    conv_share = second_grad[:, : FOLD * inner].reshape(own, blocks, FOLD, inner).transpose(0, 3, 1, 2)
    tail = local[own_in, :local_count]
    full = full[0, :full_count]
    local_parts = [tail[i * own : (i + 1) * own] for i in range(4)]
    full_parts = [full[i * own : (i + 1) * own] for i in range(8)]
    return (
        output.reshape(out_grad.shape),
        features_grad[:, None],
        tail[4 * own : 4 * own + own_in],
        tail[4 * own + own_in :],
        local[:own_in],
        local_parts[0],
        conv_share.reshape(conv_weight.shape),
        local_parts[1],
        full_parts[0],
        full_parts[1],
        attend_share.reshape(attend_weight.shape),
        local_parts[2],
        local_parts[3],
        output_share,
        full_parts[2],
        full_parts[3],
        full_parts[4],
        hidden_share,
        full[8 * own :],
        return_share,
        full_parts[5],
        full_parts[6],
        full_parts[7],
    )


def solution(mesh):
    vector, matrix, cube = P(ALL), P(ALL, None), P(ALL, None, None)
    weights = (
        vector, vector, matrix, vector, cube, vector, vector, vector, matrix, vector, vector,
        matrix, vector, vector, vector, matrix, vector, matrix, vector, vector, vector,
    )
    by_channel = P(None, "rows", None, "ch")
    by_frame = P(None, "rows", "ch", None)
    return jax.shard_map(
        per_device,
        mesh=mesh,
        in_specs=(by_channel, P(None, "rows")) + weights + (by_frame,),
        out_specs=(by_frame, by_channel) + weights,
        check_vma=False,
    )
```

```python
import functools
import math

import jax
import jax.numpy as jnp
import numpy as np
from jax import lax
from jax.experimental import pallas as pl
from jax.experimental.pallas import tpu as pltpu
from jax.sharding import PartitionSpec as P

HEAD_DIM = 64
EPS = 1e-05
NEGATIVE = -1000000000.0
FOLD = 16
ALL = ("ch", "rows")
LOW = jnp.bfloat16
MESH = pl.DeviceIdType.MESH
ROOM = 60 * 1024 * 1024


def widen(values):
    return values.astype(jnp.float32)


def dot(left, right):
    return jnp.dot(left, right, preferred_element_type=jnp.float32)


def contract(spec, left, right):
    return jnp.einsum(spec, left, right, preferred_element_type=jnp.float32)


def place(side):
    rank = lax.axis_index("rows")
    return {
        "y": lax.axis_index("ch"),
        "x": rank // (2 * side),
        "z": (rank // 2) % side,
        "k": rank % 2,
    }


def peer(spot, axis, step, sizes):
    moved = dict(spot)
    moved[axis] = (spot[axis] + step) % sizes[axis]
    return moved, (moved["y"], (moved["x"] * sizes["z"] + moved["z"]) * 2 + moved["k"])


def greet(targets):
    barrier = pltpu.get_barrier_semaphore()
    for target in targets:
        pl.semaphore_signal(barrier, inc=1, device_id=target, device_id_type=MESH)
    pl.semaphore_wait(barrier, len(targets))


def send(source, target, send_sem, recv_sem, device):
    copy = pltpu.make_async_remote_copy(
        src_ref=source, dst_ref=target, send_sem=send_sem, recv_sem=recv_sem,
        device_id=device, device_id_type=MESH,
    )
    copy.start()
    return copy


def whole(count):
    return [pl.BlockSpec(memory_space=pltpu.VMEM)] * count


def call_remote(kernel, shapes, ins, outs, scratch, ident, *values):
    return pl.pallas_call(
        kernel,
        out_shape=shapes,
        in_specs=ins,
        out_specs=outs,
        scratch_shapes=scratch,
        compiler_params=pltpu.CompilerParams(
            collective_id=ident, has_side_effects=True, vmem_limit_bytes=ROOM
        ),
    )(*values)


def over_ch(values, ident, mode, parts):
    block = values.shape if mode == "gather" else values.shape[1:]
    ring = parts == 4 and mode != "swap"
    middle = block[0] // 2
    near, far = pl.ds(0, middle), pl.ds(middle, middle)

    def direct(in_ref, out_ref, held, send_sems, recv_sems):
        here = lax.axis_index("ch")
        others = [(here + step) % parts for step in range(1, parts)]
        rank = lax.axis_index("rows")
        greet([(other, rank) for other in others])
        copies = []
        for step, other in enumerate(others):
            copies.append(
                send(in_ref.at[other], out_ref.at[here], send_sems.at[step], recv_sems.at[step],
                     (other, rank))
            )
        out_ref[here] = in_ref[here]
        for copy in copies:
            copy.wait()

    def gather(in_ref, out_ref, held, send_sems, recv_sems):
        here, rank = lax.axis_index("ch"), lax.axis_index("rows")
        right, left = (here + 1) % 4, (here + 3) % 4
        greet([(right, rank), (left, rank)])

        def move(source, target, index, other):
            return send(source, target, send_sems.at[index], recv_sems.at[index], (other, rank))

        copies = [
            move(in_ref.at[near], out_ref.at[here, near], 0, right),
            move(in_ref.at[far], out_ref.at[here, far], 1, left),
            move(in_ref.at[far], out_ref.at[here, far], 2, right),
            move(in_ref.at[near], out_ref.at[here, near], 3, left),
        ]
        out_ref[here] = in_ref[...]
        copies[0].wait_recv()
        copies.append(move(out_ref.at[left, near], out_ref.at[left, near], 4, right))
        copies[1].wait_recv()
        copies.append(move(out_ref.at[right, far], out_ref.at[right, far], 5, left))
        for copy in copies[2:]:
            copy.wait_recv()
        for copy in copies:
            copy.wait_send()

    def add(in_ref, out_ref, held, send_sems, recv_sems):
        here, rank = lax.axis_index("ch"), lax.axis_index("rows")
        right, left, across = (here + 1) % 4, (here + 3) % 4, (here + 2) % 4
        greet([(right, rank), (left, rank)])

        def move(source, index, other):
            return send(
                source, held.at[index], send_sems.at[index], recv_sems.at[index], (other, rank)
            )

        copies = [
            move(in_ref.at[across, near], 0, right),
            move(in_ref.at[across, far], 1, left),
            move(in_ref.at[right, far], 2, right),
            move(in_ref.at[left, near], 3, left),
        ]
        copies[0].wait_recv()
        held[6] = in_ref[right, near] + held[0]
        copies.append(move(held.at[6], 4, right))
        copies[1].wait_recv()
        held[7] = in_ref[left, far] + held[1]
        copies.append(move(held.at[7], 5, left))
        for copy in copies[2:]:
            copy.wait_recv()
        out_ref[near] = widen(in_ref[here, near]) + widen(held[4]) + widen(held[3])
        out_ref[far] = widen(in_ref[here, far]) + widen(held[2]) + widen(held[5])
        for copy in copies:
            copy.wait_send()

    shape = jax.ShapeDtypeStruct(
        block if mode == "add" else (parts,) + block,
        jnp.float32 if mode == "add" else values.dtype,
    )
    slots = (8, middle) + block[1:] if mode == "add" else (1, 16, 128)
    return call_remote(
        {"gather": gather, "add": add, "swap": direct}[mode], shape, whole(1), whole(1)[0],
        [
            pltpu.VMEM(slots, values.dtype),
            pltpu.SemaphoreType.DMA((6,)),
            pltpu.SemaphoreType.DMA((6,)),
        ],
        ident, values,
    )


def over_eight(blocks, pair, ident, parts):
    count = 2 * parts

    def kernel(block_ref, pair_ref, block_out, pair_out, send_sems, recv_sems):
        here, rank = lax.axis_index("ch"), lax.axis_index("rows")
        core = rank % 2
        mine = here * 2 + core
        base = rank - core
        steps = range(1, count)
        others = [(mine + step) % count for step in steps]
        devices = [(other // 2, base + other % 2) for other in others]
        greet(devices)
        copies = []
        for index, (other, device) in enumerate(zip(others, devices)):
            copies.append(
                send(block_ref.at[other], block_out.at[mine], send_sems.at[index],
                     recv_sems.at[index], device)
            )
        copies.append(
            send(pair_ref.at[1 - core], pair_out.at[core], send_sems.at[count - 1],
                 recv_sems.at[count - 1], (here, base + 1 - core))
        )
        block_out[mine] = block_ref[mine]
        pair_out[core] = pair_ref[core]
        for copy in copies:
            copy.wait()

    shapes = [jax.ShapeDtypeStruct(v.shape, v.dtype) for v in (blocks, pair)]
    return call_remote(
        kernel, shapes, whole(2), whole(2),
        [pltpu.SemaphoreType.DMA((count,)), pltpu.SemaphoreType.DMA((count,))],
        ident, blocks, pair,
    )


def job_copies(jobs, sizes):
    return sum(
        len(cuts) + sum(sizes[a] - 1 for order in orders for a in order)
        for _, cuts, orders in jobs
    )


def neighbours(jobs, spot, sizes):
    found = [peer(spot, "k", 1, sizes)[1]]
    for axis in ("y", "x", "z"):
        if any(axis in axes for axes, _, _ in jobs):
            found += [peer(spot, axis, step, sizes)[1] for step in range(1, sizes[axis])]
    return found


def window(axes, fixed, cut):
    lead = tuple(fixed.get(axis, slice(None)) for axis in axes)
    return lead + (pl.ds(cut[0], cut[1]), pl.ds(cut[2], cut[3]))


def gather_jobs(values, jobs, ident, sizes):
    total = job_copies(jobs, sizes)

    def kernel(*refs):
        count = len(jobs)
        ins, outs = refs[:count], refs[count : 2 * count]
        local, send_sems, recv_sems = refs[2 * count :]
        spot = place(sizes["z"])
        core = spot["k"]
        for number, (axes, _, _) in enumerate(jobs):
            pltpu.make_async_copy(
                ins[number],
                outs[number].at[(core,) + tuple(spot[a] for a in axes)],
                local.at[number],
            ).start()
        greet(neighbours(jobs, spot, sizes))
        for number, (axes, _, _) in enumerate(jobs):
            pltpu.make_async_copy(
                ins[number],
                outs[number].at[(core,) + tuple(spot[a] for a in axes)],
                local.at[number],
            ).wait()
        used = 0
        pending = []
        finished = []
        depth = max(len(axes) for axes, _, _ in jobs)
        waiting = {}
        for stage in range(depth + 1):
            for number, (axes, cuts, orders) in enumerate(jobs):
                for piece, (cut, order) in enumerate(zip(cuts, orders)):
                    if stage > len(order):
                        continue
                    for copy in waiting.pop((number, piece), []):
                        copy.wait_recv()
                    copies = []
                    if stage < len(order):
                        axis = order[stage]
                        fixed = {a: spot[a] for a in order[stage:]}
                        steps = range(1, sizes[axis])
                    else:
                        axis, fixed, steps = "k", {}, (1,)
                    view = outs[number].at[(core,) + window(axes, fixed, cut)]
                    for step in steps:
                        device = peer(spot, axis, step, sizes)[1]
                        copies.append(
                            send(view, view, send_sems.at[used], recv_sems.at[used], device)
                        )
                        used += 1
                    waiting[(number, piece)] = copies
                    finished += copies
        for copies in waiting.values():
            for copy in copies:
                copy.wait_recv()
        for copy in finished:
            copy.wait_send()

    shapes = [
        jax.ShapeDtypeStruct((2,) + tuple(sizes[a] for a in axes) + value.shape, value.dtype)
        for value, (axes, _, _) in zip(values, jobs)
    ]
    count = len(values)
    return call_remote(
        kernel, shapes, whole(count), whole(count),
        [
            pltpu.SemaphoreType.DMA((count,)),
            pltpu.SemaphoreType.DMA((total,)),
            pltpu.SemaphoreType.DMA((total,)),
        ],
        ident, *values,
    )


def loop_blocks(dims, body):
    count = math.prod(dims)
    if count == 1:
        body((0,) * len(dims))
        return

    def step(flat, carry):
        index = []
        rest = flat
        for size in reversed(dims):
            index.append(rest % size)
            rest = rest // size
        body(tuple(reversed(index)))
        return carry

    lax.fori_loop(0, count, step, 0)


def reduce_jobs(values, jobs, ident, sizes):
    total = job_copies(jobs, sizes)
    scratch = []
    layout = []
    for value, (axes, cuts, orders) in zip(values, jobs):
        for cut, order in zip(cuts, orders):
            block = (cut[1], cut[3])
            dims = tuple(sizes[a] for a in axes)
            entry = {"start": len(scratch)}
            scratch += [pltpu.VMEM(dims + block, LOW), pltpu.VMEM(dims + block, LOW)]
            left = list(axes)
            for axis in order:
                left.remove(axis)
                dims = tuple(sizes[a] for a in left)
                scratch.append(pltpu.VMEM((max(sizes[axis] - 1, 1),) + dims + block, LOW))
                if left:
                    scratch.append(pltpu.VMEM(dims + block, LOW))
            layout.append(entry)

    def kernel(*refs):
        count = len(jobs)
        ins, outs = refs[:count], refs[count : 2 * count]
        held = refs[2 * count : 2 * count + len(scratch)]
        local, send_sems, recv_sems = refs[2 * count + len(scratch) :]
        spot = place(sizes["z"])
        core = spot["k"]
        greet(neighbours(jobs, spot, sizes))
        used = 0
        finished = []
        states = []
        for number, (axes, cuts, orders) in enumerate(jobs):
            for cut, order in zip(cuts, orders):
                begin = layout[len(states)]["start"]
                arrived, summed = held[begin], held[begin + 1]
                cut_at = window(axes, {}, cut)
                copy = send(
                    ins[number].at[(1 - core,) + cut_at], arrived, send_sems.at[used],
                    recv_sems.at[used], peer(spot, "k", 1, sizes)[1],
                )
                mine = pltpu.make_async_copy(
                    ins[number].at[(core,) + cut_at], summed, local.at[len(states)]
                )
                mine.start()
                used += 1
                finished.append(copy)
                states.append(
                    {
                        "number": number, "axes": axes, "cut": cut, "order": order,
                        "next": begin + 2, "left": list(axes), "held": summed,
                        "arrived": arrived, "copies": [copy], "mine": mine,
                    }
                )
        depth = max(len(axes) for axes, _, _ in jobs)
        for stage in range(depth + 1):
            for state in states:
                order, left = state["order"], state["left"]
                if stage > len(order):
                    continue
                for copy in state["copies"]:
                    copy.wait_recv()
                cut = state["cut"]
                if stage == 0:
                    state["mine"].wait()
                    summed, arrived = state["held"], state["arrived"]

                    def pair(index, summed=summed, arrived=arrived):
                        summed[index] = summed[index] + arrived[index]

                    loop_blocks(tuple(sizes[a] for a in left), pair)
                else:
                    axis = order[stage - 1]
                    before, arrived = state["held"], state["arrived"]
                    spot_at = left.index(axis)
                    left.remove(axis)
                    rest = tuple(sizes[a] for a in left)
                    if left:
                        target = held[state["next"]]
                        state["next"] += 1
                    else:
                        target = None

                    def merge(
                        index, before=before, arrived=arrived, spot_at=spot_at, axis=axis,
                        target=target, cut=cut, number=state["number"], left=tuple(left),
                    ):
                        own = index[:spot_at] + (spot[axis],) + index[spot_at:] if left else (spot[axis],)
                        result = widen(before[own])
                        for step in range(sizes[axis] - 1):
                            result = result + widen(arrived[(step,) + (index if left else ())])
                        if target is None:
                            outs[number][cut[0] : cut[0] + cut[1], cut[2] : cut[2] + cut[3]] = result
                        else:
                            target[index] = result.astype(LOW)

                    loop_blocks(rest if left else (1,), merge)
                    state["held"] = target
                if stage < len(order):
                    axis = order[stage]
                    arrived = held[state["next"]]
                    state["next"] += 1
                    copies = []
                    for step in range(1, sizes[axis]):
                        moved, device = peer(spot, axis, step, sizes)
                        lead = tuple(
                            moved[axis] if a == axis else slice(None) for a in left
                        )
                        copies.append(
                            send(
                                state["held"].at[lead], arrived.at[step - 1],
                                send_sems.at[used], recv_sems.at[used], device,
                            )
                        )
                        used += 1
                    state["copies"] = copies
                    state["arrived"] = arrived
                    finished += copies
        for copy in finished:
            copy.wait_send()

    shapes = [jax.ShapeDtypeStruct(value.shape[-2:], jnp.float32) for value in values]
    count = len(values)
    pieces = len(layout)
    return call_remote(
        kernel, shapes, [pl.BlockSpec(memory_space=pl.ANY)] * count, whole(count),
        scratch
        + [
            pltpu.SemaphoreType.DMA((pieces,)),
            pltpu.SemaphoreType.DMA((total,)),
            pltpu.SemaphoreType.DMA((total,)),
        ],
        ident, *values,
    )


def dot_nt(left, right):
    return lax.dot_general(left, right, (((1,), (1,)), ((), ())), preferred_element_type=jnp.float32)


def dot_tn(left, right):
    return lax.dot_general(left, right, (((0,), (0,)), ((), ())), preferred_element_type=jnp.float32)


def pick(left, onehot):
    return dot(left, onehot).astype(LOW)


def pick_wide(values, onehot):
    high = values.astype(LOW)
    rest = (values - widen(high)).astype(LOW)
    return dot(high, onehot) + dot(rest, onehot)


def smooth(values):
    return 0.5 * values * (1.0 + lax.erf(values * 0.7071067811865476))


def smooth_slope(values):
    return 0.5 * (1.0 + lax.erf(values * 0.7071067811865476)) + values * 0.3989422804014327 * jnp.exp(
        -0.5 * values * values
    )


def norm(values):
    mean = jnp.mean(values, axis=-1, keepdims=True)
    centred = values - mean
    scale = lax.rsqrt(jnp.mean(centred * centred, axis=-1, keepdims=True) + EPS)
    return centred * scale, scale


def norm_back(incoming, normal, scale, gain):
    scaled = incoming * gain
    first = jnp.mean(scaled, axis=-1, keepdims=True)
    second = jnp.mean(scaled * normal, axis=-1, keepdims=True)
    return scale * (scaled - first - normal * second)


def norm_blocks(blocks):
    size = sum(block.shape[-1] for block in blocks)
    mean = sum(jnp.sum(block, axis=-1, keepdims=True) for block in blocks) / size
    centred = [block - mean for block in blocks]
    spread = sum(jnp.sum(block * block, axis=-1, keepdims=True) for block in centred) / size
    scale = lax.rsqrt(spread + EPS)
    return [block * scale for block in centred], scale


def column_sum(values):
    return jnp.sum(values, axis=0, keepdims=True)


def local_call(kernel, shapes, scratch, *values):
    count = len(values)
    return pl.pallas_call(
        kernel,
        out_shape=[jax.ShapeDtypeStruct(shape, kind) for shape, kind in shapes],
        in_specs=[
            pl.BlockSpec(memory_space=pltpu.SMEM if value.dtype == jnp.int32 else pltpu.VMEM)
            for value in values
        ],
        out_specs=whole(len(shapes)),
        scratch_shapes=scratch,
        compiler_params=pltpu.CompilerParams(vmem_limit_bytes=ROOM),
    )(*values)


def onehot(rows, columns):
    return (np.asarray(rows)[:, None] == np.asarray(columns)[None, :]).astype(LOW)


def natural_of(count, parts, squares):
    cells = np.arange(count).reshape(parts, squares, 2, -1)
    return cells.transpose(1, 0, 2, 3).reshape(count)


def prepare(early, second, packed, sizes, own, own_in, own_hid, thin, att, inner, blocks, count):
    parts, squares = sizes["y"], sizes["x"] * sizes["z"]
    devices = 2 * parts * squares
    width, wide_in, hidden = own * devices, own_in * devices, own_hid * devices
    quarter = width // parts
    groups = quarter // inner
    fold = second.shape[-1] - (att + -att % 128)
    rows = blocks * inner
    per = inner // own // 2
    nat_in = onehot(np.arange(wide_in), natural_of(wide_in, parts, squares))
    nat = onehot(np.arange(width), natural_of(width, parts, squares))
    lanes = np.arange(quarter)
    place_in = onehot(np.arange(256), np.where(lanes < thin, lanes, lanes - thin + 128))
    wide_att = second.shape[-1] - fold
    lanes = np.arange(2 * att)
    place_att = onehot(np.arange(2 * wide_att), np.where(lanes < att, lanes, lanes - att + wide_att))
    slab = np.arange(rows).reshape(2, per, own, blocks)
    order = [
        slab[(o // own) % 2, o // own // 2, o % own, b] for b in range(blocks) for o in range(inner)
    ]
    conv_order = onehot(order, np.arange(rows))
    lane = np.arange(packed.shape[1])
    ask = np.arange(width)
    take = (lane[:, None] < count * own) & (lane[:, None] % own == ask[None, :] % own)
    row_of = onehot(np.arange(16), np.where(lane < count * own, lane // own, -1))
    owner = onehot(np.arange(devices), ask // own)
    owner_in = onehot(np.arange(devices), np.arange(wide_in) // own_in)
    edge = count * own
    ask_in = np.arange(wide_in) % own_in
    take_in = (lane[:, None] >= edge) & (lane[:, None] < edge + 2 * own_in)
    take_in = take_in & ((lane[:, None] - edge) % own_in == ask_in[None, :])
    row_in = onehot(
        np.arange(16),
        np.where((lane >= edge) & (lane < edge + 2 * own_in), (lane - edge) // own_in, -1),
    )
    owner_hid = onehot(np.arange(devices), np.arange(hidden) // own_hid)
    take_hid = onehot(lane, edge + 2 * own_in + np.arange(hidden) % own_hid)

    def kernel(
        early_ref, second_ref, packed_ref, nat_in_ref, nat_ref, place_in_ref, place_att_ref, order_ref,
        take_ref, row_ref, owner_ref, take_in_ref, row_in_ref, owner_in_ref, take_hid_ref,
        owner_hid_ref, proj_out, attend_out, conv_out, turned_out, table_out, quarters_out, columns_out,
        edges_out, hid_out,
    ):
        for c in range(parts):
            both = [early_ref[k, c].reshape(wide_in, 128) for k in range(2)]
            slab_cols = pick(jnp.concatenate(both, axis=1), place_in_ref[...])
            proj_out[c] = pick(nat_in_ref[...], slab_cols)
        both = [second_ref[k, :, :, fold:].reshape(width, wide_att) for k in range(2)]
        slab_cols = pick(jnp.concatenate(both, axis=1), place_att_ref[...])
        attend_out[...] = pick(nat_ref[...], slab_cols)
        for g in range(groups):
            taken = second_ref[:, g * per : (g + 1) * per, :, :fold].reshape(rows, fold)
            ordered = dot(order_ref[...], taken)
            conv_out[g] = ordered.astype(LOW)
            turned_out[g] = ordered.T.astype(LOW)
        turned = packed_ref[...].T.astype(LOW)
        spread = (dot(turned, owner_ref[...]) * widen(take_ref[...])).astype(LOW)
        table = dot(row_ref[...], spread)
        table_out[...] = table
        for c in range(parts):
            quarters_out[c] = table[:, c * quarter : (c + 1) * quarter]
        columns_out[...] = jnp.concatenate(
            [table, jnp.zeros((112, width), jnp.float32)], axis=0
        ).T
        spread = (dot(turned, owner_in_ref[...]) * widen(take_in_ref[...])).astype(LOW)
        edges_out[...] = dot(row_in_ref[...], spread)
        hid_out[...] = column_sum(dot(turned, owner_hid_ref[...]) * widen(take_hid_ref[...]))

    f32 = jnp.float32
    return local_call(
        kernel,
        [
            ((parts, wide_in, quarter), LOW), ((width, 2 * att), LOW), ((groups, rows, fold), LOW),
            ((groups, fold, rows), LOW), ((16, width), f32), ((parts, 16, quarter), f32),
            ((width, 128), f32), ((16, wide_in), f32), ((1, hidden), f32),
        ],
        [],
        early, second, packed,
        *[
            jnp.asarray(v, LOW)
            for v in (nat_in, nat, place_in, place_att, conv_order, take, row_of, owner, take_in,
                      row_in, owner_in, take_hid, owner_hid)
        ],
    )


def fold_rows(padded, spread_ref, inner):
    for j in range(FOLD):
        moved = padded if j == 0 else pltpu.roll(padded, padded.shape[1] - j, 1)
        spread_ref[j * inner : (j + 1) * inner, :] = moved.astype(LOW)


def spread_blocks(padded, spread_ref, inner, blocks):
    for b in range(blocks):
        moved = padded if b == 0 else pltpu.roll(padded, FOLD * b, 1)
        spread_ref[b * inner : (b + 1) * inner, :] = moved.astype(LOW)


def front(gathered, lengths, here, proj, conv, quarters, columns, edges, micros, frames):
    parts, rows, narrow = gathered.shape
    quarter = proj.shape[2]
    groups, many, fold = conv.shape
    inner = fold // FOLD
    blocks = many // inner
    half = blocks * FOLD // 2
    span = frames + blocks * FOLD

    def kernel(
        in_ref, len_ref, here_ref, proj_ref, conv_ref, quarters_ref, columns_ref, edges_ref,
        summed_out, turned_out, before_out, spread_ref, plain_ref,
    ):
        spot = here_ref[0]
        for m in range(micros):
            at = slice(m * frames, (m + 1) * frames)
            normal, _ = norm_blocks([widen(in_ref[c, at]) for c in range(parts)])
            low = [
                (
                    block * edges_ref[0:1, c * narrow : (c + 1) * narrow]
                    + edges_ref[1:2, c * narrow : (c + 1) * narrow]
                ).astype(LOW)
                for c, block in enumerate(normal)
            ]
            result = dot(jnp.concatenate(low, axis=1), proj_ref[spot]) + quarters_ref[spot, 0:1]
            live = lax.broadcasted_iota(jnp.int32, (frames, 1), 0) < len_ref[m]
            turned = jnp.where(live, result, 0.0).T
            for g in range(groups):
                piece = turned[g * inner : (g + 1) * inner]
                plain_ref[m * groups + g] = piece
                turned_out[m * groups + g] = jnp.concatenate(
                    [
                        jnp.zeros((inner, half), jnp.float32),
                        piece.astype(LOW).astype(jnp.float32),
                        jnp.zeros((inner, half), jnp.float32),
                    ],
                    axis=1,
                )

        def one(index, carry):
            g = index % groups
            fold_rows(turned_out[index], spread_ref, inner)
            sums = dot(conv_ref[g], spread_ref[...])
            total = sums[:inner, :frames]
            for b in range(1, blocks):
                part = pltpu.roll(sums[b * inner : (b + 1) * inner], span - FOLD * b, 1)
                total = total + part[:, :frames]
            start = pl.multiple_of(spot * quarter + g * inner, 16)
            before = total + columns_ref[pl.ds(start, inner), 1:2]
            before_out[index] = before
            plain_ref[index] = plain_ref[index] + smooth(before)
            return carry

        lax.fori_loop(0, micros * groups, one, 0)
        for m in range(micros):
            both = [plain_ref[m * groups + g] for g in range(groups)]
            summed_out[m * frames : (m + 1) * frames] = jnp.concatenate(both, axis=0).T.astype(LOW)

    f32 = jnp.float32
    return local_call(
        kernel,
        [
            ((rows, quarter), LOW),
            ((micros * groups, inner, span), f32),
            ((micros * groups, inner, frames), f32),
        ],
        [pltpu.VMEM((fold, span), LOW), pltpu.VMEM((micros * groups, inner, frames), f32)],
        gathered, lengths, here, proj, conv, quarters, columns, edges,
    )


def attention(summed, lengths, here, attend, quarters, micros, frames):
    parts, rows, quarter = summed.shape
    heads = quarter // HEAD_DIM
    seg = frames // parts
    ratio = HEAD_DIM ** (-0.5)

    def kernel(in_ref, len_ref, here_ref, attend_ref, quarters_ref, low_out, joint_out, probs_out, context_out):
        spot = here_ref[0]

        def one(m, carry):
            begin = pl.multiple_of(m * frames, frames)
            at = pl.ds(begin, frames)
            normal, _ = norm_blocks([widen(in_ref[c, at]) for c in range(parts)])
            joint = jnp.zeros((frames, 3 * quarter), jnp.float32)
            for c in range(parts):
                low = (normal[c] * quarters_ref[c, 2:3] + quarters_ref[c, 3:4]).astype(LOW)
                low_out[c, at] = low
                joint = joint + dot(low, attend_ref[c * quarter : (c + 1) * quarter])
            query = joint[:, :quarter] + quarters_ref[spot, 4:5]
            keys = joint[:, quarter : 2 * quarter]
            value = joint[:, 2 * quarter :] + quarters_ref[spot, 5:6]
            joint_low = [v.astype(LOW) for v in (query, keys, value)]
            for i in range(3):
                joint_out[i, at] = joint_low[i]
            value_turned = value.T.astype(LOW)
            live = lax.broadcasted_iota(jnp.int32, (frames, 1), 0) < len_ref[m]
            results = []
            for h in range(heads):
                cols = slice(h * HEAD_DIM, (h + 1) * HEAD_DIM)
                scores = dot_nt(joint_low[1][:, cols], joint_low[0][:, cols]) * ratio
                scores = jnp.where(live, scores, NEGATIVE)
                expo = jnp.exp(scores - jnp.max(scores, axis=0, keepdims=True))
                probs = (expo / jnp.sum(expo, axis=0, keepdims=True)).astype(LOW)
                probs_out[m * heads + h] = probs
                results.append(dot(value_turned[cols], probs))
            context = jnp.concatenate(results, axis=0).T.astype(LOW)
            for d in range(parts):
                target = pl.ds(pl.multiple_of(m * seg, seg), seg)
                context_out[d, target] = context[d * seg : (d + 1) * seg]
            return carry

        lax.fori_loop(0, micros, one, 0)

    return local_call(
        kernel,
        [
            ((parts, rows, quarter), LOW), ((3, rows, quarter), LOW),
            ((micros * heads, frames, frames), LOW), ((parts, micros * seg, quarter), LOW),
        ],
        [],
        summed, lengths, here, attend, quarters,
    )


def own_frames(ref, spot, micros, frames, parts):
    seg = frames // parts
    blocks = []
    for c in range(parts):
        pieces = [
            widen(ref[c, pl.ds(pl.multiple_of(m * frames + spot * seg, seg), seg)])
            for m in range(micros)
        ]
        blocks.append(jnp.concatenate(pieces, axis=0))
    return blocks


def feed_forward(context, summed, here, upstream, weights, table, hid_bias, micros, frames, thin):
    parts, mine, quarter = context.shape
    squares, _, tall, lanes = weights.shape[1:]
    width = parts * quarter
    half, deep = width // 2, lanes - width // 2 - 128
    eight = 2 * parts
    nat = onehot(np.arange(width), natural_of(width, parts, squares))
    spots = np.arange(width)
    place = np.zeros((width // 128, 256, 128), np.float32)
    for tile in range(width // 128):
        first = tile * 128 // thin
        for lane in range(128):
            channel = tile * 128 + lane
            place[tile, (channel // thin - first) * 128 + channel % thin, lane] = 1.0
    cut = np.stack([onehot(spots, np.where(np.arange(128) < thin, j * thin + np.arange(128), -1)) for j in range(eight)])
    f32 = jnp.float32

    def kernel(
        ctx_ref, sum_ref, here_ref, up_ref, w_ref, table_ref, hid_ref, nat_ref, place_ref, cut_ref,
        out_ref, grad_out, gctx_out, slabs_out, sums_out, hid_out, pre_ref, act_ref, wout_ref,
    ):
        spot = here_ref[0]

        def block(c, k, begin, size):
            return w_ref[c, :, k, :, begin : begin + size].reshape(width, size)

        for tile in range(width // 128):
            first = tile * 128 // thin
            last = min(first + 1, eight - 1)
            both = [block(j // 2, j % 2, half + deep, 128) for j in (first, last)]
            wout_ref[:, tile * 128 : (tile + 1) * 128] = pick(jnp.concatenate(both, axis=1), place_ref[tile])
        normal, _ = norm_blocks(own_frames(sum_ref, spot, micros, frames, parts))
        encoded = jnp.concatenate(normal, axis=1) * table_ref[2:3] + table_ref[3:4]
        ctx_slab = sum(
            dot(ctx_ref[c], nat_ref[c * quarter : (c + 1) * quarter]) for c in range(parts)
        ).astype(LOW)
        attn_sum = encoded + dot(ctx_slab, wout_ref[...]) + table_ref[6:7]
        normal_att, scale_att = norm(attn_sum)
        attn_norm = normal_att * table_ref[7:8] + table_ref[8:9]
        attn_slab = pick(attn_norm.astype(LOW), nat_ref[...])
        outer = [jnp.zeros((mine, half), f32), jnp.zeros((mine, half), f32)]
        for c in range(parts):
            for k in range(2):
                begin = (2 * c + k) * deep
                pre = dot(attn_slab, block(c, k, half, deep)) + hid_ref[:, begin : begin + deep]
                pre_ref[:, begin : begin + deep] = pre
                act_ref[:, begin : begin + deep] = smooth(pre).astype(LOW)
            act = act_ref[:, 2 * c * deep : 2 * (c + 1) * deep]
            outer = [outer[k] + dot(act, block(c, k, 0, half)) for k in range(2)]
        ffn_sum = attn_norm + jnp.concatenate(outer, axis=1) + table_ref[9:10]
        normal_fin, scale_fin = norm(ffn_sum)
        out_ref[...] = (normal_fin * table_ref[10:11] + table_ref[11:12]).astype(LOW)
        up = widen(up_ref[...])
        grad_ffn = norm_back(up, normal_fin, scale_fin, table_ref[10:11])
        slope_outer = grad_ffn.astype(LOW)
        sums_out[...] = jnp.zeros_like(sums_out)
        sums_out[5:6] = column_sum(widen(slope_outer))
        sums_out[6:7] = column_sum(up * normal_fin)
        sums_out[7:8] = column_sum(up)
        grad_slab = jnp.zeros((mine, width), f32)
        attn_turned = widen(attn_slab).T.astype(LOW)
        for c in range(parts):
            columns = slice(2 * c * deep, 2 * (c + 1) * deep)
            grad_act = sum(
                dot_nt(slope_outer[:, k * half : (k + 1) * half], block(c, k, 0, half)) for k in range(2)
            )
            slope_inner = (grad_act * smooth_slope(pre_ref[:, columns])).astype(LOW)
            hid_out[:, columns] = column_sum(widen(slope_inner))
            act_turned = widen(act_ref[:, columns]).T.astype(LOW)
            for k in range(2):
                inner_k = slope_inner[:, k * deep : (k + 1) * deep]
                grad_slab = grad_slab + dot_nt(inner_k, block(c, k, half, deep))
                grad_ret = dot(act_turned, slope_outer[:, k * half : (k + 1) * half]).astype(LOW)
                slabs_out[k, c, :, :, :half] = grad_ret.reshape(squares, tall, half)
                grad_hid = dot(attn_turned, inner_k).astype(LOW)
                slabs_out[k, c, :, :, half : half + deep] = grad_hid.reshape(squares, tall, deep)
        high = grad_slab.astype(LOW)
        rest = (grad_slab - widen(high)).astype(LOW)
        grad_norm2 = grad_ffn + dot_nt(high, nat_ref[...]) + dot_nt(rest, nat_ref[...])
        sums_out[3:4] = column_sum(grad_norm2 * normal_att)
        sums_out[4:5] = column_sum(grad_norm2)
        grad_attn = norm_back(grad_norm2, normal_att, scale_att, table_ref[7:8])
        grad_out[...] = grad_attn
        slope_att = grad_attn.astype(LOW)
        sums_out[2:3] = column_sum(widen(slope_att))
        gctx_slab = dot_nt(slope_att, wout_ref[...]).astype(LOW)
        for c in range(parts):
            gctx_out[c] = dot_nt(gctx_slab, nat_ref[c * quarter : (c + 1) * quarter]).astype(LOW)
        ctx_turned = widen(ctx_slab).T.astype(LOW)
        for c in range(parts):
            for k in range(2):
                grad = dot(ctx_turned, pick(slope_att, cut_ref[2 * c + k])).astype(LOW)
                slabs_out[k, c, :, :, half + deep :] = grad.reshape(squares, tall, 128)

    hidden = eight * deep
    return local_call(
        kernel,
        [
            ((mine, width), LOW), ((mine, width), f32), ((parts, mine, quarter), LOW),
            ((2, parts, squares, tall, lanes), LOW), ((8, width), f32), ((1, hidden), f32),
        ],
        [
            pltpu.VMEM((mine, hidden), f32), pltpu.VMEM((mine, hidden), LOW),
            pltpu.VMEM((width, width), LOW),
        ],
        context, summed, here, upstream, weights, table, hid_bias,
        jnp.asarray(nat, LOW), jnp.asarray(place, LOW), jnp.asarray(cut, LOW),
    )


def attention_back(grad_context, low, joint, probs, attend, micros, frames, squares, tall):
    parts, mine, quarter = grad_context.shape
    width = parts * quarter
    rows = micros * frames
    heads = quarter // HEAD_DIM
    seg = frames // parts
    att = 3 * quarter // 2
    wide = att + -att % 128
    ratio = HEAD_DIM ** (-0.5)
    back = onehot(natural_of(width, parts, squares), np.arange(width))
    lanes = np.arange(2 * wide)
    source = np.where(lanes % wide < att, lanes // wide * att + lanes % wide, -1)
    place = onehot(np.arange(2 * att), source)

    def kernel(gctx_ref, low_ref, joint_ref, probs_ref, attend_ref, back_ref, place_ref, terms_out, grad_out, sums_out, slope_ref):
        sums_out[...] = jnp.zeros_like(sums_out)

        def one(m, carry):
            at = pl.ds(pl.multiple_of(m * frames, frames), frames)
            cells = pl.ds(pl.multiple_of(m * seg, seg), seg)
            grad = jnp.concatenate([gctx_ref[d, cells] for d in range(parts)], axis=0)
            query, keys, value = joint_ref[0, at], joint_ref[1, at], joint_ref[2, at]
            keys_turned = widen(keys).T.astype(LOW)
            queries, key_parts, values = [], [], []
            for h in range(heads):
                cols = slice(h * HEAD_DIM, (h + 1) * HEAD_DIM)
                probs_low = probs_ref[m * heads + h]
                grad_probs = dot_nt(value[:, cols], grad[:, cols])
                weighted = widen(probs_low) * grad_probs
                centre = jnp.sum(weighted, axis=0, keepdims=True)
                slope = (weighted - widen(probs_low) * centre).astype(LOW)
                values.append(dot(probs_low, grad[:, cols]))
                key_parts.append(dot(slope, query[:, cols]) * ratio)
                queries.append(dot(keys_turned[cols], slope) * ratio)
            slopes = [
                jnp.concatenate(queries, axis=0).T.astype(LOW),
                jnp.concatenate(key_parts, axis=1).astype(LOW),
                jnp.concatenate(values, axis=1).astype(LOW),
            ]
            sums_out[0:1] = sums_out[0:1] + column_sum(widen(slopes[0]))
            sums_out[1:2] = sums_out[1:2] + column_sum(widen(slopes[2]))
            slope = jnp.concatenate(slopes, axis=1)
            slope_ref[at] = slope
            terms = dot_nt(slope, attend_ref[...]).astype(LOW)
            for d in range(parts):
                terms_out[d, cells] = terms[d * seg : (d + 1) * seg]
            return carry

        lax.fori_loop(0, micros, one, 0)
        pieces = [dot_tn(low_ref[c], slope_ref[...]).astype(LOW) for c in range(parts)]
        grads = dot(back_ref[...], jnp.concatenate(pieces, axis=0)).astype(LOW)
        spread = dot(grads, place_ref[...]).astype(LOW)
        for k in range(2):
            grad_out[k] = spread[:, k * wide : (k + 1) * wide].reshape(squares, tall, wide)

    return local_call(
        kernel,
        [
            ((parts, mine, width), LOW), ((2, squares, tall, wide), LOW), ((8, quarter), jnp.float32),
        ],
        [pltpu.VMEM((rows, 3 * quarter), LOW)],
        grad_context, low, joint, probs, attend, jnp.asarray(back, LOW), jnp.asarray(place, LOW),
    )


def norm_step(terms, grad_attn, summed, here, table, sums, hid_sums, micros, frames, own, own_hid, sizes):
    parts, _, quarter = summed.shape
    mine, width = grad_attn.shape
    squares = sizes["x"] * sizes["z"]
    devices = 2 * parts * squares
    hidden = hid_sums.shape[1]
    f32 = jnp.float32
    lanes = 8 * own + own_hid
    lanes = lanes + -lanes % 128
    mask = onehot(np.arange(devices), np.arange(width) // own)
    mask_hid = onehot(np.arange(devices), np.arange(hidden) // own_hid)
    lane = np.arange(lanes)
    spread = np.stack(
        [onehot(np.arange(width) % own, np.where(lane // own == v, lane - v * own, -1)) for v in range(8)]
    )
    spread_hid = onehot(np.arange(hidden) % own_hid, np.where(lane >= 8 * own, lane - 8 * own, -1))
    order = np.arange(devices).reshape(parts, squares, 2).transpose(2, 0, 1).reshape(-1)
    rows = np.full((devices, 16), -1)
    rows[:, 0] = order
    row_of = onehot(rows.reshape(-1), np.arange(devices))

    def kernel(
        terms_ref, grad_ref, sum_ref, here_ref, table_ref, sums_ref, hid_ref, mask_ref, mask_hid_ref,
        spread_ref, spread_hid_ref, row_ref, out_ref, owned_out,
    ):
        spot = here_ref[0]
        normal, scale = norm_blocks(own_frames(sum_ref, spot, micros, frames, parts))
        normal = jnp.concatenate(normal, axis=1)
        grad = grad_ref[...] + terms_ref[...]
        result = norm_back(grad, normal, scale, table_ref[2:3]).astype(LOW)
        for c in range(parts):
            out_ref[c] = result[:, c * quarter : (c + 1) * quarter]
        vectors = [column_sum(grad * normal), column_sum(grad)]
        vectors += [sums_ref[v : v + 1] for v in range(2, 8)]
        owned = dot((widen(mask_hid_ref[...]) * hid_ref[...]).astype(LOW), spread_hid_ref[...])
        for v in range(8):
            owned = owned + dot((widen(mask_ref[...]) * vectors[v]).astype(LOW), spread_ref[v])
        owned_out[...] = dot(row_ref[...], owned.astype(LOW)).astype(LOW)

    out, owned = local_call(
        kernel,
        [((parts, mine, quarter), LOW), ((16 * devices, lanes), LOW)],
        [],
        terms, grad_attn, summed, here, table, sums, hid_sums,
        *[jnp.asarray(v, LOW) for v in (mask, mask_hid, spread, spread_hid, row_of)],
    )
    return out, owned.reshape(2, parts, sizes["x"], sizes["z"], 16, lanes)


def conv_back(grad_pos, before, padded, lengths, conv, turned, micros, frames, squares, tall, own):
    parts, mine, quarter = grad_pos.shape
    groups, many, fold = conv.shape
    inner = fold // FOLD
    blocks = many // inner
    half = blocks * FOLD // 2
    span = frames + blocks * FOLD
    seg = frames // parts
    rows = micros * frames
    per = inner // own // 2
    slab = np.arange(many).reshape(2, per, own, blocks)
    order = [
        slab[(o // own) % 2, o // own // 2, o % own, b] for b in range(blocks) for o in range(inner)
    ]
    back = onehot(np.arange(many), order)
    f32 = jnp.float32

    def kernel(
        grad_ref, before_ref, padded_ref, len_ref, turned_ref, back_ref, slope_out, grad_out, sums_out,
        spread_ref, moved_ref, grads_ref, turn_ref, weight_ref,
    ):
        sums_out[...] = jnp.zeros_like(sums_out)
        weight_ref[...] = jnp.zeros_like(weight_ref)
        for m in range(micros):
            cells = slice(m * seg, (m + 1) * seg)
            grad = jnp.concatenate([widen(grad_ref[d, cells]) for d in range(parts)], axis=0).T
            for g in range(groups):
                grads_ref[m * groups + g] = grad[g * inner : (g + 1) * inner]

        def one(index, carry):
            g, m = index % groups, index // groups
            grad = grads_ref[index]
            slope = (grad * smooth_slope(before_ref[index])).astype(LOW)
            slope = slope.astype(f32)
            turn_ref[index, :, 0:1] = jnp.sum(slope, axis=1, keepdims=True)
            wide = jnp.concatenate([slope, jnp.zeros((inner, span - frames), f32)], axis=1)
            spread_blocks(wide, moved_ref, inner, blocks)
            fold_rows(padded_ref[index], spread_ref, inner)
            weight_ref[g] = weight_ref[g] + dot_nt(moved_ref[...], spread_ref[...])
            back_sums = dot(turned_ref[g], moved_ref[...])
            total = grad
            for j in range(FOLD):
                part = pltpu.roll(
                    back_sums[j * inner : (j + 1) * inner], (span + j - half) % span, 1
                )
                total = total + part[:, :frames]
            live = lax.broadcasted_iota(jnp.int32, (1, frames), 1) < len_ref[m]
            total = jnp.where(live, total, 0.0).astype(LOW).astype(f32)
            turn_ref[index, :, 1:2] = jnp.sum(total, axis=1, keepdims=True)
            grads_ref[index] = total
            return carry

        lax.fori_loop(0, micros * groups, one, 0)
        for m in range(micros):
            both = [grads_ref[m * groups + g] for g in range(groups)]
            slope_out[m * frames : (m + 1) * frames] = jnp.concatenate(both, axis=0).T.astype(LOW)
        sums = jnp.concatenate(
            [sum(turn_ref[m * groups + g] for m in range(micros)) for g in range(groups)], axis=0
        ).T
        sums_out[...] = sums[:8]
        for g in range(groups):
            grad = dot(back_ref[...], weight_ref[g].astype(LOW)).astype(LOW)
            grad_out[:, g * per : (g + 1) * per] = grad.reshape(2, per, tall, fold)

    return local_call(
        kernel,
        [((rows, quarter), LOW), ((2, squares, tall, fold), LOW), ((8, quarter), f32)],
        [
            pltpu.VMEM((fold, span), LOW), pltpu.VMEM((many, span), LOW),
            pltpu.VMEM((micros * groups, inner, frames), f32),
            pltpu.VMEM((micros * groups, inner, 128), f32),
            pltpu.VMEM((groups, many, fold), f32),
        ],
        grad_pos, before, padded, lengths, turned, jnp.asarray(back, LOW),
    )


def finish(slopes, gathered, here, proj, edges, conv_sums, attend_sums, sizes, own, own_in):
    parts, rows, quarter = slopes.shape
    narrow = gathered.shape[2]
    squares = sizes["x"] * sizes["z"]
    ranks = 2 * squares
    width = parts * quarter
    f32 = jnp.float32
    lane = np.arange(width)
    mask = onehot(np.arange(ranks), np.arange(quarter) // own)
    spread = np.stack(
        [onehot(np.arange(quarter) % own, np.where(lane // own == v, lane - v * own, -1)) for v in range(4)]
    )
    mask_in = onehot(np.arange(ranks), np.arange(narrow) // own_in)
    begin = 4 * own
    spread_in = np.stack(
        [
            onehot(
                np.arange(narrow) % own_in,
                np.where((lane - begin) // own_in == v, lane - begin - v * own_in, -1),
            )
            for v in range(2)
        ]
    )
    high = own_in + 1 + -(own_in + 1) % 16
    order = np.arange(ranks).reshape(squares, 2).T.reshape(-1)
    proj_rows = np.full((ranks, high), -1)
    proj_rows[:, :own_in] = order[:, None] * own_in + np.arange(own_in)[None, :]
    row_proj = onehot(proj_rows.reshape(-1), np.arange(narrow))
    vector_rows = np.full((ranks, high), -1)
    vector_rows[:, own_in] = order
    row_vector = onehot(vector_rows.reshape(-1), np.arange(ranks))

    def kernel(
        slope_ref, in_ref, here_ref, proj_ref, edges_ref, conv_ref, att_ref, mask_ref, spread_ref,
        mask_in_ref, spread_in_ref, row_proj_ref, row_vector_ref, out_ref, owned_out, grad_ref,
    ):
        spot = here_ref[0]
        normal, scale = norm_blocks([widen(in_ref[c]) for c in range(parts)])
        first = jnp.zeros((rows, 1), f32)
        second = jnp.zeros((rows, 1), f32)
        for c in range(parts):
            at = slice(c * narrow, (c + 1) * narrow)
            grad = sum(dot_nt(slope_ref[b], proj_ref[b, at]) for b in range(parts))
            grad_ref[c] = grad
            scaled = grad * edges_ref[0:1, at]
            first = first + jnp.sum(scaled, axis=1, keepdims=True)
            second = second + jnp.sum(scaled * normal[c], axis=1, keepdims=True)
        size = parts * narrow
        mean = sum(jnp.sum(widen(in_ref[c]), axis=1, keepdims=True) for c in range(parts)) / size
        mine = (widen(in_ref[spot]) - mean) * scale
        at = pl.ds(pl.multiple_of(spot * narrow, narrow), narrow)
        gain, shift = edges_ref[0:1, at], edges_ref[1:2, at]
        grad = grad_ref[spot]
        out_ref[...] = scale * (grad * gain - first / size - mine * (second / size))
        low = (mine * gain + shift).astype(LOW)
        proj_grad = jnp.concatenate([dot_tn(low, slope_ref[b]) for b in range(parts)], axis=1)
        vectors = [conv_ref[1:2], conv_ref[0:1], att_ref[0:1], att_ref[1:2]]
        owned = jnp.zeros((ranks, width), f32)
        for v in range(4):
            owned = owned + dot((widen(mask_ref[...]) * vectors[v]).astype(LOW), spread_ref[v])
        edge_sums = [column_sum(grad * mine), column_sum(grad)]
        for v in range(2):
            owned = owned + dot((widen(mask_in_ref[...]) * edge_sums[v]).astype(LOW), spread_in_ref[v])
        result = dot(row_proj_ref[...], proj_grad.astype(LOW)) + dot(row_vector_ref[...], owned.astype(LOW))
        owned_out[...] = result.astype(LOW)

    out, owned = local_call(
        kernel,
        [((rows, narrow), f32), ((ranks * high, width), LOW)],
        [pltpu.VMEM((parts, rows, narrow), f32)],
        slopes, gathered, here, proj, edges, conv_sums, attend_sums,
        *[jnp.asarray(v, LOW) for v in (mask, spread, mask_in, spread_in, row_proj, row_vector)],
    )
    return out, owned.reshape(2, sizes["x"], sizes["z"], high, width)


def per_device(
    features, lengths, input_gain, input_bias, proj_weight, proj_bias, conv_weight, conv_bias,
    encoder_gain, encoder_bias, attend_weight, query_bias, value_bias, output_weight, output_bias,
    attend_gain, attend_bias, hidden_weight, hidden_bias, return_weight, return_bias, final_gain,
    final_bias, out_grad,
):
    parts = lax.axis_size("ch")
    ranks = lax.axis_size("rows")
    side = math.isqrt(ranks // 2)
    sizes = {"y": parts, "x": side, "z": side, "k": 2}
    here = lax.axis_index("ch").astype(jnp.int32).reshape(1)
    micros, _, frames, narrow = features.shape
    own = proj_bias.shape[0]
    width = proj_weight.shape[1]
    quarter = width // parts
    inner, taps = conv_weight.shape[1:]
    blocks = taps // FOLD
    hidden = hidden_weight.shape[1]
    own_in = input_gain.shape[0]
    own_hid = hidden_bias.shape[0]
    seg = out_grad.shape[2]
    eight = 2 * parts
    squares = side * side
    tall = eight * own
    deep, thin, att = hidden // eight, width // eight, 3 * quarter // 2
    half = width // 2
    rows = micros * frames
    mine = micros * seg
    fold = FOLD * inner
    spans = lengths.reshape(micros)

    cut = jnp.concatenate(
        [
            hidden_weight.reshape(own, eight, deep),
            output_weight.reshape(own, eight, thin),
            attend_weight.reshape(own, 3, parts, quarter).transpose(0, 2, 1, 3).reshape(own, eight, att),
        ],
        axis=2,
    ).transpose(1, 0, 2)
    cut = jnp.pad(cut, ((0, 0), (0, -own % 16), (0, 0)))
    first = proj_weight.reshape(own_in, eight, thin).transpose(1, 0, 2).reshape(eight, 1, -1)
    lanes_cut = cut.shape[2]
    first = jnp.pad(first, ((0, 0), (0, 0), (0, -first.shape[2] % lanes_cut)))
    first = first.reshape(eight, -1, lanes_cut)
    first = jnp.pad(first, ((0, 0), (0, -first.shape[1] % 16), (0, 0)))
    cut = jnp.concatenate([cut, first], axis=1)
    tall_cut = own + -own % 16
    pair = return_weight.reshape(-1, 2, half).transpose(1, 0, 2)
    own_ret = pair.shape[1]
    pair = jnp.pad(pair, ((0, 0), (0, -own_ret % 16), (0, 0)))
    cut, pair = over_eight(cut, pair, 0, parts)
    first = cut[:, tall_cut:].reshape(eight, -1)[:, : own_in * thin].reshape(eight * own_in, thin)
    cut = cut[:, :own].reshape(tall, lanes_cut)
    pair = pair[:, :own_ret].reshape(2 * own_ret, half)
    slab = jnp.concatenate(
        [pair, cut[:, :deep], jnp.pad(cut[:, deep : deep + thin], ((0, 0), (0, -thin % 128)))], axis=1
    )
    everything = lax.all_gather(slab, ALL, axis=0, tiled=False)
    everything = everything.reshape(parts, squares, 2, tall, -1)

    small = jnp.stack(
        [proj_bias, conv_bias, encoder_gain, encoder_bias, query_bias, value_bias, output_bias,
         attend_gain, attend_bias, return_bias, final_gain, final_bias]
    )
    packed = jnp.concatenate([small.reshape(-1), input_gain, input_bias, hidden_bias])
    spare = 128 - thin
    vector_rows = -(-packed.shape[0] // spare)
    vector_rows = vector_rows + -vector_rows % 4
    packed = jnp.pad(packed, (0, vector_rows * spare - packed.shape[0])).reshape(vector_rows, spare)
    packed = jnp.pad(packed, ((0, first.shape[0] - vector_rows), (0, 0)))
    early = jnp.concatenate([first, packed], axis=1)
    folded = conv_weight.reshape(own, inner, blocks, FOLD).transpose(0, 2, 3, 1)
    folded = folded.reshape(own * blocks, fold)
    own_att = cut[:, deep + thin :]
    second = jnp.concatenate([folded, jnp.pad(own_att, ((0, 0), (0, -att % 128)))], axis=1)
    lanes_b = second.shape[1]
    split_b = lanes_b // 256 * 128
    early, second = gather_jobs(
        [early, second],
        [
            (("y", "x", "z"), [(0, early.shape[0], 0, 128)], [("z", "x", "y")]),
            (
                ("x", "z"),
                [(0, tall, 0, split_b), (0, tall, split_b, lanes_b - split_b)],
                [("z", "x"), ("x", "z")],
            ),
        ],
        1, sizes,
    )
    early = early.reshape(2, parts, squares, -1, 128)
    second = second.reshape(2, squares, tall, lanes_b)
    vectors = early[:, :, :, :vector_rows, thin:].transpose(1, 2, 0, 3, 4)
    vectors = widen(vectors.reshape(parts * ranks, -1))
    proj, attend, conv, conv_turned, table, quarters, columns, edges, hid_bias = prepare(
        early, second, vectors, sizes, own, own_in, own_hid, thin, att, inner, blocks, small.shape[0]
    )

    gathered = over_ch(features.reshape(rows, narrow), 2, "gather", parts)
    summed, padded, before = front(
        gathered, spans, here, proj, conv, quarters, columns, edges, micros, frames
    )
    summed = over_ch(summed, 3, "gather", parts)
    low, joint, probs, context = attention(summed, spans, here, attend, quarters, micros, frames)
    context = over_ch(context, 4, "swap", parts)
    output, grad_attn, grad_context, ffn, sums, hid_sums = feed_forward(
        context, summed, here, out_grad.reshape(mine, width), everything, table, hid_bias, micros,
        frames, thin,
    )
    grad_context = over_ch(grad_context, 5, "swap", parts)
    terms, attend_grad, attend_sums = attention_back(
        grad_context, low, joint, probs, attend, micros, frames, squares, tall
    )
    terms = over_ch(terms, 6, "add", parts)
    grad_pos, full = norm_step(
        terms, grad_attn, summed, here, table, sums, hid_sums, micros, frames, own, own_hid, sizes
    )
    grad_pos = over_ch(grad_pos, 7, "swap", parts)
    slopes, conv_grad, conv_sums = conv_back(
        grad_pos, before, padded, spans, conv, conv_turned, micros, frames, squares, tall, own
    )
    slopes = over_ch(slopes, 8, "gather", parts)
    features_grad, local = finish(
        slopes, gathered, here, proj, edges, conv_sums, attend_sums, sizes, own, own_in
    )

    ffn = ffn.reshape(2, parts, side, side, tall, -1)
    conv_grad = conv_grad.reshape(2, side, side, tall, fold)
    attend_grad = attend_grad.reshape(2, side, side, tall, -1)
    third = tall // 3
    lanes_a = ffn.shape[-1]
    ffn, full, conv_share, attend_share, local = reduce_jobs(
        [ffn, full, conv_grad, attend_grad, local],
        [
            (
                ("y", "x", "z"),
                [(i * third, third, 0, lanes_a) for i in range(3)],
                [("x", "z", "y"), ("z", "y", "x"), ("y", "x", "z")],
            ),
            (("y", "x", "z"), [(0, 16, 0, full.shape[-1])], [("y", "x", "z")]),
            (
                ("x", "z"),
                [(0, tall, 0, fold // 2), (0, tall, fold // 2, fold // 2)],
                [("z", "x"), ("x", "z")],
            ),
            (("x", "z"), [(0, tall, 0, attend_grad.shape[-1])], [("x", "z")]),
            (("x", "z"), [(0, local.shape[-2], 0, width)], [("z", "x")]),
        ],
        9, sizes,
    )

    cut = jnp.concatenate(
        [ffn[:, half : half + deep], ffn[:, half + deep : half + deep + thin], attend_share[:, :att]],
        axis=1,
    ).reshape(eight, own, -1)
    cut = jnp.pad(cut, ((0, 0), (0, -own % 8), (0, 0)))
    cut, pair = over_eight(cut, ffn[:, :half].reshape(2, own_ret, half), 10, parts)
    cut = cut[:, :own].transpose(1, 0, 2)
    hidden_share = cut[:, :, :deep].reshape(hidden_weight.shape)
    output_share = cut[:, :, deep : deep + thin].reshape(output_weight.shape)
    attend_share = cut[:, :, deep + thin :].reshape(own, parts, 3, quarter).transpose(0, 2, 1, 3)
    return_share = pair.transpose(1, 0, 2).reshape(return_weight.shape)
    conv_share = conv_share.reshape(own, blocks, FOLD, inner).transpose(0, 3, 1, 2)
    tail = local[own_in]
    full = full[0]
    local_parts = [tail[i * own : (i + 1) * own] for i in range(4)]
    full_parts = [full[i * own : (i + 1) * own] for i in range(8)]
    return (
        output.reshape(out_grad.shape),
        features_grad.reshape(features.shape),
        tail[4 * own : 4 * own + own_in],
        tail[4 * own + own_in : 4 * own + 2 * own_in],
        local[:own_in],
        local_parts[0],
        conv_share.reshape(conv_weight.shape),
        local_parts[1],
        full_parts[0],
        full_parts[1],
        attend_share.reshape(attend_weight.shape),
        local_parts[2],
        local_parts[3],
        output_share,
        full_parts[2],
        full_parts[3],
        full_parts[4],
        hidden_share,
        full[8 * own : 8 * own + own_hid],
        return_share,
        full_parts[5],
        full_parts[6],
        full_parts[7],
    )


def solution(mesh):
    vector, matrix, cube = P(ALL), P(ALL, None), P(ALL, None, None)
    weights = (
        vector, vector, matrix, vector, cube, vector, vector, vector, matrix, vector, vector,
        matrix, vector, vector, vector, matrix, vector, matrix, vector, vector, vector,
    )
    by_channel = P(None, "rows", None, "ch")
    by_frame = P(None, "rows", "ch", None)
    return jax.shard_map(
        per_device,
        mesh=mesh,
        in_specs=(by_channel, P(None, "rows")) + weights + (by_frame,),
        out_specs=(by_frame, by_channel) + weights,
        check_vma=False,
    )
```

```python
import functools
import math

import jax
import jax.numpy as jnp
import numpy as np
from jax import lax
from jax.experimental import pallas as pl
from jax.experimental.pallas import tpu as pltpu
from jax.sharding import PartitionSpec as P

HEAD_DIM = 64
EPS = 1e-05
NEGATIVE = -1000000000.0
FOLD = 16
ALL = ("ch", "rows")
LOW = jnp.bfloat16
MESH = pl.DeviceIdType.MESH
ROOM = 62 * 1024 * 1024


def widen(values):
    return values.astype(jnp.float32)


def dot(left, right):
    return jnp.dot(left, right, preferred_element_type=jnp.float32)


def contract(spec, left, right):
    return jnp.einsum(spec, left, right, preferred_element_type=jnp.float32)


def place(side):
    rank = lax.axis_index("rows")
    return {
        "y": lax.axis_index("ch"),
        "x": rank // (2 * side),
        "z": (rank // 2) % side,
        "k": rank % 2,
    }


def peer(spot, axis, step, sizes):
    moved = dict(spot)
    moved[axis] = (spot[axis] + step) % sizes[axis]
    return moved, (moved["y"], (moved["x"] * sizes["z"] + moved["z"]) * 2 + moved["k"])


def greet(targets):
    barrier = pltpu.get_barrier_semaphore()
    for target in targets:
        pl.semaphore_signal(barrier, inc=1, device_id=target, device_id_type=MESH)
    pl.semaphore_wait(barrier, len(targets))


def send(source, target, send_sem, recv_sem, device):
    copy = pltpu.make_async_remote_copy(
        src_ref=source, dst_ref=target, send_sem=send_sem, recv_sem=recv_sem,
        device_id=device, device_id_type=MESH,
    )
    copy.start()
    return copy


def whole(count):
    return [pl.BlockSpec(memory_space=pltpu.VMEM)] * count


def call_remote(kernel, shapes, ins, outs, scratch, ident, *values):
    return pl.pallas_call(
        kernel,
        out_shape=shapes,
        in_specs=ins,
        out_specs=outs,
        scratch_shapes=scratch,
        compiler_params=pltpu.CompilerParams(
            collective_id=ident, has_side_effects=True, vmem_limit_bytes=ROOM
        ),
    )(*values)


def over_ch(values, ident, mode, parts):
    block = values.shape if mode == "gather" else values.shape[1:]
    ring = parts == 4 and mode != "swap"
    middle = block[0] // 2
    near, far = pl.ds(0, middle), pl.ds(middle, middle)

    def direct(in_ref, out_ref, held, send_sems, recv_sems):
        here = lax.axis_index("ch")
        others = [(here + step) % parts for step in range(1, parts)]
        rank = lax.axis_index("rows")
        greet([(other, rank) for other in others])
        copies = []
        for step, other in enumerate(others):
            copies.append(
                send(in_ref.at[other], out_ref.at[here], send_sems.at[step], recv_sems.at[step],
                     (other, rank))
            )
        out_ref[here] = in_ref[here]
        for copy in copies:
            copy.wait()

    def gather(in_ref, out_ref, held, send_sems, recv_sems):
        here, rank = lax.axis_index("ch"), lax.axis_index("rows")
        right, left = (here + 1) % 4, (here + 3) % 4
        greet([(right, rank), (left, rank)])

        def move(source, target, index, other):
            return send(source, target, send_sems.at[index], recv_sems.at[index], (other, rank))

        copies = [
            move(in_ref.at[near], out_ref.at[here, near], 0, right),
            move(in_ref.at[far], out_ref.at[here, far], 1, left),
            move(in_ref.at[far], out_ref.at[here, far], 2, right),
            move(in_ref.at[near], out_ref.at[here, near], 3, left),
        ]
        out_ref[here] = in_ref[...]
        copies[0].wait_recv()
        copies.append(move(out_ref.at[left, near], out_ref.at[left, near], 4, right))
        copies[1].wait_recv()
        copies.append(move(out_ref.at[right, far], out_ref.at[right, far], 5, left))
        for copy in copies[2:]:
            copy.wait_recv()
        for copy in copies:
            copy.wait_send()

    def add(in_ref, out_ref, held, send_sems, recv_sems):
        here, rank = lax.axis_index("ch"), lax.axis_index("rows")
        right, left, across = (here + 1) % 4, (here + 3) % 4, (here + 2) % 4
        greet([(right, rank), (left, rank)])

        def move(source, index, other):
            return send(
                source, held.at[index], send_sems.at[index], recv_sems.at[index], (other, rank)
            )

        copies = [
            move(in_ref.at[across, near], 0, right),
            move(in_ref.at[across, far], 1, left),
            move(in_ref.at[right, far], 2, right),
            move(in_ref.at[left, near], 3, left),
        ]
        copies[0].wait_recv()
        held[6] = in_ref[right, near] + held[0]
        copies.append(move(held.at[6], 4, right))
        copies[1].wait_recv()
        held[7] = in_ref[left, far] + held[1]
        copies.append(move(held.at[7], 5, left))
        for copy in copies[2:]:
            copy.wait_recv()
        out_ref[near] = widen(in_ref[here, near]) + widen(held[4]) + widen(held[3])
        out_ref[far] = widen(in_ref[here, far]) + widen(held[2]) + widen(held[5])
        for copy in copies:
            copy.wait_send()

    shape = jax.ShapeDtypeStruct(
        block if mode == "add" else (parts,) + block,
        jnp.float32 if mode == "add" else values.dtype,
    )
    slots = (8, middle) + block[1:] if mode == "add" else (1, 16, 128)
    return call_remote(
        {"gather": gather, "add": add, "swap": direct}[mode], shape, whole(1), whole(1)[0],
        [
            pltpu.VMEM(slots, values.dtype),
            pltpu.SemaphoreType.DMA((6,)),
            pltpu.SemaphoreType.DMA((6,)),
        ],
        ident, values,
    )


def over_eight(blocks, pair, ident, parts):
    count = 2 * parts

    def kernel(block_ref, pair_ref, block_out, pair_out, send_sems, recv_sems):
        here, rank = lax.axis_index("ch"), lax.axis_index("rows")
        core = rank % 2
        mine = here * 2 + core
        base = rank - core
        steps = range(1, count)
        others = [(mine + step) % count for step in steps]
        devices = [(other // 2, base + other % 2) for other in others]
        greet(devices)
        copies = []
        for index, (other, device) in enumerate(zip(others, devices)):
            copies.append(
                send(block_ref.at[other], block_out.at[mine], send_sems.at[index],
                     recv_sems.at[index], device)
            )
        copies.append(
            send(pair_ref.at[1 - core], pair_out.at[core], send_sems.at[count - 1],
                 recv_sems.at[count - 1], (here, base + 1 - core))
        )
        block_out[mine] = block_ref[mine]
        pair_out[core] = pair_ref[core]
        for copy in copies:
            copy.wait()

    shapes = [jax.ShapeDtypeStruct(v.shape, v.dtype) for v in (blocks, pair)]
    return call_remote(
        kernel, shapes, whole(2), whole(2),
        [pltpu.SemaphoreType.DMA((count,)), pltpu.SemaphoreType.DMA((count,))],
        ident, blocks, pair,
    )


def job_copies(jobs, sizes):
    return sum(
        len(cuts) + sum(sizes[a] - 1 for order in orders for a in order)
        for _, cuts, orders in jobs
    )


def neighbours(jobs, spot, sizes):
    found = [peer(spot, "k", 1, sizes)[1]]
    for axis in ("y", "x", "z"):
        if any(axis in axes for axes, _, _ in jobs):
            found += [peer(spot, axis, step, sizes)[1] for step in range(1, sizes[axis])]
    return found


def window(axes, fixed, cut):
    lead = tuple(fixed.get(axis, slice(None)) for axis in axes)
    return lead + (pl.ds(cut[0], cut[1]), pl.ds(cut[2], cut[3]))


def gather_jobs(values, jobs, ident, sizes):
    total = job_copies(jobs, sizes)

    def kernel(*refs):
        count = len(jobs)
        ins, outs = refs[:count], refs[count : 2 * count]
        local, send_sems, recv_sems = refs[2 * count :]
        spot = place(sizes["z"])
        core = spot["k"]
        for number, (axes, _, _) in enumerate(jobs):
            pltpu.make_async_copy(
                ins[number],
                outs[number].at[(core,) + tuple(spot[a] for a in axes)],
                local.at[number],
            ).start()
        greet(neighbours(jobs, spot, sizes))
        for number, (axes, _, _) in enumerate(jobs):
            pltpu.make_async_copy(
                ins[number],
                outs[number].at[(core,) + tuple(spot[a] for a in axes)],
                local.at[number],
            ).wait()
        used = 0
        pending = []
        finished = []
        depth = max(len(axes) for axes, _, _ in jobs)
        waiting = {}
        for stage in range(depth + 1):
            for number, (axes, cuts, orders) in enumerate(jobs):
                for piece, (cut, order) in enumerate(zip(cuts, orders)):
                    if stage > len(order):
                        continue
                    for copy in waiting.pop((number, piece), []):
                        copy.wait_recv()
                    copies = []
                    if stage < len(order):
                        axis = order[stage]
                        fixed = {a: spot[a] for a in order[stage:]}
                        steps = range(1, sizes[axis])
                    else:
                        axis, fixed, steps = "k", {}, (1,)
                    view = outs[number].at[(core,) + window(axes, fixed, cut)]
                    for step in steps:
                        device = peer(spot, axis, step, sizes)[1]
                        copies.append(
                            send(view, view, send_sems.at[used], recv_sems.at[used], device)
                        )
                        used += 1
                    waiting[(number, piece)] = copies
                    finished += copies
        for copies in waiting.values():
            for copy in copies:
                copy.wait_recv()
        for copy in finished:
            copy.wait_send()

    shapes = [
        jax.ShapeDtypeStruct((2,) + tuple(sizes[a] for a in axes) + value.shape, value.dtype)
        for value, (axes, _, _) in zip(values, jobs)
    ]
    count = len(values)
    return call_remote(
        kernel, shapes, whole(count), whole(count),
        [
            pltpu.SemaphoreType.DMA((count,)),
            pltpu.SemaphoreType.DMA((total,)),
            pltpu.SemaphoreType.DMA((total,)),
        ],
        ident, *values,
    )


def loop_blocks(dims, body):
    count = math.prod(dims)
    if count == 1:
        body((0,) * len(dims))
        return

    def step(flat, carry):
        index = []
        rest = flat
        for size in reversed(dims):
            index.append(rest % size)
            rest = rest // size
        body(tuple(reversed(index)))
        return carry

    lax.fori_loop(0, count, step, 0)


def dot_nt(left, right):
    return lax.dot_general(left, right, (((1,), (1,)), ((), ())), preferred_element_type=jnp.float32)


def dot_tn(left, right):
    return lax.dot_general(left, right, (((0,), (0,)), ((), ())), preferred_element_type=jnp.float32)


def pick(left, onehot):
    return dot(left, onehot).astype(LOW)


def pick_wide(values, onehot):
    high = values.astype(LOW)
    rest = (values - widen(high)).astype(LOW)
    return dot(high, onehot) + dot(rest, onehot)


def smooth(values):
    return 0.5 * values * (1.0 + lax.erf(values * 0.7071067811865476))


def smooth_slope(values):
    return 0.5 * (1.0 + lax.erf(values * 0.7071067811865476)) + values * 0.3989422804014327 * jnp.exp(
        -0.5 * values * values
    )


def norm(values):
    mean = jnp.mean(values, axis=-1, keepdims=True)
    centred = values - mean
    scale = lax.rsqrt(jnp.mean(centred * centred, axis=-1, keepdims=True) + EPS)
    return centred * scale, scale


def norm_back(incoming, normal, scale, gain):
    scaled = incoming * gain
    first = jnp.mean(scaled, axis=-1, keepdims=True)
    second = jnp.mean(scaled * normal, axis=-1, keepdims=True)
    return scale * (scaled - first - normal * second)


def norm_blocks(blocks):
    size = sum(block.shape[-1] for block in blocks)
    mean = sum(jnp.sum(block, axis=-1, keepdims=True) for block in blocks) / size
    centred = [block - mean for block in blocks]
    spread = sum(jnp.sum(block * block, axis=-1, keepdims=True) for block in centred) / size
    scale = lax.rsqrt(spread + EPS)
    return [block * scale for block in centred], scale


def column_sum(values):
    return jnp.sum(values, axis=0, keepdims=True)


def local_call(kernel, shapes, scratch, *values):
    count = len(values)
    return pl.pallas_call(
        kernel,
        out_shape=[jax.ShapeDtypeStruct(shape, kind) for shape, kind in shapes],
        in_specs=[
            pl.BlockSpec(memory_space=pltpu.SMEM if value.dtype == jnp.int32 else pltpu.VMEM)
            for value in values
        ],
        out_specs=whole(len(shapes)),
        scratch_shapes=scratch,
        compiler_params=pltpu.CompilerParams(vmem_limit_bytes=ROOM),
    )(*values)


def onehot(rows, columns):
    return (np.asarray(rows)[:, None] == np.asarray(columns)[None, :]).astype(LOW)


def natural_of(count, parts, squares):
    cells = np.arange(count).reshape(parts, squares, 2, -1)
    return cells.transpose(1, 0, 2, 3).reshape(count)


def prepare(early, second, packed, sizes, own, own_in, own_hid, thin, att, inner, blocks, count):
    parts, squares = sizes["y"], sizes["x"] * sizes["z"]
    devices = 2 * parts * squares
    width, wide_in, hidden = own * devices, own_in * devices, own_hid * devices
    quarter = width // parts
    groups = quarter // inner
    fold = second.shape[-1] - (att + -att % 128)
    rows = blocks * inner
    per = inner // own // 2
    nat_in = onehot(np.arange(wide_in), natural_of(wide_in, parts, squares))
    nat = onehot(np.arange(width), natural_of(width, parts, squares))
    lanes = np.arange(quarter)
    place_in = onehot(np.arange(256), np.where(lanes < thin, lanes, lanes - thin + 128))
    wide_att = second.shape[-1] - fold
    lanes = np.arange(2 * att)
    place_att = onehot(np.arange(2 * wide_att), np.where(lanes < att, lanes, lanes - att + wide_att))
    slab = np.arange(rows).reshape(2, per, own, blocks)
    order = [
        slab[(o // own) % 2, o // own // 2, o % own, b] for b in range(blocks) for o in range(inner)
    ]
    conv_order = onehot(order, np.arange(rows))
    lane = np.arange(packed.shape[1])
    ask = np.arange(width)
    take = (lane[:, None] < count * own) & (lane[:, None] % own == ask[None, :] % own)
    row_of = onehot(np.arange(16), np.where(lane < count * own, lane // own, -1))
    owner = onehot(np.arange(devices), ask // own)
    owner_in = onehot(np.arange(devices), np.arange(wide_in) // own_in)
    edge = count * own
    ask_in = np.arange(wide_in) % own_in
    take_in = (lane[:, None] >= edge) & (lane[:, None] < edge + 2 * own_in)
    take_in = take_in & ((lane[:, None] - edge) % own_in == ask_in[None, :])
    row_in = onehot(
        np.arange(16),
        np.where((lane >= edge) & (lane < edge + 2 * own_in), (lane - edge) // own_in, -1),
    )
    owner_hid = onehot(np.arange(devices), np.arange(hidden) // own_hid)
    take_hid = onehot(lane, edge + 2 * own_in + np.arange(hidden) % own_hid)

    def kernel(
        early_ref, second_ref, packed_ref, nat_in_ref, nat_ref, place_in_ref, place_att_ref, order_ref,
        take_ref, row_ref, owner_ref, take_in_ref, row_in_ref, owner_in_ref, take_hid_ref,
        owner_hid_ref, proj_out, attend_out, conv_out, turned_out, table_out, quarters_out, columns_out,
        edges_out, hid_out,
    ):
        for c in range(parts):
            both = [early_ref[k, c].reshape(wide_in, 128) for k in range(2)]
            slab_cols = pick(jnp.concatenate(both, axis=1), place_in_ref[...])
            proj_out[c] = pick(nat_in_ref[...], slab_cols)
        both = [second_ref[k, :, :, fold:].reshape(width, wide_att) for k in range(2)]
        slab_cols = pick(jnp.concatenate(both, axis=1), place_att_ref[...])
        attend_out[...] = pick(nat_ref[...], slab_cols)
        for g in range(groups):
            taken = second_ref[:, g * per : (g + 1) * per, :, :fold].reshape(rows, fold)
            ordered = dot(order_ref[...], taken)
            conv_out[g] = ordered.astype(LOW)
            turned_out[g] = ordered.T.astype(LOW)
        turned = packed_ref[...].T.astype(LOW)
        spread = (dot(turned, owner_ref[...]) * widen(take_ref[...])).astype(LOW)
        table = dot(row_ref[...], spread)
        table_out[...] = table
        for c in range(parts):
            quarters_out[c] = table[:, c * quarter : (c + 1) * quarter]
        columns_out[...] = jnp.concatenate(
            [table, jnp.zeros((112, width), jnp.float32)], axis=0
        ).T
        spread = (dot(turned, owner_in_ref[...]) * widen(take_in_ref[...])).astype(LOW)
        edges_out[...] = dot(row_in_ref[...], spread)
        hid_out[...] = column_sum(dot(turned, owner_hid_ref[...]) * widen(take_hid_ref[...]))

    f32 = jnp.float32
    return local_call(
        kernel,
        [
            ((parts, wide_in, quarter), LOW), ((width, 2 * att), LOW), ((groups, rows, fold), LOW),
            ((groups, fold, rows), LOW), ((16, width), f32), ((parts, 16, quarter), f32),
            ((width, 128), f32), ((16, wide_in), f32), ((1, hidden), f32),
        ],
        [],
        early, second, packed,
        *[
            jnp.asarray(v, LOW)
            for v in (nat_in, nat, place_in, place_att, conv_order, take, row_of, owner, take_in,
                      row_in, owner_in, take_hid, owner_hid)
        ],
    )


def fold_rows(padded, spread_ref, inner):
    for j in range(FOLD):
        moved = padded if j == 0 else pltpu.roll(padded, padded.shape[1] - j, 1)
        spread_ref[j * inner : (j + 1) * inner, :] = moved.astype(LOW)


def spread_blocks(padded, spread_ref, inner, blocks):
    for b in range(blocks):
        moved = padded if b == 0 else pltpu.roll(padded, FOLD * b, 1)
        spread_ref[b * inner : (b + 1) * inner, :] = moved.astype(LOW)


def front(gathered, lengths, here, proj, conv, quarters, columns, edges, micros, frames):
    parts, rows, narrow = gathered.shape
    quarter = proj.shape[2]
    groups, many, fold = conv.shape
    inner = fold // FOLD
    blocks = many // inner
    half = blocks * FOLD // 2
    span = frames + blocks * FOLD

    def kernel(
        in_ref, len_ref, here_ref, proj_ref, conv_ref, quarters_ref, columns_ref, edges_ref,
        summed_out, turned_out, before_out, spread_ref, plain_ref,
    ):
        spot = here_ref[0]
        for m in range(micros):
            at = slice(m * frames, (m + 1) * frames)
            normal, _ = norm_blocks([widen(in_ref[c, at]) for c in range(parts)])
            low = [
                (
                    block * edges_ref[0:1, c * narrow : (c + 1) * narrow]
                    + edges_ref[1:2, c * narrow : (c + 1) * narrow]
                ).astype(LOW)
                for c, block in enumerate(normal)
            ]
            result = dot(jnp.concatenate(low, axis=1), proj_ref[spot]) + quarters_ref[spot, 0:1]
            live = lax.broadcasted_iota(jnp.int32, (frames, 1), 0) < len_ref[m]
            turned = jnp.where(live, result, 0.0).T
            for g in range(groups):
                piece = turned[g * inner : (g + 1) * inner]
                plain_ref[m * groups + g] = piece
                turned_out[m * groups + g] = jnp.concatenate(
                    [
                        jnp.zeros((inner, half), LOW), piece.astype(LOW),
                        jnp.zeros((inner, half), LOW),
                    ],
                    axis=1,
                )

        def one(index, carry):
            g = index % groups
            fold_rows(widen(turned_out[index]), spread_ref, inner)
            sums = dot(conv_ref[g], spread_ref[...])
            total = sums[:inner, :frames]
            for b in range(1, blocks):
                part = pltpu.roll(sums[b * inner : (b + 1) * inner], span - FOLD * b, 1)
                total = total + part[:, :frames]
            start = pl.multiple_of(spot * quarter + g * inner, 16)
            before = total + columns_ref[pl.ds(start, inner), 1:2]
            before_out[index] = before
            plain_ref[index] = plain_ref[index] + smooth(before)
            return carry

        lax.fori_loop(0, micros * groups, one, 0)
        for m in range(micros):
            both = [plain_ref[m * groups + g] for g in range(groups)]
            summed_out[m * frames : (m + 1) * frames] = jnp.concatenate(both, axis=0).T.astype(LOW)

    f32 = jnp.float32
    return local_call(
        kernel,
        [
            ((rows, quarter), LOW),
            ((micros * groups, inner, span), LOW),
            ((micros * groups, inner, frames), f32),
        ],
        [pltpu.VMEM((fold, span), LOW), pltpu.VMEM((micros * groups, inner, frames), f32)],
        gathered, lengths, here, proj, conv, quarters, columns, edges,
    )


def attention(summed, lengths, here, attend, quarters, micros, frames):
    parts, rows, quarter = summed.shape
    heads = quarter // HEAD_DIM
    seg = frames // parts
    ratio = HEAD_DIM ** (-0.5)

    def kernel(in_ref, len_ref, here_ref, attend_ref, quarters_ref, low_out, joint_out, probs_out, context_out):
        spot = here_ref[0]

        def one(m, carry):
            begin = pl.multiple_of(m * frames, frames)
            at = pl.ds(begin, frames)
            normal, _ = norm_blocks([widen(in_ref[c, at]) for c in range(parts)])
            joint = jnp.zeros((frames, 3 * quarter), jnp.float32)
            for c in range(parts):
                low = (normal[c] * quarters_ref[c, 2:3] + quarters_ref[c, 3:4]).astype(LOW)
                low_out[c, at] = low
                joint = joint + dot(low, attend_ref[c * quarter : (c + 1) * quarter])
            query = joint[:, :quarter] + quarters_ref[spot, 4:5]
            keys = joint[:, quarter : 2 * quarter]
            value = joint[:, 2 * quarter :] + quarters_ref[spot, 5:6]
            joint_low = [v.astype(LOW) for v in (query, keys, value)]
            for i in range(3):
                joint_out[i, at] = joint_low[i]
            value_turned = value.T.astype(LOW)
            live = lax.broadcasted_iota(jnp.int32, (frames, 1), 0) < len_ref[m]
            results = []
            for h in range(heads):
                cols = slice(h * HEAD_DIM, (h + 1) * HEAD_DIM)
                scores = dot_nt(joint_low[1][:, cols], joint_low[0][:, cols]) * ratio
                scores = jnp.where(live, scores, NEGATIVE)
                expo = jnp.exp(scores - jnp.max(scores, axis=0, keepdims=True))
                probs = (expo / jnp.sum(expo, axis=0, keepdims=True)).astype(LOW)
                probs_out[m * heads + h] = probs
                results.append(dot(value_turned[cols], probs))
            context = jnp.concatenate(results, axis=0).T.astype(LOW)
            for d in range(parts):
                target = pl.ds(pl.multiple_of(m * seg, seg), seg)
                context_out[d, target] = context[d * seg : (d + 1) * seg]
            return carry

        lax.fori_loop(0, micros, one, 0)

    return local_call(
        kernel,
        [
            ((parts, rows, quarter), LOW), ((3, rows, quarter), LOW),
            ((micros * heads, frames, frames), LOW), ((parts, micros * seg, quarter), LOW),
        ],
        [],
        summed, lengths, here, attend, quarters,
    )


def own_frames(ref, spot, micros, frames, parts):
    seg = frames // parts
    blocks = []
    for c in range(parts):
        pieces = [
            widen(ref[c, pl.ds(pl.multiple_of(m * frames + spot * seg, seg), seg)])
            for m in range(micros)
        ]
        blocks.append(jnp.concatenate(pieces, axis=0))
    return blocks


def feed_forward(
    context, summed, here, upstream, weights, table, hid_bias, micros, frames, thin, own, own_hid
):
    parts, mine, quarter = context.shape
    squares, _, tall, lanes = weights.shape[1:]
    width = parts * quarter
    half, deep = width // 2, lanes - width // 2 - 128
    eight = 2 * parts
    nat = onehot(np.arange(width), natural_of(width, parts, squares))
    spots = np.arange(width)
    place = np.zeros((width // 128, 256, 128), np.float32)
    for tile in range(width // 128):
        first = tile * 128 // thin
        for lane in range(128):
            channel = tile * 128 + lane
            place[tile, (channel // thin - first) * 128 + channel % thin, lane] = 1.0
    cut = np.stack([onehot(spots, np.where(np.arange(128) < thin, j * thin + np.arange(128), -1)) for j in range(eight)])
    f32 = jnp.float32
    hidden = eight * deep
    devices = 2 * parts * squares
    lane = np.arange(8 * own + own_hid + -(8 * own + own_hid) % 128)
    mask = onehot(np.arange(devices), np.arange(width) // own)
    mask_hid = onehot(np.arange(devices), np.arange(hidden) // own_hid)
    spread = onehot(np.arange(width) % own, lane)
    spread_hid = onehot(
        np.arange(hidden) % own_hid, np.where(lane >= 8 * own, lane - 8 * own, -1)
    )

    def kernel(
        ctx_ref, sum_ref, here_ref, up_ref, w_ref, table_ref, hid_ref, nat_ref, place_ref, cut_ref,
        mask_ref, mask_hid_ref, spread_ref, spread_hid_ref,
        out_ref, grad_out, gctx_out, slabs_out, normal_out, scale_out, owned_out,
        pre_ref, act_ref, wout_ref, hid_out,
    ):
        spot = here_ref[0]

        def block(c, k, begin, size):
            return w_ref[c, :, k, :, begin : begin + size].reshape(width, size)

        for tile in range(width // 128):
            first = tile * 128 // thin
            last = min(first + 1, eight - 1)
            both = [block(j // 2, j % 2, half + deep, 128) for j in (first, last)]
            wout_ref[:, tile * 128 : (tile + 1) * 128] = pick(jnp.concatenate(both, axis=1), place_ref[tile])
        normal, scale = norm_blocks(own_frames(sum_ref, spot, micros, frames, parts))
        normal = jnp.concatenate(normal, axis=1)
        normal_out[...] = normal
        scale_out[...] = jnp.broadcast_to(scale, scale_out.shape)
        encoded = normal * table_ref[2:3] + table_ref[3:4]
        ctx_slab = sum(
            dot(ctx_ref[c], nat_ref[c * quarter : (c + 1) * quarter]) for c in range(parts)
        ).astype(LOW)
        attn_sum = encoded + dot(ctx_slab, wout_ref[...]) + table_ref[6:7]
        normal_att, scale_att = norm(attn_sum)
        attn_norm = normal_att * table_ref[7:8] + table_ref[8:9]
        attn_slab = pick(attn_norm.astype(LOW), nat_ref[...])
        outer = [jnp.zeros((mine, half), f32), jnp.zeros((mine, half), f32)]
        for c in range(parts):
            for k in range(2):
                begin = (2 * c + k) * deep
                pre = dot(attn_slab, block(c, k, half, deep)) + hid_ref[:, begin : begin + deep]
                pre_ref[:, begin : begin + deep] = pre
                act_ref[:, begin : begin + deep] = smooth(pre).astype(LOW)
            act = act_ref[:, 2 * c * deep : 2 * (c + 1) * deep]
            outer = [outer[k] + dot(act, block(c, k, 0, half)) for k in range(2)]
        ffn_sum = attn_norm + jnp.concatenate(outer, axis=1) + table_ref[9:10]
        normal_fin, scale_fin = norm(ffn_sum)
        out_ref[...] = (normal_fin * table_ref[10:11] + table_ref[11:12]).astype(LOW)
        up = widen(up_ref[...])
        grad_ffn = norm_back(up, normal_fin, scale_fin, table_ref[10:11])
        slope_outer = grad_ffn.astype(LOW)
        vectors = {
            5: column_sum(widen(slope_outer)), 6: column_sum(up * normal_fin), 7: column_sum(up)
        }
        grad_slab = jnp.zeros((mine, width), f32)
        attn_turned = widen(attn_slab).T.astype(LOW)
        for c in range(parts):
            columns = slice(2 * c * deep, 2 * (c + 1) * deep)
            grad_act = sum(
                dot_nt(slope_outer[:, k * half : (k + 1) * half], block(c, k, 0, half)) for k in range(2)
            )
            slope_inner = (grad_act * smooth_slope(pre_ref[:, columns])).astype(LOW)
            hid_out[:, columns] = column_sum(widen(slope_inner))
            act_turned = widen(act_ref[:, columns]).T.astype(LOW)
            for k in range(2):
                inner_k = slope_inner[:, k * deep : (k + 1) * deep]
                grad_slab = grad_slab + dot_nt(inner_k, block(c, k, half, deep))
                grad_ret = dot(act_turned, slope_outer[:, k * half : (k + 1) * half]).astype(LOW)
                slabs_out[k, c, :, :, :half] = grad_ret.reshape(squares, tall, half)
                grad_hid = dot(attn_turned, inner_k).astype(LOW)
                slabs_out[k, c, :, :, half : half + deep] = grad_hid.reshape(squares, tall, deep)
        high = grad_slab.astype(LOW)
        rest = (grad_slab - widen(high)).astype(LOW)
        grad_norm2 = grad_ffn + dot_nt(high, nat_ref[...]) + dot_nt(rest, nat_ref[...])
        vectors[3] = column_sum(grad_norm2 * normal_att)
        vectors[4] = column_sum(grad_norm2)
        grad_attn = norm_back(grad_norm2, normal_att, scale_att, table_ref[7:8])
        grad_out[...] = grad_attn
        slope_att = grad_attn.astype(LOW)
        vectors[2] = column_sum(widen(slope_att))
        owned = dot((widen(mask_hid_ref[...]) * hid_out[...]).astype(LOW), spread_hid_ref[...])
        for v, vector in vectors.items():
            owned = owned + owner_rows(vector, mask_ref[...], spread_ref[...], v * own)
        owned_out[...] = owned
        gctx_slab = dot_nt(slope_att, wout_ref[...]).astype(LOW)
        for c in range(parts):
            gctx_out[c] = dot_nt(gctx_slab, nat_ref[c * quarter : (c + 1) * quarter]).astype(LOW)
        ctx_turned = widen(ctx_slab).T.astype(LOW)
        for c in range(parts):
            for k in range(2):
                grad = dot(ctx_turned, pick(slope_att, cut_ref[2 * c + k])).astype(LOW)
                slabs_out[k, c, :, :, half + deep :] = grad.reshape(squares, tall, 128)

    return local_call(
        kernel,
        [
            ((mine, width), LOW), ((mine, width), f32), ((parts, mine, quarter), LOW),
            ((2, parts, squares, tall, lanes), LOW), ((mine, width), f32), ((mine, 128), f32),
            ((devices, len(lane)), f32),
        ],
        [
            pltpu.VMEM((mine, hidden), f32), pltpu.VMEM((mine, hidden), LOW),
            pltpu.VMEM((width, width), LOW), pltpu.VMEM((1, hidden), f32),
        ],
        context, summed, here, upstream, weights, table, hid_bias,
        *[jnp.asarray(v, LOW) for v in (nat, place, cut, mask, mask_hid, spread, spread_hid)],
    )


def stages_of(axes, order, sizes):
    left = list(axes)
    result = []
    for axis in order:
        where = left.index(axis)
        left = left[:where] + left[where + 1 :]
        dims = tuple(sizes[a] for a in left)
        result.append((axis, where, tuple(left), dims, sizes[axis] == 4 and len(dims) > 0))
    return result


def sum_scratch(jobs, sizes):
    scratch, copies = {}, 0
    for name, job in jobs.items():
        for part, (cut, order) in enumerate(zip(job["cuts"], job["orders"])):
            block = (cut[1], cut[3])
            dims = tuple(sizes[a] for a in job["axes"])
            key = f"{name}{part}"
            scratch[key + "got"] = pltpu.VMEM(dims + block, LOW)
            if job["far"]:
                scratch[key + "own"] = pltpu.VMEM((2,) + dims[1:] + block, LOW)
            copies += 1
            for number, (axis, _, _, dims, ring) in enumerate(stages_of(job["axes"], order, sizes)):
                if ring:
                    half = (dims[0] // 2,) + dims[1:] + block
                    scratch[f"{key}got{number}"] = pltpu.VMEM((6,) + half, LOW)
                    copies += 6
                else:
                    scratch[f"{key}got{number}"] = pltpu.VMEM((max(sizes[axis] - 1, 1),) + dims + block, LOW)
                    copies += sizes[axis] - 1
                if dims:
                    scratch[f"{key}sum{number}"] = pltpu.VMEM(dims + block, LOW)
    return scratch, copies


class Sums:
    def __init__(self, refs, jobs, spot, sizes, sources, sinks, local):
        self.refs, self.jobs, self.spot, self.sizes = refs, jobs, spot, sizes
        self.sources, self.sinks, self.local = sources, sinks, local
        self.states, self.finished = {}, []

    def move(self, source, target, device):
        copy = self.refs["move"](source, target, device)
        self.finished.append(copy)
        return copy

    def start(self, name):
        job, core = self.jobs[name], self.spot["k"]
        sibling = peer(self.spot, "k", 1, self.sizes)[1]
        states = []
        for part, (cut, order) in enumerate(zip(job["cuts"], job["orders"])):
            key = f"{name}{part}"
            window_at = window(job["axes"], {}, cut)
            got = self.refs[key + "got"]
            copy = self.move(self.sources[name].at[(1 - core,) + window_at], got, sibling)
            near = None
            if job["far"]:

                def near(number, slot, window_at=window_at, key=key, part=part):
                    return pltpu.make_async_copy(
                        self.sources[name].at[(core, number) + window_at[1:]],
                        self.refs[key + "own"].at[slot], self.local.at[2 * part + slot],
                    )

                near(0, 0).start()
            states.append(
                {
                    "key": key, "cut": cut, "held": got, "left": job["axes"], "step": 0, "near": near,
                    "copies": [copy], "half": False,
                    "stages": stages_of(job["axes"], order, self.sizes),
                }
            )
        self.states[name] = states

    def pump(self, *names):
        for name in names:
            for state in self.states[name]:
                self.advance(name, state)

    def drain(self, *names):
        while any(s["step"] <= len(s["stages"]) for name in names for s in self.states[name]):
            self.pump(*names)

    def advance(self, name, state):
        step, stages = state["step"], state["stages"]
        if step > len(stages):
            return
        if step == 0:
            self.add_own(name, state)
        elif state["half"]:
            self.relay(state, stages[step - 1], step - 1)
            return
        else:
            self.add_stage(name, state, stages[step - 1], step - 1)
        if step < len(stages):
            self.send_stage(state, stages[step], step)
        state["step"] = step + 1

    def add_own(self, name, state):
        for copy in state["copies"]:
            copy.wait_recv()
        held, cut = state["held"], state["cut"]
        dims = tuple(self.sizes[a] for a in state["left"])
        if state["near"] is not None:
            near, own = state["near"], self.refs[state["key"] + "own"]
            for number in range(dims[0]):
                slot = number % 2
                if number + 1 < dims[0]:
                    near(number + 1, 1 - slot).start()
                near(number, slot).wait()

                def add(index, number=number, slot=slot):
                    held[(number,) + index] = held[(number,) + index] + own[(slot,) + index]

                loop_blocks(dims[1:], add)
            return
        else:
            source, core = self.sources[name], self.spot["k"]

            def add(index):
                rows, lanes = slice(cut[0], cut[0] + cut[1]), slice(cut[2], cut[2] + cut[3])
                held[index] = held[index] + source[(core,) + index + (rows, lanes)]

        loop_blocks(dims, add)

    def send_stage(self, state, stage, number):
        axis, _, left, dims, ring = stage
        held, got = state["held"], self.refs[f"{state['key']}got{number}"]
        before = state["left"]
        state["copies"] = []
        if not ring:
            for step in range(1, self.sizes[axis]):
                moved, device = peer(self.spot, axis, step, self.sizes)
                at = tuple(moved[a] if a == axis else slice(None) for a in before)
                state["copies"].append(self.move(held.at[at], got.at[step - 1], device))
        else:
            size = dims[0] // 2
            near, far = pl.ds(0, size), pl.ds(size, size)

            def piece(step, half):
                moved = peer(self.spot, axis, step, self.sizes)[0]
                return held.at[
                    tuple(
                        moved[a] if a == axis else (half if a == left[0] else slice(None)) for a in before
                    )
                ]

            right = peer(self.spot, axis, 1, self.sizes)[1]
            back = peer(self.spot, axis, 3, self.sizes)[1]
            state["copies"] = [
                self.move(piece(2, near), got.at[0], right),
                self.move(piece(2, far), got.at[1], back),
                self.move(piece(1, far), got.at[2], right),
                self.move(piece(3, near), got.at[3], back),
            ]
            state["half"] = True

    def relay(self, state, stage, number):
        axis, where, left, dims, _ = stage
        held = state["held"]
        got = self.refs[f"{state['key']}got{number}"]
        size = dims[0] // 2
        ahead, right = peer(self.spot, axis, 1, self.sizes)
        behind, back = peer(self.spot, axis, 3, self.sizes)
        for slot, spot, offset in ((0, ahead, 0), (1, behind, size)):
            state["copies"][slot].wait_recv()

            def add(index, slot=slot, spot=spot, offset=offset):
                full = (index[0] + offset,) + index[1:]
                full = full[:where] + (spot[axis],) + full[where:]
                held[full] = held[full] + got[(slot,) + index]

            loop_blocks((size,) + dims[1:], add)
            at = tuple(
                spot[a] if a == axis else (pl.ds(offset, size) if a == left[0] else slice(None))
                for a in state["left"]
            )
            state["copies"].append(
                self.move(held.at[at], got.at[4 + slot], (right, back)[slot])
            )
        state["half"] = False

    def add_stage(self, name, state, stage, number):
        axis, where, left, dims, ring = stage
        held, cut = state["held"], state["cut"]
        got = self.refs[f"{state['key']}got{number}"]
        target = self.refs[f"{state['key']}sum{number}"] if dims else None
        mine = self.spot[axis]
        for copy in state["copies"][2 if ring else 0 :]:
            copy.wait_recv()
        if ring:
            size = dims[0] // 2
            for offset, first, second in ((0, 4, 3), (size, 2, 5)):

                def add(index, offset=offset, first=first, second=second):
                    full = (index[0] + offset,) + index[1:]
                    own = full[:where] + (mine,) + full[where:]
                    result = widen(held[own]) + widen(got[(first,) + index]) + widen(got[(second,) + index])
                    target[full] = result.astype(LOW)

                loop_blocks((size,) + dims[1:], add)
        else:

            def add(index):
                index = index if dims else ()
                result = widen(held[index[:where] + (mine,) + index[where:]])
                for step in range(self.sizes[axis] - 1):
                    result = result + widen(got[(step,) + index])
                if target is None:
                    rows, lanes = slice(cut[0], cut[0] + cut[1]), slice(cut[2], cut[2] + cut[3])
                    self.sinks[name][rows, lanes] = result
                else:
                    target[index] = result.astype(LOW)

            loop_blocks(dims if dims else (1,), add)
        state["held"], state["left"] = target, left

    def close(self):
        for copy in self.finished:
            copy.wait_send()


def attention_back_step(r, micros, frames):
    parts, mine, quarter = r["gctx"].shape
    heads = quarter // HEAD_DIM
    seg = frames // parts
    ratio = HEAD_DIM ** (-0.5)
    r["att_sums"][...] = jnp.zeros_like(r["att_sums"])
    r["slope_joint"][...] = jnp.zeros_like(r["slope_joint"])

    def one(m, carry):
        at = pl.ds(pl.multiple_of(m * frames, frames), frames)
        cells = pl.ds(pl.multiple_of(m * seg, seg), seg)
        grad = jnp.concatenate([r["gctx_in"][d, cells] for d in range(parts)], axis=0)
        query, keys, value = r["joint"][0, at], r["joint"][1, at], r["joint"][2, at]
        keys_turned = widen(keys).T.astype(LOW)
        queries, key_parts, values = [], [], []
        for h in range(heads):
            cols = slice(h * HEAD_DIM, (h + 1) * HEAD_DIM)
            probs_low = r["probs"][m * heads + h]
            grad_probs = dot_nt(value[:, cols], grad[:, cols])
            weighted = widen(probs_low) * grad_probs
            centre = jnp.sum(weighted, axis=0, keepdims=True)
            slope = (weighted - widen(probs_low) * centre).astype(LOW)
            values.append(dot(probs_low, grad[:, cols]))
            key_parts.append(dot(slope, query[:, cols]) * ratio)
            queries.append(dot(keys_turned[cols], slope) * ratio)
        slopes = [
            jnp.concatenate(queries, axis=0).T.astype(LOW),
            jnp.concatenate(key_parts, axis=1).astype(LOW),
            jnp.concatenate(values, axis=1).astype(LOW),
        ]
        r["att_sums"][0:1] = r["att_sums"][0:1] + column_sum(widen(slopes[0]))
        r["att_sums"][1:2] = r["att_sums"][1:2] + column_sum(widen(slopes[2]))
        slope = jnp.concatenate(slopes, axis=1)
        size = slope.shape[1] // 2
        for k in range(2):
            r["slope_joint"][k, at, :size] = slope[:, k * size : (k + 1) * size]
        terms = dot_nt(slope, r["attend"][...]).astype(LOW)
        for d in range(parts):
            r["terms"][d, cells] = terms[d * seg : (d + 1) * seg]
        return carry

    lax.fori_loop(0, micros, one, 0)


def attention_weight_step(r):
    parts = r["low"].shape[0]
    for k in range(2):
        pieces = [dot_tn(r["low"][c], r["slope_joint"][k]).astype(LOW) for c in range(parts)]
        grads = dot(r["back_att"][...], jnp.concatenate(pieces, axis=0)).astype(LOW)
        r["att_grad"][k] = grads.reshape(r["att_grad"].shape[1:])


def norm_back_step(r):
    parts, _, quarter = r["gpos"].shape
    normal, scale = r["normal"][...], r["scale"][:, 0:1]
    grad = r["grad_attn"][...] + r["terms_sum"][...]
    result = norm_back(grad, normal, scale, r["table"][2:3]).astype(LOW)
    for c in range(parts):
        r["gpos"][c] = result[:, c * quarter : (c + 1) * quarter]
    r["sums_own"][0:1] = column_sum(grad * normal)
    r["sums_own"][1:2] = column_sum(grad)


def owner_rows(vector, mask, spread, place):
    cells = dot((widen(mask) * vector).astype(LOW), spread)
    return cells if place == 0 else pltpu.roll(cells, place, 1)


def vectors_step(r, own):
    owned = r["owned"][...]
    for v in range(2):
        owned = owned + owner_rows(r["sums_own"][v : v + 1], r["mask"][...], r["spread"][...], v * own)
    r["full"][...] = dot(r["row_full"][...], owned.astype(LOW)).astype(LOW).reshape(r["full"].shape)


def conv_back_step(r, here, micros, frames, tall, per):
    parts, mine, quarter = r["gpos"].shape
    groups, fold, many = r["conv_turned"].shape
    inner = fold // FOLD
    blocks = many // inner
    half = blocks * FOLD // 2
    span = frames + blocks * FOLD
    seg = frames // parts
    side = r["conv_grad"].shape[2]
    f32 = jnp.float32
    for m in range(micros):
        cells = slice(m * seg, (m + 1) * seg)
        grad = jnp.concatenate([widen(r["gpos_in"][d, cells]) for d in range(parts)], axis=0).T
        for g in range(groups):
            r["grads"][m * groups + g] = grad[g * inner : (g + 1) * inner]

    def one(g, carry):
        weight = 0.0
        for m in range(micros):
            index = m * groups + g
            grad = r["grads"][index]
            slope = (grad * smooth_slope(r["before"][index])).astype(LOW).astype(f32)
            r["turn"][index, :, 0:1] = jnp.sum(slope, axis=1, keepdims=True)
            wide = jnp.concatenate([slope, jnp.zeros((inner, span - frames), f32)], axis=1)
            spread_blocks(wide, r["moved"], inner, blocks)
            fold_rows(widen(r["padded"][index]), r["folded"], inner)
            weight = weight + dot_nt(r["moved"][...], r["folded"][...])
            back_sums = dot(r["conv_turned"][g], r["moved"][...])
            total = grad
            for j in range(FOLD):
                part = pltpu.roll(back_sums[j * inner : (j + 1) * inner], (span + j - half) % span, 1)
                total = total + part[:, :frames]
            live = lax.broadcasted_iota(jnp.int32, (1, frames), 1) < r["spans"][m]
            total = jnp.where(live, total, 0.0).astype(LOW).astype(f32)
            r["turn"][index, :, 1:2] = jnp.sum(total, axis=1, keepdims=True)
            r["grads"][index] = total
        weight = dot(r["back_conv"][...], weight.astype(LOW)).astype(LOW).reshape(2, per, tall, fold)
        for n in range(per):
            xz = g * per + n
            for k in range(2):
                r["conv_grad"][k, xz // side, xz % side] = weight[k, n]
        return carry

    lax.fori_loop(0, groups, one, 0)
    for m in range(micros):
        both = [r["grads"][m * groups + g] for g in range(groups)]
        r["slopes_all"][here, m * frames : (m + 1) * frames] = jnp.concatenate(both, axis=0).T.astype(LOW)
    sums = jnp.concatenate(
        [sum(r["turn"][m * groups + g] for m in range(micros)) for g in range(groups)], axis=0
    ).T
    r["conv_sums"][...] = sums[:8]


def finish_step(r, spot, own, own_in):
    parts, rows, narrow = r["gathered"].shape
    ranks, quarter = r["mask_ch"].shape
    width = parts * quarter
    f32 = jnp.float32
    here = spot["y"]
    size = parts * narrow
    chunk = 256
    mine_at = pl.ds(pl.multiple_of(here * narrow, narrow), narrow)
    gain, shift = r["edges"][0:1, mine_at], r["edges"][1:2, mine_at]
    r["edge_sums"][...] = jnp.zeros_like(r["edge_sums"])
    r["proj_grad"][...] = jnp.zeros_like(r["proj_grad"])

    def one(number, carry):
        at = pl.ds(pl.multiple_of(number * chunk, chunk), chunk)
        blocks = [widen(r["gathered"][c, at]) for c in range(parts)]
        slopes = [r["slopes_all"][b, at] for b in range(parts)]
        normal, scale = norm_blocks(blocks)
        first = jnp.zeros((chunk, 1), f32)
        second = jnp.zeros((chunk, 1), f32)
        for c in range(parts):
            lanes = slice(c * narrow, (c + 1) * narrow)
            grad = sum(dot_nt(slopes[b], r["proj"][b, lanes]) for b in range(parts))
            scaled = grad * r["edges"][0:1, lanes]
            first = first + jnp.sum(scaled, axis=1, keepdims=True)
            second = second + jnp.sum(scaled * normal[c], axis=1, keepdims=True)
        mean = sum(jnp.sum(block, axis=1, keepdims=True) for block in blocks) / size
        mine = (widen(r["gathered"][here, at]) - mean) * scale
        grad = sum(dot_nt(slopes[b], r["proj"][b, mine_at]) for b in range(parts))
        r["features_grad"][at] = scale * (grad * gain - first / size - mine * (second / size))
        low = (mine * gain + shift).astype(LOW)
        r["proj_grad"][...] = r["proj_grad"][...] + jnp.concatenate(
            [dot_tn(low, slopes[b]) for b in range(parts)], axis=1
        )
        r["edge_sums"][0:1] = r["edge_sums"][0:1] + column_sum(grad * mine)
        r["edge_sums"][1:2] = r["edge_sums"][1:2] + column_sum(grad)
        return carry

    lax.fori_loop(0, rows // chunk, one, 0)
    vectors = [
        r["conv_sums"][1:2], r["conv_sums"][0:1], r["att_sums"][0:1], r["att_sums"][1:2],
    ]
    owned = 0.0
    for v in range(4):
        owned = owned + owner_rows(vectors[v], r["mask_ch"][...], r["spread_ch"][...], v * own)
    for v in range(2):
        owned = owned + owner_rows(
            r["edge_sums"][v : v + 1], r["mask_in"][...], r["spread_in"][...], 4 * own + v * own_in
        )
    lanes = owned.shape[1]
    owned = jnp.concatenate([owned, jnp.zeros((ranks, width - lanes), f32)], axis=1)
    result = dot(r["row_proj"][...], r["proj_grad"][...].astype(LOW))
    result = result + dot(r["row_vector"][...], owned.astype(LOW))
    r["local"][...] = result.astype(LOW).reshape(r["local"].shape)


def backward_rest(values, sizes, ident, micros, frames, own, own_in, own_hid, own_ret, thin):
    parts, squares, side = sizes["y"], sizes["x"] * sizes["z"], sizes["z"]
    devices, ranks = 2 * parts * squares, 2 * squares
    _, mine, quarter = values["gctx"].shape
    width = parts * quarter
    rows = micros * frames
    narrow = values["gathered"].shape[2]
    groups, fold, many = values["conv_turned"].shape
    inner = fold // FOLD
    blocks = many // inner
    span = frames + blocks * FOLD
    per = inner // own // 2
    tall, lanes_a = values["ffn"].shape[-2:]
    half, deep = width // 2, lanes_a - width // 2 - 128
    att = 3 * quarter // 2
    wide = att + -att % 128
    eight = 2 * parts
    f32 = jnp.float32

    ones = {}
    ones["back_att"] = onehot(natural_of(width, parts, squares), np.arange(width))
    slab = np.arange(many).reshape(2, per, own, blocks)
    ones["back_conv"] = onehot(
        np.arange(many),
        [slab[(o // own) % 2, o // own // 2, o % own, b] for b in range(blocks) for o in range(inner)],
    )
    count = 8 * own + own_hid
    lane = np.arange(count + -count % 128)
    ones["mask"] = onehot(np.arange(devices), np.arange(width) // own)
    ones["spread"] = onehot(np.arange(width) % own, lane)
    full_rows = np.full((devices, 16), -1)
    full_rows[:, 0] = np.arange(devices).reshape(parts, squares, 2).transpose(2, 0, 1).reshape(-1)
    ones["row_full"] = onehot(full_rows.reshape(-1), np.arange(devices))
    few = 4 * own + 2 * own_in
    few = np.arange(few + -few % 128)
    ones["mask_ch"] = onehot(np.arange(ranks), np.arange(quarter) // own)
    ones["spread_ch"] = onehot(np.arange(quarter) % own, few)
    ones["mask_in"] = onehot(np.arange(ranks), np.arange(narrow) // own_in)
    ones["spread_in"] = onehot(np.arange(narrow) % own_in, few)
    high = own_in + 1 + -(own_in + 1) % 16
    order = np.arange(ranks).reshape(squares, 2).T.reshape(-1)
    proj_rows = np.full((ranks, high), -1)
    proj_rows[:, :own_in] = order[:, None] * own_in + np.arange(own_in)[None, :]
    ones["row_proj"] = onehot(proj_rows.reshape(-1), np.arange(narrow))
    vector_rows = np.full((ranks, high), -1)
    vector_rows[:, own_in] = order
    ones["row_vector"] = onehot(vector_rows.reshape(-1), np.arange(ranks))

    cut_lanes = lanes_a // 256 * 128 + 128 * (lanes_a // 128 % 2)
    jobs = {
        "ffn": {
            "axes": ("y", "x", "z"), "far": True,
            "cuts": [(0, tall, 0, cut_lanes), (0, tall, cut_lanes, lanes_a - cut_lanes)],
            "orders": [("x", "z", "y"), ("z", "x", "y")],
        },
        "full": {
            "axes": ("y", "x", "z"), "far": False, "cuts": [(0, 16, 0, len(lane))],
            "orders": [("z", "x", "y")],
        },
        "att": {
            "axes": ("x", "z"), "far": False, "cuts": [(0, tall, 0, wide)], "orders": [("x", "z")],
        },
        "conv": {
            "axes": ("x", "z"), "far": False,
            "cuts": [(0, tall, 0, fold // 2), (0, tall, fold // 2, fold // 2)],
            "orders": [("x", "z"), ("z", "x")],
        },
        "local": {
            "axes": ("x", "z"), "far": False, "cuts": [(0, high, 0, width)], "orders": [("z", "x")],
        },
    }
    scratch, copies = sum_scratch(jobs, sizes)
    copies += 3 * (parts - 1) + 12 + eight
    lead = {"y": parts, "x": sizes["x"], "z": sizes["z"]}
    low_rows = own + -own % 8
    block_lanes = deep + 128 + wide
    scratch.update(
        {
            "gctx_in": pltpu.VMEM((parts, mine, quarter), LOW),
            "terms": pltpu.VMEM((parts, mine, width), LOW),
            "terms_held": pltpu.VMEM((6, mine // 2, width), LOW),
            "terms_sum": pltpu.VMEM((mine, width), f32),
            "slope_joint": pltpu.VMEM((2, rows, wide), LOW),
            "att_grad": pltpu.VMEM((2, sizes["x"], sizes["z"], tall, wide), LOW),
            "att_sums": pltpu.VMEM((8, quarter), f32),
            "gpos": pltpu.VMEM((parts, mine, quarter), LOW),
            "gpos_in": pltpu.VMEM((parts, mine, quarter), LOW),
            "sums_own": pltpu.VMEM((8, width), f32),
            "full": pltpu.VMEM((2, parts, sizes["x"], sizes["z"], 16, len(lane)), LOW),
            "grads": pltpu.VMEM((micros * groups, inner, frames), f32),
            "turn": pltpu.VMEM((micros * groups, inner, 128), f32),
            "moved": pltpu.VMEM((many, span), LOW),
            "folded": pltpu.VMEM((fold, span), LOW),
            "slopes_all": pltpu.VMEM((parts, rows, quarter), LOW),
            "conv_sums": pltpu.VMEM((8, quarter), f32),
            "conv_grad": pltpu.VMEM((2, sizes["x"], sizes["z"], tall, fold), LOW),
            "proj_grad": pltpu.VMEM((narrow, width), f32),
            "edge_sums": pltpu.VMEM((8, narrow), f32),
            "local": pltpu.VMEM((2, sizes["x"], sizes["z"], high, width), LOW),
            "ffn_sum": pltpu.VMEM((tall, lanes_a), f32),
            "att_sum": pltpu.VMEM((tall, wide), f32),
            "block": pltpu.VMEM((eight, low_rows, block_lanes), f32),
            "pair": pltpu.VMEM((2, own_ret, half), f32),
        }
    )
    outs = {
        "features_grad": ((rows, narrow), f32),
        "full_sum": ((16, len(lane)), f32),
        "conv_sum": ((tall, fold), f32),
        "local_sum": ((high, width), f32),
        "block_in": ((eight, low_rows, block_lanes), f32),
        "pair_in": ((2, own_ret, half), f32),
    }
    ins = dict(values)
    ins.update({name: jnp.asarray(value, LOW) for name, value in ones.items()})
    spaces = {"spans": pltpu.SMEM, "ffn": pl.ANY}
    names = list(ins) + list(outs) + list(scratch)

    def kernel(*refs):
        r = dict(zip(names, refs))
        local, send_sems, recv_sems = refs[len(names) :]
        spot = place(side)
        here, core, rank = spot["y"], spot["k"], lax.axis_index("rows")
        base = rank - core
        used = [0]

        def move(source, target, device):
            index = used[0]
            used[0] += 1
            return send(source, target, send_sems.at[index], recv_sems.at[index], device)

        r["move"] = move
        sources = {
            "ffn": r["ffn"], "full": r["full"], "att": r["att_grad"], "conv": r["conv_grad"],
            "local": r["local"],
        }
        sinks = {
            "ffn": r["ffn_sum"], "full": r["full_sum"], "att": r["att_sum"], "conv": r["conv_sum"],
            "local": r["local_sum"],
        }
        sums = Sums(r, jobs, spot, sizes, sources, sinks, local)
        ring = [peer(spot, "y", step, sizes)[1] for step in range(1, parts)]
        others = [(here + step) % parts for step in range(1, parts)]
        number = here * 2 + core
        eights = [(number + step) % eight for step in range(1, eight)]
        eight_at = [(other // 2, base + other % 2) for other in eights]
        greet(
            eight_at
            + [peer(spot, axis, step, sizes)[1] for axis in ("x", "z") for step in range(1, sizes[axis])]
        )
        sent = []

        def swap(source, target):
            target_copies = [
                move(source.at[other], target.at[here], device) for other, device in zip(others, ring)
            ]
            target[here] = source[here]
            sent.extend(target_copies)
            return target_copies

        swapped = swap(r["gctx"], r["gctx_in"])
        sums.start("ffn")
        for copy in swapped:
            copy.wait_recv()
        attention_back_step(r, micros, frames)

        terms, held = r["terms"], r["terms_held"]
        middle = mine // 2
        near, far = pl.ds(0, middle), pl.ds(middle, middle)
        right, across, left = [(here + step) % 4 for step in (1, 2, 3)]
        to_right, to_left = ring[0], ring[2]
        ringing = [
            move(terms.at[across, near], held.at[0], to_right),
            move(terms.at[across, far], held.at[1], to_left),
            move(terms.at[right, far], held.at[2], to_right),
            move(terms.at[left, near], held.at[3], to_left),
        ]
        attention_weight_step(r)
        ringing[0].wait_recv()
        terms[right, near] = terms[right, near] + held[0]
        ringing.append(move(terms.at[right, near], held.at[4], to_right))
        ringing[1].wait_recv()
        terms[left, far] = terms[left, far] + held[1]
        ringing.append(move(terms.at[left, far], held.at[5], to_left))
        sums.pump("ffn")
        sums.start("att")
        for copy in ringing[2:]:
            copy.wait_recv()
        r["terms_sum"][near] = widen(terms[here, near]) + widen(held[4]) + widen(held[3])
        r["terms_sum"][far] = widen(terms[here, far]) + widen(held[2]) + widen(held[5])
        sent.extend(ringing)
        norm_back_step(r)
        swapped = swap(r["gpos"], r["gpos_in"])
        vectors_step(r, own)
        sums.start("full")
        sums.pump("ffn")
        sums.pump("att")
        for copy in swapped:
            copy.wait_recv()
        conv_back_step(r, here, micros, frames, tall, per)
        sums.start("conv")

        target = r["slopes_all"]
        middle = rows // 2
        near, far = pl.ds(0, middle), pl.ds(middle, middle)
        ringing = [
            move(target.at[here, near], target.at[here, near], to_right),
            move(target.at[here, far], target.at[here, far], to_left),
            move(target.at[here, far], target.at[here, far], to_right),
            move(target.at[here, near], target.at[here, near], to_left),
        ]
        ringing[0].wait_recv()
        ringing.append(move(target.at[left, near], target.at[left, near], to_right))
        ringing[1].wait_recv()
        ringing.append(move(target.at[right, far], target.at[right, far], to_left))
        sums.pump("ffn", "att", "full")
        sums.pump("conv")
        for copy in ringing[2:]:
            copy.wait_recv()
        sent.extend(ringing)
        sums.pump("ffn", "att", "full")
        finish_step(r, spot, own, own_in)
        sums.start("local")
        sums.pump("conv", "ffn", "att", "full")
        sums.pump("local")
        sums.drain("ffn", "att")

        for j in range(eight):
            at = slice(j * own, (j + 1) * own)
            r["block"][j, :own, : deep + 128] = r["ffn_sum"][at, half:]
            r["block"][j, :own, deep + 128 :] = r["att_sum"][at]
        for k in range(2):
            r["pair"][k] = r["ffn_sum"][k * own_ret : (k + 1) * own_ret, :half]
        last = [
            move(r["block"].at[other], r["block_in"].at[number], device)
            for other, device in zip(eights, eight_at)
        ]
        last.append(move(r["pair"].at[1 - core], r["pair_in"].at[core], (here, base + 1 - core)))
        r["block_in"][number] = r["block"][number]
        r["pair_in"][core] = r["pair"][core]
        sums.drain("conv", "full", "local")
        for copy in last:
            copy.wait()
        for copy in sent:
            copy.wait_send()
        sums.close()

    return dict(
        zip(
            outs,
            call_remote(
                kernel,
                [jax.ShapeDtypeStruct(shape, kind) for shape, kind in outs.values()],
                [pl.BlockSpec(memory_space=spaces.get(name, pltpu.VMEM)) for name in ins],
                whole(len(outs)),
                list(scratch.values())
                + [
                    pltpu.SemaphoreType.DMA((4,)),
                    pltpu.SemaphoreType.DMA((copies,)),
                    pltpu.SemaphoreType.DMA((copies,)),
                ],
                ident, *ins.values(),
            ),
        )
    )


def per_device(
    features, lengths, input_gain, input_bias, proj_weight, proj_bias, conv_weight, conv_bias,
    encoder_gain, encoder_bias, attend_weight, query_bias, value_bias, output_weight, output_bias,
    attend_gain, attend_bias, hidden_weight, hidden_bias, return_weight, return_bias, final_gain,
    final_bias, out_grad,
):
    parts = lax.axis_size("ch")
    ranks = lax.axis_size("rows")
    side = math.isqrt(ranks // 2)
    sizes = {"y": parts, "x": side, "z": side, "k": 2}
    here = lax.axis_index("ch").astype(jnp.int32).reshape(1)
    micros, _, frames, narrow = features.shape
    own = proj_bias.shape[0]
    width = proj_weight.shape[1]
    quarter = width // parts
    inner, taps = conv_weight.shape[1:]
    blocks = taps // FOLD
    hidden = hidden_weight.shape[1]
    own_in = input_gain.shape[0]
    own_hid = hidden_bias.shape[0]
    seg = out_grad.shape[2]
    eight = 2 * parts
    squares = side * side
    tall = eight * own
    deep, thin, att = hidden // eight, width // eight, 3 * quarter // 2
    half = width // 2
    rows = micros * frames
    mine = micros * seg
    fold = FOLD * inner
    spans = lengths.reshape(micros)

    cut = jnp.concatenate(
        [
            hidden_weight.reshape(own, eight, deep),
            output_weight.reshape(own, eight, thin),
            attend_weight.reshape(own, 3, parts, quarter).transpose(0, 2, 1, 3).reshape(own, eight, att),
        ],
        axis=2,
    ).transpose(1, 0, 2)
    cut = jnp.pad(cut, ((0, 0), (0, -own % 16), (0, 0)))
    first = proj_weight.reshape(own_in, eight, thin).transpose(1, 0, 2).reshape(eight, 1, -1)
    lanes_cut = cut.shape[2]
    first = jnp.pad(first, ((0, 0), (0, 0), (0, -first.shape[2] % lanes_cut)))
    first = first.reshape(eight, -1, lanes_cut)
    first = jnp.pad(first, ((0, 0), (0, -first.shape[1] % 16), (0, 0)))
    cut = jnp.concatenate([cut, first], axis=1)
    tall_cut = own + -own % 16
    pair = return_weight.reshape(-1, 2, half).transpose(1, 0, 2)
    own_ret = pair.shape[1]
    pair = jnp.pad(pair, ((0, 0), (0, -own_ret % 16), (0, 0)))
    cut, pair = over_eight(cut, pair, 0, parts)
    first = cut[:, tall_cut:].reshape(eight, -1)[:, : own_in * thin].reshape(eight * own_in, thin)
    cut = cut[:, :own].reshape(tall, lanes_cut)
    pair = pair[:, :own_ret].reshape(2 * own_ret, half)
    slab = jnp.concatenate(
        [pair, cut[:, :deep], jnp.pad(cut[:, deep : deep + thin], ((0, 0), (0, -thin % 128)))], axis=1
    )
    everything = lax.all_gather(slab, ALL, axis=0, tiled=False)
    everything = everything.reshape(parts, squares, 2, tall, -1)

    small = jnp.stack(
        [proj_bias, conv_bias, encoder_gain, encoder_bias, query_bias, value_bias, output_bias,
         attend_gain, attend_bias, return_bias, final_gain, final_bias]
    )
    packed = jnp.concatenate([small.reshape(-1), input_gain, input_bias, hidden_bias])
    spare = 128 - thin
    vector_rows = -(-packed.shape[0] // spare)
    vector_rows = vector_rows + -vector_rows % 4
    packed = jnp.pad(packed, (0, vector_rows * spare - packed.shape[0])).reshape(vector_rows, spare)
    packed = jnp.pad(packed, ((0, first.shape[0] - vector_rows), (0, 0)))
    early = jnp.concatenate([first, packed], axis=1)
    folded = conv_weight.reshape(own, inner, blocks, FOLD).transpose(0, 2, 3, 1)
    folded = folded.reshape(own * blocks, fold)
    own_att = cut[:, deep + thin :]
    second = jnp.concatenate([folded, jnp.pad(own_att, ((0, 0), (0, -att % 128)))], axis=1)
    lanes_b = second.shape[1]
    split_b = lanes_b // 256 * 128
    early, second = gather_jobs(
        [early, second],
        [
            (("y", "x", "z"), [(0, early.shape[0], 0, 128)], [("z", "x", "y")]),
            (
                ("x", "z"),
                [(0, tall, 0, split_b), (0, tall, split_b, lanes_b - split_b)],
                [("z", "x"), ("x", "z")],
            ),
        ],
        1, sizes,
    )
    early = early.reshape(2, parts, squares, -1, 128)
    second = second.reshape(2, squares, tall, lanes_b)
    vectors = early[:, :, :, :vector_rows, thin:].transpose(1, 2, 0, 3, 4)
    vectors = widen(vectors.reshape(parts * ranks, -1))
    proj, attend, conv, conv_turned, table, quarters, columns, edges, hid_bias = prepare(
        early, second, vectors, sizes, own, own_in, own_hid, thin, att, inner, blocks, small.shape[0]
    )

    gathered = over_ch(features.reshape(rows, narrow), 2, "gather", parts)
    summed, padded, before = front(
        gathered, spans, here, proj, conv, quarters, columns, edges, micros, frames
    )
    summed = over_ch(summed, 3, "gather", parts)
    low, joint, probs, context = attention(summed, spans, here, attend, quarters, micros, frames)
    context = over_ch(context, 4, "swap", parts)
    output, grad_attn, grad_context, ffn, normal, scale, owned = feed_forward(
        context, summed, here, out_grad.reshape(mine, width), everything, table, hid_bias, micros,
        frames, thin, own, own_hid,
    )
    third = backward_rest(
        {
            "gctx": grad_context, "low": low, "joint": joint, "probs": probs, "attend": attend,
            "grad_attn": grad_attn, "normal": normal, "scale": scale, "table": table, "owned": owned,
            "before": before, "padded": padded, "spans": spans,
            "conv_turned": conv_turned, "gathered": gathered, "proj": proj, "edges": edges,
            "ffn": ffn.reshape(2, parts, side, side, tall, -1),
        },
        sizes, 9, micros, frames, own, own_in, own_hid, own_ret, thin,
    )

    cut = third["block_in"][:, :own].transpose(1, 0, 2)
    hidden_share = cut[:, :, :deep].reshape(hidden_weight.shape)
    output_share = cut[:, :, deep : deep + thin].reshape(output_weight.shape)
    attend_share = cut[:, :, deep + 128 : deep + 128 + att]
    attend_share = attend_share.reshape(own, parts, 3, quarter).transpose(0, 2, 1, 3)
    return_share = third["pair_in"].transpose(1, 0, 2).reshape(return_weight.shape)
    conv_share = third["conv_sum"].reshape(own, blocks, FOLD, inner).transpose(0, 3, 1, 2)
    features_grad = third["features_grad"]
    local = third["local_sum"]
    tail = local[own_in]
    full = third["full_sum"][0]
    local_parts = [tail[i * own : (i + 1) * own] for i in range(4)]
    full_parts = [full[i * own : (i + 1) * own] for i in range(8)]
    return (
        output.reshape(out_grad.shape),
        features_grad.reshape(features.shape),
        tail[4 * own : 4 * own + own_in],
        tail[4 * own + own_in : 4 * own + 2 * own_in],
        local[:own_in],
        local_parts[0],
        conv_share.reshape(conv_weight.shape),
        local_parts[1],
        full_parts[0],
        full_parts[1],
        attend_share.reshape(attend_weight.shape),
        local_parts[2],
        local_parts[3],
        output_share,
        full_parts[2],
        full_parts[3],
        full_parts[4],
        hidden_share,
        full[8 * own : 8 * own + own_hid],
        return_share,
        full_parts[5],
        full_parts[6],
        full_parts[7],
    )


def solution(mesh):
    vector, matrix, cube = P(ALL), P(ALL, None), P(ALL, None, None)
    weights = (
        vector, vector, matrix, vector, cube, vector, vector, vector, matrix, vector, vector,
        matrix, vector, vector, vector, matrix, vector, matrix, vector, vector, vector,
    )
    by_channel = P(None, "rows", None, "ch")
    by_frame = P(None, "rows", "ch", None)
    return jax.shard_map(
        per_device,
        mesh=mesh,
        in_specs=(by_channel, P(None, "rows")) + weights + (by_frame,),
        out_specs=(by_frame, by_channel) + weights,
        check_vma=False,
    )
```

```python
import functools
import math

import jax
import jax.numpy as jnp
import numpy as np
from jax import lax
from jax.experimental import pallas as pl
from jax.experimental.pallas import tpu as pltpu
from jax.sharding import PartitionSpec as P

HEAD_DIM = 64
EPS = 1e-05
NEGATIVE = -1000000000.0
FOLD = 16
ALL = ("ch", "rows")
LOW = jnp.bfloat16
MESH = pl.DeviceIdType.MESH
ROOM = 62 * 1024 * 1024


def widen(values):
    return values.astype(jnp.float32)


def dot(left, right):
    return jnp.dot(left, right, preferred_element_type=jnp.float32)


def contract(spec, left, right):
    return jnp.einsum(spec, left, right, preferred_element_type=jnp.float32)


def place(side):
    rank = lax.axis_index("rows")
    return {
        "y": lax.axis_index("ch"),
        "x": rank // (2 * side),
        "z": (rank // 2) % side,
        "k": rank % 2,
    }


def peer(spot, axis, step, sizes):
    moved = dict(spot)
    moved[axis] = (spot[axis] + step) % sizes[axis]
    return moved, (moved["y"], (moved["x"] * sizes["z"] + moved["z"]) * 2 + moved["k"])


def greet(targets):
    barrier = pltpu.get_barrier_semaphore()
    for target in targets:
        pl.semaphore_signal(barrier, inc=1, device_id=target, device_id_type=MESH)
    pl.semaphore_wait(barrier, len(targets))


def send(source, target, send_sem, recv_sem, device):
    copy = pltpu.make_async_remote_copy(
        src_ref=source, dst_ref=target, send_sem=send_sem, recv_sem=recv_sem,
        device_id=device, device_id_type=MESH,
    )
    copy.start()
    return copy


def whole(count):
    return [pl.BlockSpec(memory_space=pltpu.VMEM)] * count


def call_remote(kernel, shapes, ins, outs, scratch, ident, *values):
    return pl.pallas_call(
        kernel,
        out_shape=shapes,
        in_specs=ins,
        out_specs=outs,
        scratch_shapes=scratch,
        compiler_params=pltpu.CompilerParams(
            collective_id=ident, has_side_effects=True, vmem_limit_bytes=ROOM
        ),
    )(*values)


def window(axes, fixed, cut):
    lead = tuple(fixed.get(axis, slice(None)) for axis in axes)
    return lead + (pl.ds(cut[0], cut[1]), pl.ds(cut[2], cut[3]))


def loop_blocks(dims, body):
    count = math.prod(dims)
    if count == 1:
        body((0,) * len(dims))
        return

    def step(flat, carry):
        index = []
        rest = flat
        for size in reversed(dims):
            index.append(rest % size)
            rest = rest // size
        body(tuple(reversed(index)))
        return carry

    lax.fori_loop(0, count, step, 0)


def dot_nt(left, right):
    return lax.dot_general(left, right, (((1,), (1,)), ((), ())), preferred_element_type=jnp.float32)


def dot_tn(left, right):
    return lax.dot_general(left, right, (((0,), (0,)), ((), ())), preferred_element_type=jnp.float32)


def pick(left, onehot):
    return dot(left, onehot).astype(LOW)


def pick_wide(values, onehot):
    high = values.astype(LOW)
    rest = (values - widen(high)).astype(LOW)
    return dot(high, onehot) + dot(rest, onehot)


def smooth(values):
    return 0.5 * values * (1.0 + lax.erf(values * 0.7071067811865476))


def smooth_slope(values):
    return 0.5 * (1.0 + lax.erf(values * 0.7071067811865476)) + values * 0.3989422804014327 * jnp.exp(
        -0.5 * values * values
    )


def norm(values):
    mean = jnp.mean(values, axis=-1, keepdims=True)
    centred = values - mean
    scale = lax.rsqrt(jnp.mean(centred * centred, axis=-1, keepdims=True) + EPS)
    return centred * scale, scale


def norm_back(incoming, normal, scale, gain):
    scaled = incoming * gain
    first = jnp.mean(scaled, axis=-1, keepdims=True)
    second = jnp.mean(scaled * normal, axis=-1, keepdims=True)
    return scale * (scaled - first - normal * second)


def norm_blocks(blocks):
    size = sum(block.shape[-1] for block in blocks)
    mean = sum(jnp.sum(block, axis=-1, keepdims=True) for block in blocks) / size
    centred = [block - mean for block in blocks]
    spread = sum(jnp.sum(block * block, axis=-1, keepdims=True) for block in centred) / size
    scale = lax.rsqrt(spread + EPS)
    return [block * scale for block in centred], scale


def column_sum(values):
    return jnp.sum(values, axis=0, keepdims=True)


def local_call(kernel, shapes, scratch, *values):
    count = len(values)
    return pl.pallas_call(
        kernel,
        out_shape=[jax.ShapeDtypeStruct(shape, kind) for shape, kind in shapes],
        in_specs=[
            pl.BlockSpec(memory_space=pltpu.SMEM if value.dtype == jnp.int32 else pltpu.VMEM)
            for value in values
        ],
        out_specs=whole(len(shapes)),
        scratch_shapes=scratch,
        compiler_params=pltpu.CompilerParams(vmem_limit_bytes=ROOM),
    )(*values)


def onehot(rows, columns):
    return (np.asarray(rows)[:, None] == np.asarray(columns)[None, :]).astype(LOW)


def natural_of(count, parts, squares):
    cells = np.arange(count).reshape(parts, squares, 2, -1)
    return cells.transpose(1, 0, 2, 3).reshape(count)


def fold_rows(padded, spread_ref, inner):
    for j in range(FOLD):
        moved = padded if j == 0 else pltpu.roll(padded, padded.shape[1] - j, 1)
        spread_ref[j * inner : (j + 1) * inner, :] = moved.astype(LOW)


def spread_blocks(padded, spread_ref, inner, blocks):
    for b in range(blocks):
        moved = padded if b == 0 else pltpu.roll(padded, FOLD * b, 1)
        spread_ref[b * inner : (b + 1) * inner, :] = moved.astype(LOW)


def own_frames(ref, spot, micros, frames, parts):
    seg = frames // parts
    blocks = []
    for c in range(parts):
        pieces = [
            widen(ref[c, pl.ds(pl.multiple_of(m * frames + spot * seg, seg), seg)])
            for m in range(micros)
        ]
        blocks.append(jnp.concatenate(pieces, axis=0))
    return blocks


def feed_forward(
    context, summed, here, upstream, weights, table, hid_bias, micros, frames, thin, own, own_hid
):
    parts, mine, quarter = context.shape
    weights = weights.reshape(2, parts, -1, *weights.shape[-2:])
    squares, tall, lanes = weights.shape[2:]
    width = parts * quarter
    half, deep = width // 2, lanes - width // 2 - 128
    eight = 2 * parts
    nat = onehot(np.arange(width), natural_of(width, parts, squares))
    spots = np.arange(width)
    place = np.zeros((width // 128, 256, 128), np.float32)
    for tile in range(width // 128):
        first = tile * 128 // thin
        for lane in range(128):
            channel = tile * 128 + lane
            place[tile, (channel // thin - first) * 128 + channel % thin, lane] = 1.0
    cut = np.stack([onehot(spots, np.where(np.arange(128) < thin, j * thin + np.arange(128), -1)) for j in range(eight)])
    f32 = jnp.float32
    hidden = eight * deep
    devices = 2 * parts * squares
    lane = np.arange(8 * own + own_hid + -(8 * own + own_hid) % 128)
    mask = onehot(np.arange(devices), np.arange(width) // own)
    mask_hid = onehot(np.arange(devices), np.arange(hidden) // own_hid)
    spread = onehot(np.arange(width) % own, lane)
    spread_hid = onehot(
        np.arange(hidden) % own_hid, np.where(lane >= 8 * own, lane - 8 * own, -1)
    )

    def kernel(
        ctx_ref, sum_ref, here_ref, up_ref, w_ref, table_ref, hid_ref, nat_ref, place_ref, cut_ref,
        mask_ref, mask_hid_ref, spread_ref, spread_hid_ref,
        out_ref, grad_out, gctx_out, slabs_out, normal_out, scale_out, owned_out,
        pre_ref, act_ref, wout_ref, hid_out,
    ):
        spot = here_ref[0]

        def block(c, k, begin, size):
            return w_ref[k, c, :, :, begin : begin + size].reshape(width, size)

        for tile in range(width // 128):
            first = tile * 128 // thin
            last = min(first + 1, eight - 1)
            both = [block(j // 2, j % 2, half + deep, 128) for j in (first, last)]
            wout_ref[:, tile * 128 : (tile + 1) * 128] = pick(jnp.concatenate(both, axis=1), place_ref[tile])
        normal, scale = norm_blocks(own_frames(sum_ref, spot, micros, frames, parts))
        normal = jnp.concatenate(normal, axis=1)
        normal_out[...] = normal
        scale_out[...] = jnp.broadcast_to(scale, scale_out.shape)
        encoded = normal * table_ref[2:3] + table_ref[3:4]
        ctx_slab = sum(
            dot(ctx_ref[c], nat_ref[c * quarter : (c + 1) * quarter]) for c in range(parts)
        ).astype(LOW)
        attn_sum = encoded + dot(ctx_slab, wout_ref[...]) + table_ref[6:7]
        normal_att, scale_att = norm(attn_sum)
        attn_norm = normal_att * table_ref[7:8] + table_ref[8:9]
        attn_slab = pick(attn_norm.astype(LOW), nat_ref[...])
        outer = [jnp.zeros((mine, half), f32), jnp.zeros((mine, half), f32)]
        for c in range(parts):
            for k in range(2):
                begin = (2 * c + k) * deep
                pre = dot(attn_slab, block(c, k, half, deep)) + hid_ref[:, begin : begin + deep]
                pre_ref[:, begin : begin + deep] = pre
                act_ref[:, begin : begin + deep] = smooth(pre).astype(LOW)
            act = act_ref[:, 2 * c * deep : 2 * (c + 1) * deep]
            outer = [outer[k] + dot(act, block(c, k, 0, half)) for k in range(2)]
        ffn_sum = attn_norm + jnp.concatenate(outer, axis=1) + table_ref[9:10]
        normal_fin, scale_fin = norm(ffn_sum)
        out_ref[...] = (normal_fin * table_ref[10:11] + table_ref[11:12]).astype(LOW)
        up = widen(up_ref[...])
        grad_ffn = norm_back(up, normal_fin, scale_fin, table_ref[10:11])
        slope_outer = grad_ffn.astype(LOW)
        vectors = {
            5: column_sum(widen(slope_outer)), 6: column_sum(up * normal_fin), 7: column_sum(up)
        }
        grad_slab = jnp.zeros((mine, width), f32)
        attn_turned = widen(attn_slab).T.astype(LOW)
        for c in range(parts):
            columns = slice(2 * c * deep, 2 * (c + 1) * deep)
            grad_act = sum(
                dot_nt(slope_outer[:, k * half : (k + 1) * half], block(c, k, 0, half)) for k in range(2)
            )
            slope_inner = (grad_act * smooth_slope(pre_ref[:, columns])).astype(LOW)
            hid_out[:, columns] = column_sum(widen(slope_inner))
            act_turned = widen(act_ref[:, columns]).T.astype(LOW)
            for k in range(2):
                inner_k = slope_inner[:, k * deep : (k + 1) * deep]
                grad_slab = grad_slab + dot_nt(inner_k, block(c, k, half, deep))
                grad_ret = dot(act_turned, slope_outer[:, k * half : (k + 1) * half]).astype(LOW)
                slabs_out[k, c, :, :, :half] = grad_ret.reshape(squares, tall, half)
                grad_hid = dot(attn_turned, inner_k).astype(LOW)
                slabs_out[k, c, :, :, half : half + deep] = grad_hid.reshape(squares, tall, deep)
        high = grad_slab.astype(LOW)
        rest = (grad_slab - widen(high)).astype(LOW)
        grad_norm2 = grad_ffn + dot_nt(high, nat_ref[...]) + dot_nt(rest, nat_ref[...])
        vectors[3] = column_sum(grad_norm2 * normal_att)
        vectors[4] = column_sum(grad_norm2)
        grad_attn = norm_back(grad_norm2, normal_att, scale_att, table_ref[7:8])
        grad_out[...] = grad_attn
        slope_att = grad_attn.astype(LOW)
        vectors[2] = column_sum(widen(slope_att))
        owned = dot((widen(mask_hid_ref[...]) * hid_out[...]).astype(LOW), spread_hid_ref[...])
        for v, vector in vectors.items():
            owned = owned + owner_rows(vector, mask_ref[...], spread_ref[...], v * own)
        owned_out[...] = owned
        gctx_slab = dot_nt(slope_att, wout_ref[...]).astype(LOW)
        for c in range(parts):
            gctx_out[c] = dot_nt(gctx_slab, nat_ref[c * quarter : (c + 1) * quarter]).astype(LOW)
        ctx_turned = widen(ctx_slab).T.astype(LOW)
        for c in range(parts):
            for k in range(2):
                grad = dot(ctx_turned, pick(slope_att, cut_ref[2 * c + k])).astype(LOW)
                slabs_out[k, c, :, :, half + deep :] = grad.reshape(squares, tall, 128)

    return local_call(
        kernel,
        [
            ((mine, width), LOW), ((mine, width), f32), ((parts, mine, quarter), LOW),
            ((2, parts, squares, tall, lanes), LOW), ((mine, width), f32), ((mine, 128), f32),
            ((devices, len(lane)), f32),
        ],
        [
            pltpu.VMEM((mine, hidden), f32), pltpu.VMEM((mine, hidden), LOW),
            pltpu.VMEM((width, width), LOW), pltpu.VMEM((1, hidden), f32),
        ],
        context, summed, here, upstream, weights, table, hid_bias,
        *[jnp.asarray(v, LOW) for v in (nat, place, cut, mask, mask_hid, spread, spread_hid)],
    )


def gather_copies(jobs, sizes):
    total = 0
    for job in jobs.values():
        for order in job["orders"]:
            total += 1
            for number, axis in enumerate(order):
                total += 6 if number > 0 and sizes[axis] == 4 else sizes[axis] - 1
    return total


class Gathers:
    def __init__(self, buffers, jobs, spot, sizes, move):
        self.buffers, self.jobs, self.spot, self.sizes, self.move = buffers, jobs, spot, sizes, move
        self.states, self.finished = {}, []

    def send(self, name, cut, fixed, device):
        axes = self.jobs[name]["axes"]
        view = self.buffers[name].at[(self.spot["k"],) + window(axes, fixed, cut)]
        copy = self.move(view, view, device)
        self.finished.append(copy)
        return copy

    def own(self, name):
        axes = self.jobs[name]["axes"]
        return self.buffers[name].at[(self.spot["k"],) + tuple(self.spot[a] for a in axes)]

    def start(self, name):
        job = self.jobs[name]
        self.states[name] = [
            {"cut": cut, "order": order, "step": 0, "copies": [], "half": False}
            for cut, order in zip(job["cuts"], job["orders"])
        ]
        self.pump(name)

    def pump(self, *names):
        for name in names:
            for state in self.states[name]:
                self.advance(name, state)

    def drain(self, *names):
        while any(s["step"] <= len(s["order"]) + 1 for name in names for s in self.states[name]):
            self.pump(*names)

    def advance(self, name, state):
        step, order, cut = state["step"], state["order"], state["cut"]
        if step > len(order) + 1:
            return
        if state["half"]:
            axis, halved, near, far, fixed = state["half"]
            for slot, turn, half in ((0, 3, near), (1, 1, far)):
                state["copies"][slot].wait_recv()
                spot = peer(self.spot, axis, turn, self.sizes)[0]
                device = peer(self.spot, axis, 4 - turn, self.sizes)[1]
                at = dict(fixed)
                at[axis], at[halved] = spot[axis], half
                state["copies"].append(self.send(name, cut, at, device))
            state["half"] = False
            return
        for copy in state["copies"][2 if len(state["copies"]) == 6 else 0 :]:
            copy.wait_recv()
        state["copies"] = []
        state["step"] = step + 1
        if step > len(order):
            return
        if step == len(order):
            device = peer(self.spot, "k", 1, self.sizes)[1]
            state["copies"] = [self.send(name, cut, {}, device)]
            return
        axis = order[step]
        fixed = {a: self.spot[a] for a in order[step:]}
        if step > 0 and self.sizes[axis] == 4:
            halved = order[0]
            size = self.sizes[halved] // 2
            near, far = pl.ds(0, size), pl.ds(size, size)
            for half, turn in ((near, 1), (far, 3), (far, 1), (near, 3)):
                at = dict(fixed)
                at[halved] = half
                device = peer(self.spot, axis, turn, self.sizes)[1]
                state["copies"].append(self.send(name, cut, at, device))
            state["half"] = (axis, halved, near, far, fixed)
        else:
            for turn in range(1, self.sizes[axis]):
                device = peer(self.spot, axis, turn, self.sizes)[1]
                state["copies"].append(self.send(name, cut, fixed, device))

    def close(self):
        for copy in self.finished:
            copy.wait_send()


class Ring:
    def __init__(self, move, buffer, begin, count, here, to_right, to_left):
        self.move, self.buffer, self.here = move, buffer, here
        self.to_right, self.to_left = to_right, to_left
        half = count // 2
        self.near, self.far = pl.ds(begin, half), pl.ds(begin + half, half)
        self.copies = [
            self.shift(here, self.near, to_right), self.shift(here, self.far, to_left),
            self.shift(here, self.far, to_right), self.shift(here, self.near, to_left),
        ]

    def shift(self, block, rows, device):
        view = self.buffer.at[block, rows]
        return self.move(view, view, device)

    def relay(self):
        self.copies[0].wait_recv()
        self.copies.append(self.shift((self.here + 3) % 4, self.near, self.to_right))
        self.copies[1].wait_recv()
        self.copies.append(self.shift((self.here + 1) % 4, self.far, self.to_left))

    def finish(self):
        for copy in self.copies[2:]:
            copy.wait_recv()

    def close(self):
        for copy in self.copies:
            copy.wait_send()


def slabs_step(r, own, deep, thin, att):
    f32 = jnp.float32
    blocks = r["blocks_in"][...].reshape(-1, r["blocks_in"].shape[2])
    main = dot(r["slab_rows"][...], blocks)
    pair = dot(r["pair_rows"][...], r["pair_in"][...].reshape(-1, r["pair_in"].shape[2]))
    tall = main.shape[0]
    r["ffn_slab"][...] = jnp.concatenate(
        [pair, main[:, :deep], main[:, deep : deep + thin], jnp.zeros((tall, 128 - thin), f32)], axis=1
    ).astype(LOW)
    att_slab = jnp.concatenate(
        [main[:, deep + thin :], jnp.zeros((tall, -att % 128), f32)], axis=1
    ).astype(LOW)
    early = (dot(r["first_rows"][...], blocks[:, :128]) + widen(r["packed"][...])).astype(LOW)
    return att_slab, early


def vectors_ready_step(r, parts, quarter):
    wide_in = r["nat_in"].shape[0]
    width = r["table"].shape[1]
    for c in range(parts):
        both = [r["early_all"][k, c].reshape(wide_in, 128) for k in range(2)]
        slab_cols = pick(jnp.concatenate(both, axis=1), r["place_in"][...])
        r["proj"][c] = pick(r["nat_in"][...], slab_cols)
    devices = r["vector_rows"].shape[1]
    high = r["vector_rows"].shape[2] // devices
    cells = widen(r["early_all"][...].reshape(devices, -1, 128)[:, : -(-high // 16) * 16])
    cells = cells[:, :high].reshape(devices * high, 128).astype(LOW)
    turned = []
    for number in range(r["vector_rows"].shape[0]):
        turned.append(dot(r["vector_rows"][number], cells))
    lanes = jnp.concatenate([piece[:, -(128 - r["thin"]) :] for piece in turned], axis=1)
    turned = lanes.T.astype(LOW)
    spread = (dot(turned, r["owner"][...]) * widen(r["take"][...])).astype(LOW)
    table = dot(r["row_of"][...], spread)
    r["table"][...] = table
    for c in range(parts):
        r["quarters"][c] = table[:, c * quarter : (c + 1) * quarter]
    r["columns"][...] = jnp.concatenate([table, jnp.zeros((112, width), jnp.float32)], axis=0).T
    spread = (dot(turned, r["owner_in"][...]) * widen(r["take_in"][...])).astype(LOW)
    r["edges"][...] = dot(r["row_in"][...], spread)
    r["hid_bias"][...] = column_sum(dot(turned, r["owner_hid"][...]) * widen(r["take_hid"][...]))


def conv_ready_step(r, per, side):
    groups, rows, fold = r["conv"].shape
    for g in range(groups):
        taken = jnp.concatenate(
            [
                r["conv_all"][k, (g * per + n) // side, (g * per + n) % side]
                for k in range(2) for n in range(per)
            ],
            axis=0,
        )
        r["conv"][g] = dot(r["conv_order"][...], taken).astype(LOW)


def conv_turned_step(r):
    for g in range(r["conv"].shape[0]):
        r["conv_turned"][g] = widen(r["conv"][g]).T.astype(LOW)


def attend_ready_step(r):
    width = r["nat"].shape[0]
    both = [r["att_all"][k].reshape(width, -1) for k in range(2)]
    slab_cols = pick(jnp.concatenate(both, axis=1), r["place_att"][...])
    r["attend"][...] = pick(r["nat"][...], slab_cols)


def project_step(r, here, m, frames):
    parts, _, narrow = r["gathered"].shape
    groups, _, fold = r["conv"].shape
    inner = fold // FOLD
    half = (r["padded"].shape[2] - frames) // 2
    at = slice(m * frames, (m + 1) * frames)
    normal, _ = norm_blocks([widen(r["gathered"][c, at]) for c in range(parts)])
    low = []
    for c, block in enumerate(normal):
        lanes = slice(c * narrow, (c + 1) * narrow)
        low.append((block * r["edges"][0:1, lanes] + r["edges"][1:2, lanes]).astype(LOW))
    result = dot(jnp.concatenate(low, axis=1), r["proj"][here]) + r["quarters"][here, 0:1]
    live = lax.broadcasted_iota(jnp.int32, (frames, 1), 0) < r["spans"][m]
    turned = jnp.where(live, result, 0.0).T
    for g in range(groups):
        piece = turned[g * inner : (g + 1) * inner]
        r["plain"][m * groups + g] = piece
        edge = jnp.zeros((inner, half), LOW)
        r["padded"][m * groups + g] = jnp.concatenate([edge, piece.astype(LOW), edge], axis=1)


def conv_step(r, here, m, frames):
    groups, many, fold = r["conv"].shape
    inner = fold // FOLD
    blocks = many // inner
    span = r["padded"].shape[2]
    quarter = groups * inner

    def one(g, carry):
        index = m * groups + g
        fold_rows(widen(r["padded"][index]), r["folded"], inner)
        sums = dot(r["conv"][g], r["folded"][...])
        total = sums[:inner, :frames]
        for b in range(1, blocks):
            part = pltpu.roll(sums[b * inner : (b + 1) * inner], span - FOLD * b, 1)
            total = total + part[:, :frames]
        start = pl.multiple_of(here * quarter + g * inner, 16)
        before = total + r["columns"][pl.ds(start, inner), 1:2]
        r["before"][index] = before
        r["plain"][index] = r["plain"][index] + smooth(before)
        return carry

    lax.fori_loop(0, groups, one, 0)
    both = [r["plain"][m * groups + g] for g in range(groups)]
    r["summed"][here, m * frames : (m + 1) * frames] = jnp.concatenate(both, axis=0).T.astype(LOW)


def attention_step(r, here, m, frames):
    parts, _, quarter = r["summed"].shape
    heads = quarter // HEAD_DIM
    seg = frames // parts
    ratio = HEAD_DIM ** (-0.5)
    at = slice(m * frames, (m + 1) * frames)
    normal, _ = norm_blocks([widen(r["summed"][c, at]) for c in range(parts)])
    joint = jnp.zeros((frames, 3 * quarter), jnp.float32)
    for c in range(parts):
        low = (normal[c] * r["quarters"][c, 2:3] + r["quarters"][c, 3:4]).astype(LOW)
        r["low"][c, at] = low
        joint = joint + dot(low, r["attend"][c * quarter : (c + 1) * quarter])
    query = joint[:, :quarter] + r["quarters"][here, 4:5]
    keys = joint[:, quarter : 2 * quarter]
    value = joint[:, 2 * quarter :] + r["quarters"][here, 5:6]
    joint_low = [v.astype(LOW) for v in (query, keys, value)]
    for i in range(3):
        r["joint"][i, at] = joint_low[i]
    value_turned = value.T.astype(LOW)
    live = lax.broadcasted_iota(jnp.int32, (frames, 1), 0) < r["spans"][m]
    results = []
    for h in range(heads):
        cols = slice(h * HEAD_DIM, (h + 1) * HEAD_DIM)
        scores = dot_nt(joint_low[1][:, cols], joint_low[0][:, cols]) * ratio
        scores = jnp.where(live, scores, NEGATIVE)
        expo = jnp.exp(scores - jnp.max(scores, axis=0, keepdims=True))
        probs = (expo / jnp.sum(expo, axis=0, keepdims=True)).astype(LOW)
        r["probs"][m * heads + h] = probs
        results.append(dot(value_turned[cols], probs))
    context = jnp.concatenate(results, axis=0).T.astype(LOW)
    for d in range(parts):
        r["context"][d, m * seg : (m + 1) * seg] = context[d * seg : (d + 1) * seg]


def forward_start(values, sizes, ident, micros, frames, own, own_in, own_hid, own_ret, count):
    parts, squares, side = sizes["y"], sizes["x"] * sizes["z"], sizes["z"]
    devices = 2 * parts * squares
    rows, narrow = values["features"].shape
    eight, tall_block, lanes_cut = values["blocks"].shape
    tall_pair, half = values["pair"].shape[1:]
    tall, fold = values["conv_own"].shape
    width, wide_in, hidden = own * devices, own_in * devices, own_hid * devices
    quarter = width // parts
    inner, blocks = fold // FOLD, tall // own
    groups = quarter // inner
    many = blocks * inner
    per = inner // own // 2
    heads = quarter // HEAD_DIM
    span = frames + blocks * FOLD
    seg = frames // parts
    mine = micros * seg
    deep, thin, att = hidden // eight, width // eight, 3 * quarter // 2
    wide = att + -att % 128
    lanes_a = half + deep + 128
    spare = 128 - thin
    f32 = jnp.float32

    ones = {}
    j, s = np.divmod(np.arange(tall), own)
    ones["slab_rows"] = onehot(j * tall_block + s, np.arange(eight * tall_block))
    j, s = np.divmod(np.arange(eight * own_in), own_in)
    ones["first_rows"] = onehot(j * tall_block + own + s, np.arange(eight * tall_block))
    j, s = np.divmod(np.arange(2 * own_ret), own_ret)
    ones["pair_rows"] = onehot(j * tall_pair + s, np.arange(2 * tall_pair))
    ones["nat_in"] = onehot(np.arange(wide_in), natural_of(wide_in, parts, squares))
    ones["nat"] = onehot(np.arange(width), natural_of(width, parts, squares))
    lanes = np.arange(quarter)
    ones["place_in"] = onehot(np.arange(256), np.where(lanes < thin, lanes, lanes - thin + 128))
    lanes = np.arange(2 * att)
    ones["place_att"] = onehot(np.arange(2 * wide), np.where(lanes < att, lanes, lanes - att + wide))
    slab = np.arange(many).reshape(2, per, own, blocks)
    ones["conv_order"] = onehot(
        [slab[(o // own) % 2, o // own // 2, o % own, b] for b in range(blocks) for o in range(inner)],
        np.arange(many),
    )
    early_rows = eight * own_in
    vector_rows = -(-(count * own + 2 * own_in + own_hid) // spare)
    vector_rows = vector_rows + -vector_rows % (128 // spare)
    spots = np.arange(devices).reshape(2, parts, squares).transpose(1, 2, 0).reshape(-1)
    high = vector_rows + -vector_rows % 8
    ones["vector_rows"] = np.stack(
        [onehot(spots * high + i, np.arange(devices * high)) for i in range(vector_rows)]
    )
    lane = np.arange(vector_rows * spare)
    ask = np.arange(width)
    edge = count * own
    ones["take"] = (lane[:, None] < edge) & (lane[:, None] % own == ask[None, :] % own)
    ones["row_of"] = onehot(np.arange(16), np.where(lane < edge, lane // own, -1))
    ones["owner"] = onehot(np.arange(devices), ask // own)
    ones["owner_in"] = onehot(np.arange(devices), np.arange(wide_in) // own_in)
    ends = (lane >= edge) & (lane < edge + 2 * own_in)
    ones["take_in"] = ends[:, None] & (
        (lane[:, None] - edge) % own_in == (np.arange(wide_in) % own_in)[None, :]
    )
    ones["row_in"] = onehot(np.arange(16), np.where(ends, (lane - edge) // own_in, -1))
    ones["owner_hid"] = onehot(np.arange(devices), np.arange(hidden) // own_hid)
    ones["take_hid"] = onehot(lane, edge + 2 * own_in + np.arange(hidden) % own_hid)

    all_axes, row_axes = ("y", "x", "z"), ("x", "z")
    cut_a = lanes_a // 256 * 128 + 128 * (lanes_a // 128 % 2)
    jobs = {
        "conv_all": {
            "axes": row_axes,
            "cuts": [(0, tall, 0, fold // 2), (0, tall, fold // 2, fold // 2)],
            "orders": [("z", "x"), ("x", "z")],
        },
        "early_all": {
            "axes": all_axes, "cuts": [(0, early_rows, 0, 128)], "orders": [("z", "x", "y")],
        },
        "att_all": {"axes": row_axes, "cuts": [(0, tall, 0, wide)], "orders": [("x", "z")]},
        "weights": {
            "axes": all_axes,
            "cuts": [(0, tall, 0, cut_a), (0, tall, cut_a, lanes_a - cut_a)],
            "orders": [("y", "z", "x"), ("y", "x", "z")],
        },
    }
    copies = gather_copies(jobs, sizes) + eight + 6 * (1 + micros) + micros * (parts - 1)
    lead = (sizes["x"], sizes["z"])
    scratch = {
        "blocks_in": pltpu.VMEM(values["blocks"].shape, LOW),
        "pair_in": pltpu.VMEM(values["pair"].shape, LOW),
        "ffn_slab": pltpu.VMEM((tall, lanes_a), LOW),
        "early_all": pltpu.VMEM((2, parts) + lead + (early_rows, 128), LOW),
        "conv_all": pltpu.VMEM((2,) + lead + (tall, fold), LOW),
        "att_all": pltpu.VMEM((2,) + lead + (tall, wide), LOW),
        "quarters": pltpu.VMEM((parts, 16, quarter), f32),
        "columns": pltpu.VMEM((width, 128), f32),
        "conv": pltpu.VMEM((groups, many, fold), LOW),
        "plain": pltpu.VMEM((micros * groups, inner, frames), f32),
        "folded": pltpu.VMEM((fold, span), LOW),
        "context": pltpu.VMEM((parts, mine, quarter), LOW),
    }
    outs = {
        "weights": ((2, parts) + lead + (tall, lanes_a), LOW),
        "gathered": ((parts, rows, narrow), LOW),
        "proj": ((parts, wide_in, quarter), LOW),
        "table": ((16, width), f32),
        "edges": ((16, wide_in), f32),
        "hid_bias": ((1, hidden), f32),
        "attend": ((width, 3 * quarter), LOW),
        "conv_turned": ((groups, fold, many), LOW),
        "padded": ((micros * groups, inner, span), LOW),
        "before": ((micros * groups, inner, frames), f32),
        "summed": ((parts, rows, quarter), LOW),
        "low": ((parts, rows, quarter), LOW),
        "joint": ((3, rows, quarter), LOW),
        "probs": ((micros * heads, frames, frames), LOW),
        "context_in": ((parts, mine, quarter), LOW),
    }
    ins = dict(values)
    ins.update({name: jnp.asarray(value, LOW) for name, value in ones.items()})
    spaces = {"spans": pltpu.SMEM, "weights": pl.ANY}
    names = list(ins) + list(outs) + list(scratch)

    def kernel(*refs):
        r = dict(zip(names, refs))
        local, send_sems, recv_sems = refs[len(names) :]
        r["thin"] = thin
        spot = place(side)
        here, core, rank = spot["y"], spot["k"], lax.axis_index("rows")
        base = rank - core
        used = [0]

        def move(source, target, device):
            index = used[0]
            used[0] += 1
            return send(source, target, send_sems.at[index], recv_sems.at[index], device)

        gathers = Gathers({name: r[name] for name in jobs}, jobs, spot, sizes, move)
        ring = [peer(spot, "y", step, sizes)[1] for step in range(1, parts)]
        others = [(here + step) % parts for step in range(1, parts)]
        to_right, to_left = ring[0], ring[2]
        number = here * 2 + core
        eights = [(number + step) % eight for step in range(1, eight)]
        eight_at = [(other // 2, base + other % 2) for other in eights]
        r["gathered"][here] = r["features"][...]
        gathers.own("conv_all")[...] = r["conv_own"][...]
        greet(
            eight_at
            + [peer(spot, axis, step, sizes)[1] for axis in ("x", "z") for step in range(1, sizes[axis])]
        )
        sent = [
            move(r["blocks"].at[other], r["blocks_in"].at[number], device)
            for other, device in zip(eights, eight_at)
        ]
        sent.append(move(r["pair"].at[1 - core], r["pair_in"].at[core], (here, base + 1 - core)))
        features = Ring(move, r["gathered"], 0, rows, here, to_right, to_left)
        gathers.start("conv_all")
        r["blocks_in"][number] = r["blocks"][number]
        r["pair_in"][core] = r["pair"][core]
        for copy in sent:
            copy.wait_recv()
        att_slab, early = slabs_step(r, own, deep, thin, att)
        gathers.own("early_all")[...] = early
        gathers.start("early_all")
        gathers.own("att_all")[...] = att_slab
        keep = pltpu.make_async_copy(r["ffn_slab"], gathers.own("weights"), local)
        keep.start()
        gathers.pump("early_all")
        gathers.pump("conv_all")
        gathers.pump("early_all")
        features.relay()
        gathers.pump("early_all")
        gathers.start("att_all")
        gathers.pump("early_all", "conv_all")
        gathers.drain("early_all")
        keep.wait()
        gathers.start("weights")
        vectors_ready_step(r, parts, quarter)
        gathers.pump("conv_all", "att_all")
        features.finish()
        for m in range(micros):
            project_step(r, here, m, frames)
            gathers.pump("conv_all", "att_all", "weights")
        gathers.drain("conv_all")
        conv_ready_step(r, per, side)
        gathers.pump("att_all", "weights")
        rings = []
        for m in range(micros):
            conv_step(r, here, m, frames)
            rings.append(Ring(move, r["summed"], m * frames, frames, here, to_right, to_left))
            if m > 0:
                rings[m - 1].relay()
            gathers.pump("att_all", "weights")
        gathers.drain("att_all")
        attend_ready_step(r)
        rings[-1].relay()
        gathers.pump("weights")
        conv_turned_step(r)
        swaps = []
        for m in range(micros):
            rings[m].finish()
            attention_step(r, here, m, frames)
            cells = pl.ds(m * seg, seg)
            swaps += [
                move(r["context"].at[other, cells], r["context_in"].at[here, cells], device)
                for other, device in zip(others, ring)
            ]
            r["context_in"][here, cells] = r["context"][here, cells]
            gathers.pump("weights")
        gathers.drain("weights")
        for copy in swaps:
            copy.wait()
        for copy in sent:
            copy.wait_send()
        for item in rings + [features, gathers]:
            item.close()

    return dict(
        zip(
            outs,
            call_remote(
                kernel,
                [jax.ShapeDtypeStruct(shape, kind) for shape, kind in outs.values()],
                [pl.BlockSpec(memory_space=spaces.get(name, pltpu.VMEM)) for name in ins],
                [pl.BlockSpec(memory_space=spaces.get(name, pltpu.VMEM)) for name in outs],
                list(scratch.values())
                + [
                    pltpu.SemaphoreType.DMA,
                    pltpu.SemaphoreType.DMA((copies,)),
                    pltpu.SemaphoreType.DMA((copies,)),
                ],
                ident, *ins.values(),
            ),
        )
    )


def stages_of(axes, order, sizes):
    left = list(axes)
    result = []
    for axis in order:
        where = left.index(axis)
        left = left[:where] + left[where + 1 :]
        dims = tuple(sizes[a] for a in left)
        result.append((axis, where, tuple(left), dims, sizes[axis] == 4 and len(dims) > 0))
    return result


def sum_scratch(jobs, sizes):
    scratch, copies = {}, 0
    for name, job in jobs.items():
        for part, (cut, order) in enumerate(zip(job["cuts"], job["orders"])):
            block = (cut[1], cut[3])
            dims = tuple(sizes[a] for a in job["axes"])
            key = f"{name}{part}"
            scratch[key + "got"] = pltpu.VMEM(dims + block, LOW)
            if job["far"]:
                scratch[key + "own"] = pltpu.VMEM((2,) + dims[1:] + block, LOW)
            copies += 1
            for number, (axis, _, _, dims, ring) in enumerate(stages_of(job["axes"], order, sizes)):
                if ring:
                    half = (dims[0] // 2,) + dims[1:] + block
                    scratch[f"{key}got{number}"] = pltpu.VMEM((6,) + half, LOW)
                    copies += 6
                else:
                    scratch[f"{key}got{number}"] = pltpu.VMEM((max(sizes[axis] - 1, 1),) + dims + block, LOW)
                    copies += sizes[axis] - 1
                if dims:
                    scratch[f"{key}sum{number}"] = pltpu.VMEM(dims + block, LOW)
    return scratch, copies


class Sums:
    def __init__(self, refs, jobs, spot, sizes, sources, sinks, local):
        self.refs, self.jobs, self.spot, self.sizes = refs, jobs, spot, sizes
        self.sources, self.sinks, self.local = sources, sinks, local
        self.states, self.finished = {}, []

    def move(self, source, target, device):
        copy = self.refs["move"](source, target, device)
        self.finished.append(copy)
        return copy

    def start(self, name):
        job, core = self.jobs[name], self.spot["k"]
        sibling = peer(self.spot, "k", 1, self.sizes)[1]
        states = []
        for part, (cut, order) in enumerate(zip(job["cuts"], job["orders"])):
            key = f"{name}{part}"
            window_at = window(job["axes"], {}, cut)
            got = self.refs[key + "got"]
            copy = self.move(self.sources[name].at[(1 - core,) + window_at], got, sibling)
            near = None
            if job["far"]:

                def near(number, slot, window_at=window_at, key=key, part=part):
                    return pltpu.make_async_copy(
                        self.sources[name].at[(core, number) + window_at[1:]],
                        self.refs[key + "own"].at[slot], self.local.at[2 * part + slot],
                    )

                near(0, 0).start()
            states.append(
                {
                    "key": key, "cut": cut, "held": got, "left": job["axes"], "step": 0, "near": near,
                    "copies": [copy], "half": False,
                    "stages": stages_of(job["axes"], order, self.sizes),
                }
            )
        self.states[name] = states

    def pump(self, *names):
        for name in names:
            for state in self.states[name]:
                self.advance(name, state)

    def drain(self, *names):
        while any(s["step"] <= len(s["stages"]) for name in names for s in self.states[name]):
            self.pump(*names)

    def advance(self, name, state):
        step, stages = state["step"], state["stages"]
        if step > len(stages):
            return
        if step == 0:
            self.add_own(name, state)
        elif state["half"]:
            self.relay(state, stages[step - 1], step - 1)
            return
        else:
            self.add_stage(name, state, stages[step - 1], step - 1)
        if step < len(stages):
            self.send_stage(state, stages[step], step)
        state["step"] = step + 1

    def add_own(self, name, state):
        for copy in state["copies"]:
            copy.wait_recv()
        held, cut = state["held"], state["cut"]
        dims = tuple(self.sizes[a] for a in state["left"])
        if state["near"] is not None:
            near, own = state["near"], self.refs[state["key"] + "own"]
            for number in range(dims[0]):
                slot = number % 2
                if number + 1 < dims[0]:
                    near(number + 1, 1 - slot).start()
                near(number, slot).wait()

                def add(index, number=number, slot=slot):
                    held[(number,) + index] = held[(number,) + index] + own[(slot,) + index]

                loop_blocks(dims[1:], add)
            return
        else:
            source, core = self.sources[name], self.spot["k"]

            def add(index):
                rows, lanes = slice(cut[0], cut[0] + cut[1]), slice(cut[2], cut[2] + cut[3])
                held[index] = held[index] + source[(core,) + index + (rows, lanes)]

        loop_blocks(dims, add)

    def send_stage(self, state, stage, number):
        axis, _, left, dims, ring = stage
        held, got = state["held"], self.refs[f"{state['key']}got{number}"]
        before = state["left"]
        state["copies"] = []
        if not ring:
            for step in range(1, self.sizes[axis]):
                moved, device = peer(self.spot, axis, step, self.sizes)
                at = tuple(moved[a] if a == axis else slice(None) for a in before)
                state["copies"].append(self.move(held.at[at], got.at[step - 1], device))
        else:
            size = dims[0] // 2
            near, far = pl.ds(0, size), pl.ds(size, size)

            def piece(step, half):
                moved = peer(self.spot, axis, step, self.sizes)[0]
                return held.at[
                    tuple(
                        moved[a] if a == axis else (half if a == left[0] else slice(None)) for a in before
                    )
                ]

            right = peer(self.spot, axis, 1, self.sizes)[1]
            back = peer(self.spot, axis, 3, self.sizes)[1]
            state["copies"] = [
                self.move(piece(2, near), got.at[0], right),
                self.move(piece(2, far), got.at[1], back),
                self.move(piece(1, far), got.at[2], right),
                self.move(piece(3, near), got.at[3], back),
            ]
            state["half"] = True

    def relay(self, state, stage, number):
        axis, where, left, dims, _ = stage
        held = state["held"]
        got = self.refs[f"{state['key']}got{number}"]
        size = dims[0] // 2
        ahead, right = peer(self.spot, axis, 1, self.sizes)
        behind, back = peer(self.spot, axis, 3, self.sizes)
        for slot, spot, offset in ((0, ahead, 0), (1, behind, size)):
            state["copies"][slot].wait_recv()

            def add(index, slot=slot, spot=spot, offset=offset):
                full = (index[0] + offset,) + index[1:]
                full = full[:where] + (spot[axis],) + full[where:]
                held[full] = held[full] + got[(slot,) + index]

            loop_blocks((size,) + dims[1:], add)
            at = tuple(
                spot[a] if a == axis else (pl.ds(offset, size) if a == left[0] else slice(None))
                for a in state["left"]
            )
            state["copies"].append(
                self.move(held.at[at], got.at[4 + slot], (right, back)[slot])
            )
        state["half"] = False

    def add_stage(self, name, state, stage, number):
        axis, where, left, dims, ring = stage
        held, cut = state["held"], state["cut"]
        got = self.refs[f"{state['key']}got{number}"]
        target = self.refs[f"{state['key']}sum{number}"] if dims else None
        mine = self.spot[axis]
        for copy in state["copies"][2 if ring else 0 :]:
            copy.wait_recv()
        if ring:
            size = dims[0] // 2
            for offset, first, second in ((0, 4, 3), (size, 2, 5)):

                def add(index, offset=offset, first=first, second=second):
                    full = (index[0] + offset,) + index[1:]
                    own = full[:where] + (mine,) + full[where:]
                    result = widen(held[own]) + widen(got[(first,) + index]) + widen(got[(second,) + index])
                    target[full] = result.astype(LOW)

                loop_blocks((size,) + dims[1:], add)
        else:

            def add(index):
                index = index if dims else ()
                result = widen(held[index[:where] + (mine,) + index[where:]])
                for step in range(self.sizes[axis] - 1):
                    result = result + widen(got[(step,) + index])
                if target is None:
                    rows, lanes = slice(cut[0], cut[0] + cut[1]), slice(cut[2], cut[2] + cut[3])
                    self.sinks[name][rows, lanes] = result
                else:
                    target[index] = result.astype(LOW)

            loop_blocks(dims if dims else (1,), add)
        state["held"], state["left"] = target, left

    def close(self):
        for copy in self.finished:
            copy.wait_send()


def attention_back_step(r, micros, frames):
    parts, mine, quarter = r["gctx"].shape
    heads = quarter // HEAD_DIM
    seg = frames // parts
    ratio = HEAD_DIM ** (-0.5)
    r["att_sums"][...] = jnp.zeros_like(r["att_sums"])
    r["slope_joint"][...] = jnp.zeros_like(r["slope_joint"])

    def one(m, carry):
        at = pl.ds(pl.multiple_of(m * frames, frames), frames)
        cells = pl.ds(pl.multiple_of(m * seg, seg), seg)
        grad = jnp.concatenate([r["gctx_in"][d, cells] for d in range(parts)], axis=0)
        query, keys, value = r["joint"][0, at], r["joint"][1, at], r["joint"][2, at]
        keys_turned = widen(keys).T.astype(LOW)
        queries, key_parts, values = [], [], []
        for h in range(heads):
            cols = slice(h * HEAD_DIM, (h + 1) * HEAD_DIM)
            probs_low = r["probs"][m * heads + h]
            grad_probs = dot_nt(value[:, cols], grad[:, cols])
            weighted = widen(probs_low) * grad_probs
            centre = jnp.sum(weighted, axis=0, keepdims=True)
            slope = (weighted - widen(probs_low) * centre).astype(LOW)
            values.append(dot(probs_low, grad[:, cols]))
            key_parts.append(dot(slope, query[:, cols]) * ratio)
            queries.append(dot(keys_turned[cols], slope) * ratio)
        slopes = [
            jnp.concatenate(queries, axis=0).T.astype(LOW),
            jnp.concatenate(key_parts, axis=1).astype(LOW),
            jnp.concatenate(values, axis=1).astype(LOW),
        ]
        r["att_sums"][0:1] = r["att_sums"][0:1] + column_sum(widen(slopes[0]))
        r["att_sums"][1:2] = r["att_sums"][1:2] + column_sum(widen(slopes[2]))
        slope = jnp.concatenate(slopes, axis=1)
        size = slope.shape[1] // 2
        for k in range(2):
            r["slope_joint"][k, at, :size] = slope[:, k * size : (k + 1) * size]
        terms = dot_nt(slope, r["attend"][...]).astype(LOW)
        for d in range(parts):
            r["terms"][d, cells] = terms[d * seg : (d + 1) * seg]
        return carry

    lax.fori_loop(0, micros, one, 0)


def attention_weight_step(r):
    parts = r["low"].shape[0]
    for k in range(2):
        pieces = [dot_tn(r["low"][c], r["slope_joint"][k]).astype(LOW) for c in range(parts)]
        grads = dot(r["back_att"][...], jnp.concatenate(pieces, axis=0)).astype(LOW)
        r["att_grad"][k] = grads.reshape(r["att_grad"].shape[1:])


def norm_back_step(r):
    parts, _, quarter = r["gpos"].shape
    normal, scale = r["normal"][...], r["scale"][:, 0:1]
    grad = r["grad_attn"][...] + r["terms_sum"][...]
    result = norm_back(grad, normal, scale, r["table"][2:3]).astype(LOW)
    for c in range(parts):
        r["gpos"][c] = result[:, c * quarter : (c + 1) * quarter]
    r["sums_own"][0:1] = column_sum(grad * normal)
    r["sums_own"][1:2] = column_sum(grad)


def owner_rows(vector, mask, spread, place):
    cells = dot((widen(mask) * vector).astype(LOW), spread)
    return cells if place == 0 else pltpu.roll(cells, place, 1)


def vectors_step(r, own):
    owned = r["owned"][...]
    for v in range(2):
        owned = owned + owner_rows(r["sums_own"][v : v + 1], r["mask"][...], r["spread"][...], v * own)
    r["full"][...] = dot(r["row_full"][...], owned.astype(LOW)).astype(LOW).reshape(r["full"].shape)


def conv_back_step(r, here, micros, frames, tall, per):
    parts, mine, quarter = r["gpos"].shape
    groups, fold, many = r["conv_turned"].shape
    inner = fold // FOLD
    blocks = many // inner
    half = blocks * FOLD // 2
    span = frames + blocks * FOLD
    seg = frames // parts
    side = r["conv_grad"].shape[2]
    f32 = jnp.float32
    for m in range(micros):
        cells = slice(m * seg, (m + 1) * seg)
        grad = jnp.concatenate([widen(r["gpos_in"][d, cells]) for d in range(parts)], axis=0).T
        for g in range(groups):
            r["grads"][m * groups + g] = grad[g * inner : (g + 1) * inner]

    def one(g, carry):
        weight = 0.0
        for m in range(micros):
            index = m * groups + g
            grad = r["grads"][index]
            slope = (grad * smooth_slope(r["before"][index])).astype(LOW).astype(f32)
            r["turn"][index, :, 0:1] = jnp.sum(slope, axis=1, keepdims=True)
            wide = jnp.concatenate([slope, jnp.zeros((inner, span - frames), f32)], axis=1)
            spread_blocks(wide, r["moved"], inner, blocks)
            fold_rows(widen(r["padded"][index]), r["folded"], inner)
            weight = weight + dot_nt(r["moved"][...], r["folded"][...])
            back_sums = dot(r["conv_turned"][g], r["moved"][...])
            total = grad
            for j in range(FOLD):
                part = pltpu.roll(back_sums[j * inner : (j + 1) * inner], (span + j - half) % span, 1)
                total = total + part[:, :frames]
            live = lax.broadcasted_iota(jnp.int32, (1, frames), 1) < r["spans"][m]
            total = jnp.where(live, total, 0.0).astype(LOW).astype(f32)
            r["turn"][index, :, 1:2] = jnp.sum(total, axis=1, keepdims=True)
            r["grads"][index] = total
        weight = dot(r["back_conv"][...], weight.astype(LOW)).astype(LOW).reshape(2, per, tall, fold)
        for n in range(per):
            xz = g * per + n
            for k in range(2):
                r["conv_grad"][k, xz // side, xz % side] = weight[k, n]
        return carry

    lax.fori_loop(0, groups, one, 0)
    for m in range(micros):
        both = [r["grads"][m * groups + g] for g in range(groups)]
        r["slopes_all"][here, m * frames : (m + 1) * frames] = jnp.concatenate(both, axis=0).T.astype(LOW)
    sums = jnp.concatenate(
        [sum(r["turn"][m * groups + g] for m in range(micros)) for g in range(groups)], axis=0
    ).T
    r["conv_sums"][...] = sums[:8]


def finish_step(r, spot, own, own_in):
    parts, rows, narrow = r["gathered"].shape
    ranks, quarter = r["mask_ch"].shape
    width = parts * quarter
    f32 = jnp.float32
    here = spot["y"]
    size = parts * narrow
    chunk = 256
    mine_at = pl.ds(pl.multiple_of(here * narrow, narrow), narrow)
    gain, shift = r["edges"][0:1, mine_at], r["edges"][1:2, mine_at]
    r["edge_sums"][...] = jnp.zeros_like(r["edge_sums"])
    r["proj_grad"][...] = jnp.zeros_like(r["proj_grad"])

    def one(number, carry):
        at = pl.ds(pl.multiple_of(number * chunk, chunk), chunk)
        blocks = [widen(r["gathered"][c, at]) for c in range(parts)]
        slopes = [r["slopes_all"][b, at] for b in range(parts)]
        normal, scale = norm_blocks(blocks)
        first = jnp.zeros((chunk, 1), f32)
        second = jnp.zeros((chunk, 1), f32)
        for c in range(parts):
            lanes = slice(c * narrow, (c + 1) * narrow)
            grad = sum(dot_nt(slopes[b], r["proj"][b, lanes]) for b in range(parts))
            scaled = grad * r["edges"][0:1, lanes]
            first = first + jnp.sum(scaled, axis=1, keepdims=True)
            second = second + jnp.sum(scaled * normal[c], axis=1, keepdims=True)
        mean = sum(jnp.sum(block, axis=1, keepdims=True) for block in blocks) / size
        mine = (widen(r["gathered"][here, at]) - mean) * scale
        grad = sum(dot_nt(slopes[b], r["proj"][b, mine_at]) for b in range(parts))
        r["features_grad"][at] = scale * (grad * gain - first / size - mine * (second / size))
        low = (mine * gain + shift).astype(LOW)
        r["proj_grad"][...] = r["proj_grad"][...] + jnp.concatenate(
            [dot_tn(low, slopes[b]) for b in range(parts)], axis=1
        )
        r["edge_sums"][0:1] = r["edge_sums"][0:1] + column_sum(grad * mine)
        r["edge_sums"][1:2] = r["edge_sums"][1:2] + column_sum(grad)
        return carry

    lax.fori_loop(0, rows // chunk, one, 0)
    vectors = [
        r["conv_sums"][1:2], r["conv_sums"][0:1], r["att_sums"][0:1], r["att_sums"][1:2],
    ]
    owned = 0.0
    for v in range(4):
        owned = owned + owner_rows(vectors[v], r["mask_ch"][...], r["spread_ch"][...], v * own)
    for v in range(2):
        owned = owned + owner_rows(
            r["edge_sums"][v : v + 1], r["mask_in"][...], r["spread_in"][...], 4 * own + v * own_in
        )
    lanes = owned.shape[1]
    owned = jnp.concatenate([owned, jnp.zeros((ranks, width - lanes), f32)], axis=1)
    result = dot(r["row_proj"][...], r["proj_grad"][...].astype(LOW))
    result = result + dot(r["row_vector"][...], owned.astype(LOW))
    r["local"][...] = result.astype(LOW).reshape(r["local"].shape)


def backward_rest(values, sizes, ident, micros, frames, own, own_in, own_hid, own_ret, thin):
    parts, squares, side = sizes["y"], sizes["x"] * sizes["z"], sizes["z"]
    devices, ranks = 2 * parts * squares, 2 * squares
    _, mine, quarter = values["gctx"].shape
    width = parts * quarter
    rows = micros * frames
    narrow = values["gathered"].shape[2]
    groups, fold, many = values["conv_turned"].shape
    inner = fold // FOLD
    blocks = many // inner
    span = frames + blocks * FOLD
    per = inner // own // 2
    tall, lanes_a = values["ffn"].shape[-2:]
    half, deep = width // 2, lanes_a - width // 2 - 128
    att = 3 * quarter // 2
    wide = att + -att % 128
    eight = 2 * parts
    f32 = jnp.float32

    ones = {}
    ones["back_att"] = onehot(natural_of(width, parts, squares), np.arange(width))
    slab = np.arange(many).reshape(2, per, own, blocks)
    ones["back_conv"] = onehot(
        np.arange(many),
        [slab[(o // own) % 2, o // own // 2, o % own, b] for b in range(blocks) for o in range(inner)],
    )
    count = 8 * own + own_hid
    lane = np.arange(count + -count % 128)
    ones["mask"] = onehot(np.arange(devices), np.arange(width) // own)
    ones["spread"] = onehot(np.arange(width) % own, lane)
    full_rows = np.full((devices, 16), -1)
    full_rows[:, 0] = np.arange(devices).reshape(parts, squares, 2).transpose(2, 0, 1).reshape(-1)
    ones["row_full"] = onehot(full_rows.reshape(-1), np.arange(devices))
    few = 4 * own + 2 * own_in
    few = np.arange(few + -few % 128)
    ones["mask_ch"] = onehot(np.arange(ranks), np.arange(quarter) // own)
    ones["spread_ch"] = onehot(np.arange(quarter) % own, few)
    ones["mask_in"] = onehot(np.arange(ranks), np.arange(narrow) // own_in)
    ones["spread_in"] = onehot(np.arange(narrow) % own_in, few)
    high = own_in + 1 + -(own_in + 1) % 16
    order = np.arange(ranks).reshape(squares, 2).T.reshape(-1)
    proj_rows = np.full((ranks, high), -1)
    proj_rows[:, :own_in] = order[:, None] * own_in + np.arange(own_in)[None, :]
    ones["row_proj"] = onehot(proj_rows.reshape(-1), np.arange(narrow))
    vector_rows = np.full((ranks, high), -1)
    vector_rows[:, own_in] = order
    ones["row_vector"] = onehot(vector_rows.reshape(-1), np.arange(ranks))

    cut_lanes = lanes_a // 256 * 128 + 128 * (lanes_a // 128 % 2)
    jobs = {
        "ffn": {
            "axes": ("y", "x", "z"), "far": True,
            "cuts": [(0, tall, 0, cut_lanes), (0, tall, cut_lanes, lanes_a - cut_lanes)],
            "orders": [("x", "z", "y"), ("z", "x", "y")],
        },
        "full": {
            "axes": ("y", "x", "z"), "far": False, "cuts": [(0, 16, 0, len(lane))],
            "orders": [("z", "x", "y")],
        },
        "att": {
            "axes": ("x", "z"), "far": False, "cuts": [(0, tall, 0, wide)], "orders": [("x", "z")],
        },
        "conv": {
            "axes": ("x", "z"), "far": False,
            "cuts": [(0, tall, 0, fold // 2), (0, tall, fold // 2, fold // 2)],
            "orders": [("x", "z"), ("z", "x")],
        },
        "local": {
            "axes": ("x", "z"), "far": False, "cuts": [(0, high, 0, width)], "orders": [("z", "x")],
        },
    }
    scratch, copies = sum_scratch(jobs, sizes)
    copies += 3 * (parts - 1) + 12 + eight
    lead = {"y": parts, "x": sizes["x"], "z": sizes["z"]}
    low_rows = own + -own % 8
    block_lanes = deep + 128 + wide
    scratch.update(
        {
            "gctx_in": pltpu.VMEM((parts, mine, quarter), LOW),
            "terms": pltpu.VMEM((parts, mine, width), LOW),
            "terms_held": pltpu.VMEM((6, mine // 2, width), LOW),
            "terms_sum": pltpu.VMEM((mine, width), f32),
            "slope_joint": pltpu.VMEM((2, rows, wide), LOW),
            "att_grad": pltpu.VMEM((2, sizes["x"], sizes["z"], tall, wide), LOW),
            "att_sums": pltpu.VMEM((8, quarter), f32),
            "gpos": pltpu.VMEM((parts, mine, quarter), LOW),
            "gpos_in": pltpu.VMEM((parts, mine, quarter), LOW),
            "sums_own": pltpu.VMEM((8, width), f32),
            "full": pltpu.VMEM((2, parts, sizes["x"], sizes["z"], 16, len(lane)), LOW),
            "grads": pltpu.VMEM((micros * groups, inner, frames), f32),
            "turn": pltpu.VMEM((micros * groups, inner, 128), f32),
            "moved": pltpu.VMEM((many, span), LOW),
            "folded": pltpu.VMEM((fold, span), LOW),
            "slopes_all": pltpu.VMEM((parts, rows, quarter), LOW),
            "conv_sums": pltpu.VMEM((8, quarter), f32),
            "conv_grad": pltpu.VMEM((2, sizes["x"], sizes["z"], tall, fold), LOW),
            "proj_grad": pltpu.VMEM((narrow, width), f32),
            "edge_sums": pltpu.VMEM((8, narrow), f32),
            "local": pltpu.VMEM((2, sizes["x"], sizes["z"], high, width), LOW),
            "ffn_sum": pltpu.VMEM((tall, lanes_a), f32),
            "att_sum": pltpu.VMEM((tall, wide), f32),
            "block": pltpu.VMEM((eight, low_rows, block_lanes), f32),
            "pair": pltpu.VMEM((2, own_ret, half), f32),
        }
    )
    outs = {
        "features_grad": ((rows, narrow), f32),
        "full_sum": ((16, len(lane)), f32),
        "conv_sum": ((tall, fold), f32),
        "local_sum": ((high, width), f32),
        "block_in": ((eight, low_rows, block_lanes), f32),
        "pair_in": ((2, own_ret, half), f32),
    }
    ins = dict(values)
    ins.update({name: jnp.asarray(value, LOW) for name, value in ones.items()})
    spaces = {"spans": pltpu.SMEM, "ffn": pl.ANY}
    names = list(ins) + list(outs) + list(scratch)

    def kernel(*refs):
        r = dict(zip(names, refs))
        local, send_sems, recv_sems = refs[len(names) :]
        spot = place(side)
        here, core, rank = spot["y"], spot["k"], lax.axis_index("rows")
        base = rank - core
        used = [0]

        def move(source, target, device):
            index = used[0]
            used[0] += 1
            return send(source, target, send_sems.at[index], recv_sems.at[index], device)

        r["move"] = move
        sources = {
            "ffn": r["ffn"], "full": r["full"], "att": r["att_grad"], "conv": r["conv_grad"],
            "local": r["local"],
        }
        sinks = {
            "ffn": r["ffn_sum"], "full": r["full_sum"], "att": r["att_sum"], "conv": r["conv_sum"],
            "local": r["local_sum"],
        }
        sums = Sums(r, jobs, spot, sizes, sources, sinks, local)
        ring = [peer(spot, "y", step, sizes)[1] for step in range(1, parts)]
        others = [(here + step) % parts for step in range(1, parts)]
        number = here * 2 + core
        eights = [(number + step) % eight for step in range(1, eight)]
        eight_at = [(other // 2, base + other % 2) for other in eights]
        greet(
            eight_at
            + [peer(spot, axis, step, sizes)[1] for axis in ("x", "z") for step in range(1, sizes[axis])]
        )
        sent = []

        def swap(source, target):
            target_copies = [
                move(source.at[other], target.at[here], device) for other, device in zip(others, ring)
            ]
            target[here] = source[here]
            sent.extend(target_copies)
            return target_copies

        swapped = swap(r["gctx"], r["gctx_in"])
        sums.start("ffn")
        for copy in swapped:
            copy.wait_recv()
        attention_back_step(r, micros, frames)

        terms, held = r["terms"], r["terms_held"]
        middle = mine // 2
        near, far = pl.ds(0, middle), pl.ds(middle, middle)
        right, across, left = [(here + step) % 4 for step in (1, 2, 3)]
        to_right, to_left = ring[0], ring[2]
        ringing = [
            move(terms.at[across, near], held.at[0], to_right),
            move(terms.at[across, far], held.at[1], to_left),
            move(terms.at[right, far], held.at[2], to_right),
            move(terms.at[left, near], held.at[3], to_left),
        ]
        attention_weight_step(r)
        ringing[0].wait_recv()
        terms[right, near] = terms[right, near] + held[0]
        ringing.append(move(terms.at[right, near], held.at[4], to_right))
        ringing[1].wait_recv()
        terms[left, far] = terms[left, far] + held[1]
        ringing.append(move(terms.at[left, far], held.at[5], to_left))
        sums.pump("ffn")
        sums.start("att")
        for copy in ringing[2:]:
            copy.wait_recv()
        r["terms_sum"][near] = widen(terms[here, near]) + widen(held[4]) + widen(held[3])
        r["terms_sum"][far] = widen(terms[here, far]) + widen(held[2]) + widen(held[5])
        sent.extend(ringing)
        norm_back_step(r)
        swapped = swap(r["gpos"], r["gpos_in"])
        vectors_step(r, own)
        sums.start("full")
        sums.pump("ffn")
        sums.pump("att")
        for copy in swapped:
            copy.wait_recv()
        conv_back_step(r, here, micros, frames, tall, per)
        sums.start("conv")

        target = r["slopes_all"]
        middle = rows // 2
        near, far = pl.ds(0, middle), pl.ds(middle, middle)
        ringing = [
            move(target.at[here, near], target.at[here, near], to_right),
            move(target.at[here, far], target.at[here, far], to_left),
            move(target.at[here, far], target.at[here, far], to_right),
            move(target.at[here, near], target.at[here, near], to_left),
        ]
        ringing[0].wait_recv()
        ringing.append(move(target.at[left, near], target.at[left, near], to_right))
        ringing[1].wait_recv()
        ringing.append(move(target.at[right, far], target.at[right, far], to_left))
        sums.pump("ffn", "att", "full")
        sums.pump("conv")
        for copy in ringing[2:]:
            copy.wait_recv()
        sent.extend(ringing)
        sums.pump("ffn", "att", "full")
        finish_step(r, spot, own, own_in)
        sums.start("local")
        sums.pump("conv", "ffn", "att", "full")
        sums.pump("local")
        sums.drain("ffn", "att")

        for j in range(eight):
            at = slice(j * own, (j + 1) * own)
            r["block"][j, :own, : deep + 128] = r["ffn_sum"][at, half:]
            r["block"][j, :own, deep + 128 :] = r["att_sum"][at]
        for k in range(2):
            r["pair"][k] = r["ffn_sum"][k * own_ret : (k + 1) * own_ret, :half]
        last = [
            move(r["block"].at[other], r["block_in"].at[number], device)
            for other, device in zip(eights, eight_at)
        ]
        last.append(move(r["pair"].at[1 - core], r["pair_in"].at[core], (here, base + 1 - core)))
        r["block_in"][number] = r["block"][number]
        r["pair_in"][core] = r["pair"][core]
        sums.drain("conv", "full", "local")
        for copy in last:
            copy.wait()
        for copy in sent:
            copy.wait_send()
        sums.close()

    return dict(
        zip(
            outs,
            call_remote(
                kernel,
                [jax.ShapeDtypeStruct(shape, kind) for shape, kind in outs.values()],
                [pl.BlockSpec(memory_space=spaces.get(name, pltpu.VMEM)) for name in ins],
                whole(len(outs)),
                list(scratch.values())
                + [
                    pltpu.SemaphoreType.DMA((4,)),
                    pltpu.SemaphoreType.DMA((copies,)),
                    pltpu.SemaphoreType.DMA((copies,)),
                ],
                ident, *ins.values(),
            ),
        )
    )


def per_device(
    features, lengths, input_gain, input_bias, proj_weight, proj_bias, conv_weight, conv_bias,
    encoder_gain, encoder_bias, attend_weight, query_bias, value_bias, output_weight, output_bias,
    attend_gain, attend_bias, hidden_weight, hidden_bias, return_weight, return_bias, final_gain,
    final_bias, out_grad,
):
    parts = lax.axis_size("ch")
    ranks = lax.axis_size("rows")
    side = math.isqrt(ranks // 2)
    sizes = {"y": parts, "x": side, "z": side, "k": 2}
    here = lax.axis_index("ch").astype(jnp.int32).reshape(1)
    micros, _, frames, narrow = features.shape
    own = proj_bias.shape[0]
    width = proj_weight.shape[1]
    quarter = width // parts
    inner, taps = conv_weight.shape[1:]
    blocks = taps // FOLD
    hidden = hidden_weight.shape[1]
    own_in = input_gain.shape[0]
    own_hid = hidden_bias.shape[0]
    seg = out_grad.shape[2]
    eight = 2 * parts
    squares = side * side
    tall = eight * own
    deep, thin, att = hidden // eight, width // eight, 3 * quarter // 2
    half = width // 2
    rows = micros * frames
    mine = micros * seg
    fold = FOLD * inner
    spans = lengths.reshape(micros)

    cut = jnp.concatenate(
        [
            hidden_weight.reshape(own, eight, deep),
            output_weight.reshape(own, eight, thin),
            attend_weight.reshape(own, 3, parts, quarter).transpose(0, 2, 1, 3).reshape(own, eight, att),
        ],
        axis=2,
    )
    first = jnp.pad(proj_weight.reshape(own_in, eight, thin), ((0, 0), (0, 0), (0, deep + att)))
    cut = jnp.concatenate([cut, first], axis=0).transpose(1, 0, 2)
    cut = jnp.pad(cut, ((0, 0), (0, -cut.shape[1] % 16), (0, 0)))
    pair = return_weight.reshape(-1, 2, half).transpose(1, 0, 2)
    own_ret = pair.shape[1]
    pair = jnp.pad(pair, ((0, 0), (0, -own_ret % 16), (0, 0)))
    small = (proj_bias, conv_bias, encoder_gain, encoder_bias, query_bias, value_bias, output_bias,
             attend_gain, attend_bias, return_bias, final_gain, final_bias)
    packed = jnp.concatenate(small + (input_gain, input_bias, hidden_bias))
    spare = 128 - thin
    packed = jnp.pad(packed, (0, eight * own_in * spare - packed.shape[0])).reshape(-1, spare)
    packed = jnp.pad(packed, ((0, 0), (thin, 0)))
    folded = conv_weight.reshape(own, inner, blocks, FOLD).transpose(0, 2, 3, 1)
    f = forward_start(
        {
            "features": features.reshape(rows, narrow), "blocks": cut, "pair": pair,
            "packed": packed, "conv_own": folded.reshape(own * blocks, fold), "spans": spans,
        },
        sizes, 0, micros, frames, own, own_in, own_hid, own_ret, len(small),
    )
    output, grad_attn, grad_context, ffn, normal, scale, owned = feed_forward(
        f["context_in"], f["summed"], here, out_grad.reshape(mine, width), f["weights"], f["table"],
        f["hid_bias"], micros, frames, thin, own, own_hid,
    )
    third = backward_rest(
        {
            "gctx": grad_context, "grad_attn": grad_attn, "normal": normal, "scale": scale,
            "owned": owned, "spans": spans,
            **{
                name: f[name]
                for name in ("low", "joint", "probs", "attend", "table", "before", "padded",
                             "conv_turned", "gathered", "proj", "edges")
            },
            "ffn": ffn.reshape(2, parts, side, side, tall, -1),
        },
        sizes, 9, micros, frames, own, own_in, own_hid, own_ret, thin,
    )

    cut = third["block_in"][:, :own].transpose(1, 0, 2)
    hidden_share = cut[:, :, :deep].reshape(hidden_weight.shape)
    output_share = cut[:, :, deep : deep + thin].reshape(output_weight.shape)
    attend_share = cut[:, :, deep + 128 : deep + 128 + att]
    attend_share = attend_share.reshape(own, parts, 3, quarter).transpose(0, 2, 1, 3)
    return_share = third["pair_in"].transpose(1, 0, 2).reshape(return_weight.shape)
    conv_share = third["conv_sum"].reshape(own, blocks, FOLD, inner).transpose(0, 3, 1, 2)
    features_grad = third["features_grad"]
    local = third["local_sum"]
    tail = local[own_in]
    full = third["full_sum"][0]
    local_parts = [tail[i * own : (i + 1) * own] for i in range(4)]
    full_parts = [full[i * own : (i + 1) * own] for i in range(8)]
    return (
        output.reshape(out_grad.shape),
        features_grad.reshape(features.shape),
        tail[4 * own : 4 * own + own_in],
        tail[4 * own + own_in : 4 * own + 2 * own_in],
        local[:own_in],
        local_parts[0],
        conv_share.reshape(conv_weight.shape),
        local_parts[1],
        full_parts[0],
        full_parts[1],
        attend_share.reshape(attend_weight.shape),
        local_parts[2],
        local_parts[3],
        output_share,
        full_parts[2],
        full_parts[3],
        full_parts[4],
        hidden_share,
        full[8 * own : 8 * own + own_hid],
        return_share,
        full_parts[5],
        full_parts[6],
        full_parts[7],
    )


def solution(mesh):
    vector, matrix, cube = P(ALL), P(ALL, None), P(ALL, None, None)
    weights = (
        vector, vector, matrix, vector, cube, vector, vector, vector, matrix, vector, vector,
        matrix, vector, vector, vector, matrix, vector, matrix, vector, vector, vector,
    )
    by_channel = P(None, "rows", None, "ch")
    by_frame = P(None, "rows", "ch", None)
    return jax.shard_map(
        per_device,
        mesh=mesh,
        in_specs=(by_channel, P(None, "rows")) + weights + (by_frame,),
        out_specs=(by_frame, by_channel) + weights,
        check_vma=False,
    )
```

```python
import functools
import math

import jax
import jax.numpy as jnp
import numpy as np
from jax import lax
from jax.experimental import pallas as pl
from jax.experimental.pallas import tpu as pltpu
from jax.sharding import PartitionSpec as P

HEAD_DIM = 64
EPS = 1e-05
NEGATIVE = -1000000000.0
FOLD = 16
ALL = ("ch", "rows")
LOW = jnp.bfloat16
MESH = pl.DeviceIdType.MESH
ROOM = 62 * 1024 * 1024


def widen(values):
    return values.astype(jnp.float32)


def dot(left, right):
    return jnp.dot(left, right, preferred_element_type=jnp.float32)


def contract(spec, left, right):
    return jnp.einsum(spec, left, right, preferred_element_type=jnp.float32)


def place(side):
    rank = lax.axis_index("rows")
    return {
        "y": lax.axis_index("ch"),
        "x": rank // (2 * side),
        "z": (rank // 2) % side,
        "k": rank % 2,
    }


def peer(spot, axis, step, sizes):
    moved = dict(spot)
    moved[axis] = (spot[axis] + step) % sizes[axis]
    return moved, (moved["y"], (moved["x"] * sizes["z"] + moved["z"]) * 2 + moved["k"])


def greet(targets):
    barrier = pltpu.get_barrier_semaphore()
    for target in targets:
        pl.semaphore_signal(barrier, inc=1, device_id=target, device_id_type=MESH)
    pl.semaphore_wait(barrier, len(targets))


def send(source, target, send_sem, recv_sem, device):
    copy = pltpu.make_async_remote_copy(
        src_ref=source, dst_ref=target, send_sem=send_sem, recv_sem=recv_sem,
        device_id=device, device_id_type=MESH,
    )
    copy.start()
    return copy


def whole(count):
    return [pl.BlockSpec(memory_space=pltpu.VMEM)] * count


def call_remote(kernel, shapes, ins, outs, scratch, ident, *values):
    return pl.pallas_call(
        kernel,
        out_shape=shapes,
        in_specs=ins,
        out_specs=outs,
        scratch_shapes=scratch,
        compiler_params=pltpu.CompilerParams(
            collective_id=ident, has_side_effects=True, vmem_limit_bytes=ROOM
        ),
    )(*values)


def window(axes, fixed, cut):
    lead = tuple(fixed.get(axis, slice(None)) for axis in axes)
    return lead + (pl.ds(cut[0], cut[1]), pl.ds(cut[2], cut[3]))


def loop_blocks(dims, body):
    count = math.prod(dims)
    if count == 1:
        body((0,) * len(dims))
        return

    def step(flat, carry):
        index = []
        rest = flat
        for size in reversed(dims):
            index.append(rest % size)
            rest = rest // size
        body(tuple(reversed(index)))
        return carry

    lax.fori_loop(0, count, step, 0)


def dot_nt(left, right):
    return lax.dot_general(left, right, (((1,), (1,)), ((), ())), preferred_element_type=jnp.float32)


def dot_tn(left, right):
    return lax.dot_general(left, right, (((0,), (0,)), ((), ())), preferred_element_type=jnp.float32)


def pick(left, onehot):
    return dot(left, onehot).astype(LOW)


def pick_wide(values, onehot):
    high = values.astype(LOW)
    rest = (values - widen(high)).astype(LOW)
    return dot(high, onehot) + dot(rest, onehot)


def smooth(values):
    return 0.5 * values * (1.0 + lax.erf(values * 0.7071067811865476))


def smooth_slope(values):
    return 0.5 * (1.0 + lax.erf(values * 0.7071067811865476)) + values * 0.3989422804014327 * jnp.exp(
        -0.5 * values * values
    )


def norm(values):
    mean = jnp.mean(values, axis=-1, keepdims=True)
    centred = values - mean
    scale = lax.rsqrt(jnp.mean(centred * centred, axis=-1, keepdims=True) + EPS)
    return centred * scale, scale


def norm_back(incoming, normal, scale, gain):
    scaled = incoming * gain
    first = jnp.mean(scaled, axis=-1, keepdims=True)
    second = jnp.mean(scaled * normal, axis=-1, keepdims=True)
    return scale * (scaled - first - normal * second)


def norm_blocks(blocks):
    size = sum(block.shape[-1] for block in blocks)
    mean = sum(jnp.sum(block, axis=-1, keepdims=True) for block in blocks) / size
    centred = [block - mean for block in blocks]
    spread = sum(jnp.sum(block * block, axis=-1, keepdims=True) for block in centred) / size
    scale = lax.rsqrt(spread + EPS)
    return [block * scale for block in centred], scale


def column_sum(values):
    return jnp.sum(values, axis=0, keepdims=True)


def local_call(kernel, shapes, scratch, *values):
    count = len(values)
    return pl.pallas_call(
        kernel,
        out_shape=[jax.ShapeDtypeStruct(shape, kind) for shape, kind in shapes],
        in_specs=[
            pl.BlockSpec(memory_space=pltpu.SMEM if value.dtype == jnp.int32 else pltpu.VMEM)
            for value in values
        ],
        out_specs=whole(len(shapes)),
        scratch_shapes=scratch,
        compiler_params=pltpu.CompilerParams(vmem_limit_bytes=ROOM),
    )(*values)


def onehot(rows, columns):
    return (np.asarray(rows)[:, None] == np.asarray(columns)[None, :]).astype(LOW)


def natural_of(count, parts, squares):
    cells = np.arange(count).reshape(parts, squares, 2, -1)
    return cells.transpose(1, 0, 2, 3).reshape(count)


def fold_rows(padded, spread_ref, inner):
    for j in range(FOLD):
        moved = padded if j == 0 else pltpu.roll(padded, padded.shape[1] - j, 1)
        spread_ref[j * inner : (j + 1) * inner, :] = moved


def spread_blocks(padded, spread_ref, inner, blocks):
    for b in range(blocks):
        moved = padded if b == 0 else pltpu.roll(padded, FOLD * b, 1)
        spread_ref[b * inner : (b + 1) * inner, :] = moved


def own_frames(ref, spot, micros, frames, parts):
    seg = frames // parts
    blocks = []
    for c in range(parts):
        pieces = [
            widen(ref[c, pl.ds(pl.multiple_of(m * frames + spot * seg, seg), seg)])
            for m in range(micros)
        ]
        blocks.append(jnp.concatenate(pieces, axis=0))
    return blocks


def feed_forward(
    context, summed, here, upstream, weights, table, hid_bias, micros, frames, thin, own, own_hid
):
    parts, mine, quarter = context.shape
    weights = weights.reshape(2, parts, -1, *weights.shape[-2:])
    squares, tall, lanes = weights.shape[2:]
    width = parts * quarter
    half, deep = width // 2, lanes - width // 2 - 128
    eight = 2 * parts
    nat = onehot(np.arange(width), natural_of(width, parts, squares))
    spots = np.arange(width)
    place = np.zeros((width // 128, 256, 128), np.float32)
    for tile in range(width // 128):
        first = tile * 128 // thin
        for lane in range(128):
            channel = tile * 128 + lane
            place[tile, (channel // thin - first) * 128 + channel % thin, lane] = 1.0
    cut = np.stack([onehot(spots, np.where(np.arange(128) < thin, j * thin + np.arange(128), -1)) for j in range(eight)])
    f32 = jnp.float32
    hidden = eight * deep
    devices = 2 * parts * squares
    lane = np.arange(8 * own + own_hid + -(8 * own + own_hid) % 128)
    mask = onehot(np.arange(devices), np.arange(width) // own)
    mask_hid = onehot(np.arange(devices), np.arange(hidden) // own_hid)
    spread = onehot(np.arange(width) % own, lane)
    spread_hid = onehot(
        np.arange(hidden) % own_hid, np.where(lane >= 8 * own, lane - 8 * own, -1)
    )

    def kernel(
        ctx_ref, sum_ref, here_ref, up_ref, w_ref, table_ref, hid_ref, nat_ref, place_ref, cut_ref,
        mask_ref, mask_hid_ref, spread_ref, spread_hid_ref,
        out_ref, grad_out, gctx_out, slabs_out, normal_out, scale_out, owned_out,
        pre_ref, act_ref, wout_ref, hid_out,
    ):
        spot = here_ref[0]

        def block(c, k, begin, size):
            return w_ref[k, c, :, :, begin : begin + size].reshape(width, size)

        for tile in range(width // 128):
            first = tile * 128 // thin
            last = min(first + 1, eight - 1)
            both = [block(j // 2, j % 2, half + deep, 128) for j in (first, last)]
            wout_ref[:, tile * 128 : (tile + 1) * 128] = pick(jnp.concatenate(both, axis=1), place_ref[tile])
        normal, scale = norm_blocks(own_frames(sum_ref, spot, micros, frames, parts))
        normal = jnp.concatenate(normal, axis=1)
        normal_out[...] = normal
        scale_out[...] = jnp.broadcast_to(scale, scale_out.shape)
        encoded = normal * table_ref[2:3] + table_ref[3:4]
        ctx_slab = sum(
            dot(ctx_ref[c], nat_ref[c * quarter : (c + 1) * quarter]) for c in range(parts)
        ).astype(LOW)
        attn_sum = encoded + dot(ctx_slab, wout_ref[...]) + table_ref[6:7]
        normal_att, scale_att = norm(attn_sum)
        attn_norm = normal_att * table_ref[7:8] + table_ref[8:9]
        attn_slab = pick(attn_norm.astype(LOW), nat_ref[...])
        outer = [jnp.zeros((mine, half), f32), jnp.zeros((mine, half), f32)]
        for c in range(parts):
            for k in range(2):
                begin = (2 * c + k) * deep
                pre = dot(attn_slab, block(c, k, half, deep)) + hid_ref[:, begin : begin + deep]
                share = 0.5 * (1.0 + lax.erf(pre * 0.7071067811865476))
                pre_ref[:, begin : begin + deep] = share + pre * 0.3989422804014327 * jnp.exp(-0.5 * pre * pre)
                act_ref[:, begin : begin + deep] = (pre * share).astype(LOW)
            act = act_ref[:, 2 * c * deep : 2 * (c + 1) * deep]
            outer = [outer[k] + dot(act, block(c, k, 0, half)) for k in range(2)]
        ffn_sum = attn_norm + jnp.concatenate(outer, axis=1) + table_ref[9:10]
        normal_fin, scale_fin = norm(ffn_sum)
        out_ref[...] = (normal_fin * table_ref[10:11] + table_ref[11:12]).astype(LOW)
        up = widen(up_ref[...])
        grad_ffn = norm_back(up, normal_fin, scale_fin, table_ref[10:11])
        slope_outer = grad_ffn.astype(LOW)
        vectors = {
            5: column_sum(widen(slope_outer)), 6: column_sum(up * normal_fin), 7: column_sum(up)
        }
        grad_slab = jnp.zeros((mine, width), f32)
        attn_turned = widen(attn_slab).T.astype(LOW)
        for c in range(parts):
            columns = slice(2 * c * deep, 2 * (c + 1) * deep)
            grad_act = sum(
                dot_nt(slope_outer[:, k * half : (k + 1) * half], block(c, k, 0, half)) for k in range(2)
            )
            slope_inner = (grad_act * pre_ref[:, columns]).astype(LOW)
            hid_out[:, columns] = column_sum(widen(slope_inner))
            act_turned = widen(act_ref[:, columns]).T.astype(LOW)
            for k in range(2):
                inner_k = slope_inner[:, k * deep : (k + 1) * deep]
                grad_slab = grad_slab + dot_nt(inner_k, block(c, k, half, deep))
                grad_ret = dot(act_turned, slope_outer[:, k * half : (k + 1) * half]).astype(LOW)
                slabs_out[k, c, :, :, :half] = grad_ret.reshape(squares, tall, half)
                grad_hid = dot(attn_turned, inner_k).astype(LOW)
                slabs_out[k, c, :, :, half : half + deep] = grad_hid.reshape(squares, tall, deep)
        high = grad_slab.astype(LOW)
        rest = (grad_slab - widen(high)).astype(LOW)
        grad_norm2 = grad_ffn + dot_nt(high, nat_ref[...]) + dot_nt(rest, nat_ref[...])
        vectors[3] = column_sum(grad_norm2 * normal_att)
        vectors[4] = column_sum(grad_norm2)
        grad_attn = norm_back(grad_norm2, normal_att, scale_att, table_ref[7:8])
        grad_out[...] = grad_attn
        slope_att = grad_attn.astype(LOW)
        vectors[2] = column_sum(widen(slope_att))
        owned = dot((widen(mask_hid_ref[...]) * hid_out[...]).astype(LOW), spread_hid_ref[...])
        for v, vector in vectors.items():
            owned = owned + owner_rows(vector, mask_ref[...], spread_ref[...], v * own)
        owned_out[...] = owned
        gctx_slab = dot_nt(slope_att, wout_ref[...]).astype(LOW)
        for c in range(parts):
            gctx_out[c] = dot_nt(gctx_slab, nat_ref[c * quarter : (c + 1) * quarter]).astype(LOW)
        ctx_turned = widen(ctx_slab).T.astype(LOW)
        for c in range(parts):
            for k in range(2):
                grad = dot(ctx_turned, pick(slope_att, cut_ref[2 * c + k])).astype(LOW)
                slabs_out[k, c, :, :, half + deep :] = grad.reshape(squares, tall, 128)

    return local_call(
        kernel,
        [
            ((mine, width), LOW), ((mine, width), f32), ((parts, mine, quarter), LOW),
            ((2, parts, squares, tall, lanes), LOW), ((mine, width), f32), ((mine, 128), f32),
            ((devices, len(lane)), f32),
        ],
        [
            pltpu.VMEM((mine, hidden), f32), pltpu.VMEM((mine, hidden), LOW),
            pltpu.VMEM((width, width), LOW), pltpu.VMEM((1, hidden), f32),
        ],
        context, summed, here, upstream, weights, table, hid_bias,
        *[jnp.asarray(v, LOW) for v in (nat, place, cut, mask, mask_hid, spread, spread_hid)],
    )


def gather_copies(jobs, sizes):
    total = 0
    for job in jobs.values():
        for order in job["orders"]:
            total += 1
            for number, axis in enumerate(order):
                total += 6 if number > 0 and sizes[axis] == 4 else sizes[axis] - 1
    return total


class Gathers:
    def __init__(self, buffers, jobs, spot, sizes, move):
        self.buffers, self.jobs, self.spot, self.sizes, self.move = buffers, jobs, spot, sizes, move
        self.states, self.finished = {}, []

    def send(self, name, cut, fixed, device):
        axes = self.jobs[name]["axes"]
        view = self.buffers[name].at[(self.spot["k"],) + window(axes, fixed, cut)]
        copy = self.move(view, view, device)
        self.finished.append(copy)
        return copy

    def own(self, name):
        axes = self.jobs[name]["axes"]
        return self.buffers[name].at[(self.spot["k"],) + tuple(self.spot[a] for a in axes)]

    def start(self, name):
        job = self.jobs[name]
        self.states[name] = [
            {"cut": cut, "order": order, "step": 0, "copies": [], "half": False}
            for cut, order in zip(job["cuts"], job["orders"])
        ]
        self.pump(name)

    def pump(self, *names):
        for name in names:
            for state in self.states[name]:
                self.advance(name, state)

    def drain(self, *names):
        while any(s["step"] <= len(s["order"]) + 1 for name in names for s in self.states[name]):
            self.pump(*names)

    def advance(self, name, state):
        step, order, cut = state["step"], state["order"], state["cut"]
        if step > len(order) + 1:
            return
        if state["half"]:
            axis, halved, near, far, fixed = state["half"]
            for slot, turn, half in ((0, 3, near), (1, 1, far)):
                state["copies"][slot].wait_recv()
                spot = peer(self.spot, axis, turn, self.sizes)[0]
                device = peer(self.spot, axis, 4 - turn, self.sizes)[1]
                at = dict(fixed)
                at[axis], at[halved] = spot[axis], half
                state["copies"].append(self.send(name, cut, at, device))
            state["half"] = False
            return
        for copy in state["copies"][2 if len(state["copies"]) == 6 else 0 :]:
            copy.wait_recv()
        state["copies"] = []
        state["step"] = step + 1
        if step > len(order):
            return
        if step == len(order):
            device = peer(self.spot, "k", 1, self.sizes)[1]
            state["copies"] = [self.send(name, cut, {}, device)]
            return
        axis = order[step]
        fixed = {a: self.spot[a] for a in order[step:]}
        if step > 0 and self.sizes[axis] == 4:
            halved = order[0]
            size = self.sizes[halved] // 2
            near, far = pl.ds(0, size), pl.ds(size, size)
            for half, turn in ((near, 1), (far, 3), (far, 1), (near, 3)):
                at = dict(fixed)
                at[halved] = half
                device = peer(self.spot, axis, turn, self.sizes)[1]
                state["copies"].append(self.send(name, cut, at, device))
            state["half"] = (axis, halved, near, far, fixed)
        else:
            for turn in range(1, self.sizes[axis]):
                device = peer(self.spot, axis, turn, self.sizes)[1]
                state["copies"].append(self.send(name, cut, fixed, device))

    def close(self):
        for copy in self.finished:
            copy.wait_send()


class Ring:
    def __init__(self, move, buffer, begin, count, here, to_right, to_left):
        self.move, self.buffer, self.here = move, buffer, here
        self.to_right, self.to_left = to_right, to_left
        half = count // 2
        self.near, self.far = pl.ds(begin, half), pl.ds(begin + half, half)
        self.copies = [
            self.shift(here, self.near, to_right), self.shift(here, self.far, to_left),
            self.shift(here, self.far, to_right), self.shift(here, self.near, to_left),
        ]

    def shift(self, block, rows, device):
        view = self.buffer.at[block, rows]
        return self.move(view, view, device)

    def relay(self):
        self.copies[0].wait_recv()
        self.copies.append(self.shift((self.here + 3) % 4, self.near, self.to_right))
        self.copies[1].wait_recv()
        self.copies.append(self.shift((self.here + 1) % 4, self.far, self.to_left))

    def finish(self):
        for copy in self.copies[2:]:
            copy.wait_recv()

    def close(self):
        for copy in self.copies:
            copy.wait_send()


def shards_step(r, parts, own, own_in, deep, thin, att, quarter, spare):
    f32 = jnp.float32
    eight = 2 * parts
    width = thin * eight
    half = width // 2
    hid, out, joint = [widen(r[name][...]) for name in ("hidden_raw", "output_raw", "attend_raw")]
    proj, ret = widen(r["proj_raw"][...]), widen(r["return_raw"][...])
    tall, lanes = r["blocks"].shape[1:]
    for c in range(parts):
        both = jnp.concatenate(
            [joint[:, i * width + c * quarter : i * width + (c + 1) * quarter] for i in range(3)], axis=1
        )
        for k in range(2):
            j = 2 * c + k
            top = [
                hid[:, j * deep : (j + 1) * deep], out[:, j * thin : (j + 1) * thin],
                both[:, k * att : (k + 1) * att],
            ]
            low = [proj[:, j * thin : (j + 1) * thin], jnp.zeros((own_in, lanes - thin), f32)]
            rows = [jnp.concatenate(top, axis=1), jnp.concatenate(low, axis=1)]
            if tall > own + own_in:
                rows.append(jnp.zeros((tall - own - own_in, lanes), f32))
            r["blocks"][j] = jnp.concatenate(rows, axis=0).astype(LOW)
    for k in range(2):
        rows = [ret[:, k * half : (k + 1) * half]]
        if r["pair"].shape[1] > ret.shape[0]:
            rows.append(jnp.zeros((r["pair"].shape[1] - ret.shape[0], half), f32))
        r["pair"][k] = jnp.concatenate(rows, axis=0).astype(LOW)
    small, ends = widen(r["small"][...]), widen(r["ends"][...])
    row = [small[i : i + 1] for i in range(small.shape[0])] + [ends[0:1], ends[1:2]]
    row = jnp.concatenate(row + [widen(r["hid_own"][...])], axis=1)
    count = -(-row.shape[1] // spare)
    row = jnp.concatenate([row, jnp.zeros((1, count * spare - row.shape[1]), f32)], axis=1)
    rows = [row[:, i * spare : (i + 1) * spare] for i in range(count)]
    rows.append(jnp.zeros((r["packed"].shape[0] - count, spare), f32))
    rows = jnp.concatenate(rows, axis=0)
    rows = [jnp.zeros((rows.shape[0], 128 - spare), f32), rows]
    r["packed"][...] = jnp.concatenate(rows, axis=1)


def fold_own_step(r, target):
    own, inner, taps = r["conv_raw"].shape
    blocks = taps // FOLD
    rows = []
    for o in range(own):
        r["taps"][o] = widen(r["conv_raw"][o]).T
        pieces = [r["taps"][o, pl.ds(j, blocks, stride=FOLD), :] for j in range(FOLD)]
        rows.append(jnp.concatenate(pieces, axis=1))
    target[...] = jnp.concatenate(rows, axis=0).astype(LOW)


def slabs_step(r, own, deep, thin, att):
    f32 = jnp.float32
    blocks = r["blocks_in"][...].reshape(-1, r["blocks_in"].shape[2])
    main = dot(r["slab_rows"][...], blocks)
    pair = dot(r["pair_rows"][...], r["pair_in"][...].reshape(-1, r["pair_in"].shape[2]))
    tall = main.shape[0]
    r["ffn_slab"][...] = jnp.concatenate(
        [pair, main[:, :deep], main[:, deep : deep + thin], jnp.zeros((tall, 128 - thin), f32)], axis=1
    ).astype(LOW)
    att_slab = jnp.concatenate(
        [main[:, deep + thin :], jnp.zeros((tall, -att % 128), f32)], axis=1
    ).astype(LOW)
    early = (dot(r["first_rows"][...], blocks[:, :128]) + r["packed"][...]).astype(LOW)
    return att_slab, early


def vectors_ready_step(r, parts, quarter):
    wide_in = r["nat_in"].shape[0]
    width = r["table"].shape[1]
    for c in range(parts):
        both = [r["early_all"][k, c].reshape(wide_in, 128) for k in range(2)]
        slab_cols = pick(jnp.concatenate(both, axis=1), r["place_in"][...])
        r["proj"][c] = pick(r["nat_in"][...], slab_cols)
    devices = r["vector_rows"].shape[1]
    high = r["vector_rows"].shape[2] // devices
    cells = widen(r["early_all"][...].reshape(devices, -1, 128)[:, : -(-high // 16) * 16])
    cells = cells[:, :high].reshape(devices * high, 128).astype(LOW)
    turned = []
    for number in range(r["vector_rows"].shape[0]):
        turned.append(dot(r["vector_rows"][number], cells))
    lanes = jnp.concatenate([piece[:, -(128 - r["thin"]) :] for piece in turned], axis=1)
    turned = lanes.T.astype(LOW)
    spread = (dot(turned, r["owner"][...]) * widen(r["take"][...])).astype(LOW)
    table = dot(r["row_of"][...], spread)
    r["table"][...] = table
    for c in range(parts):
        r["quarters"][c] = table[:, c * quarter : (c + 1) * quarter]
    r["columns"][...] = jnp.concatenate([table, jnp.zeros((112, width), jnp.float32)], axis=0).T
    spread = (dot(turned, r["owner_in"][...]) * widen(r["take_in"][...])).astype(LOW)
    r["edges"][...] = dot(r["row_in"][...], spread)
    r["hid_bias"][...] = column_sum(dot(turned, r["owner_hid"][...]) * widen(r["take_hid"][...]))


def conv_ready_step(r, per, side):
    groups, rows, fold = r["conv"].shape
    for g in range(groups):
        taken = jnp.concatenate(
            [
                r["conv_all"][k, (g * per + n) // side, (g * per + n) % side]
                for k in range(2) for n in range(per)
            ],
            axis=0,
        )
        r["conv"][g] = dot(r["conv_order"][...], taken).astype(LOW)


def conv_turned_step(r):
    for g in range(r["conv"].shape[0]):
        r["conv_turned"][g] = widen(r["conv"][g]).T.astype(LOW)


def attend_ready_step(r):
    width = r["nat"].shape[0]
    both = [r["att_all"][k].reshape(width, -1) for k in range(2)]
    slab_cols = pick(jnp.concatenate(both, axis=1), r["place_att"][...])
    r["attend"][...] = pick(r["nat"][...], slab_cols)


def project_step(r, here, m, frames):
    parts, _, narrow = r["gathered"].shape
    groups, _, fold = r["conv"].shape
    inner = fold // FOLD
    half = (r["padded"].shape[2] - frames) // 2
    at = slice(m * frames, (m + 1) * frames)
    normal, _ = norm_blocks([widen(r["gathered"][c, at]) for c in range(parts)])
    low = []
    for c, block in enumerate(normal):
        lanes = slice(c * narrow, (c + 1) * narrow)
        low.append((block * r["edges"][0:1, lanes] + r["edges"][1:2, lanes]).astype(LOW))
    result = dot(jnp.concatenate(low, axis=1), r["proj"][here]) + r["quarters"][here, 0:1]
    live = lax.broadcasted_iota(jnp.int32, (frames, 1), 0) < r["spans"][m]
    turned = jnp.where(live, result, 0.0).T
    for g in range(groups):
        piece = turned[g * inner : (g + 1) * inner]
        r["plain"][m * groups + g] = piece
        edge = jnp.zeros((inner, half), LOW)
        r["padded"][m * groups + g] = jnp.concatenate([edge, piece.astype(LOW), edge], axis=1)


def conv_step(r, here, m, frames):
    groups, many, fold = r["conv"].shape
    inner = fold // FOLD
    blocks = many // inner
    span = r["padded"].shape[2]
    quarter = groups * inner

    def one(g, carry):
        index = m * groups + g
        fold_rows(r["padded"][index], r["folded"], inner)
        sums = dot(r["conv"][g], r["folded"][...])
        total = sums[:inner, :frames]
        for b in range(1, blocks):
            part = pltpu.roll(sums[b * inner : (b + 1) * inner], span - FOLD * b, 1)
            total = total + part[:, :frames]
        start = pl.multiple_of(here * quarter + g * inner, 16)
        before = total + r["columns"][pl.ds(start, inner), 1:2]
        r["before"][index] = before
        r["plain"][index] = r["plain"][index] + smooth(before)
        return carry

    lax.fori_loop(0, groups, one, 0)
    both = [r["plain"][m * groups + g] for g in range(groups)]
    r["summed"][here, m * frames : (m + 1) * frames] = jnp.concatenate(both, axis=0).T.astype(LOW)


def attention_step(r, here, m, frames):
    parts, _, quarter = r["summed"].shape
    heads = quarter // HEAD_DIM
    seg = frames // parts
    ratio = HEAD_DIM ** (-0.5)
    at = slice(m * frames, (m + 1) * frames)
    normal, _ = norm_blocks([widen(r["summed"][c, at]) for c in range(parts)])
    joint = jnp.zeros((frames, 3 * quarter), jnp.float32)
    for c in range(parts):
        low = (normal[c] * r["quarters"][c, 2:3] + r["quarters"][c, 3:4]).astype(LOW)
        r["low"][c, at] = low
        joint = joint + dot(low, r["attend"][c * quarter : (c + 1) * quarter])
    query = joint[:, :quarter] + r["quarters"][here, 4:5]
    keys = joint[:, quarter : 2 * quarter]
    value = joint[:, 2 * quarter :] + r["quarters"][here, 5:6]
    joint_low = [v.astype(LOW) for v in (query, keys, value)]
    for i in range(3):
        r["joint"][i, at] = joint_low[i]
    value_turned = value.T.astype(LOW)
    live = lax.broadcasted_iota(jnp.int32, (frames, 1), 0) < r["spans"][m]
    results = []
    for h in range(heads):
        cols = slice(h * HEAD_DIM, (h + 1) * HEAD_DIM)
        scores = dot_nt(joint_low[1][:, cols], joint_low[0][:, cols]) * ratio
        scores = jnp.where(live, scores, NEGATIVE)
        expo = jnp.exp(scores - jnp.max(scores, axis=0, keepdims=True))
        probs = (expo / jnp.sum(expo, axis=0, keepdims=True)).astype(LOW)
        r["probs"][m * heads + h] = probs
        results.append(dot(value_turned[cols], probs))
    context = jnp.concatenate(results, axis=0).T.astype(LOW)
    for d in range(parts):
        r["context"][d, m * seg : (m + 1) * seg] = context[d * seg : (d + 1) * seg]


def forward_start(values, sizes, ident, micros, frames, own, own_in, own_hid, own_ret, count):
    parts, squares, side = sizes["y"], sizes["x"] * sizes["z"], sizes["z"]
    devices = 2 * parts * squares
    rows, narrow = values["features"].shape
    _, inner, taps = values["conv_raw"].shape
    eight, blocks, fold = 2 * parts, taps // FOLD, inner * FOLD
    tall_block, tall_pair = own + own_in, own_ret
    tall_block, tall_pair = tall_block + -tall_block % 16, tall_pair + -tall_pair % 16
    tall = eight * own
    width, wide_in, hidden = own * devices, own_in * devices, own_hid * devices
    quarter = width // parts
    half = width // 2
    groups = quarter // inner
    many = blocks * inner
    per = inner // own // 2
    heads = quarter // HEAD_DIM
    span = frames + blocks * FOLD
    seg = frames // parts
    mine = micros * seg
    deep, thin, att = hidden // eight, width // eight, 3 * quarter // 2
    wide = att + -att % 128
    lanes_a = half + deep + 128
    spare = 128 - thin
    f32 = jnp.float32

    ones = {}
    j, s = np.divmod(np.arange(tall), own)
    ones["slab_rows"] = onehot(j * tall_block + s, np.arange(eight * tall_block))
    j, s = np.divmod(np.arange(eight * own_in), own_in)
    ones["first_rows"] = onehot(j * tall_block + own + s, np.arange(eight * tall_block))
    j, s = np.divmod(np.arange(2 * own_ret), own_ret)
    ones["pair_rows"] = onehot(j * tall_pair + s, np.arange(2 * tall_pair))
    ones["nat_in"] = onehot(np.arange(wide_in), natural_of(wide_in, parts, squares))
    ones["nat"] = onehot(np.arange(width), natural_of(width, parts, squares))
    lanes = np.arange(quarter)
    ones["place_in"] = onehot(np.arange(256), np.where(lanes < thin, lanes, lanes - thin + 128))
    lanes = np.arange(2 * att)
    ones["place_att"] = onehot(np.arange(2 * wide), np.where(lanes < att, lanes, lanes - att + wide))
    slab = np.arange(many).reshape(2, per, own, blocks)
    ones["conv_order"] = onehot(
        [slab[(o // own) % 2, o // own // 2, o % own, b] for b in range(blocks) for o in range(inner)],
        np.arange(many),
    )
    early_rows = eight * own_in
    vector_rows = -(-(count * own + 2 * own_in + own_hid) // spare)
    vector_rows = vector_rows + -vector_rows % (128 // spare)
    spots = np.arange(devices).reshape(2, parts, squares).transpose(1, 2, 0).reshape(-1)
    high = vector_rows + -vector_rows % 8
    ones["vector_rows"] = np.stack(
        [onehot(spots * high + i, np.arange(devices * high)) for i in range(vector_rows)]
    )
    lane = np.arange(vector_rows * spare)
    ask = np.arange(width)
    edge = count * own
    ones["take"] = (lane[:, None] < edge) & (lane[:, None] % own == ask[None, :] % own)
    ones["row_of"] = onehot(np.arange(16), np.where(lane < edge, lane // own, -1))
    ones["owner"] = onehot(np.arange(devices), ask // own)
    ones["owner_in"] = onehot(np.arange(devices), np.arange(wide_in) // own_in)
    ends = (lane >= edge) & (lane < edge + 2 * own_in)
    ones["take_in"] = ends[:, None] & (
        (lane[:, None] - edge) % own_in == (np.arange(wide_in) % own_in)[None, :]
    )
    ones["row_in"] = onehot(np.arange(16), np.where(ends, (lane - edge) // own_in, -1))
    ones["owner_hid"] = onehot(np.arange(devices), np.arange(hidden) // own_hid)
    ones["take_hid"] = onehot(lane, edge + 2 * own_in + np.arange(hidden) % own_hid)

    all_axes, row_axes = ("y", "x", "z"), ("x", "z")
    cut_a = lanes_a // 256 * 128 + 128 * (lanes_a // 128 % 2)
    jobs = {
        "conv_all": {
            "axes": row_axes,
            "cuts": [(0, tall, 0, fold // 2), (0, tall, fold // 2, fold // 2)],
            "orders": [("z", "x"), ("x", "z")],
        },
        "early_all": {
            "axes": all_axes, "cuts": [(0, early_rows, 0, 128)], "orders": [("z", "x", "y")],
        },
        "att_all": {"axes": row_axes, "cuts": [(0, tall, 0, wide)], "orders": [("x", "z")]},
        "weights": {
            "axes": all_axes,
            "cuts": [(0, tall, 0, cut_a), (0, tall, cut_a, lanes_a - cut_a)],
            "orders": [("y", "z", "x"), ("y", "x", "z")],
        },
    }
    copies = gather_copies(jobs, sizes) + eight + 6 * (1 + micros) + micros * (parts - 1)
    lead = (sizes["x"], sizes["z"])
    lanes_cut = deep + thin + att
    scratch = {
        "blocks": pltpu.VMEM((eight, tall_block, lanes_cut), LOW),
        "pair": pltpu.VMEM((2, tall_pair, half), LOW),
        "packed": pltpu.VMEM((early_rows, 128), f32),
        "taps": pltpu.VMEM((own, taps, inner), f32),
        "blocks_in": pltpu.VMEM((eight, tall_block, lanes_cut), LOW),
        "pair_in": pltpu.VMEM((2, tall_pair, half), LOW),
        "ffn_slab": pltpu.VMEM((tall, lanes_a), LOW),
        "early_all": pltpu.VMEM((2, parts) + lead + (early_rows, 128), LOW),
        "conv_all": pltpu.VMEM((2,) + lead + (tall, fold), LOW),
        "att_all": pltpu.VMEM((2,) + lead + (tall, wide), LOW),
        "quarters": pltpu.VMEM((parts, 16, quarter), f32),
        "columns": pltpu.VMEM((width, 128), f32),
        "conv": pltpu.VMEM((groups, many, fold), LOW),
        "plain": pltpu.VMEM((micros * groups, inner, frames), f32),
        "folded": pltpu.VMEM((fold, span), LOW),
        "context": pltpu.VMEM((parts, mine, quarter), LOW),
    }
    outs = {
        "weights": ((2, parts) + lead + (tall, lanes_a), LOW),
        "gathered": ((parts, rows, narrow), LOW),
        "proj": ((parts, wide_in, quarter), LOW),
        "table": ((16, width), f32),
        "edges": ((16, wide_in), f32),
        "hid_bias": ((1, hidden), f32),
        "attend": ((width, 3 * quarter), LOW),
        "conv_turned": ((groups, fold, many), LOW),
        "padded": ((micros * groups, inner, span), LOW),
        "before": ((micros * groups, inner, frames), f32),
        "summed": ((parts, rows, quarter), LOW),
        "low": ((parts, rows, quarter), LOW),
        "joint": ((3, rows, quarter), LOW),
        "probs": ((micros * heads, frames, frames), LOW),
        "context_in": ((parts, mine, quarter), LOW),
    }
    ins = dict(values)
    ins.update({name: jnp.asarray(value, LOW) for name, value in ones.items()})
    spaces = {"spans": pltpu.SMEM, "weights": pl.ANY}
    names = list(ins) + list(outs) + list(scratch)

    def kernel(*refs):
        r = dict(zip(names, refs))
        local, send_sems, recv_sems = refs[len(names) :]
        r["thin"] = thin
        spot = place(side)
        here, core, rank = spot["y"], spot["k"], lax.axis_index("rows")
        base = rank - core
        used = [0]

        def move(source, target, device):
            index = used[0]
            used[0] += 1
            return send(source, target, send_sems.at[index], recv_sems.at[index], device)

        gathers = Gathers({name: r[name] for name in jobs}, jobs, spot, sizes, move)
        ring = [peer(spot, "y", step, sizes)[1] for step in range(1, parts)]
        others = [(here + step) % parts for step in range(1, parts)]
        to_right, to_left = ring[0], ring[2]
        number = here * 2 + core
        eights = [(number + step) % eight for step in range(1, eight)]
        eight_at = [(other // 2, base + other % 2) for other in eights]
        r["gathered"][here] = r["features"][...]
        shards_step(r, parts, own, own_in, deep, thin, att, quarter, spare)
        fold_own_step(r, gathers.own("conv_all"))
        greet(
            eight_at
            + [peer(spot, axis, step, sizes)[1] for axis in ("x", "z") for step in range(1, sizes[axis])]
        )
        sent = [
            move(r["blocks"].at[other], r["blocks_in"].at[number], device)
            for other, device in zip(eights, eight_at)
        ]
        sent.append(move(r["pair"].at[1 - core], r["pair_in"].at[core], (here, base + 1 - core)))
        features = Ring(move, r["gathered"], 0, rows, here, to_right, to_left)
        gathers.start("conv_all")
        r["blocks_in"][number] = r["blocks"][number]
        r["pair_in"][core] = r["pair"][core]
        for copy in sent:
            copy.wait_recv()
        att_slab, early = slabs_step(r, own, deep, thin, att)
        gathers.own("early_all")[...] = early
        gathers.start("early_all")
        gathers.own("att_all")[...] = att_slab
        keep = pltpu.make_async_copy(r["ffn_slab"], gathers.own("weights"), local)
        keep.start()
        gathers.pump("early_all")
        gathers.pump("conv_all")
        gathers.pump("early_all")
        features.relay()
        gathers.pump("early_all")
        gathers.start("att_all")
        gathers.pump("early_all", "conv_all")
        gathers.drain("early_all")
        keep.wait()
        gathers.start("weights")
        vectors_ready_step(r, parts, quarter)
        gathers.pump("conv_all", "att_all")
        features.finish()
        for m in range(micros):
            project_step(r, here, m, frames)
            gathers.pump("conv_all", "att_all", "weights")
        gathers.drain("conv_all")
        conv_ready_step(r, per, side)
        gathers.pump("att_all", "weights")
        rings = []
        for m in range(micros):
            conv_step(r, here, m, frames)
            rings.append(Ring(move, r["summed"], m * frames, frames, here, to_right, to_left))
            if m > 0:
                rings[m - 1].relay()
            gathers.pump("att_all", "weights")
        gathers.drain("att_all")
        attend_ready_step(r)
        rings[-1].relay()
        gathers.pump("weights")
        conv_turned_step(r)
        swaps = []
        for m in range(micros):
            rings[m].finish()
            attention_step(r, here, m, frames)
            cells = pl.ds(m * seg, seg)
            swaps += [
                move(r["context"].at[other, cells], r["context_in"].at[here, cells], device)
                for other, device in zip(others, ring)
            ]
            r["context_in"][here, cells] = r["context"][here, cells]
            gathers.pump("weights")
        gathers.drain("weights")
        for copy in swaps:
            copy.wait()
        for copy in sent:
            copy.wait_send()
        for item in rings + [features, gathers]:
            item.close()

    return dict(
        zip(
            outs,
            call_remote(
                kernel,
                [jax.ShapeDtypeStruct(shape, kind) for shape, kind in outs.values()],
                [pl.BlockSpec(memory_space=spaces.get(name, pltpu.VMEM)) for name in ins],
                [pl.BlockSpec(memory_space=spaces.get(name, pltpu.VMEM)) for name in outs],
                list(scratch.values())
                + [
                    pltpu.SemaphoreType.DMA,
                    pltpu.SemaphoreType.DMA((copies,)),
                    pltpu.SemaphoreType.DMA((copies,)),
                ],
                ident, *ins.values(),
            ),
        )
    )


def stages_of(axes, order, sizes):
    left = list(axes)
    result = []
    for axis in order:
        where = left.index(axis)
        left = left[:where] + left[where + 1 :]
        dims = tuple(sizes[a] for a in left)
        result.append((axis, where, tuple(left), dims, sizes[axis] == 4 and len(dims) > 0))
    return result


def sum_scratch(jobs, sizes):
    scratch, copies = {}, 0
    for name, job in jobs.items():
        for part, (cut, order) in enumerate(zip(job["cuts"], job["orders"])):
            block = (cut[1], cut[3])
            dims = tuple(sizes[a] for a in job["axes"])
            key = f"{name}{part}"
            scratch[key + "got"] = pltpu.VMEM(dims + block, LOW)
            if job["far"]:
                scratch[key + "own"] = pltpu.VMEM((2,) + dims[1:] + block, LOW)
            copies += 1
            for number, (axis, _, _, dims, ring) in enumerate(stages_of(job["axes"], order, sizes)):
                if ring:
                    half = (dims[0] // 2,) + dims[1:] + block
                    scratch[f"{key}got{number}"] = pltpu.VMEM((6,) + half, LOW)
                    copies += 6
                else:
                    scratch[f"{key}got{number}"] = pltpu.VMEM((max(sizes[axis] - 1, 1),) + dims + block, LOW)
                    copies += sizes[axis] - 1
                if dims:
                    scratch[f"{key}sum{number}"] = pltpu.VMEM(dims + block, LOW)
    return scratch, copies


class Sums:
    def __init__(self, refs, jobs, spot, sizes, sources, sinks, local):
        self.refs, self.jobs, self.spot, self.sizes = refs, jobs, spot, sizes
        self.sources, self.sinks, self.local = sources, sinks, local
        self.states, self.finished = {}, []

    def move(self, source, target, device):
        copy = self.refs["move"](source, target, device)
        self.finished.append(copy)
        return copy

    def start(self, name):
        job, core = self.jobs[name], self.spot["k"]
        sibling = peer(self.spot, "k", 1, self.sizes)[1]
        states = []
        for part, (cut, order) in enumerate(zip(job["cuts"], job["orders"])):
            key = f"{name}{part}"
            window_at = window(job["axes"], {}, cut)
            got = self.refs[key + "got"]
            copy = self.move(self.sources[name].at[(1 - core,) + window_at], got, sibling)
            near = None
            if job["far"]:

                def near(number, slot, window_at=window_at, key=key, part=part):
                    return pltpu.make_async_copy(
                        self.sources[name].at[(core, number) + window_at[1:]],
                        self.refs[key + "own"].at[slot], self.local.at[2 * part + slot],
                    )

                near(0, 0).start()
            states.append(
                {
                    "key": key, "cut": cut, "held": got, "left": job["axes"], "step": 0, "near": near,
                    "copies": [copy], "half": False,
                    "stages": stages_of(job["axes"], order, self.sizes),
                }
            )
        self.states[name] = states

    def pump(self, *names):
        for name in names:
            for state in self.states[name]:
                self.advance(name, state)

    def drain(self, *names):
        while any(s["step"] <= len(s["stages"]) for name in names for s in self.states[name]):
            self.pump(*names)

    def advance(self, name, state):
        step, stages = state["step"], state["stages"]
        if step > len(stages):
            return
        if step == 0:
            self.add_own(name, state)
        elif state["half"]:
            self.relay(state, stages[step - 1], step - 1)
            return
        else:
            self.add_stage(name, state, stages[step - 1], step - 1)
        if step < len(stages):
            self.send_stage(state, stages[step], step)
        state["step"] = step + 1

    def add_own(self, name, state):
        for copy in state["copies"]:
            copy.wait_recv()
        held, cut = state["held"], state["cut"]
        dims = tuple(self.sizes[a] for a in state["left"])
        if state["near"] is not None:
            near, own = state["near"], self.refs[state["key"] + "own"]
            for number in range(dims[0]):
                slot = number % 2
                if number + 1 < dims[0]:
                    near(number + 1, 1 - slot).start()
                near(number, slot).wait()

                def add(index, number=number, slot=slot):
                    held[(number,) + index] = held[(number,) + index] + own[(slot,) + index]

                loop_blocks(dims[1:], add)
            return
        else:
            source, core = self.sources[name], self.spot["k"]

            def add(index):
                rows, lanes = slice(cut[0], cut[0] + cut[1]), slice(cut[2], cut[2] + cut[3])
                held[index] = held[index] + source[(core,) + index + (rows, lanes)]

        loop_blocks(dims, add)

    def send_stage(self, state, stage, number):
        axis, _, left, dims, ring = stage
        held, got = state["held"], self.refs[f"{state['key']}got{number}"]
        before = state["left"]
        state["copies"] = []
        if not ring:
            for step in range(1, self.sizes[axis]):
                moved, device = peer(self.spot, axis, step, self.sizes)
                at = tuple(moved[a] if a == axis else slice(None) for a in before)
                state["copies"].append(self.move(held.at[at], got.at[step - 1], device))
        else:
            size = dims[0] // 2
            near, far = pl.ds(0, size), pl.ds(size, size)

            def piece(step, half):
                moved = peer(self.spot, axis, step, self.sizes)[0]
                return held.at[
                    tuple(
                        moved[a] if a == axis else (half if a == left[0] else slice(None)) for a in before
                    )
                ]

            right = peer(self.spot, axis, 1, self.sizes)[1]
            back = peer(self.spot, axis, 3, self.sizes)[1]
            state["copies"] = [
                self.move(piece(2, near), got.at[0], right),
                self.move(piece(2, far), got.at[1], back),
                self.move(piece(1, far), got.at[2], right),
                self.move(piece(3, near), got.at[3], back),
            ]
            state["half"] = True

    def relay(self, state, stage, number):
        axis, where, left, dims, _ = stage
        held = state["held"]
        got = self.refs[f"{state['key']}got{number}"]
        size = dims[0] // 2
        ahead, right = peer(self.spot, axis, 1, self.sizes)
        behind, back = peer(self.spot, axis, 3, self.sizes)
        for slot, spot, offset in ((0, ahead, 0), (1, behind, size)):
            state["copies"][slot].wait_recv()

            def add(index, slot=slot, spot=spot, offset=offset):
                full = (index[0] + offset,) + index[1:]
                full = full[:where] + (spot[axis],) + full[where:]
                held[full] = held[full] + got[(slot,) + index]

            loop_blocks((size,) + dims[1:], add)
            at = tuple(
                spot[a] if a == axis else (pl.ds(offset, size) if a == left[0] else slice(None))
                for a in state["left"]
            )
            state["copies"].append(
                self.move(held.at[at], got.at[4 + slot], (right, back)[slot])
            )
        state["half"] = False

    def add_stage(self, name, state, stage, number):
        axis, where, left, dims, ring = stage
        held, cut = state["held"], state["cut"]
        got = self.refs[f"{state['key']}got{number}"]
        target = self.refs[f"{state['key']}sum{number}"] if dims else None
        mine = self.spot[axis]
        for copy in state["copies"][2 if ring else 0 :]:
            copy.wait_recv()
        if ring:
            size = dims[0] // 2
            for offset, first, second in ((0, 4, 3), (size, 2, 5)):

                def add(index, offset=offset, first=first, second=second):
                    full = (index[0] + offset,) + index[1:]
                    own = full[:where] + (mine,) + full[where:]
                    result = widen(held[own]) + widen(got[(first,) + index]) + widen(got[(second,) + index])
                    target[full] = result.astype(LOW)

                loop_blocks((size,) + dims[1:], add)
        else:

            def add(index):
                index = index if dims else ()
                result = widen(held[index[:where] + (mine,) + index[where:]])
                for step in range(self.sizes[axis] - 1):
                    result = result + widen(got[(step,) + index])
                if target is None:
                    rows, lanes = slice(cut[0], cut[0] + cut[1]), slice(cut[2], cut[2] + cut[3])
                    self.sinks[name][rows, lanes] = result
                else:
                    target[index] = result.astype(LOW)

            loop_blocks(dims if dims else (1,), add)
        state["held"], state["left"] = target, left

    def close(self):
        for copy in self.finished:
            copy.wait_send()


def attention_back_step(r, m, frames):
    parts, mine, quarter = r["gctx"].shape
    heads = quarter // HEAD_DIM
    seg = frames // parts
    ratio = HEAD_DIM ** (-0.5)
    at, cells = slice(m * frames, (m + 1) * frames), slice(m * seg, (m + 1) * seg)
    grad = jnp.concatenate([r["gctx_in"][d, cells] for d in range(parts)], axis=0)
    query, keys, value = r["joint"][0, at], r["joint"][1, at], r["joint"][2, at]
    keys_turned = widen(keys).T.astype(LOW)
    queries, key_parts, values = [], [], []
    for h in range(heads):
        cols = slice(h * HEAD_DIM, (h + 1) * HEAD_DIM)
        probs_low = r["probs"][m * heads + h]
        grad_probs = dot_nt(value[:, cols], grad[:, cols])
        weighted = widen(probs_low) * grad_probs
        centre = jnp.sum(weighted, axis=0, keepdims=True)
        slope = (weighted - widen(probs_low) * centre).astype(LOW)
        values.append(dot(probs_low, grad[:, cols]))
        key_parts.append(dot(slope, query[:, cols]) * ratio)
        queries.append(dot(keys_turned[cols], slope) * ratio)
    slopes = [
        jnp.concatenate(queries, axis=0).T.astype(LOW),
        jnp.concatenate(key_parts, axis=1).astype(LOW),
        jnp.concatenate(values, axis=1).astype(LOW),
    ]
    for i, source in enumerate((0, 2)):
        found = column_sum(widen(slopes[source]))
        r["att_sums"][i : i + 1] = found if m == 0 else r["att_sums"][i : i + 1] + found
    slope = jnp.concatenate(slopes, axis=1)
    size = slope.shape[1] // 2
    for k in range(2):
        r["slope_joint"][k, at, :size] = slope[:, k * size : (k + 1) * size]
        r["slope_joint"][k, at, size:] = jnp.zeros((frames, r["slope_joint"].shape[2] - size), LOW)
    terms = dot_nt(slope, r["attend"][...]).astype(LOW)
    for d in range(parts):
        r["terms"][d, cells] = terms[d * seg : (d + 1) * seg]


def attention_weight_step(r):
    parts = r["low"].shape[0]
    for k in range(2):
        pieces = [dot_tn(r["low"][c], r["slope_joint"][k]).astype(LOW) for c in range(parts)]
        grads = dot(r["back_att"][...], jnp.concatenate(pieces, axis=0)).astype(LOW)
        r["att_grad"][k] = grads.reshape(r["att_grad"].shape[1:])


def norm_back_step(r, m, seg):
    parts, _, quarter = r["gpos"].shape
    cells = slice(m * seg, (m + 1) * seg)
    normal, scale = r["normal"][cells], r["scale"][cells, 0:1]
    grad = r["grad_attn"][cells] + r["terms_sum"][...]
    result = norm_back(grad, normal, scale, r["table"][2:3]).astype(LOW)
    for c in range(parts):
        r["gpos"][c, cells] = result[:, c * quarter : (c + 1) * quarter]
    for i, found in enumerate((column_sum(grad * normal), column_sum(grad))):
        r["sums_own"][i : i + 1] = found if m == 0 else r["sums_own"][i : i + 1] + found


def owner_rows(vector, mask, spread, place):
    cells = dot((widen(mask) * vector).astype(LOW), spread)
    return cells if place == 0 else pltpu.roll(cells, place, 1)


def vectors_step(r, own):
    owned = r["owned"][...]
    for v in range(2):
        owned = owned + owner_rows(r["sums_own"][v : v + 1], r["mask"][...], r["spread"][...], v * own)
    r["full"][...] = dot(r["row_full"][...], owned.astype(LOW)).astype(LOW).reshape(r["full"].shape)


def conv_back_step(r, here, m, frames, tall, per):
    parts, mine, quarter = r["gpos"].shape
    groups, fold, many = r["conv_turned"].shape
    inner = fold // FOLD
    blocks = many // inner
    half = blocks * FOLD // 2
    span = frames + blocks * FOLD
    seg = frames // parts
    side = r["conv_grad"].shape[2]
    f32 = jnp.float32
    cells = slice(m * seg, (m + 1) * seg)
    grad = jnp.concatenate([widen(r["gpos_in"][d, cells]) for d in range(parts)], axis=0).T
    for g in range(groups):
        r["grads"][g] = grad[g * inner : (g + 1) * inner]
    live = lax.broadcasted_iota(jnp.int32, (1, frames), 1) < r["spans"][m]

    def one(g, carry):
        index = m * groups + g
        grad = r["grads"][g]
        slope = (grad * smooth_slope(r["before"][index])).astype(LOW)
        r["turn"][index, :, 0:1] = jnp.sum(widen(slope), axis=1, keepdims=True)
        wide = jnp.concatenate([slope, jnp.zeros((inner, span - frames), LOW)], axis=1)
        spread_blocks(wide, r["moved"], inner, blocks)
        fold_rows(r["padded"][index], r["folded"], inner)
        weight = dot_nt(r["moved"][...], r["folded"][...])
        back_sums = dot(r["conv_turned"][g], r["moved"][...])
        total = grad
        for j in range(FOLD):
            part = pltpu.roll(back_sums[j * inner : (j + 1) * inner], (span + j - half) % span, 1)
            total = total + part[:, :frames]
        total = jnp.where(live, total, 0.0).astype(LOW).astype(f32)
        r["turn"][index, :, 1:2] = jnp.sum(total, axis=1, keepdims=True)
        r["grads"][g] = total
        weight = dot(r["back_conv"][...], weight.astype(LOW)).reshape(2, per, tall, fold)
        for n in range(per):
            xz = g * per + n
            for k in range(2):
                piece = weight[k, n]
                if m > 0:
                    piece = piece + widen(r["conv_grad"][k, xz // side, xz % side])
                r["conv_grad"][k, xz // side, xz % side] = piece.astype(LOW)
        return carry

    lax.fori_loop(0, groups, one, 0)
    both = [r["grads"][g] for g in range(groups)]
    r["slopes_all"][here, m * frames : (m + 1) * frames] = jnp.concatenate(both, axis=0).T.astype(LOW)


def conv_sums_step(r, micros):
    groups = r["turn"].shape[0] // micros
    sums = jnp.concatenate(
        [sum(r["turn"][m * groups + g] for m in range(micros)) for g in range(groups)], axis=0
    ).T
    r["conv_sums"][...] = sums[:8]


def finish_step(r, here, m, frames):
    parts, _, narrow = r["gathered"].shape
    f32 = jnp.float32
    size = parts * narrow
    chunk = 256
    mine_at = pl.ds(pl.multiple_of(here * narrow, narrow), narrow)
    gain, shift = r["edges"][0:1, mine_at], r["edges"][1:2, mine_at]
    if m == 0:
        r["edge_sums"][...] = jnp.zeros_like(r["edge_sums"])
        r["proj_grad"][...] = jnp.zeros_like(r["proj_grad"])

    def one(number, carry):
        at = pl.ds(pl.multiple_of(m * frames + number * chunk, chunk), chunk)
        blocks = [widen(r["gathered"][c, at]) for c in range(parts)]
        slopes = [r["slopes_all"][b, at] for b in range(parts)]
        normal, scale = norm_blocks(blocks)
        first = jnp.zeros((chunk, 1), f32)
        second = jnp.zeros((chunk, 1), f32)
        for c in range(parts):
            lanes = slice(c * narrow, (c + 1) * narrow)
            grad = sum(dot_nt(slopes[b], r["proj"][b, lanes]) for b in range(parts))
            scaled = grad * r["edges"][0:1, lanes]
            first = first + jnp.sum(scaled, axis=1, keepdims=True)
            second = second + jnp.sum(scaled * normal[c], axis=1, keepdims=True)
        mean = sum(jnp.sum(block, axis=1, keepdims=True) for block in blocks) / size
        mine = (widen(r["gathered"][here, at]) - mean) * scale
        grad = sum(dot_nt(slopes[b], r["proj"][b, mine_at]) for b in range(parts))
        r["features_grad"][at] = scale * (grad * gain - first / size - mine * (second / size))
        low = (mine * gain + shift).astype(LOW)
        r["proj_grad"][...] = r["proj_grad"][...] + jnp.concatenate(
            [dot_tn(low, slopes[b]) for b in range(parts)], axis=1
        )
        r["edge_sums"][0:1] = r["edge_sums"][0:1] + column_sum(grad * mine)
        r["edge_sums"][1:2] = r["edge_sums"][1:2] + column_sum(grad)
        return carry

    lax.fori_loop(0, frames // chunk, one, 0)


def local_step(r, own, own_in):
    ranks, quarter = r["mask_ch"].shape
    width = r["proj_grad"].shape[1]
    f32 = jnp.float32
    vectors = [
        r["conv_sums"][1:2], r["conv_sums"][0:1], r["att_sums"][0:1], r["att_sums"][1:2],
    ]
    owned = 0.0
    for v in range(4):
        owned = owned + owner_rows(vectors[v], r["mask_ch"][...], r["spread_ch"][...], v * own)
    for v in range(2):
        owned = owned + owner_rows(
            r["edge_sums"][v : v + 1], r["mask_in"][...], r["spread_in"][...], 4 * own + v * own_in
        )
    lanes = owned.shape[1]
    owned = jnp.concatenate([owned, jnp.zeros((ranks, width - lanes), f32)], axis=1)
    result = dot(r["row_proj"][...], r["proj_grad"][...].astype(LOW))
    result = result + dot(r["row_vector"][...], owned.astype(LOW))
    r["local"][...] = result.astype(LOW).reshape(r["local"].shape)


def owners_step(r, parts, own, own_in, deep, thin, att, quarter, fold):
    inner = fold // FOLD
    eight = 2 * parts
    width = quarter * parts
    for j in range(eight):
        r["hidden_out"][:, j * deep : (j + 1) * deep] = r["block_in"][j, :own, :deep]
    pieces = [r["block_in"][j, :own, deep : deep + thin] for j in range(eight)]
    r["output_out"][...] = jnp.concatenate(pieces, axis=1)
    for c in range(parts):
        both = [r["block_in"][2 * c + k, :own, deep + 128 : deep + 128 + att] for k in range(2)]
        both = jnp.concatenate(both, axis=1)
        for i in range(3):
            at = slice(i * width + c * quarter, i * width + (c + 1) * quarter)
            r["attend_out"][:, at] = both[:, i * quarter : (i + 1) * quarter]
    for k in range(2):
        half = width // 2
        r["return_out"][:, k * half : (k + 1) * half] = r["pair_in"][k]


def owners_conv_step(r, own, own_in, fold):
    inner = fold // FOLD
    blocks = r["taps"].shape[0] // FOLD
    for o in range(own):
        rows = r["conv_sum"][o * blocks : (o + 1) * blocks]
        for j in range(FOLD):
            r["taps"][pl.ds(j, blocks, stride=FOLD), :] = rows[:, j * inner : (j + 1) * inner]
        r["conv_out"][o] = r["taps"][...].T
    r["proj_out"][...] = r["local_sum"][:own_in]
    r["few_row"][...] = r["local_sum"][own_in : own_in + 1, : r["few_row"].shape[1]]
    r["full_row"][...] = r["full_sum"][0:1]


def backward_rest(values, sizes, ident, micros, frames, own, own_in, own_hid, own_ret, thin):
    parts, squares, side = sizes["y"], sizes["x"] * sizes["z"], sizes["z"]
    devices, ranks = 2 * parts * squares, 2 * squares
    _, mine, quarter = values["gctx"].shape
    width = parts * quarter
    rows = micros * frames
    narrow = values["gathered"].shape[2]
    groups, fold, many = values["conv_turned"].shape
    inner = fold // FOLD
    blocks = many // inner
    span = frames + blocks * FOLD
    per = inner // own // 2
    tall, lanes_a = values["ffn"].shape[-2:]
    half, deep = width // 2, lanes_a - width // 2 - 128
    att = 3 * quarter // 2
    wide = att + -att % 128
    eight = 2 * parts
    seg = frames // parts
    f32 = jnp.float32

    ones = {}
    ones["back_att"] = onehot(natural_of(width, parts, squares), np.arange(width))
    slab = np.arange(many).reshape(2, per, own, blocks)
    ones["back_conv"] = onehot(
        np.arange(many),
        [slab[(o // own) % 2, o // own // 2, o % own, b] for b in range(blocks) for o in range(inner)],
    )
    count = 8 * own + own_hid
    lane = np.arange(count + -count % 128)
    ones["mask"] = onehot(np.arange(devices), np.arange(width) // own)
    ones["spread"] = onehot(np.arange(width) % own, lane)
    full_rows = np.full((devices, 16), -1)
    full_rows[:, 0] = np.arange(devices).reshape(parts, squares, 2).transpose(2, 0, 1).reshape(-1)
    ones["row_full"] = onehot(full_rows.reshape(-1), np.arange(devices))
    few = 4 * own + 2 * own_in
    few = np.arange(few + -few % 128)
    ones["mask_ch"] = onehot(np.arange(ranks), np.arange(quarter) // own)
    ones["spread_ch"] = onehot(np.arange(quarter) % own, few)
    ones["mask_in"] = onehot(np.arange(ranks), np.arange(narrow) // own_in)
    ones["spread_in"] = onehot(np.arange(narrow) % own_in, few)
    high = own_in + 1 + -(own_in + 1) % 16
    order = np.arange(ranks).reshape(squares, 2).T.reshape(-1)
    proj_rows = np.full((ranks, high), -1)
    proj_rows[:, :own_in] = order[:, None] * own_in + np.arange(own_in)[None, :]
    ones["row_proj"] = onehot(proj_rows.reshape(-1), np.arange(narrow))
    vector_rows = np.full((ranks, high), -1)
    vector_rows[:, own_in] = order
    ones["row_vector"] = onehot(vector_rows.reshape(-1), np.arange(ranks))

    cut_lanes = lanes_a // 256 * 128 + 128 * (lanes_a // 128 % 2)
    jobs = {
        "ffn": {
            "axes": ("y", "x", "z"), "far": True,
            "cuts": [(0, tall, 0, cut_lanes), (0, tall, cut_lanes, lanes_a - cut_lanes)],
            "orders": [("x", "z", "y"), ("z", "x", "y")],
        },
        "full": {
            "axes": ("y", "x", "z"), "far": False, "cuts": [(0, 16, 0, len(lane))],
            "orders": [("z", "x", "y")],
        },
        "att": {
            "axes": ("x", "z"), "far": False, "cuts": [(0, tall, 0, wide)], "orders": [("x", "z")],
        },
        "conv": {
            "axes": ("x", "z"), "far": False,
            "cuts": [(0, tall, 0, fold // 2), (0, tall, fold // 2, fold // 2)],
            "orders": [("x", "z"), ("z", "x")],
        },
        "local": {
            "axes": ("x", "z"), "far": False, "cuts": [(0, high, 0, width)], "orders": [("z", "x")],
        },
    }
    scratch, copies = sum_scratch(jobs, sizes)
    copies += micros * (2 * (parts - 1) + 12) + eight
    lead = {"y": parts, "x": sizes["x"], "z": sizes["z"]}
    low_rows = own + -own % 8
    block_lanes = deep + 128 + wide
    scratch.update(
        {
            "gctx_in": pltpu.VMEM((parts, mine, quarter), LOW),
            "terms": pltpu.VMEM((parts, mine, width), LOW),
            "terms_held": pltpu.VMEM((micros, 6, seg // 2, width), LOW),
            "terms_sum": pltpu.VMEM((seg, width), f32),
            "slope_joint": pltpu.VMEM((2, rows, wide), LOW),
            "att_grad": pltpu.VMEM((2, sizes["x"], sizes["z"], tall, wide), LOW),
            "att_sums": pltpu.VMEM((8, quarter), f32),
            "gpos": pltpu.VMEM((parts, mine, quarter), LOW),
            "gpos_in": pltpu.VMEM((parts, mine, quarter), LOW),
            "sums_own": pltpu.VMEM((8, width), f32),
            "full": pltpu.VMEM((2, parts, sizes["x"], sizes["z"], 16, len(lane)), LOW),
            "grads": pltpu.VMEM((groups, inner, frames), f32),
            "turn": pltpu.VMEM((micros * groups, inner, 128), f32),
            "moved": pltpu.VMEM((many, span), LOW),
            "folded": pltpu.VMEM((fold, span), LOW),
            "slopes_all": pltpu.VMEM((parts, rows, quarter), LOW),
            "conv_sums": pltpu.VMEM((8, quarter), f32),
            "conv_grad": pltpu.VMEM((2, sizes["x"], sizes["z"], tall, fold), LOW),
            "proj_grad": pltpu.VMEM((narrow, width), f32),
            "edge_sums": pltpu.VMEM((8, narrow), f32),
            "local": pltpu.VMEM((2, sizes["x"], sizes["z"], high, width), LOW),
            "ffn_sum": pltpu.VMEM((tall, lanes_a), f32),
            "full_sum": pltpu.VMEM((16, len(lane)), f32),
            "conv_sum": pltpu.VMEM((tall, fold), f32),
            "local_sum": pltpu.VMEM((high, width), f32),
            "block_in": pltpu.VMEM((eight, low_rows, block_lanes), f32),
            "pair_in": pltpu.VMEM((2, own_ret, half), f32),
            "taps": pltpu.VMEM((blocks * FOLD, inner), f32),
            "att_sum": pltpu.VMEM((tall, wide), f32),
            "block": pltpu.VMEM((eight, low_rows, block_lanes), f32),
            "pair": pltpu.VMEM((2, own_ret, half), f32),
        }
    )
    outs = {
        "features_grad": ((rows, narrow), f32),
        "full_row": ((1, len(lane)), f32),
        "few_row": ((1, len(few)), f32),
        "proj_out": ((own_in, width), f32),
        "conv_out": ((own, inner, blocks * FOLD), f32),
        "hidden_out": ((own, eight * deep), f32),
        "output_out": ((own, width), f32),
        "attend_out": ((own, 3 * width), f32),
        "return_out": ((own_ret, width), f32),
    }
    ins = dict(values)
    ins.update({name: jnp.asarray(value, LOW) for name, value in ones.items()})
    spaces = {"spans": pltpu.SMEM, "ffn": pl.ANY}
    names = list(ins) + list(outs) + list(scratch)

    def kernel(*refs):
        r = dict(zip(names, refs))
        local, send_sems, recv_sems = refs[len(names) :]
        spot = place(side)
        here, core, rank = spot["y"], spot["k"], lax.axis_index("rows")
        base = rank - core
        used = [0]

        def move(source, target, device):
            index = used[0]
            used[0] += 1
            return send(source, target, send_sems.at[index], recv_sems.at[index], device)

        r["move"] = move
        sources = {
            "ffn": r["ffn"], "full": r["full"], "att": r["att_grad"], "conv": r["conv_grad"],
            "local": r["local"],
        }
        sinks = {
            "ffn": r["ffn_sum"], "full": r["full_sum"], "att": r["att_sum"], "conv": r["conv_sum"],
            "local": r["local_sum"],
        }
        sums = Sums(r, jobs, spot, sizes, sources, sinks, local)
        ring = [peer(spot, "y", step, sizes)[1] for step in range(1, parts)]
        others = [(here + step) % parts for step in range(1, parts)]
        number = here * 2 + core
        eights = [(number + step) % eight for step in range(1, eight)]
        eight_at = [(other // 2, base + other % 2) for other in eights]
        greet(
            eight_at
            + [peer(spot, axis, step, sizes)[1] for axis in ("x", "z") for step in range(1, sizes[axis])]
        )
        sent = []

        def swap(source, target, m):
            cells = pl.ds(m * seg, seg)
            copies = [
                move(source.at[other, cells], target.at[here, cells], device)
                for other, device in zip(others, ring)
            ]
            target[here, cells] = source[here, cells]
            sent.extend(copies)
            return copies

        def arrived(copies):
            for copy in copies:
                copy.wait_recv()

        to_right, to_left = ring[0], ring[2]
        right, across, left = [(here + step) % 4 for step in (1, 2, 3)]
        terms = r["terms"]

        def ring_add(m):
            held, size = r["terms_held"], seg // 2
            near, far = pl.ds(m * seg, size), pl.ds(m * seg + size, size)
            return [
                move(terms.at[across, near], held.at[m, 0], to_right),
                move(terms.at[across, far], held.at[m, 1], to_left),
                move(terms.at[right, far], held.at[m, 2], to_right),
                move(terms.at[left, near], held.at[m, 3], to_left),
            ]

        def ring_relay(m, copies):
            held, size = r["terms_held"], seg // 2
            near, far = pl.ds(m * seg, size), pl.ds(m * seg + size, size)
            copies[0].wait_recv()
            terms[right, near] = terms[right, near] + held[m, 0]
            copies.append(move(terms.at[right, near], held.at[m, 4], to_right))
            copies[1].wait_recv()
            terms[left, far] = terms[left, far] + held[m, 1]
            copies.append(move(terms.at[left, far], held.at[m, 5], to_left))

        def ring_end(m, copies):
            held, size = r["terms_held"], seg // 2
            near, far = pl.ds(m * seg, size), pl.ds(m * seg + size, size)
            arrived(copies[2:])
            sent.extend(copies)
            r["terms_sum"][:size] = widen(terms[here, near]) + widen(held[m, 4]) + widen(held[m, 3])
            r["terms_sum"][size:] = widen(terms[here, far]) + widen(held[m, 2]) + widen(held[m, 5])

        swapped = [swap(r["gctx"], r["gctx_in"], m) for m in range(micros)]
        sums.start("ffn")
        added = []
        for m in range(micros):
            arrived(swapped[m])
            attention_back_step(r, m, frames)
            added.append(ring_add(m))
            if m > 0:
                ring_relay(m - 1, added[m - 1])
        attention_weight_step(r)
        ring_relay(micros - 1, added[-1])
        sums.start("att")
        sums.pump("ffn")
        swapped = []
        for m in range(micros):
            ring_end(m, added[m])
            norm_back_step(r, m, seg)
            swapped.append(swap(r["gpos"], r["gpos_in"], m))
        vectors_step(r, own)
        sums.start("full")
        sums.pump("att")
        rings = []
        for m in range(micros):
            arrived(swapped[m])
            conv_back_step(r, here, m, frames, tall, per)
            rings.append(Ring(move, r["slopes_all"], m * frames, frames, here, to_right, to_left))
            if m > 0:
                rings[m - 1].relay()
            sums.pump("ffn", "att", "full")
        sums.start("conv")
        conv_sums_step(r, micros)
        sums.pump("ffn", "att", "full")
        rings[-1].relay()
        for m in range(micros):
            rings[m].finish()
            finish_step(r, here, m, frames)
            sums.pump("conv", "ffn", "att", "full")
        local_step(r, own, own_in)
        sums.start("local")
        sums.pump("conv", "ffn", "att", "full")
        sums.pump("local")
        sums.drain("ffn", "att")

        for j in range(eight):
            at = slice(j * own, (j + 1) * own)
            r["block"][j, :own, : deep + 128] = r["ffn_sum"][at, half:]
            r["block"][j, :own, deep + 128 :] = r["att_sum"][at]
        for k in range(2):
            r["pair"][k] = r["ffn_sum"][k * own_ret : (k + 1) * own_ret, :half]
        last = [
            move(r["block"].at[other], r["block_in"].at[number], device)
            for other, device in zip(eights, eight_at)
        ]
        last.append(move(r["pair"].at[1 - core], r["pair_in"].at[core], (here, base + 1 - core)))
        r["block_in"][number] = r["block"][number]
        r["pair_in"][core] = r["pair"][core]
        sums.drain("conv", "full", "local")
        owners_conv_step(r, own, own_in, fold)
        for copy in last:
            copy.wait()
        owners_step(r, parts, own, own_in, deep, thin, att, quarter, fold)
        for copy in sent:
            copy.wait_send()
        for item in rings + [sums]:
            item.close()

    return dict(
        zip(
            outs,
            call_remote(
                kernel,
                [jax.ShapeDtypeStruct(shape, kind) for shape, kind in outs.values()],
                [pl.BlockSpec(memory_space=spaces.get(name, pltpu.VMEM)) for name in ins],
                whole(len(outs)),
                list(scratch.values())
                + [
                    pltpu.SemaphoreType.DMA((4,)),
                    pltpu.SemaphoreType.DMA((copies,)),
                    pltpu.SemaphoreType.DMA((copies,)),
                ],
                ident, *ins.values(),
            ),
        )
    )


def per_device(
    features, lengths, input_gain, input_bias, proj_weight, proj_bias, conv_weight, conv_bias,
    encoder_gain, encoder_bias, attend_weight, query_bias, value_bias, output_weight, output_bias,
    attend_gain, attend_bias, hidden_weight, hidden_bias, return_weight, return_bias, final_gain,
    final_bias, out_grad,
):
    parts = lax.axis_size("ch")
    ranks = lax.axis_size("rows")
    side = math.isqrt(ranks // 2)
    sizes = {"y": parts, "x": side, "z": side, "k": 2}
    here = lax.axis_index("ch").astype(jnp.int32).reshape(1)
    micros, _, frames, narrow = features.shape
    own = proj_bias.shape[0]
    width = proj_weight.shape[1]
    quarter = width // parts
    inner, taps = conv_weight.shape[1:]
    blocks = taps // FOLD
    hidden = hidden_weight.shape[1]
    own_in = input_gain.shape[0]
    own_hid = hidden_bias.shape[0]
    seg = out_grad.shape[2]
    eight = 2 * parts
    squares = side * side
    tall = eight * own
    deep, thin, att = hidden // eight, width // eight, 3 * quarter // 2
    half = width // 2
    rows = micros * frames
    mine = micros * seg
    fold = FOLD * inner
    spans = lengths.reshape(micros)

    small = (proj_bias, conv_bias, encoder_gain, encoder_bias, query_bias, value_bias, output_bias,
             attend_gain, attend_bias, return_bias, final_gain, final_bias)
    own_ret = return_weight.shape[0]
    f = forward_start(
        {
            "features": features.reshape(rows, narrow), "hidden_raw": hidden_weight,
            "output_raw": output_weight, "attend_raw": attend_weight, "proj_raw": proj_weight,
            "return_raw": return_weight, "conv_raw": conv_weight, "small": jnp.stack(small),
            "ends": jnp.stack([input_gain, input_bias]), "hid_own": hidden_bias.reshape(1, own_hid),
            "spans": spans,
        },
        sizes, 0, micros, frames, own, own_in, own_hid, own_ret, len(small),
    )
    output, grad_attn, grad_context, ffn, normal, scale, owned = feed_forward(
        f["context_in"], f["summed"], here, out_grad.reshape(mine, width), f["weights"], f["table"],
        f["hid_bias"], micros, frames, thin, own, own_hid,
    )
    third = backward_rest(
        {
            "gctx": grad_context, "grad_attn": grad_attn, "normal": normal, "scale": scale,
            "owned": owned, "spans": spans,
            **{
                name: f[name]
                for name in ("low", "joint", "probs", "attend", "table", "before", "padded",
                             "conv_turned", "gathered", "proj", "edges")
            },
            "ffn": ffn.reshape(2, parts, side, side, tall, -1),
        },
        sizes, 9, micros, frames, own, own_in, own_hid, own_ret, thin,
    )

    tail, full = third["few_row"][0], third["full_row"][0]
    local_parts = [tail[i * own : (i + 1) * own] for i in range(4)]
    full_parts = [full[i * own : (i + 1) * own] for i in range(8)]
    return (
        output.reshape(out_grad.shape),
        third["features_grad"].reshape(features.shape),
        tail[4 * own : 4 * own + own_in],
        tail[4 * own + own_in : 4 * own + 2 * own_in],
        third["proj_out"],
        local_parts[0],
        third["conv_out"],
        local_parts[1],
        full_parts[0],
        full_parts[1],
        third["attend_out"],
        local_parts[2],
        local_parts[3],
        third["output_out"],
        full_parts[2],
        full_parts[3],
        full_parts[4],
        third["hidden_out"],
        full[8 * own : 8 * own + own_hid],
        third["return_out"],
        full_parts[5],
        full_parts[6],
        full_parts[7],
    )


def solution(mesh):
    vector, matrix, cube = P(ALL), P(ALL, None), P(ALL, None, None)
    weights = (
        vector, vector, matrix, vector, cube, vector, vector, vector, matrix, vector, vector,
        matrix, vector, vector, vector, matrix, vector, matrix, vector, vector, vector,
    )
    by_channel = P(None, "rows", None, "ch")
    by_frame = P(None, "rows", "ch", None)
    return jax.shard_map(
        per_device,
        mesh=mesh,
        in_specs=(by_channel, P(None, "rows")) + weights + (by_frame,),
        out_specs=(by_frame, by_channel) + weights,
        check_vma=False,
    )
```

```python
import functools
import math

import jax
import jax.numpy as jnp
import numpy as np
from jax import lax
from jax.experimental import pallas as pl
from jax.experimental.pallas import tpu as pltpu
from jax.sharding import PartitionSpec as P

HEAD_DIM = 64
EPS = 1e-05
NEGATIVE = -1000000000.0
FOLD = 16
ALL = ("ch", "rows")
LOW = jnp.bfloat16
MESH = pl.DeviceIdType.MESH
ROOM = 62 * 1024 * 1024


def widen(values):
    return values.astype(jnp.float32)


def dot(left, right):
    return jnp.dot(left, right, preferred_element_type=jnp.float32)


def contract(spec, left, right):
    return jnp.einsum(spec, left, right, preferred_element_type=jnp.float32)


def place(side):
    rank = lax.axis_index("rows")
    return {
        "y": lax.axis_index("ch"),
        "x": rank // (2 * side),
        "z": (rank // 2) % side,
        "k": rank % 2,
    }


def peer(spot, axis, step, sizes):
    moved = dict(spot)
    moved[axis] = (spot[axis] + step) % sizes[axis]
    return moved, (moved["y"], (moved["x"] * sizes["z"] + moved["z"]) * 2 + moved["k"])


def greet(targets):
    barrier = pltpu.get_barrier_semaphore()
    for target in targets:
        pl.semaphore_signal(barrier, inc=1, device_id=target, device_id_type=MESH)
    pl.semaphore_wait(barrier, len(targets))


def send(source, target, send_sem, recv_sem, device):
    copy = pltpu.make_async_remote_copy(
        src_ref=source, dst_ref=target, send_sem=send_sem, recv_sem=recv_sem,
        device_id=device, device_id_type=MESH,
    )
    copy.start()
    return copy


def whole(count):
    return [pl.BlockSpec(memory_space=pltpu.VMEM)] * count


def call_remote(kernel, shapes, ins, outs, scratch, ident, *values):
    return pl.pallas_call(
        kernel,
        out_shape=shapes,
        in_specs=ins,
        out_specs=outs,
        scratch_shapes=scratch,
        compiler_params=pltpu.CompilerParams(
            collective_id=ident, has_side_effects=True, vmem_limit_bytes=ROOM
        ),
    )(*values)


def staged_call(ident, ins, outs, scratch, copies, body, spaces, kept=(), keeps=0):
    lazy = [
        name for name, value in ins.items()
        if name not in spaces and value.size * value.dtype.itemsize >= 49152
    ]
    names = [name + "@" if name in lazy else name for name in ins]
    names += [name + "@" if name in kept else name for name in outs]
    scratch = dict(scratch)
    scratch.update({name: pltpu.VMEM(ins[name].shape, ins[name].dtype) for name in lazy})
    scratch.update({name: pltpu.VMEM(*outs[name]) for name in kept})
    names += list(scratch)

    def kernel(*refs):
        r = dict(zip(names, refs))
        load_sems, keep_sems, send_sems, recv_sems = refs[len(names) :]
        loads, stores, used = {}, [], [0]
        for number, name in enumerate(lazy):
            loads[name] = pltpu.make_async_copy(r[name + "@"], r[name], load_sems.at[number])
            loads[name].start()

        def need(*wanted):
            for name in wanted:
                if name in loads:
                    loads.pop(name).wait()

        def copy_here(source, target):
            copy = pltpu.make_async_copy(source, target, keep_sems.at[len(stores)])
            copy.start()
            stores.append(copy)
            return copy

        def keep(name, at=None):
            if at is None:
                copy_here(r[name], r[name + "@"])
            else:
                copy_here(r[name].at[at], r[name + "@"].at[at])

        def move(source, target, device):
            index = used[0]
            used[0] += 1
            return send(source, target, send_sems.at[index], recv_sems.at[index], device)

        waited = body(r, move, need, keep, copy_here)
        need(*list(loads))
        for copy in stores:
            if not any(copy is other for other in waited):
                copy.wait()

    space = lambda name: pl.ANY if name in lazy or name in kept else spaces.get(name, pltpu.VMEM)
    results = call_remote(
        kernel,
        [jax.ShapeDtypeStruct(shape, kind) for shape, kind in outs.values()],
        [pl.BlockSpec(memory_space=space(name)) for name in ins],
        [pl.BlockSpec(memory_space=space(name)) for name in outs],
        list(scratch.values())
        + [
            pltpu.SemaphoreType.DMA((max(len(lazy), 1),)),
            pltpu.SemaphoreType.DMA((max(keeps, 1),)),
            pltpu.SemaphoreType.DMA((copies,)),
            pltpu.SemaphoreType.DMA((copies,)),
        ],
        ident, *ins.values(),
    )
    return dict(zip(outs, results))


def plane(spot, sizes):
    found = []
    for step in range(1, sizes["x"] * sizes["z"]):
        moved = dict(spot)
        moved["x"] = (spot["x"] + step // sizes["z"]) % sizes["x"]
        moved["z"] = (spot["z"] + step % sizes["z"]) % sizes["z"]
        found.append((moved, (moved["y"], (moved["x"] * sizes["z"] + moved["z"]) * 2 + moved["k"])))
    return found


def window(axes, fixed, cut):
    lead = tuple(fixed.get(axis, slice(None)) for axis in axes)
    return lead + (pl.ds(cut[0], cut[1]), pl.ds(cut[2], cut[3]))


def loop_blocks(dims, body):
    count = math.prod(dims)
    if count == 1:
        body((0,) * len(dims))
        return

    def step(flat, carry):
        index = []
        rest = flat
        for size in reversed(dims):
            index.append(rest % size)
            rest = rest // size
        body(tuple(reversed(index)))
        return carry

    lax.fori_loop(0, count, step, 0)


def dot_nt(left, right):
    return lax.dot_general(left, right, (((1,), (1,)), ((), ())), preferred_element_type=jnp.float32)


def dot_tn(left, right):
    return lax.dot_general(left, right, (((0,), (0,)), ((), ())), preferred_element_type=jnp.float32)


def pick(left, onehot):
    return dot(left, onehot).astype(LOW)


def pick_wide(values, onehot):
    high = values.astype(LOW)
    rest = (values - widen(high)).astype(LOW)
    return dot(high, onehot) + dot(rest, onehot)


def smooth(values):
    return 0.5 * values * (1.0 + lax.erf(values * 0.7071067811865476))


def smooth_slope(values):
    return 0.5 * (1.0 + lax.erf(values * 0.7071067811865476)) + values * 0.3989422804014327 * jnp.exp(
        -0.5 * values * values
    )


def norm(values):
    mean = jnp.mean(values, axis=-1, keepdims=True)
    centred = values - mean
    scale = lax.rsqrt(jnp.mean(centred * centred, axis=-1, keepdims=True) + EPS)
    return centred * scale, scale


def norm_back(incoming, normal, scale, gain):
    scaled = incoming * gain
    first = jnp.mean(scaled, axis=-1, keepdims=True)
    second = jnp.mean(scaled * normal, axis=-1, keepdims=True)
    return scale * (scaled - first - normal * second)


def norm_blocks(blocks):
    size = sum(block.shape[-1] for block in blocks)
    mean = sum(jnp.sum(block, axis=-1, keepdims=True) for block in blocks) / size
    centred = [block - mean for block in blocks]
    spread = sum(jnp.sum(block * block, axis=-1, keepdims=True) for block in centred) / size
    scale = lax.rsqrt(spread + EPS)
    return [block * scale for block in centred], scale


def column_sum(values):
    return jnp.sum(values, axis=0, keepdims=True)


def local_call(kernel, shapes, scratch, *values):
    count = len(values)
    return pl.pallas_call(
        kernel,
        out_shape=[jax.ShapeDtypeStruct(shape, kind) for shape, kind in shapes],
        in_specs=[
            pl.BlockSpec(memory_space=pltpu.SMEM if value.dtype == jnp.int32 else pltpu.VMEM)
            for value in values
        ],
        out_specs=whole(len(shapes)),
        scratch_shapes=scratch,
        compiler_params=pltpu.CompilerParams(vmem_limit_bytes=ROOM),
    )(*values)


def onehot(rows, columns):
    return (np.asarray(rows)[:, None] == np.asarray(columns)[None, :]).astype(LOW)


def natural_of(count, parts, squares):
    cells = np.arange(count).reshape(parts, squares, 2, -1)
    return cells.transpose(1, 0, 2, 3).reshape(count)


def fold_rows(padded, spread_ref, inner):
    for j in range(FOLD):
        moved = padded if j == 0 else pltpu.roll(padded, padded.shape[1] - j, 1)
        spread_ref[j * inner : (j + 1) * inner, :] = moved


def spread_blocks(padded, spread_ref, inner, blocks):
    for b in range(blocks):
        moved = padded if b == 0 else pltpu.roll(padded, FOLD * b, 1)
        spread_ref[b * inner : (b + 1) * inner, :] = moved


def own_frames(ref, spot, micros, frames, parts):
    seg = frames // parts
    blocks = []
    for c in range(parts):
        pieces = [
            widen(ref[c, pl.ds(pl.multiple_of(m * frames + spot * seg, seg), seg)])
            for m in range(micros)
        ]
        blocks.append(jnp.concatenate(pieces, axis=0))
    return blocks


def feed_forward(
    context, summed, upstream, weights, table, hid_bias, sizes, ident, micros, frames, thin, own, own_hid
):
    parts, mine, quarter = context.shape
    squares, side = sizes["x"] * sizes["z"], sizes["z"]
    weights = weights.reshape(2, parts, squares, *weights.shape[-2:])
    tall, lanes = weights.shape[-2:]
    width = parts * quarter
    half, deep = width // 2, lanes - width // 2 - 128
    most = half + deep
    eight = 2 * parts
    seg = frames // parts
    f32 = jnp.float32
    hidden = eight * deep
    devices = 2 * parts * squares
    ones = {"nat": onehot(np.arange(width), natural_of(width, parts, squares))}
    ones["place"] = np.zeros((width // 128, 256, 128), np.float32)
    for tile in range(width // 128):
        first = tile * 128 // thin
        for lane in range(128):
            channel = tile * 128 + lane
            ones["place"][tile, (channel // thin - first) * 128 + channel % thin, lane] = 1.0
    lane = np.arange(128)
    ones["cut"] = np.stack(
        [onehot(np.arange(width), np.where(lane < thin, j * thin + lane, -1)) for j in range(eight)]
    )
    lane = np.arange(8 * own + own_hid + -(8 * own + own_hid) % 128)
    ones["mask"] = onehot(np.arange(devices), np.arange(width) // own)
    ones["mask_hid"] = onehot(np.arange(devices), np.arange(hidden) // own_hid)
    ones["spread"] = onehot(np.arange(width) % own, lane)
    ones["spread_hid"] = onehot(
        np.arange(hidden) % own_hid, np.where(lane >= 8 * own, lane - 8 * own, -1)
    )
    ins = {
        "nat": None, "place": None, "context": context, "table": table, "hid_bias": hid_bias,
        "summed": summed, "weights": weights, "upstream": upstream,
    }
    ins.update({name: jnp.asarray(value, LOW) for name, value in ones.items()})
    outs = {
        "output": ((mine, width), LOW),
        "grad_attn": ((mine, width), f32),
        "gctx_in": ((parts, mine, quarter), LOW),
        "slabs": ((2, parts, squares, tall, lanes), LOW),
        "normal": ((mine, width), f32),
        "scale": ((mine, 128), f32),
        "owned": ((devices, len(lane)), f32),
    }
    scratch = {
        "own_rows": pltpu.VMEM((parts, mine, quarter), LOW),
        "w": pltpu.VMEM((2, parts, squares, tall, most), LOW),
        "w_out": pltpu.VMEM((2, parts, squares, tall, 128), LOW),
        "joined": pltpu.VMEM((width, width), LOW),
        "pre": pltpu.VMEM((mine, hidden), f32),
        "act": pltpu.VMEM((mine, hidden), LOW),
        "inner": pltpu.VMEM((mine, hidden), LOW),
        "hid_sums": pltpu.VMEM((1, hidden), f32),
        "gctx": pltpu.VMEM((parts, mine, quarter), LOW),
    }

    def body(r, move, need, keep, copy_here):
        spot = place(side)
        here = spot["y"]
        loads = [
            copy_here(
                r["summed"].at[:, pl.ds(pl.multiple_of(m * frames + here * seg, seg), seg)],
                r["own_rows"].at[:, pl.ds(m * seg, seg)],
            )
            for m in range(micros)
        ]
        loads.append(copy_here(r["weights"].at[:, :, :, :, pl.ds(most, 128)], r["w_out"]))
        chunks = [
            copy_here(r["weights"].at[:, c, :, :, pl.ds(0, most)], r["w"].at[:, c]) for c in range(parts)
        ]
        ring = [peer(spot, "y", step, sizes)[1] for step in range(1, parts)]
        others = [(here + step) % parts for step in range(1, parts)]
        greet(ring)

        def block(c, k, begin, size):
            return r["w"][k, c, :, :, begin : begin + size].reshape(width, size)

        table = r["table"]
        for copy in loads[:micros]:
            copy.wait()
        normal, scale = norm_blocks([widen(r["own_rows"][c]) for c in range(parts)])
        normal = jnp.concatenate(normal, axis=1)
        r["normal"][...] = normal
        r["scale"][...] = jnp.broadcast_to(scale, r["scale"].shape)
        keep("normal")
        keep("scale")
        encoded = normal * table[2:3] + table[3:4]
        need("nat", "place")
        nat = r["nat"]
        ctx_slab = sum(
            dot(r["context"][c], nat[c * quarter : (c + 1) * quarter]) for c in range(parts)
        ).astype(LOW)
        loads[micros].wait()
        for tile in range(width // 128):
            first = tile * 128 // thin
            last = min(first + 1, eight - 1)
            both = [r["w_out"][j % 2, j // 2].reshape(width, 128) for j in (first, last)]
            r["joined"][:, tile * 128 : (tile + 1) * 128] = pick(
                jnp.concatenate(both, axis=1), r["place"][tile]
            )
        attn_sum = encoded + dot(ctx_slab, r["joined"][...]) + table[6:7]
        normal_att, scale_att = norm(attn_sum)
        attn_norm = normal_att * table[7:8] + table[8:9]
        attn_slab = pick(attn_norm.astype(LOW), nat[...])
        outer = [jnp.zeros((mine, half), f32), jnp.zeros((mine, half), f32)]
        for c in range(parts):
            chunks[c].wait()
            for k in range(2):
                begin = (2 * c + k) * deep
                pre = dot(attn_slab, block(c, k, half, deep)) + r["hid_bias"][:, begin : begin + deep]
                share = 0.5 * (1.0 + lax.erf(pre * 0.7071067811865476))
                r["pre"][:, begin : begin + deep] = share + pre * 0.3989422804014327 * jnp.exp(-0.5 * pre * pre)
                r["act"][:, begin : begin + deep] = (pre * share).astype(LOW)
            act = r["act"][:, 2 * c * deep : 2 * (c + 1) * deep]
            outer = [outer[k] + dot(act, block(c, k, 0, half)) for k in range(2)]
        ffn_sum = attn_norm + jnp.concatenate(outer, axis=1) + table[9:10]
        normal_fin, scale_fin = norm(ffn_sum)
        need("upstream")
        r["output"][...] = (normal_fin * table[10:11] + table[11:12]).astype(LOW)
        keep("output")
        up = widen(r["upstream"][...])
        grad_ffn = norm_back(up, normal_fin, scale_fin, table[10:11])
        slope_outer = grad_ffn.astype(LOW)
        vectors = {
            5: column_sum(widen(slope_outer)), 6: column_sum(up * normal_fin), 7: column_sum(up)
        }
        grad_slab = jnp.zeros((mine, width), f32)
        for c in range(parts):
            columns = slice(2 * c * deep, 2 * (c + 1) * deep)
            grad_act = sum(
                dot_nt(slope_outer[:, k * half : (k + 1) * half], block(c, k, 0, half)) for k in range(2)
            )
            slope_inner = (grad_act * r["pre"][:, columns]).astype(LOW)
            r["inner"][:, columns] = slope_inner
            r["hid_sums"][:, columns] = column_sum(widen(slope_inner))
            for k in range(2):
                grad_slab = grad_slab + dot_nt(
                    slope_inner[:, k * deep : (k + 1) * deep], block(c, k, half, deep)
                )
        high = grad_slab.astype(LOW)
        rest = (grad_slab - widen(high)).astype(LOW)
        grad_norm2 = grad_ffn + dot_nt(high, nat[...]) + dot_nt(rest, nat[...])
        vectors[3] = column_sum(grad_norm2 * normal_att)
        vectors[4] = column_sum(grad_norm2)
        grad_attn = norm_back(grad_norm2, normal_att, scale_att, table[7:8])
        r["grad_attn"][...] = grad_attn
        keep("grad_attn")
        slope_att = grad_attn.astype(LOW)
        vectors[2] = column_sum(widen(slope_att))
        gctx_slab = dot_nt(slope_att, r["joined"][...]).astype(LOW)
        for c in range(parts):
            r["gctx"][c] = dot_nt(gctx_slab, nat[c * quarter : (c + 1) * quarter]).astype(LOW)
        swaps = [
            move(r["gctx"].at[other], r["gctx_in"].at[here], device)
            for other, device in zip(others, ring)
        ]
        r["gctx_in"][here] = r["gctx"][here]

        attn_turned = widen(attn_slab).T.astype(LOW)
        for c in range(parts):
            columns = slice(2 * c * deep, 2 * (c + 1) * deep)
            act_turned = widen(r["act"][:, columns]).T.astype(LOW)
            for k in range(2):
                begin = (2 * c + k) * deep
                grad_ret = dot(act_turned, slope_outer[:, k * half : (k + 1) * half]).astype(LOW)
                r["slabs"][k, c, :, :, :half] = grad_ret.reshape(squares, tall, half)
                grad_hid = dot(attn_turned, r["inner"][:, begin : begin + deep]).astype(LOW)
                r["slabs"][k, c, :, :, half:most] = grad_hid.reshape(squares, tall, deep)
                keep("slabs", (k, c, slice(None), slice(None), pl.ds(0, most)))
        need("cut", "mask", "mask_hid", "spread", "spread_hid")
        ctx_turned = widen(ctx_slab).T.astype(LOW)
        for c in range(parts):
            for k in range(2):
                grad = dot(ctx_turned, pick(slope_att, r["cut"][2 * c + k])).astype(LOW)
                r["slabs"][k, c, :, :, most:] = grad.reshape(squares, tall, 128)
        keep("slabs", (slice(None), slice(None), slice(None), slice(None), pl.ds(most, 128)))
        owned = dot((widen(r["mask_hid"][...]) * r["hid_sums"][...]).astype(LOW), r["spread_hid"][...])
        for v, vector in vectors.items():
            owned = owned + owner_rows(vector, r["mask"][...], r["spread"][...], v * own)
        r["owned"][...] = owned
        for copy in swaps:
            copy.wait()
        return loads + chunks

    results = staged_call(
        ident, ins, outs, scratch, parts - 1, body,
        {"summed": pl.ANY, "weights": pl.ANY, "context": pltpu.VMEM, "table": pltpu.VMEM},
        ("output", "grad_attn", "slabs", "normal", "scale"), 32,
    )
    return tuple(
        results[name]
        for name in ("output", "grad_attn", "gctx_in", "slabs", "normal", "scale", "owned")
    )


def gather_copies(jobs, sizes):
    total = 0
    for job in jobs.values():
        for order in job["orders"]:
            total += 1
            for number, axis in enumerate(order):
                if axis == "p":
                    total += sizes["x"] * sizes["z"] - 1
                else:
                    total += 6 if number > 0 and sizes[axis] == 4 else sizes[axis] - 1
    return total


class Gathers:
    def __init__(self, buffers, jobs, spot, sizes, move):
        self.buffers, self.jobs, self.spot, self.sizes, self.move = buffers, jobs, spot, sizes, move
        self.states, self.finished = {}, []

    def send(self, name, cut, fixed, device):
        axes = self.jobs[name]["axes"]
        view = self.buffers[name].at[(self.spot["k"],) + window(axes, fixed, cut)]
        copy = self.move(view, view, device)
        self.finished.append(copy)
        return copy

    def own(self, name):
        axes = self.jobs[name]["axes"]
        return self.buffers[name].at[(self.spot["k"],) + tuple(self.spot[a] for a in axes)]

    def start(self, name):
        job = self.jobs[name]
        self.states[name] = [
            {"cut": cut, "order": order, "step": 0, "copies": [], "half": False, "ring": False}
            for cut, order in zip(job["cuts"], job["orders"])
        ]
        self.pump(name)

    def pump(self, *names):
        for name in names:
            for state in self.states[name]:
                self.advance(name, state)

    def drain(self, *names):
        while any(s["step"] <= len(s["order"]) + 1 for name in names for s in self.states[name]):
            self.pump(*names)

    def advance(self, name, state):
        step, order, cut = state["step"], state["order"], state["cut"]
        if step > len(order) + 1:
            return
        if state["half"]:
            axis, halved, near, far, fixed = state["half"]
            for slot, turn, half in ((0, 3, near), (1, 1, far)):
                state["copies"][slot].wait_recv()
                spot = peer(self.spot, axis, turn, self.sizes)[0]
                device = peer(self.spot, axis, 4 - turn, self.sizes)[1]
                at = dict(fixed)
                at[axis], at[halved] = spot[axis], half
                state["copies"].append(self.send(name, cut, at, device))
            state["half"] = False
            return
        for copy in state["copies"][2 if state["ring"] else 0 :]:
            copy.wait_recv()
        state["copies"], state["ring"] = [], False
        state["step"] = step + 1
        if step > len(order):
            return
        if step == len(order):
            device = peer(self.spot, "k", 1, self.sizes)[1]
            state["copies"] = [self.send(name, cut, {}, device)]
            return
        axis = order[step]
        if axis == "p":
            fixed = {"x": self.spot["x"], "z": self.spot["z"]}
            for _, device in plane(self.spot, self.sizes):
                state["copies"].append(self.send(name, cut, fixed, device))
            return
        fixed = {a: self.spot[a] for a in order[step:]}
        if step > 0 and self.sizes[axis] == 4:
            halved = order[0]
            size = self.sizes[halved] // 2
            near, far = pl.ds(0, size), pl.ds(size, size)
            for half, turn in ((near, 1), (far, 3), (far, 1), (near, 3)):
                at = dict(fixed)
                at[halved] = half
                device = peer(self.spot, axis, turn, self.sizes)[1]
                state["copies"].append(self.send(name, cut, at, device))
            state["half"], state["ring"] = (axis, halved, near, far, fixed), True
        else:
            for turn in range(1, self.sizes[axis]):
                device = peer(self.spot, axis, turn, self.sizes)[1]
                state["copies"].append(self.send(name, cut, fixed, device))

    def close(self):
        for copy in self.finished:
            copy.wait_send()


class Ring:
    def __init__(self, move, buffer, begin, count, here, to_right, to_left):
        self.move, self.buffer, self.here = move, buffer, here
        self.to_right, self.to_left = to_right, to_left
        half = count // 2
        self.near, self.far = pl.ds(begin, half), pl.ds(begin + half, half)
        self.copies = [
            self.shift(here, self.near, to_right), self.shift(here, self.far, to_left),
            self.shift(here, self.far, to_right), self.shift(here, self.near, to_left),
        ]

    def shift(self, block, rows, device):
        view = self.buffer.at[block, rows]
        return self.move(view, view, device)

    def relay(self):
        self.copies[0].wait_recv()
        self.copies.append(self.shift((self.here + 3) % 4, self.near, self.to_right))
        self.copies[1].wait_recv()
        self.copies.append(self.shift((self.here + 1) % 4, self.far, self.to_left))

    def finish(self):
        for copy in self.copies[2:]:
            copy.wait_recv()

    def close(self):
        for copy in self.copies:
            copy.wait_send()


def shards_step(r, parts, own, own_in, deep, thin, att, quarter):
    f32 = jnp.float32
    eight = 2 * parts
    width = thin * eight
    half = width // 2
    hid, out, joint = [widen(r[name][...]) for name in ("hidden_raw", "output_raw", "attend_raw")]
    proj, ret = widen(r["proj_raw"][...]), widen(r["return_raw"][...])
    tall, lanes = r["blocks"].shape[1:]
    small, ends = widen(r["small"][...]), widen(r["ends"][...])
    row = [small[i : i + 1] for i in range(small.shape[0])] + [ends[0:1], ends[1:2]]
    row = jnp.concatenate(row + [widen(r["hid_own"][...])], axis=1)
    row = jnp.concatenate([row, jnp.zeros((1, lanes - row.shape[1]), f32)], axis=1)
    for c in range(parts):
        both = jnp.concatenate(
            [joint[:, i * width + c * quarter : i * width + (c + 1) * quarter] for i in range(3)], axis=1
        )
        for k in range(2):
            j = 2 * c + k
            top = [
                hid[:, j * deep : (j + 1) * deep], out[:, j * thin : (j + 1) * thin],
                both[:, k * att : (k + 1) * att],
            ]
            low = [proj[:, k * half : (k + 1) * half], jnp.zeros((own_in, lanes - half), f32)]
            rows = [jnp.concatenate(top, axis=1), jnp.concatenate(low, axis=1), row]
            if tall > own + own_in + 1:
                rows.append(jnp.zeros((tall - own - own_in - 1, lanes), f32))
            r["blocks"][j] = jnp.concatenate(rows, axis=0).astype(LOW)
    for k in range(2):
        rows = [ret[:, k * half : (k + 1) * half]]
        if r["pair"].shape[1] > ret.shape[0]:
            rows.append(jnp.zeros((r["pair"].shape[1] - ret.shape[0], half), f32))
        r["pair"][k] = jnp.concatenate(rows, axis=0).astype(LOW)


def fold_own_step(r, target):
    own, inner, taps = r["conv_raw"].shape
    blocks = taps // FOLD
    rows = []
    for o in range(own):
        r["taps"][o] = widen(r["conv_raw"][o]).T
        pieces = [r["taps"][o, pl.ds(j, blocks, stride=FOLD), :] for j in range(FOLD)]
        rows.append(jnp.concatenate(pieces, axis=1))
    target[...] = jnp.concatenate(rows, axis=0).astype(LOW)


def slabs_step(r, own, deep, thin, att):
    f32 = jnp.float32
    blocks = r["blocks_in"][...].reshape(-1, r["blocks_in"].shape[2])
    main = dot(r["slab_rows"][...], blocks)
    pair = dot(r["pair_rows"][...], r["pair_in"][...].reshape(-1, r["pair_in"].shape[2]))
    tall = main.shape[0]
    r["ffn_slab"][...] = jnp.concatenate(
        [pair, main[:, :deep], main[:, deep : deep + thin], jnp.zeros((tall, 128 - thin), f32)], axis=1
    ).astype(LOW)
    att_slab = jnp.concatenate(
        [main[:, deep + thin :], jnp.zeros((tall, -att % 128), f32)], axis=1
    ).astype(LOW)
    early = dot(r["first_rows"][...], blocks[:, : r["early_all"].shape[-1]]).astype(LOW)
    return att_slab, early


def vectors_ready_step(r, parts, quarter):
    wide_in = r["nat_in"].shape[0]
    width = r["table"].shape[1]
    devices = r["vector_rows"].shape[0]
    early, half = r["early_all"], width // 2
    tall = 2 * parts * wide_in // devices
    both = [
        pick(r["nat_in"][...], early[k, :, :, :tall, :half].reshape(wide_in, half)) for k in range(2)
    ]
    both = jnp.concatenate(both, axis=1)
    for c in range(parts):
        r["proj"][c] = both[:, c * quarter : (c + 1) * quarter]
    lanes = early.shape[-1]
    cells = widen(early[0, :, :, tall:].reshape(-1, early.shape[-2] - tall, lanes))
    cells = cells[:, : 2 * parts].reshape(devices, lanes).astype(LOW)
    turned = dot(r["vector_rows"][...], cells).T.astype(LOW)
    spread = (dot(turned, r["owner"][...]) * widen(r["take"][...])).astype(LOW)
    table = dot(r["row_of"][...], spread)
    r["table"][...] = table
    for c in range(parts):
        r["quarters"][c] = table[:, c * quarter : (c + 1) * quarter]
    r["columns"][...] = jnp.concatenate([table, jnp.zeros((112, width), jnp.float32)], axis=0).T
    spread = (dot(turned, r["owner_in"][...]) * widen(r["take_in"][...])).astype(LOW)
    r["edges"][...] = dot(r["row_in"][...], spread)
    r["hid_bias"][...] = column_sum(dot(turned, r["owner_hid"][...]) * widen(r["take_hid"][...]))


def conv_ready_step(r, per, side):
    groups, rows, fold = r["conv"].shape
    for g in range(groups):
        taken = jnp.concatenate(
            [
                r["conv_all"][k, (g * per + n) // side, (g * per + n) % side]
                for k in range(2) for n in range(per)
            ],
            axis=0,
        )
        r["conv"][g] = dot(r["conv_order"][...], taken).astype(LOW)


def conv_turned_step(r):
    for g in range(r["conv"].shape[0]):
        r["conv_turned"][g] = widen(r["conv"][g]).T.astype(LOW)


def attend_ready_step(r):
    width = r["nat"].shape[0]
    both = [r["att_all"][k].reshape(width, -1) for k in range(2)]
    slab_cols = pick(jnp.concatenate(both, axis=1), r["place_att"][...])
    r["attend"][...] = pick(r["nat"][...], slab_cols)


def project_step(r, here, m, frames):
    parts, _, narrow = r["gathered"].shape
    groups, _, fold = r["conv"].shape
    inner = fold // FOLD
    half = (r["padded"].shape[2] - frames) // 2
    at = slice(m * frames, (m + 1) * frames)
    normal, _ = norm_blocks([widen(r["gathered"][c, at]) for c in range(parts)])
    low = []
    for c, block in enumerate(normal):
        lanes = slice(c * narrow, (c + 1) * narrow)
        low.append((block * r["edges"][0:1, lanes] + r["edges"][1:2, lanes]).astype(LOW))
    result = dot(jnp.concatenate(low, axis=1), r["proj"][here]) + r["quarters"][here, 0:1]
    live = lax.broadcasted_iota(jnp.int32, (frames, 1), 0) < r["spans"][m]
    turned = jnp.where(live, result, 0.0).T
    for g in range(groups):
        piece = turned[g * inner : (g + 1) * inner]
        r["plain"][m * groups + g] = piece
        edge = jnp.zeros((inner, half), LOW)
        r["padded"][m * groups + g] = jnp.concatenate([edge, piece.astype(LOW), edge], axis=1)


def conv_step(r, here, m, frames):
    groups, many, fold = r["conv"].shape
    inner = fold // FOLD
    blocks = many // inner
    span = r["padded"].shape[2]
    quarter = groups * inner

    def one(g, carry):
        index = m * groups + g
        fold_rows(r["padded"][index], r["folded"], inner)
        sums = dot(r["conv"][g], r["folded"][...])
        total = sums[:inner, :frames]
        for b in range(1, blocks):
            part = pltpu.roll(sums[b * inner : (b + 1) * inner], span - FOLD * b, 1)
            total = total + part[:, :frames]
        start = pl.multiple_of(here * quarter + g * inner, 16)
        before = total + r["columns"][pl.ds(start, inner), 1:2]
        r["before"][index] = before
        r["plain"][index] = r["plain"][index] + smooth(before)
        return carry

    lax.fori_loop(0, groups, one, 0)
    both = [r["plain"][m * groups + g] for g in range(groups)]
    r["summed"][here, m * frames : (m + 1) * frames] = jnp.concatenate(both, axis=0).T.astype(LOW)


def attention_step(r, here, m, frames):
    parts, _, quarter = r["summed"].shape
    heads = quarter // HEAD_DIM
    seg = frames // parts
    ratio = HEAD_DIM ** (-0.5)
    at = slice(m * frames, (m + 1) * frames)
    normal, _ = norm_blocks([widen(r["summed"][c, at]) for c in range(parts)])
    joint = jnp.zeros((frames, 3 * quarter), jnp.float32)
    for c in range(parts):
        low = (normal[c] * r["quarters"][c, 2:3] + r["quarters"][c, 3:4]).astype(LOW)
        r["low"][c, at] = low
        joint = joint + dot(low, r["attend"][c * quarter : (c + 1) * quarter])
    query = joint[:, :quarter] + r["quarters"][here, 4:5]
    keys = joint[:, quarter : 2 * quarter]
    value = joint[:, 2 * quarter :] + r["quarters"][here, 5:6]
    joint_low = [v.astype(LOW) for v in (query, keys, value)]
    for i in range(3):
        r["joint"][i, at] = joint_low[i]
    value_turned = value.T.astype(LOW)
    live = lax.broadcasted_iota(jnp.int32, (frames, 1), 0) < r["spans"][m]
    results = []
    for h in range(heads):
        cols = slice(h * HEAD_DIM, (h + 1) * HEAD_DIM)
        scores = dot_nt(joint_low[1][:, cols], joint_low[0][:, cols]) * ratio
        scores = jnp.where(live, scores, NEGATIVE)
        expo = jnp.exp(scores - jnp.max(scores, axis=0, keepdims=True))
        probs = (expo / jnp.sum(expo, axis=0, keepdims=True)).astype(LOW)
        r["probs"][m * heads + h] = probs
        results.append(dot(value_turned[cols], probs))
    context = jnp.concatenate(results, axis=0).T.astype(LOW)
    for d in range(parts):
        r["context"][d, m * seg : (m + 1) * seg] = context[d * seg : (d + 1) * seg]


def forward_start(values, sizes, ident, micros, frames, own, own_in, own_hid, own_ret, count):
    parts, squares, side = sizes["y"], sizes["x"] * sizes["z"], sizes["z"]
    devices = 2 * parts * squares
    rows, narrow = values["features"].shape
    _, inner, taps = values["conv_raw"].shape
    eight, blocks, fold = 2 * parts, taps // FOLD, inner * FOLD
    tall_block, tall_pair = own + own_in + 1, own_ret
    tall_block, tall_pair = tall_block + -tall_block % 16, tall_pair + -tall_pair % 16
    tall = eight * own
    width, wide_in, hidden = own * devices, own_in * devices, own_hid * devices
    quarter = width // parts
    half = width // 2
    groups = quarter // inner
    many = blocks * inner
    per = inner // own // 2
    heads = quarter // HEAD_DIM
    span = frames + blocks * FOLD
    seg = frames // parts
    mine = micros * seg
    deep, thin, att = hidden // eight, width // eight, 3 * quarter // 2
    wide = att + -att % 128
    lanes_a = half + deep + 128
    f32 = jnp.float32

    ones = {}
    j, s = np.divmod(np.arange(tall), own)
    ones["slab_rows"] = onehot(j * tall_block + s, np.arange(eight * tall_block))
    early_rows = eight * own_in + eight + -(eight * own_in + eight) % 16
    j, s = np.divmod(np.arange(eight * own_in), own_in)
    from_rows = np.full(early_rows, -1)
    from_rows[: eight * own_in] = j * tall_block + own + s
    from_rows[eight * own_in : eight * own_in + eight] = np.arange(eight) * tall_block + own + own_in
    ones["first_rows"] = onehot(from_rows, np.arange(eight * tall_block))
    j, s = np.divmod(np.arange(2 * own_ret), own_ret)
    ones["pair_rows"] = onehot(j * tall_pair + s, np.arange(2 * tall_pair))
    ones["nat_in"] = onehot(np.arange(wide_in), natural_of(wide_in, parts, squares))
    ones["nat"] = onehot(np.arange(width), natural_of(width, parts, squares))
    lanes = np.arange(2 * att)
    ones["place_att"] = onehot(np.arange(2 * wide), np.where(lanes < att, lanes, lanes - att + wide))
    slab = np.arange(many).reshape(2, per, own, blocks)
    ones["conv_order"] = onehot(
        [slab[(o // own) % 2, o // own // 2, o % own, b] for b in range(blocks) for o in range(inner)],
        np.arange(many),
    )
    vector_lanes = count * own + 2 * own_in + own_hid
    early_lanes = max(half, vector_lanes + -vector_lanes % 128)
    spots = np.arange(devices).reshape(squares, parts, 2).transpose(1, 0, 2).reshape(-1)
    ones["vector_rows"] = onehot(spots, np.arange(devices))
    lane = np.arange(early_lanes)
    ask = np.arange(width)
    edge = count * own
    ones["take"] = (lane[:, None] < edge) & (lane[:, None] % own == ask[None, :] % own)
    ones["row_of"] = onehot(np.arange(16), np.where(lane < edge, lane // own, -1))
    ones["owner"] = onehot(np.arange(devices), ask // own)
    ones["owner_in"] = onehot(np.arange(devices), np.arange(wide_in) // own_in)
    ends = (lane >= edge) & (lane < edge + 2 * own_in)
    ones["take_in"] = ends[:, None] & (
        (lane[:, None] - edge) % own_in == (np.arange(wide_in) % own_in)[None, :]
    )
    ones["row_in"] = onehot(np.arange(16), np.where(ends, (lane - edge) // own_in, -1))
    ones["owner_hid"] = onehot(np.arange(devices), np.arange(hidden) // own_hid)
    ones["take_hid"] = onehot(lane, edge + 2 * own_in + np.arange(hidden) % own_hid)

    all_axes, row_axes = ("y", "x", "z"), ("x", "z")
    cut_a = lanes_a // 256 * 128 + 128 * (lanes_a // 128 % 2)
    jobs = {
        "conv_all": {
            "axes": row_axes,
            "cuts": [(0, tall, 0, fold // 2), (0, tall, fold // 2, fold // 2)],
            "orders": [("z", "x"), ("x", "z")],
        },
        "early_all": {
            "axes": row_axes, "cuts": [(0, early_rows, 0, early_lanes)], "orders": [("p",)],
        },
        "att_all": {"axes": row_axes, "cuts": [(0, tall, 0, wide)], "orders": [("p",)]},
        "weights": {
            "axes": all_axes,
            "cuts": [(0, tall, 0, cut_a), (0, tall, cut_a, lanes_a - cut_a)],
            "orders": [("y", "z", "x"), ("y", "x", "z")],
        },
    }
    copies = gather_copies(jobs, sizes) + eight + 6 * (1 + micros) + micros * (parts - 1)
    lead = (sizes["x"], sizes["z"])
    lanes_cut = deep + thin + att
    scratch = {
        "blocks": pltpu.VMEM((eight, tall_block, lanes_cut), LOW),
        "pair": pltpu.VMEM((2, tall_pair, half), LOW),
        "taps": pltpu.VMEM((own, taps, inner), f32),
        "blocks_in": pltpu.VMEM((eight, tall_block, lanes_cut), LOW),
        "pair_in": pltpu.VMEM((2, tall_pair, half), LOW),
        "ffn_slab": pltpu.VMEM((tall, lanes_a), LOW),
        "early_all": pltpu.VMEM((2,) + lead + (early_rows, early_lanes), LOW),
        "conv_all": pltpu.VMEM((2,) + lead + (tall, fold), LOW),
        "att_all": pltpu.VMEM((2,) + lead + (tall, wide), LOW),
        "quarters": pltpu.VMEM((parts, 16, quarter), f32),
        "columns": pltpu.VMEM((width, 128), f32),
        "conv": pltpu.VMEM((groups, many, fold), LOW),
        "plain": pltpu.VMEM((micros * groups, inner, frames), f32),
        "folded": pltpu.VMEM((fold, span), LOW),
        "context": pltpu.VMEM((parts, mine, quarter), LOW),
    }
    outs = {
        "weights": ((2, parts) + lead + (tall, lanes_a), LOW),
        "gathered": ((parts, rows, narrow), LOW),
        "proj": ((parts, wide_in, quarter), LOW),
        "table": ((16, width), f32),
        "edges": ((16, wide_in), f32),
        "hid_bias": ((1, hidden), f32),
        "attend": ((width, 3 * quarter), LOW),
        "conv_turned": ((groups, fold, many), LOW),
        "padded": ((micros * groups, inner, span), LOW),
        "before": ((micros * groups, inner, frames), f32),
        "summed": ((parts, rows, quarter), LOW),
        "low": ((parts, rows, quarter), LOW),
        "joint": ((3, rows, quarter), LOW),
        "probs": ((micros * heads, frames, frames), LOW),
        "context_in": ((parts, mine, quarter), LOW),
    }
    ins = dict(values)
    ins.update({name: jnp.asarray(value, LOW) for name, value in ones.items()})
    kept = ("gathered", "proj", "table", "edges", "hid_bias", "attend", "conv_turned", "padded",
            "before", "summed", "low", "joint", "probs")

    def body(r, move, need, keep, copy_here):
        spot = place(side)
        here, core, rank = spot["y"], spot["k"], lax.axis_index("rows")
        base = rank - core
        gathers = Gathers({name: r[name] for name in jobs}, jobs, spot, sizes, move)
        ring = [peer(spot, "y", step, sizes)[1] for step in range(1, parts)]
        others = [(here + step) % parts for step in range(1, parts)]
        to_right, to_left = ring[0], ring[2]
        number = here * 2 + core
        eights = [(number + step) % eight for step in range(1, eight)]
        eight_at = [(other // 2, base + other % 2) for other in eights]
        shards_step(r, parts, own, own_in, deep, thin, att, quarter)
        need("features")
        r["gathered"][here] = r["features"][...]
        greet(eight_at + [device for _, device in plane(spot, sizes)])
        sent = [
            move(r["blocks"].at[other], r["blocks_in"].at[number], device)
            for other, device in zip(eights, eight_at)
        ]
        sent.append(move(r["pair"].at[1 - core], r["pair_in"].at[core], (here, base + 1 - core)))
        features = Ring(move, r["gathered"], 0, rows, here, to_right, to_left)
        r["blocks_in"][number] = r["blocks"][number]
        r["pair_in"][core] = r["pair"][core]
        need("conv_raw")
        fold_own_step(r, gathers.own("conv_all"))
        gathers.start("conv_all")
        need("slab_rows", "first_rows", "pair_rows")
        for copy in sent:
            copy.wait_recv()
        att_slab, early = slabs_step(r, own, deep, thin, att)
        gathers.own("early_all")[...] = early
        gathers.start("early_all")
        first = copy_here(r["ffn_slab"], gathers.own("weights"))
        gathers.own("att_all")[...] = att_slab
        gathers.start("att_all")
        first.wait()
        gathers.start("weights")
        gathers.pump("conv_all")
        features.relay()
        gathers.pump("early_all", "weights")
        gathers.drain("early_all")
        gathers.pump("conv_all")
        need("nat_in", "vector_rows", "owner", "take", "row_of", "owner_in", "take_in", "row_in",
             "owner_hid", "take_hid")
        vectors_ready_step(r, parts, quarter)
        for name in ("proj", "table", "edges", "hid_bias"):
            keep(name)
        gathers.pump("weights")
        features.finish()
        keep("gathered")
        project_step(r, here, 0, frames)
        gathers.pump("conv_all", "att_all")
        for m in range(1, micros):
            project_step(r, here, m, frames)
        keep("padded")
        gathers.drain("conv_all")
        gathers.pump("weights")
        need("conv_order")
        conv_ready_step(r, per, side)
        rings = []
        for m in range(micros):
            conv_step(r, here, m, frames)
            rings.append(Ring(move, r["summed"], m * frames, frames, here, to_right, to_left))
        keep("before")
        gathers.drain("att_all")
        need("nat", "place_att")
        attend_ready_step(r)
        keep("attend")
        rings[0].relay()
        conv_turned_step(r)
        keep("conv_turned")
        gathers.pump("weights")
        for item in rings[1:]:
            item.relay()
        swaps = []
        for m in range(micros):
            rings[m].finish()
            attention_step(r, here, m, frames)
            cells = pl.ds(m * seg, seg)
            swaps += [
                move(r["context"].at[other, cells], r["context_in"].at[here, cells], device)
                for other, device in zip(others, ring)
            ]
            r["context_in"][here, cells] = r["context"][here, cells]
            at = pl.ds(m * frames, frames)
            for name in ("low", "joint"):
                keep(name, (slice(None), at))
            keep("probs", pl.ds(m * heads, heads))
            if m == 0:
                gathers.pump("weights")
        keep("summed")
        gathers.drain("weights")
        for copy in swaps:
            copy.wait()
        for copy in sent:
            copy.wait_send()
        for item in rings + [features, gathers]:
            item.close()
        return [first]

    return staged_call(
        ident, ins, outs, scratch, copies, body,
        {"spans": pltpu.SMEM, "weights": pl.ANY, "small": pltpu.VMEM}, kept, 32,
    )


def stages_of(axes, order, sizes):
    left = list(axes)
    result = []
    for axis in order:
        if axis == "p":
            result.append((axis, 0, (), (), False))
            continue
        where = left.index(axis)
        left = left[:where] + left[where + 1 :]
        dims = tuple(sizes[a] for a in left)
        result.append((axis, where, tuple(left), dims, sizes[axis] == 4 and len(dims) > 0))
    return result


def sum_scratch(jobs, sizes):
    scratch, copies = {}, 0
    for name, job in jobs.items():
        for part, (cut, order) in enumerate(zip(job["cuts"], job["orders"])):
            block = (cut[1], cut[3])
            dims = tuple(sizes[a] for a in job["axes"])
            key = f"{name}{part}"
            scratch[key + "got"] = pltpu.VMEM(dims + block, LOW)
            if job["far"]:
                scratch[key + "own"] = pltpu.VMEM((2,) + dims[1:] + block, LOW)
            copies += 1
            for number, (axis, _, _, dims, ring) in enumerate(stages_of(job["axes"], order, sizes)):
                if ring:
                    half = (dims[0] // 2,) + dims[1:] + block
                    scratch[f"{key}got{number}"] = pltpu.VMEM((6,) + half, LOW)
                    copies += 6
                else:
                    others = sizes["x"] * sizes["z"] - 1 if axis == "p" else sizes[axis] - 1
                    scratch[f"{key}got{number}"] = pltpu.VMEM((max(others, 1),) + dims + block, LOW)
                    copies += others
                if dims:
                    scratch[f"{key}sum{number}"] = pltpu.VMEM(dims + block, LOW)
    return scratch, copies


class Sums:
    def __init__(self, refs, jobs, spot, sizes, sources, sinks, local):
        self.refs, self.jobs, self.spot, self.sizes = refs, jobs, spot, sizes
        self.sources, self.sinks, self.local = sources, sinks, local
        self.states, self.finished = {}, []

    def move(self, source, target, device):
        copy = self.refs["move"](source, target, device)
        self.finished.append(copy)
        return copy

    def start(self, name):
        job, core = self.jobs[name], self.spot["k"]
        sibling = peer(self.spot, "k", 1, self.sizes)[1]
        states = []
        for part, (cut, order) in enumerate(zip(job["cuts"], job["orders"])):
            key = f"{name}{part}"
            window_at = window(job["axes"], {}, cut)
            got = self.refs[key + "got"]
            copy = self.move(self.sources[name].at[(1 - core,) + window_at], got, sibling)
            near = None
            if job["far"]:

                def near(number, slot, window_at=window_at, key=key, part=part):
                    return pltpu.make_async_copy(
                        self.sources[name].at[(core, number) + window_at[1:]],
                        self.refs[key + "own"].at[slot], self.local.at[2 * part + slot],
                    )

                near(0, 0).start()
            states.append(
                {
                    "key": key, "cut": cut, "held": got, "left": job["axes"], "step": 0, "near": near,
                    "copies": [copy], "half": False,
                    "stages": stages_of(job["axes"], order, self.sizes),
                }
            )
        self.states[name] = states

    def pump(self, *names):
        for name in names:
            for state in self.states[name]:
                self.advance(name, state)

    def drain(self, *names):
        while any(s["step"] <= len(s["stages"]) for name in names for s in self.states[name]):
            self.pump(*names)

    def advance(self, name, state):
        step, stages = state["step"], state["stages"]
        if step > len(stages):
            return
        if step == 0:
            self.add_own(name, state)
        elif state["half"]:
            self.relay(state, stages[step - 1], step - 1)
            return
        else:
            self.add_stage(name, state, stages[step - 1], step - 1)
        if step < len(stages):
            self.send_stage(state, stages[step], step)
        state["step"] = step + 1

    def add_own(self, name, state):
        for copy in state["copies"]:
            copy.wait_recv()
        held, cut = state["held"], state["cut"]
        dims = tuple(self.sizes[a] for a in state["left"])
        if state["near"] is not None:
            near, own = state["near"], self.refs[state["key"] + "own"]
            for number in range(dims[0]):
                slot = number % 2
                if number + 1 < dims[0]:
                    near(number + 1, 1 - slot).start()
                near(number, slot).wait()

                def add(index, number=number, slot=slot):
                    held[(number,) + index] = held[(number,) + index] + own[(slot,) + index]

                loop_blocks(dims[1:], add)
            return
        else:
            source, core = self.sources[name], self.spot["k"]

            def add(index):
                rows, lanes = slice(cut[0], cut[0] + cut[1]), slice(cut[2], cut[2] + cut[3])
                held[index] = held[index] + source[(core,) + index + (rows, lanes)]

        loop_blocks(dims, add)

    def send_stage(self, state, stage, number):
        axis, _, left, dims, ring = stage
        held, got = state["held"], self.refs[f"{state['key']}got{number}"]
        before = state["left"]
        state["copies"] = []
        if axis == "p":
            for number, (moved, device) in enumerate(plane(self.spot, self.sizes)):
                source = held.at[moved["x"], moved["z"]]
                state["copies"].append(self.move(source, got.at[number], device))
        elif not ring:
            for step in range(1, self.sizes[axis]):
                moved, device = peer(self.spot, axis, step, self.sizes)
                at = tuple(moved[a] if a == axis else slice(None) for a in before)
                state["copies"].append(self.move(held.at[at], got.at[step - 1], device))
        else:
            size = dims[0] // 2
            near, far = pl.ds(0, size), pl.ds(size, size)

            def piece(step, half):
                moved = peer(self.spot, axis, step, self.sizes)[0]
                return held.at[
                    tuple(
                        moved[a] if a == axis else (half if a == left[0] else slice(None)) for a in before
                    )
                ]

            right = peer(self.spot, axis, 1, self.sizes)[1]
            back = peer(self.spot, axis, 3, self.sizes)[1]
            state["copies"] = [
                self.move(piece(2, near), got.at[0], right),
                self.move(piece(2, far), got.at[1], back),
                self.move(piece(1, far), got.at[2], right),
                self.move(piece(3, near), got.at[3], back),
            ]
            state["half"] = True

    def relay(self, state, stage, number):
        axis, where, left, dims, _ = stage
        held = state["held"]
        got = self.refs[f"{state['key']}got{number}"]
        size = dims[0] // 2
        ahead, right = peer(self.spot, axis, 1, self.sizes)
        behind, back = peer(self.spot, axis, 3, self.sizes)
        for slot, spot, offset in ((0, ahead, 0), (1, behind, size)):
            state["copies"][slot].wait_recv()

            def add(index, slot=slot, spot=spot, offset=offset):
                full = (index[0] + offset,) + index[1:]
                full = full[:where] + (spot[axis],) + full[where:]
                held[full] = held[full] + got[(slot,) + index]

            loop_blocks((size,) + dims[1:], add)
            at = tuple(
                spot[a] if a == axis else (pl.ds(offset, size) if a == left[0] else slice(None))
                for a in state["left"]
            )
            state["copies"].append(
                self.move(held.at[at], got.at[4 + slot], (right, back)[slot])
            )
        state["half"] = False

    def add_stage(self, name, state, stage, number):
        axis, where, left, dims, ring = stage
        held, cut = state["held"], state["cut"]
        got = self.refs[f"{state['key']}got{number}"]
        target = self.refs[f"{state['key']}sum{number}"] if dims else None
        mine = None if axis == "p" else self.spot[axis]
        for copy in state["copies"][2 if ring else 0 :]:
            copy.wait_recv()
        if ring:
            size = dims[0] // 2
            for offset, first, second in ((0, 4, 3), (size, 2, 5)):

                def add(index, offset=offset, first=first, second=second):
                    full = (index[0] + offset,) + index[1:]
                    own = full[:where] + (mine,) + full[where:]
                    result = widen(held[own]) + widen(got[(first,) + index]) + widen(got[(second,) + index])
                    target[full] = result.astype(LOW)

                loop_blocks((size,) + dims[1:], add)
        else:

            def add(index):
                index = index if dims else ()
                if axis == "p":
                    result = widen(held[self.spot["x"], self.spot["z"]])
                else:
                    result = widen(held[index[:where] + (mine,) + index[where:]])
                for step in range(len(state["copies"])):
                    result = result + widen(got[(step,) + index])
                if target is None:
                    rows, lanes = slice(cut[0], cut[0] + cut[1]), slice(cut[2], cut[2] + cut[3])
                    self.sinks[name][rows, lanes] = result
                else:
                    target[index] = result.astype(LOW)

            loop_blocks(dims if dims else (1,), add)
        state["held"], state["left"] = target, left

    def close(self):
        for copy in self.finished:
            copy.wait_send()


def attention_back_step(r, m, frames):
    parts, mine, quarter = r["gctx_in"].shape
    heads = quarter // HEAD_DIM
    seg = frames // parts
    ratio = HEAD_DIM ** (-0.5)
    at, cells = slice(m * frames, (m + 1) * frames), slice(m * seg, (m + 1) * seg)
    grad = jnp.concatenate([r["gctx_in"][d, cells] for d in range(parts)], axis=0)
    query, keys, value = r["joint"][0, at], r["joint"][1, at], r["joint"][2, at]
    keys_turned = widen(keys).T.astype(LOW)
    queries, key_parts, values = [], [], []
    for h in range(heads):
        cols = slice(h * HEAD_DIM, (h + 1) * HEAD_DIM)
        probs_low = r["probs"][m * heads + h]
        grad_probs = dot_nt(value[:, cols], grad[:, cols])
        weighted = widen(probs_low) * grad_probs
        centre = jnp.sum(weighted, axis=0, keepdims=True)
        slope = (weighted - widen(probs_low) * centre).astype(LOW)
        values.append(dot(probs_low, grad[:, cols]))
        key_parts.append(dot(slope, query[:, cols]) * ratio)
        queries.append(dot(keys_turned[cols], slope) * ratio)
    slopes = [
        jnp.concatenate(queries, axis=0).T.astype(LOW),
        jnp.concatenate(key_parts, axis=1).astype(LOW),
        jnp.concatenate(values, axis=1).astype(LOW),
    ]
    for i, source in enumerate((0, 2)):
        found = column_sum(widen(slopes[source]))
        r["att_sums"][i : i + 1] = found if m == 0 else r["att_sums"][i : i + 1] + found
    slope = jnp.concatenate(slopes, axis=1)
    size = slope.shape[1] // 2
    for k in range(2):
        r["slope_joint"][k, at, :size] = slope[:, k * size : (k + 1) * size]
        r["slope_joint"][k, at, size:] = jnp.zeros((frames, r["slope_joint"].shape[2] - size), LOW)
    terms = dot_nt(slope, r["attend"][...]).astype(LOW)
    for d in range(parts):
        r["terms"][d, cells] = terms[d * seg : (d + 1) * seg]


def attention_weight_step(r):
    parts = r["low"].shape[0]
    for k in range(2):
        pieces = [dot_tn(r["low"][c], r["slope_joint"][k]).astype(LOW) for c in range(parts)]
        grads = dot(r["back_att"][...], jnp.concatenate(pieces, axis=0)).astype(LOW)
        r["att_grad"][k] = grads.reshape(r["att_grad"].shape[1:])


def norm_back_step(r, m, seg):
    parts, _, quarter = r["gpos"].shape
    cells = slice(m * seg, (m + 1) * seg)
    normal, scale = r["normal"][cells], r["scale"][cells, 0:1]
    grad = r["grad_attn"][cells] + r["terms_sum"][...]
    result = norm_back(grad, normal, scale, r["table"][2:3]).astype(LOW)
    for c in range(parts):
        r["gpos"][c, cells] = result[:, c * quarter : (c + 1) * quarter]
    for i, found in enumerate((column_sum(grad * normal), column_sum(grad))):
        r["sums_own"][i : i + 1] = found if m == 0 else r["sums_own"][i : i + 1] + found


def owner_rows(vector, mask, spread, place):
    cells = dot((widen(mask) * vector).astype(LOW), spread)
    return cells if place == 0 else pltpu.roll(cells, place, 1)


def vectors_step(r, own):
    owned = r["owned"][...]
    for v in range(2):
        owned = owned + owner_rows(r["sums_own"][v : v + 1], r["mask"][...], r["spread"][...], v * own)
    r["full"][...] = dot(r["row_full"][...], owned.astype(LOW)).astype(LOW).reshape(r["full"].shape)


def conv_back_step(r, here, m, frames, tall, per):
    parts, mine, quarter = r["gpos"].shape
    groups, fold, many = r["conv_turned"].shape
    inner = fold // FOLD
    blocks = many // inner
    half = blocks * FOLD // 2
    span = frames + blocks * FOLD
    seg = frames // parts
    side = r["conv_grad"].shape[2]
    f32 = jnp.float32
    cells = slice(m * seg, (m + 1) * seg)
    grad = jnp.concatenate([widen(r["gpos_in"][d, cells]) for d in range(parts)], axis=0).T
    for g in range(groups):
        r["grads"][g] = grad[g * inner : (g + 1) * inner]
    live = lax.broadcasted_iota(jnp.int32, (1, frames), 1) < r["spans"][m]

    def one(g, carry):
        index = m * groups + g
        grad = r["grads"][g]
        slope = (grad * smooth_slope(r["before"][index])).astype(LOW)
        r["turn"][index, :, 0:1] = jnp.sum(widen(slope), axis=1, keepdims=True)
        wide = jnp.concatenate([slope, jnp.zeros((inner, span - frames), LOW)], axis=1)
        spread_blocks(wide, r["moved"], inner, blocks)
        fold_rows(r["padded"][index], r["folded"], inner)
        weight = dot_nt(r["moved"][...], r["folded"][...])
        back_sums = dot(r["conv_turned"][g], r["moved"][...])
        total = grad
        for j in range(FOLD):
            part = pltpu.roll(back_sums[j * inner : (j + 1) * inner], (span + j - half) % span, 1)
            total = total + part[:, :frames]
        total = jnp.where(live, total, 0.0).astype(LOW).astype(f32)
        r["turn"][index, :, 1:2] = jnp.sum(total, axis=1, keepdims=True)
        r["grads"][g] = total
        weight = dot(r["back_conv"][...], weight.astype(LOW)).reshape(2, per, tall, fold)
        for n in range(per):
            xz = g * per + n
            for k in range(2):
                piece = weight[k, n]
                if m > 0:
                    piece = piece + widen(r["conv_grad"][k, xz // side, xz % side])
                r["conv_grad"][k, xz // side, xz % side] = piece.astype(LOW)
        return carry

    lax.fori_loop(0, groups, one, 0)
    both = [r["grads"][g] for g in range(groups)]
    r["slopes_all"][here, m * frames : (m + 1) * frames] = jnp.concatenate(both, axis=0).T.astype(LOW)


def conv_sums_step(r, micros):
    groups = r["turn"].shape[0] // micros
    sums = jnp.concatenate(
        [sum(r["turn"][m * groups + g] for m in range(micros)) for g in range(groups)], axis=0
    ).T
    r["conv_sums"][...] = sums[:8]


def finish_step(r, here, m, frames):
    parts, _, narrow = r["gathered"].shape
    f32 = jnp.float32
    size = parts * narrow
    chunk = 256
    mine_at = pl.ds(pl.multiple_of(here * narrow, narrow), narrow)
    gain, shift = r["edges"][0:1, mine_at], r["edges"][1:2, mine_at]
    if m == 0:
        r["edge_sums"][...] = jnp.zeros_like(r["edge_sums"])
        r["proj_grad"][...] = jnp.zeros_like(r["proj_grad"])

    def one(number, carry):
        at = pl.ds(pl.multiple_of(m * frames + number * chunk, chunk), chunk)
        blocks = [widen(r["gathered"][c, at]) for c in range(parts)]
        slopes = [r["slopes_all"][b, at] for b in range(parts)]
        normal, scale = norm_blocks(blocks)
        first = jnp.zeros((chunk, 1), f32)
        second = jnp.zeros((chunk, 1), f32)
        for c in range(parts):
            lanes = slice(c * narrow, (c + 1) * narrow)
            grad = sum(dot_nt(slopes[b], r["proj"][b, lanes]) for b in range(parts))
            scaled = grad * r["edges"][0:1, lanes]
            first = first + jnp.sum(scaled, axis=1, keepdims=True)
            second = second + jnp.sum(scaled * normal[c], axis=1, keepdims=True)
        mean = sum(jnp.sum(block, axis=1, keepdims=True) for block in blocks) / size
        mine = (widen(r["gathered"][here, at]) - mean) * scale
        grad = sum(dot_nt(slopes[b], r["proj"][b, mine_at]) for b in range(parts))
        r["features_grad"][at] = scale * (grad * gain - first / size - mine * (second / size))
        low = (mine * gain + shift).astype(LOW)
        r["proj_grad"][...] = r["proj_grad"][...] + jnp.concatenate(
            [dot_tn(low, slopes[b]) for b in range(parts)], axis=1
        )
        r["edge_sums"][0:1] = r["edge_sums"][0:1] + column_sum(grad * mine)
        r["edge_sums"][1:2] = r["edge_sums"][1:2] + column_sum(grad)
        return carry

    lax.fori_loop(0, frames // chunk, one, 0)


def local_step(r, own, own_in):
    ranks, quarter = r["mask_ch"].shape
    width = r["proj_grad"].shape[1]
    f32 = jnp.float32
    vectors = [
        r["conv_sums"][1:2], r["conv_sums"][0:1], r["att_sums"][0:1], r["att_sums"][1:2],
    ]
    owned = 0.0
    for v in range(4):
        owned = owned + owner_rows(vectors[v], r["mask_ch"][...], r["spread_ch"][...], v * own)
    for v in range(2):
        owned = owned + owner_rows(
            r["edge_sums"][v : v + 1], r["mask_in"][...], r["spread_in"][...], 4 * own + v * own_in
        )
    lanes = owned.shape[1]
    owned = jnp.concatenate([owned, jnp.zeros((ranks, width - lanes), f32)], axis=1)
    result = dot(r["row_proj"][...], r["proj_grad"][...].astype(LOW))
    result = result + dot(r["row_vector"][...], owned.astype(LOW))
    r["local"][...] = result.astype(LOW).reshape(r["local"].shape)


def backward_rest(values, sizes, ident, micros, frames, own, own_in, own_hid, own_ret, thin):
    parts, squares, side = sizes["y"], sizes["x"] * sizes["z"], sizes["z"]
    devices, ranks = 2 * parts * squares, 2 * squares
    _, mine, quarter = values["gctx_in"].shape
    width = parts * quarter
    rows = micros * frames
    narrow = values["gathered"].shape[2]
    groups, fold, many = values["conv_turned"].shape
    inner = fold // FOLD
    blocks = many // inner
    span = frames + blocks * FOLD
    per = inner // own // 2
    tall, lanes_a = values["ffn"].shape[-2:]
    half, deep = width // 2, lanes_a - width // 2 - 128
    att = 3 * quarter // 2
    wide = att + -att % 128
    eight = 2 * parts
    seg = frames // parts
    f32 = jnp.float32

    ones = {}
    ones["back_att"] = onehot(natural_of(width, parts, squares), np.arange(width))
    slab = np.arange(many).reshape(2, per, own, blocks)
    ones["back_conv"] = onehot(
        np.arange(many),
        [slab[(o // own) % 2, o // own // 2, o % own, b] for b in range(blocks) for o in range(inner)],
    )
    count = 8 * own + own_hid
    lane = np.arange(count + -count % 128)
    ones["mask"] = onehot(np.arange(devices), np.arange(width) // own)
    ones["spread"] = onehot(np.arange(width) % own, lane)
    full_rows = np.full((devices, 16), -1)
    full_rows[:, 0] = np.arange(devices).reshape(parts, squares, 2).transpose(2, 0, 1).reshape(-1)
    ones["row_full"] = onehot(full_rows.reshape(-1), np.arange(devices))
    few = 4 * own + 2 * own_in
    few = np.arange(few + -few % 128)
    ones["mask_ch"] = onehot(np.arange(ranks), np.arange(quarter) // own)
    ones["spread_ch"] = onehot(np.arange(quarter) % own, few)
    ones["mask_in"] = onehot(np.arange(ranks), np.arange(narrow) // own_in)
    ones["spread_in"] = onehot(np.arange(narrow) % own_in, few)
    high = own_in + 1 + -(own_in + 1) % 16
    order = np.arange(ranks).reshape(squares, 2).T.reshape(-1)
    proj_rows = np.full((ranks, high), -1)
    proj_rows[:, :own_in] = order[:, None] * own_in + np.arange(own_in)[None, :]
    ones["row_proj"] = onehot(proj_rows.reshape(-1), np.arange(narrow))
    vector_rows = np.full((ranks, high), -1)
    vector_rows[:, own_in] = order
    ones["row_vector"] = onehot(vector_rows.reshape(-1), np.arange(ranks))

    cut_lanes = lanes_a // 256 * 128 + 128 * (lanes_a // 128 % 2)
    jobs = {
        "ffn": {
            "axes": ("y", "x", "z"), "far": True,
            "cuts": [(0, tall, 0, cut_lanes), (0, tall, cut_lanes, lanes_a - cut_lanes)],
            "orders": [("x", "z", "y"), ("z", "x", "y")],
        },
        "full": {
            "axes": ("y", "x", "z"), "far": False, "cuts": [(0, 16, 0, len(lane))],
            "orders": [("z", "x", "y")],
        },
        "att": {
            "axes": ("x", "z"), "far": False, "cuts": [(0, tall, 0, wide)], "orders": [("x", "z")],
        },
        "conv": {
            "axes": ("x", "z"), "far": False,
            "cuts": [(0, tall, 0, fold // 2), (0, tall, fold // 2, fold // 2)],
            "orders": [("x", "z"), ("z", "x")],
        },
        "local": {
            "axes": ("x", "z"), "far": False, "cuts": [(0, high, 0, width)], "orders": [("p",)],
        },
    }
    scratch, copies = sum_scratch(jobs, sizes)
    copies += micros * (parts - 1 + 12) + eight
    lead = {"y": parts, "x": sizes["x"], "z": sizes["z"]}
    low_rows = own + -own % 8
    block_lanes = deep + 128 + wide
    scratch.update(
        {
            "terms": pltpu.VMEM((parts, mine, width), LOW),
            "terms_held": pltpu.VMEM((micros, 6, seg // 2, width), LOW),
            "terms_sum": pltpu.VMEM((seg, width), f32),
            "slope_joint": pltpu.VMEM((2, rows, wide), LOW),
            "att_grad": pltpu.VMEM((2, sizes["x"], sizes["z"], tall, wide), LOW),
            "att_sums": pltpu.VMEM((8, quarter), f32),
            "gpos": pltpu.VMEM((parts, mine, quarter), LOW),
            "gpos_in": pltpu.VMEM((parts, mine, quarter), LOW),
            "sums_own": pltpu.VMEM((8, width), f32),
            "full": pltpu.VMEM((2, parts, sizes["x"], sizes["z"], 16, len(lane)), LOW),
            "grads": pltpu.VMEM((groups, inner, frames), f32),
            "turn": pltpu.VMEM((micros * groups, inner, 128), f32),
            "moved": pltpu.VMEM((many, span), LOW),
            "folded": pltpu.VMEM((fold, span), LOW),
            "slopes_all": pltpu.VMEM((parts, rows, quarter), LOW),
            "conv_sums": pltpu.VMEM((8, quarter), f32),
            "conv_grad": pltpu.VMEM((2, sizes["x"], sizes["z"], tall, fold), LOW),
            "proj_grad": pltpu.VMEM((narrow, width), f32),
            "edge_sums": pltpu.VMEM((8, narrow), f32),
            "local": pltpu.VMEM((2, sizes["x"], sizes["z"], high, width), LOW),
            "ffn_sum": pltpu.VMEM((tall, lanes_a), f32),
            "att_sum": pltpu.VMEM((tall, wide), f32),
            "block": pltpu.VMEM((eight, low_rows, block_lanes), f32),
            "pair": pltpu.VMEM((2, own_ret, half), f32),
        }
    )
    outs = {
        "features_grad": ((rows, narrow), f32),
        "full_sum": ((16, len(lane)), f32),
        "conv_sum": ((tall, fold), f32),
        "local_sum": ((high, width), f32),
        "block_in": ((eight, low_rows, block_lanes), f32),
        "pair_in": ((2, own_ret, half), f32),
    }
    ins = dict(values)
    ins.update({name: jnp.asarray(value, LOW) for name, value in ones.items()})

    def body(r, move, need, keep, copy_here):
        spot = place(side)
        here, core, rank = spot["y"], spot["k"], lax.axis_index("rows")
        base = rank - core
        local = r["local_sems"]
        r["move"] = move
        sources = {
            "ffn": r["ffn"], "full": r["full"], "att": r["att_grad"], "conv": r["conv_grad"],
            "local": r["local"],
        }
        sinks = {
            "ffn": r["ffn_sum"], "full": r["full_sum"], "att": r["att_sum"], "conv": r["conv_sum"],
            "local": r["local_sum"],
        }
        sums = Sums(r, jobs, spot, sizes, sources, sinks, local)
        ring = [peer(spot, "y", step, sizes)[1] for step in range(1, parts)]
        others = [(here + step) % parts for step in range(1, parts)]
        number = here * 2 + core
        eights = [(number + step) % eight for step in range(1, eight)]
        eight_at = [(other // 2, base + other % 2) for other in eights]
        greet(eight_at + [device for _, device in plane(spot, sizes)])
        sent = []

        def swap(source, target, m):
            cells = pl.ds(m * seg, seg)
            copies = [
                move(source.at[other, cells], target.at[here, cells], device)
                for other, device in zip(others, ring)
            ]
            target[here, cells] = source[here, cells]
            sent.extend(copies)
            return copies

        def arrived(copies):
            for copy in copies:
                copy.wait_recv()

        to_right, to_left = ring[0], ring[2]
        right, across, left = [(here + step) % 4 for step in (1, 2, 3)]
        terms = r["terms"]

        def ring_add(m):
            held, size = r["terms_held"], seg // 2
            near, far = pl.ds(m * seg, size), pl.ds(m * seg + size, size)
            return [
                move(terms.at[across, near], held.at[m, 0], to_right),
                move(terms.at[across, far], held.at[m, 1], to_left),
                move(terms.at[right, far], held.at[m, 2], to_right),
                move(terms.at[left, near], held.at[m, 3], to_left),
            ]

        def ring_relay(m, copies):
            held, size = r["terms_held"], seg // 2
            near, far = pl.ds(m * seg, size), pl.ds(m * seg + size, size)
            copies[0].wait_recv()
            terms[right, near] = terms[right, near] + held[m, 0]
            copies.append(move(terms.at[right, near], held.at[m, 4], to_right))
            copies[1].wait_recv()
            terms[left, far] = terms[left, far] + held[m, 1]
            copies.append(move(terms.at[left, far], held.at[m, 5], to_left))

        def ring_end(m, copies):
            held, size = r["terms_held"], seg // 2
            near, far = pl.ds(m * seg, size), pl.ds(m * seg + size, size)
            arrived(copies[2:])
            sent.extend(copies)
            r["terms_sum"][:size] = widen(terms[here, near]) + widen(held[m, 4]) + widen(held[m, 3])
            r["terms_sum"][size:] = widen(terms[here, far]) + widen(held[m, 2]) + widen(held[m, 5])

        sums.start("ffn")
        need("joint", "probs", "attend")
        added = []
        for m in range(micros):
            attention_back_step(r, m, frames)
            added.append(ring_add(m))
            if m > 0:
                ring_relay(m - 1, added[m - 1])
        need("low", "back_att")
        attention_weight_step(r)
        ring_relay(micros - 1, added[-1])
        sums.start("att")
        sums.pump("ffn")
        swapped = []
        need("normal", "scale", "grad_attn", "table")
        for m in range(micros):
            ring_end(m, added[m])
            norm_back_step(r, m, seg)
            swapped.append(swap(r["gpos"], r["gpos_in"], m))
        need("owned", "mask", "spread", "row_full")
        vectors_step(r, own)
        sums.start("full")
        sums.pump("att")
        rings = []
        need("conv_turned", "before", "padded", "back_conv")
        for m in range(micros):
            arrived(swapped[m])
            conv_back_step(r, here, m, frames, tall, per)
            rings.append(Ring(move, r["slopes_all"], m * frames, frames, here, to_right, to_left))
            if m > 0:
                rings[m - 1].relay()
            sums.pump("ffn", "att", "full")
        sums.start("conv")
        conv_sums_step(r, micros)
        sums.pump("ffn", "att", "full")
        rings[-1].relay()
        need("gathered", "proj", "edges")
        for m in range(micros):
            rings[m].finish()
            finish_step(r, here, m, frames)
            sums.pump("conv", "ffn", "att", "full")
        need("mask_ch", "spread_ch", "mask_in", "spread_in", "row_proj", "row_vector")
        local_step(r, own, own_in)
        sums.start("local")
        sums.pump("conv", "ffn", "att", "full")
        sums.pump("local")
        sums.drain("ffn", "att")

        for j in range(eight):
            at = slice(j * own, (j + 1) * own)
            r["block"][j, :own, : deep + 128] = r["ffn_sum"][at, half:]
            r["block"][j, :own, deep + 128 :] = r["att_sum"][at]
        for k in range(2):
            r["pair"][k] = r["ffn_sum"][k * own_ret : (k + 1) * own_ret, :half]
        last = [
            move(r["block"].at[other], r["block_in"].at[number], device)
            for other, device in zip(eights, eight_at)
        ]
        last.append(move(r["pair"].at[1 - core], r["pair_in"].at[core], (here, base + 1 - core)))
        r["block_in"][number] = r["block"][number]
        r["pair_in"][core] = r["pair"][core]
        sums.drain("conv", "full", "local")
        for copy in last:
            copy.wait()
        for copy in sent:
            copy.wait_send()
        for item in rings + [sums]:
            item.close()
        return []

    scratch["local_sems"] = pltpu.SemaphoreType.DMA((4,))
    return staged_call(
        ident, ins, outs, scratch, copies, body,
        {"spans": pltpu.SMEM, "ffn": pl.ANY, "gctx_in": pltpu.VMEM},
    )


def owners(sums, own, own_in, own_hid, deep, thin, att, quarter, inner, taps, order):
    f32 = jnp.float32
    eight, _, lanes = sums["block_in"].shape
    parts, width, half = eight // 2, quarter * eight // 2, quarter * eight // 4
    blocks = taps // FOLD
    own_ret = sums["pair_in"].shape[1]
    names = list(sums)
    shapes = {
        "features_grad": sums["features_grad"].shape, "proj": (own_in, width),
        "conv": (own, inner, taps), "hidden": (own, eight * deep), "output": (own, width),
        "attend": (own, 3 * width), "return": (own_ret, width),
    }
    places = {}
    for name, source, begin, size in order:
        shapes[name] = (1, size)
        places[name] = (source, begin, size)

    def kernel(*refs):
        r = dict(zip(names, refs))
        o = dict(zip(shapes, refs[len(names) :]))
        folded = refs[-1]
        o["features_grad"][...] = r["features_grad"][...]
        for j in range(eight):
            o["hidden"][:, j * deep : (j + 1) * deep] = r["block_in"][j, :own, :deep]
        pieces = [r["block_in"][j, :own, deep : deep + thin] for j in range(eight)]
        o["output"][...] = jnp.concatenate(pieces, axis=1)
        for c in range(parts):
            both = [r["block_in"][2 * c + k, :own, deep + 128 : deep + 128 + att] for k in range(2)]
            both = jnp.concatenate(both, axis=1)
            for i in range(3):
                at = slice(i * width + c * quarter, i * width + (c + 1) * quarter)
                o["attend"][:, at] = both[:, i * quarter : (i + 1) * quarter]
        for k in range(2):
            o["return"][:, k * half : (k + 1) * half] = r["pair_in"][k]
        for i in range(own):
            rows = r["conv_sum"][i * blocks : (i + 1) * blocks]
            for j in range(FOLD):
                folded[pl.ds(j, blocks, stride=FOLD), :] = rows[:, j * inner : (j + 1) * inner]
            o["conv"][i] = folded[...].T
        o["proj"][...] = r["local_sum"][:own_in]
        rows = {"local": r["local_sum"][own_in : own_in + 1], "full": r["full_sum"][0:1]}
        for name, (source, begin, size) in places.items():
            o[name][...] = rows[source][:, begin : begin + size]

    results = local_call(
        kernel, [(shape, f32) for shape in shapes.values()], [pltpu.VMEM((taps, inner), f32)],
        *sums.values(),
    )
    return dict(zip(shapes, results))


def per_device(
    features, lengths, input_gain, input_bias, proj_weight, proj_bias, conv_weight, conv_bias,
    encoder_gain, encoder_bias, attend_weight, query_bias, value_bias, output_weight, output_bias,
    attend_gain, attend_bias, hidden_weight, hidden_bias, return_weight, return_bias, final_gain,
    final_bias, out_grad,
):
    parts = lax.axis_size("ch")
    ranks = lax.axis_size("rows")
    side = math.isqrt(ranks // 2)
    sizes = {"y": parts, "x": side, "z": side, "k": 2}
    micros, _, frames, narrow = features.shape
    own = proj_bias.shape[0]
    width = proj_weight.shape[1]
    quarter = width // parts
    inner, taps = conv_weight.shape[1:]
    blocks = taps // FOLD
    hidden = hidden_weight.shape[1]
    own_in = input_gain.shape[0]
    own_hid = hidden_bias.shape[0]
    seg = out_grad.shape[2]
    eight = 2 * parts
    squares = side * side
    tall = eight * own
    deep, thin, att = hidden // eight, width // eight, 3 * quarter // 2
    half = width // 2
    rows = micros * frames
    mine = micros * seg
    fold = FOLD * inner
    spans = lengths.reshape(micros)

    small = (proj_bias, conv_bias, encoder_gain, encoder_bias, query_bias, value_bias, output_bias,
             attend_gain, attend_bias, return_bias, final_gain, final_bias)
    own_ret = return_weight.shape[0]
    f = forward_start(
        {
            "features": features.reshape(rows, narrow), "hidden_raw": hidden_weight,
            "output_raw": output_weight, "attend_raw": attend_weight, "proj_raw": proj_weight,
            "return_raw": return_weight, "conv_raw": conv_weight, "small": jnp.stack(small),
            "ends": jnp.stack([input_gain, input_bias]), "hid_own": hidden_bias.reshape(1, own_hid),
            "spans": spans,
        },
        sizes, 0, micros, frames, own, own_in, own_hid, own_ret, len(small),
    )
    output, grad_attn, grad_context, ffn, normal, scale, owned = feed_forward(
        f["context_in"], f["summed"], out_grad.reshape(mine, width), f["weights"], f["table"],
        f["hid_bias"], sizes, 1, micros, frames, thin, own, own_hid,
    )
    third = backward_rest(
        {
            "gctx_in": grad_context, "grad_attn": grad_attn, "normal": normal, "scale": scale,
            "owned": owned, "spans": spans,
            **{
                name: f[name]
                for name in ("low", "joint", "probs", "attend", "table", "before", "padded",
                             "conv_turned", "gathered", "proj", "edges")
            },
            "ffn": ffn.reshape(2, parts, side, side, tall, -1),
        },
        sizes, 9, micros, frames, own, own_in, own_hid, own_ret, thin,
    )

    full, local = ("full", "local")
    order = []
    for number, name in enumerate(("proj_bias", "conv_bias", "query_bias", "value_bias")):
        order.append((name, local, number * own, own))
    for number, name in enumerate(("input_gain", "input_bias")):
        order.append((name, local, 4 * own + number * own_in, own_in))
    names = ("encoder_gain", "encoder_bias", "output_bias", "attend_gain", "attend_bias",
             "return_bias", "final_gain", "final_bias")
    for number, name in enumerate(names):
        order.append((name, full, number * own, own))
    order.append(("hidden_bias", full, 8 * own, own_hid))
    o = owners(
        third, own, own_in, own_hid, deep, thin, att, quarter, inner, taps, order
    )
    for name, _, _, size in order:
        o[name] = o[name].reshape(size)
    return (
        output.reshape(out_grad.shape), o["features_grad"].reshape(features.shape),
        o["input_gain"], o["input_bias"], o["proj"], o["proj_bias"], o["conv"], o["conv_bias"],
        o["encoder_gain"], o["encoder_bias"], o["attend"], o["query_bias"], o["value_bias"],
        o["output"], o["output_bias"], o["attend_gain"], o["attend_bias"], o["hidden"],
        o["hidden_bias"], o["return"], o["return_bias"], o["final_gain"], o["final_bias"],
    )


def solution(mesh):
    vector, matrix, cube = P(ALL), P(ALL, None), P(ALL, None, None)
    weights = (
        vector, vector, matrix, vector, cube, vector, vector, vector, matrix, vector, vector,
        matrix, vector, vector, vector, matrix, vector, matrix, vector, vector, vector,
    )
    by_channel = P(None, "rows", None, "ch")
    by_frame = P(None, "rows", "ch", None)
    return jax.shard_map(
        per_device,
        mesh=mesh,
        in_specs=(by_channel, P(None, "rows")) + weights + (by_frame,),
        out_specs=(by_frame, by_channel) + weights,
        check_vma=False,
    )
```

```python
import functools
import math

import jax
import jax.numpy as jnp
import numpy as np
from jax import lax
from jax.experimental import pallas as pl
from jax.experimental.pallas import tpu as pltpu
from jax.sharding import PartitionSpec as P

HEAD_DIM = 64
EPS = 1e-05
NEGATIVE = -1000000000.0
FOLD = 16
ALL = ("ch", "rows")
LOW = jnp.bfloat16
MESH = pl.DeviceIdType.MESH
ROOM = 62 * 1024 * 1024


def widen(values):
    return values.astype(jnp.float32)


def dot(left, right):
    return jnp.dot(left, right, preferred_element_type=jnp.float32)


def contract(spec, left, right):
    return jnp.einsum(spec, left, right, preferred_element_type=jnp.float32)


def place(side):
    rank = lax.axis_index("rows")
    return {
        "y": lax.axis_index("ch"),
        "x": rank // (2 * side),
        "z": (rank // 2) % side,
        "k": rank % 2,
    }


def peer(spot, axis, step, sizes):
    moved = dict(spot)
    moved[axis] = (spot[axis] + step) % sizes[axis]
    return moved, (moved["y"], (moved["x"] * sizes["z"] + moved["z"]) * 2 + moved["k"])


def call_out(targets):
    barrier = pltpu.get_barrier_semaphore()
    for target in targets:
        pl.semaphore_signal(barrier, inc=1, device_id=target, device_id_type=MESH)


def greet(targets):
    pl.semaphore_wait(pltpu.get_barrier_semaphore(), len(targets))


def send(source, target, send_sem, recv_sem, device):
    copy = pltpu.make_async_remote_copy(
        src_ref=source, dst_ref=target, send_sem=send_sem, recv_sem=recv_sem,
        device_id=device, device_id_type=MESH,
    )
    copy.start()
    return copy


def whole(count):
    return [pl.BlockSpec(memory_space=pltpu.VMEM)] * count


def call_remote(kernel, shapes, ins, outs, scratch, ident, *values):
    return pl.pallas_call(
        kernel,
        out_shape=shapes,
        in_specs=ins,
        out_specs=outs,
        scratch_shapes=scratch,
        compiler_params=pltpu.CompilerParams(
            collective_id=ident, has_side_effects=True, vmem_limit_bytes=ROOM
        ),
    )(*values)


def staged_call(ident, ins, outs, scratch, copies, body, spaces, kept=(), keeps=0):
    lazy = [
        name for name, value in ins.items()
        if name not in spaces and value.size * value.dtype.itemsize >= 49152
    ]
    names = [name + "@" if name in lazy else name for name in ins]
    names += [name + "@" if name in kept else name for name in outs]
    scratch = dict(scratch)
    scratch.update({name: pltpu.VMEM(ins[name].shape, ins[name].dtype) for name in lazy})
    scratch.update({name: pltpu.VMEM(*outs[name]) for name in kept})
    names += list(scratch)

    def kernel(*refs):
        r = dict(zip(names, refs))
        load_sems, keep_sems, send_sems, recv_sems = refs[len(names) :]
        loads, stores, used = {}, [], [0]
        for number, name in enumerate(lazy):
            loads[name] = pltpu.make_async_copy(r[name + "@"], r[name], load_sems.at[number])
            loads[name].start()

        def need(*wanted):
            for name in wanted:
                if name in loads:
                    loads.pop(name).wait()

        def copy_here(source, target):
            copy = pltpu.make_async_copy(source, target, keep_sems.at[len(stores)])
            copy.start()
            stores.append(copy)
            return copy

        def keep(name, at=None):
            if at is None:
                copy_here(r[name], r[name + "@"])
            else:
                copy_here(r[name].at[at], r[name + "@"].at[at])

        def move(source, target, device):
            index = used[0]
            used[0] += 1
            return send(source, target, send_sems.at[index], recv_sems.at[index], device)

        waited = body(r, move, need, keep, copy_here)
        need(*list(loads))
        for copy in stores:
            if not any(copy is other for other in waited):
                copy.wait()

    space = lambda name: pl.ANY if name in lazy or name in kept else spaces.get(name, pltpu.VMEM)
    results = call_remote(
        kernel,
        [jax.ShapeDtypeStruct(shape, kind) for shape, kind in outs.values()],
        [pl.BlockSpec(memory_space=space(name)) for name in ins],
        [pl.BlockSpec(memory_space=space(name)) for name in outs],
        list(scratch.values())
        + [
            pltpu.SemaphoreType.DMA((max(len(lazy), 1),)),
            pltpu.SemaphoreType.DMA((max(keeps, 1),)),
            pltpu.SemaphoreType.DMA((copies,)),
            pltpu.SemaphoreType.DMA((copies,)),
        ],
        ident, *ins.values(),
    )
    return dict(zip(outs, results))


def plane(spot, sizes):
    found = []
    for step in range(1, sizes["x"] * sizes["z"]):
        moved = dict(spot)
        moved["x"] = (spot["x"] + step // sizes["z"]) % sizes["x"]
        moved["z"] = (spot["z"] + step % sizes["z"]) % sizes["z"]
        found.append((moved, (moved["y"], (moved["x"] * sizes["z"] + moved["z"]) * 2 + moved["k"])))
    return found


def window(axes, fixed, cut):
    lead = tuple(fixed.get(axis, slice(None)) for axis in axes)
    return lead + (pl.ds(cut[0], cut[1]), pl.ds(cut[2], cut[3]))


def loop_blocks(dims, body):
    count = math.prod(dims)
    if count == 1:
        body((0,) * len(dims))
        return

    def step(flat, carry):
        index = []
        rest = flat
        for size in reversed(dims):
            index.append(rest % size)
            rest = rest // size
        body(tuple(reversed(index)))
        return carry

    lax.fori_loop(0, count, step, 0)


def dot_nt(left, right):
    return lax.dot_general(left, right, (((1,), (1,)), ((), ())), preferred_element_type=jnp.float32)


def dot_tn(left, right):
    return lax.dot_general(left, right, (((0,), (0,)), ((), ())), preferred_element_type=jnp.float32)


def pick(left, onehot):
    return dot(left, onehot).astype(LOW)


def pick_wide(values, onehot):
    high = values.astype(LOW)
    rest = (values - widen(high)).astype(LOW)
    return dot(high, onehot) + dot(rest, onehot)


def smooth(values):
    return 0.5 * values * (1.0 + lax.erf(values * 0.7071067811865476))


def smooth_slope(values):
    return 0.5 * (1.0 + lax.erf(values * 0.7071067811865476)) + values * 0.3989422804014327 * jnp.exp(
        -0.5 * values * values
    )


def norm(values):
    mean = jnp.mean(values, axis=-1, keepdims=True)
    centred = values - mean
    scale = lax.rsqrt(jnp.mean(centred * centred, axis=-1, keepdims=True) + EPS)
    return centred * scale, scale


def norm_back(incoming, normal, scale, gain):
    scaled = incoming * gain
    first = jnp.mean(scaled, axis=-1, keepdims=True)
    second = jnp.mean(scaled * normal, axis=-1, keepdims=True)
    return scale * (scaled - first - normal * second)


def norm_blocks(blocks):
    size = sum(block.shape[-1] for block in blocks)
    mean = sum(jnp.sum(block, axis=-1, keepdims=True) for block in blocks) / size
    centred = [block - mean for block in blocks]
    spread = sum(jnp.sum(block * block, axis=-1, keepdims=True) for block in centred) / size
    scale = lax.rsqrt(spread + EPS)
    return [block * scale for block in centred], scale


def column_sum(values):
    return jnp.sum(values, axis=0, keepdims=True)


def local_call(kernel, shapes, scratch, *values):
    count = len(values)
    return pl.pallas_call(
        kernel,
        out_shape=[jax.ShapeDtypeStruct(shape, kind) for shape, kind in shapes],
        in_specs=[
            pl.BlockSpec(memory_space=pltpu.SMEM if value.dtype == jnp.int32 else pltpu.VMEM)
            for value in values
        ],
        out_specs=whole(len(shapes)),
        scratch_shapes=scratch,
        compiler_params=pltpu.CompilerParams(vmem_limit_bytes=ROOM),
    )(*values)


def onehot(rows, columns):
    return (np.asarray(rows)[:, None] == np.asarray(columns)[None, :]).astype(LOW)


def natural_of(count, parts, squares):
    cells = np.arange(count).reshape(parts, squares, 2, -1)
    return cells.transpose(1, 0, 2, 3).reshape(count)


def fold_rows(padded, spread_ref, inner):
    for j in range(FOLD):
        moved = padded if j == 0 else pltpu.roll(padded, padded.shape[1] - j, 1)
        spread_ref[j * inner : (j + 1) * inner, :] = moved


def spread_blocks(padded, spread_ref, inner, blocks):
    for b in range(blocks):
        moved = padded if b == 0 else pltpu.roll(padded, FOLD * b, 1)
        spread_ref[b * inner : (b + 1) * inner, :] = moved


def own_frames(ref, spot, micros, frames, parts):
    seg = frames // parts
    blocks = []
    for c in range(parts):
        pieces = [
            widen(ref[c, pl.ds(pl.multiple_of(m * frames + spot * seg, seg), seg)])
            for m in range(micros)
        ]
        blocks.append(jnp.concatenate(pieces, axis=0))
    return blocks


def feed_forward(
    context, summed, upstream, weights, table, hid_bias, sizes, ident, micros, frames, thin, own, own_hid
):
    parts, mine, quarter = context.shape
    squares, side = sizes["x"] * sizes["z"], sizes["z"]
    weights = weights.reshape(parts, squares, *weights.shape[-2:])
    tall, lanes = weights.shape[-2:]
    width = parts * quarter
    half, deep = width // 2, lanes - width // 2 - 128
    most = half + deep
    eight = 2 * parts
    seg = frames // parts
    f32 = jnp.float32
    hidden = eight * deep
    devices = 2 * parts * squares
    ones = {"nat": onehot(np.arange(width), natural_of(width, parts, squares))}
    ones["place"] = np.zeros((width // 128, 256, 128), np.float32)
    for tile in range(width // 128):
        first = tile * 128 // thin
        for lane in range(128):
            channel = tile * 128 + lane
            ones["place"][tile, (channel // thin - first) * 128 + channel % thin, lane] = 1.0
    lane = np.arange(128)
    ones["cut"] = np.stack(
        [onehot(np.arange(width), np.where(lane < thin, j * thin + lane, -1)) for j in range(eight)]
    )
    lane = np.arange(8 * own + own_hid + -(8 * own + own_hid) % 128)
    ones["mask"] = onehot(np.arange(devices), np.arange(width) // own)
    ones["mask_hid"] = onehot(np.arange(devices), np.arange(hidden) // own_hid)
    ones["spread"] = onehot(np.arange(width) % own, lane)
    ones["spread_hid"] = onehot(
        np.arange(hidden) % own_hid, np.where(lane >= 8 * own, lane - 8 * own, -1)
    )
    ins = {
        "nat": None, "place": None, "context": context, "table": table, "hid_bias": hid_bias,
        "summed": summed, "weights": weights, "upstream": upstream,
    }
    ins.update({name: jnp.asarray(value, LOW) for name, value in ones.items()})
    outs = {
        "output": ((mine, width), LOW),
        "grad_attn": ((mine, width), f32),
        "gctx_in": ((parts, mine, quarter), LOW),
        "slabs": ((2, parts, squares, tall, lanes), LOW),
        "normal": ((mine, width), f32),
        "scale": ((mine, 128), f32),
        "owned": ((devices, len(lane)), f32),
    }
    scratch = {
        "own_rows": pltpu.VMEM((parts, mine, quarter), LOW),
        "w_ret": pltpu.VMEM((parts, squares, tall, 2 * half), LOW),
        "w_hid": pltpu.VMEM((parts, squares, tall, 2 * deep), LOW),
        "w_out": pltpu.VMEM((2, parts, squares, tall, 128), LOW),
        "joined": pltpu.VMEM((width, width), LOW),
        "pre": pltpu.VMEM((mine, hidden), f32),
        "act": pltpu.VMEM((mine, hidden), LOW),
        "inner": pltpu.VMEM((mine, hidden), LOW),
        "hid_sums": pltpu.VMEM((1, hidden), f32),
        "gctx": pltpu.VMEM((parts, mine, quarter), LOW),
    }

    def body(r, move, need, keep, copy_here):
        spot = place(side)
        here = spot["y"]
        loads = [
            copy_here(
                r["summed"].at[:, pl.ds(pl.multiple_of(m * frames + here * seg, seg), seg)],
                r["own_rows"].at[:, pl.ds(m * seg, seg)],
            )
            for m in range(micros)
        ]
        core = spot["k"]
        sibling = peer(spot, "k", 1, sizes)[1]
        ring = [peer(spot, "y", step, sizes)[1] for step in range(1, parts)]
        others = [(here + step) % parts for step in range(1, parts)]
        call_out(ring + [sibling])
        greet(ring + [sibling])

        def fetch(source, target):
            return [copy_here(source, target), move(source, target, sibling)]

        pairs = {"w_out": fetch(r["weights"].at[:, :, :, pl.ds(most, 128)], r["w_out"].at[core])}
        for c in range(parts):
            for name, begin, size in (("w_hid", half, deep), ("w_ret", 0, half)):
                at = pl.ds(pl.multiple_of(core * size, size), size)
                pairs[name, c] = fetch(
                    r["weights"].at[c, :, :, pl.ds(begin, size)], r[name].at[c, :, :, at]
                )

        def have(*key):
            for copy in pairs[key if len(key) > 1 else key[0]]:
                copy.wait()

        def block(name, c):
            return r[name][c].reshape(width, r[name].shape[-1])

        table = r["table"]
        for copy in loads[:micros]:
            copy.wait()
        normal, scale = norm_blocks([widen(r["own_rows"][c]) for c in range(parts)])
        normal = jnp.concatenate(normal, axis=1)
        r["normal"][...] = normal
        r["scale"][...] = jnp.broadcast_to(scale, r["scale"].shape)
        keep("normal")
        keep("scale")
        encoded = normal * table[2:3] + table[3:4]
        need("nat", "place")
        nat = r["nat"]
        ctx_slab = sum(
            dot(r["context"][c], nat[c * quarter : (c + 1) * quarter]) for c in range(parts)
        ).astype(LOW)
        have("w_out")
        for tile in range(width // 128):
            first = tile * 128 // thin
            last = min(first + 1, eight - 1)
            both = [r["w_out"][j % 2, j // 2].reshape(width, 128) for j in (first, last)]
            r["joined"][:, tile * 128 : (tile + 1) * 128] = pick(
                jnp.concatenate(both, axis=1), r["place"][tile]
            )
        attn_sum = encoded + dot(ctx_slab, r["joined"][...]) + table[6:7]
        normal_att, scale_att = norm(attn_sum)
        attn_norm = normal_att * table[7:8] + table[8:9]
        attn_slab = pick(attn_norm.astype(LOW), nat[...])
        outer = jnp.zeros((mine, width), f32)
        for c in range(parts):
            columns = slice(2 * c * deep, 2 * (c + 1) * deep)
            have("w_hid", c)
            pre = dot(attn_slab, block("w_hid", c)) + r["hid_bias"][:, columns]
            share = 0.5 * (1.0 + lax.erf(pre * 0.7071067811865476))
            r["pre"][:, columns] = share + pre * 0.3989422804014327 * jnp.exp(-0.5 * pre * pre)
            r["act"][:, columns] = (pre * share).astype(LOW)
            have("w_ret", c)
            outer = outer + dot(r["act"][:, columns], block("w_ret", c))
        ffn_sum = attn_norm + outer + table[9:10]
        normal_fin, scale_fin = norm(ffn_sum)
        need("upstream")
        r["output"][...] = (normal_fin * table[10:11] + table[11:12]).astype(LOW)
        keep("output")
        up = widen(r["upstream"][...])
        grad_ffn = norm_back(up, normal_fin, scale_fin, table[10:11])
        slope_outer = grad_ffn.astype(LOW)
        vectors = {
            5: column_sum(widen(slope_outer)), 6: column_sum(up * normal_fin), 7: column_sum(up)
        }
        grad_slab = jnp.zeros((mine, width), f32)
        for c in range(parts):
            columns = slice(2 * c * deep, 2 * (c + 1) * deep)
            grad_act = dot_nt(slope_outer, block("w_ret", c))
            slope_inner = (grad_act * r["pre"][:, columns]).astype(LOW)
            r["inner"][:, columns] = slope_inner
            r["hid_sums"][:, columns] = column_sum(widen(slope_inner))
            grad_slab = grad_slab + dot_nt(slope_inner, block("w_hid", c))
        high = grad_slab.astype(LOW)
        rest = (grad_slab - widen(high)).astype(LOW)
        grad_norm2 = grad_ffn + dot_nt(high, nat[...]) + dot_nt(rest, nat[...])
        vectors[3] = column_sum(grad_norm2 * normal_att)
        vectors[4] = column_sum(grad_norm2)
        grad_attn = norm_back(grad_norm2, normal_att, scale_att, table[7:8])
        r["grad_attn"][...] = grad_attn
        keep("grad_attn")
        slope_att = grad_attn.astype(LOW)
        vectors[2] = column_sum(widen(slope_att))
        gctx_slab = dot_nt(slope_att, r["joined"][...]).astype(LOW)
        for c in range(parts):
            r["gctx"][c] = dot_nt(gctx_slab, nat[c * quarter : (c + 1) * quarter]).astype(LOW)
        swaps = [
            move(r["gctx"].at[other], r["gctx_in"].at[here], device)
            for other, device in zip(others, ring)
        ]
        r["gctx_in"][here] = r["gctx"][here]

        attn_turned = widen(attn_slab).T.astype(LOW)
        for c in range(parts):
            columns = slice(2 * c * deep, 2 * (c + 1) * deep)
            act_turned = widen(r["act"][:, columns]).T.astype(LOW)
            grad_ret = dot(act_turned, slope_outer).astype(LOW)
            grad_hid = dot(attn_turned, r["inner"][:, columns]).astype(LOW)
            for k in range(2):
                piece = grad_ret[:, k * half : (k + 1) * half]
                r["slabs"][k, c, :, :, :half] = piece.reshape(squares, tall, half)
                piece = grad_hid[:, k * deep : (k + 1) * deep]
                r["slabs"][k, c, :, :, half:most] = piece.reshape(squares, tall, deep)
                keep("slabs", (k, c, slice(None), slice(None), pl.ds(0, most)))
        need("cut", "mask", "mask_hid", "spread", "spread_hid")
        ctx_turned = widen(ctx_slab).T.astype(LOW)
        for c in range(parts):
            for k in range(2):
                grad = dot(ctx_turned, pick(slope_att, r["cut"][2 * c + k])).astype(LOW)
                r["slabs"][k, c, :, :, most:] = grad.reshape(squares, tall, 128)
        keep("slabs", (slice(None), slice(None), slice(None), slice(None), pl.ds(most, 128)))
        owned = dot((widen(r["mask_hid"][...]) * r["hid_sums"][...]).astype(LOW), r["spread_hid"][...])
        for v, vector in vectors.items():
            owned = owned + owner_rows(vector, r["mask"][...], r["spread"][...], v * own)
        r["owned"][...] = owned
        for copy in swaps:
            copy.wait()
        return loads + [two[0] for two in pairs.values()]

    results = staged_call(
        ident, ins, outs, scratch, 3 * parts, body,
        {"summed": pl.ANY, "weights": pl.ANY, "context": pltpu.VMEM, "table": pltpu.VMEM},
        ("output", "grad_attn", "slabs", "normal", "scale"), 48,
    )
    return tuple(
        results[name]
        for name in ("output", "grad_attn", "gctx_in", "slabs", "normal", "scale", "owned")
    )


def gather_copies(jobs, sizes):
    total = 0
    for job in jobs.values():
        for order in job["orders"]:
            total += 1
            for number, axis in enumerate(order):
                if axis == "p":
                    total += sizes["x"] * sizes["z"] - 1
                else:
                    total += 6 if number > 0 and sizes[axis] == 4 else sizes[axis] - 1
    return total


class Gathers:
    def __init__(self, buffers, jobs, spot, sizes, move):
        self.buffers, self.jobs, self.spot, self.sizes, self.move = buffers, jobs, spot, sizes, move
        self.states, self.finished = {}, []

    def send(self, name, cut, fixed, device):
        axes = self.jobs[name]["axes"]
        view = self.buffers[name].at[self.lead(name) + window(axes, fixed, cut)]
        copy = self.move(view, view, device)
        self.finished.append(copy)
        return copy

    def lead(self, name):
        return () if self.jobs[name].get("half") else (self.spot["k"],)

    def own(self, name):
        axes = self.jobs[name]["axes"]
        return self.buffers[name].at[self.lead(name) + tuple(self.spot[a] for a in axes)]

    def start(self, name):
        job = self.jobs[name]
        self.states[name] = [
            {"cut": cut, "order": order, "step": 0, "copies": [], "half": False, "ring": False}
            for cut, order in zip(job["cuts"], job["orders"])
        ]
        self.pump(name)

    def pump(self, *names):
        for name in names:
            for state in self.states[name]:
                self.advance(name, state)

    def drain(self, *names):
        while any(s["step"] <= len(s["order"]) + 1 for name in names for s in self.states[name]):
            self.pump(*names)

    def advance(self, name, state):
        step, order, cut = state["step"], state["order"], state["cut"]
        if step > len(order) + 1:
            return
        if state["half"]:
            axis, halved, near, far, fixed = state["half"]
            for slot, turn, half in ((0, 3, near), (1, 1, far)):
                state["copies"][slot].wait_recv()
                spot = peer(self.spot, axis, turn, self.sizes)[0]
                device = peer(self.spot, axis, 4 - turn, self.sizes)[1]
                at = dict(fixed)
                at[axis], at[halved] = spot[axis], half
                state["copies"].append(self.send(name, cut, at, device))
            state["half"] = False
            return
        for copy in state["copies"][2 if state["ring"] else 0 :]:
            copy.wait_recv()
        state["copies"], state["ring"] = [], False
        state["step"] = step + 1
        if step > len(order):
            return
        if step == len(order) and self.jobs[name].get("half"):
            state["step"] = step + 2
            return
        if step == len(order):
            device = peer(self.spot, "k", 1, self.sizes)[1]
            state["copies"] = [self.send(name, cut, {}, device)]
            return
        axis = order[step]
        if axis == "p":
            fixed = {"x": self.spot["x"], "z": self.spot["z"]}
            for _, device in plane(self.spot, self.sizes):
                state["copies"].append(self.send(name, cut, fixed, device))
            return
        fixed = {a: self.spot[a] for a in order[step:]}
        if step > 0 and self.sizes[axis] == 4:
            halved = order[0]
            size = self.sizes[halved] // 2
            near, far = pl.ds(0, size), pl.ds(size, size)
            for half, turn in ((near, 1), (far, 3), (far, 1), (near, 3)):
                at = dict(fixed)
                at[halved] = half
                device = peer(self.spot, axis, turn, self.sizes)[1]
                state["copies"].append(self.send(name, cut, at, device))
            state["half"], state["ring"] = (axis, halved, near, far, fixed), True
        else:
            for turn in range(1, self.sizes[axis]):
                device = peer(self.spot, axis, turn, self.sizes)[1]
                state["copies"].append(self.send(name, cut, fixed, device))

    def close(self):
        for copy in self.finished:
            copy.wait_send()


class Ring:
    def __init__(self, move, buffer, begin, count, here, to_right, to_left):
        self.move, self.buffer, self.here = move, buffer, here
        self.to_right, self.to_left = to_right, to_left
        half = count // 2
        self.near, self.far = pl.ds(begin, half), pl.ds(begin + half, half)
        self.copies = [
            self.shift(here, self.near, to_right), self.shift(here, self.far, to_left),
            self.shift(here, self.far, to_right), self.shift(here, self.near, to_left),
        ]

    def shift(self, block, rows, device):
        view = self.buffer.at[block, rows]
        return self.move(view, view, device)

    def relay(self):
        self.copies[0].wait_recv()
        self.copies.append(self.shift((self.here + 3) % 4, self.near, self.to_right))
        self.copies[1].wait_recv()
        self.copies.append(self.shift((self.here + 1) % 4, self.far, self.to_left))

    def finish(self):
        for copy in self.copies[2:]:
            copy.wait_recv()

    def close(self):
        for copy in self.copies:
            copy.wait_send()


def shards_step(r, parts, own, own_in, deep, thin, att, quarter):
    f32 = jnp.float32
    eight = 2 * parts
    width = thin * eight
    half = width // 2
    hid, out, joint = [widen(r[name][...]) for name in ("hidden_raw", "output_raw", "attend_raw")]
    proj, ret = widen(r["proj_raw"][...]), widen(r["return_raw"][...])
    tall, lanes = r["blocks"].shape[1:]
    small, ends = widen(r["small"][...]), widen(r["ends"][...])
    row = [small[i : i + 1] for i in range(small.shape[0])] + [ends[0:1], ends[1:2]]
    row = jnp.concatenate(row + [widen(r["hid_own"][...])], axis=1)
    row = jnp.concatenate([row, jnp.zeros((1, lanes - row.shape[1]), f32)], axis=1)
    for c in range(parts):
        both = jnp.concatenate(
            [joint[:, i * width + c * quarter : i * width + (c + 1) * quarter] for i in range(3)], axis=1
        )
        for k in range(2):
            j = 2 * c + k
            top = [
                hid[:, j * deep : (j + 1) * deep], out[:, j * thin : (j + 1) * thin],
                both[:, k * att : (k + 1) * att],
            ]
            low = [proj[:, k * half : (k + 1) * half], jnp.zeros((own_in, lanes - half), f32)]
            rows = [jnp.concatenate(top, axis=1), jnp.concatenate(low, axis=1), row]
            if tall > own + own_in + 1:
                rows.append(jnp.zeros((tall - own - own_in - 1, lanes), f32))
            r["blocks"][j] = jnp.concatenate(rows, axis=0).astype(LOW)
    for k in range(2):
        rows = [ret[:, k * half : (k + 1) * half]]
        if r["pair"].shape[1] > ret.shape[0]:
            rows.append(jnp.zeros((r["pair"].shape[1] - ret.shape[0], half), f32))
        r["pair"][k] = jnp.concatenate(rows, axis=0).astype(LOW)


def fold_own_step(r, target):
    own, inner, taps = r["conv_raw"].shape
    blocks = taps // FOLD
    rows = []
    for o in range(own):
        r["taps"][o, :taps] = widen(r["conv_raw"][o]).T
        pieces = [r["taps"][o, pl.ds(j, blocks, stride=FOLD), :] for j in range(FOLD)]
        rows.append(jnp.concatenate(pieces, axis=1))
    target[...] = jnp.concatenate(rows, axis=0).astype(LOW)


def slabs_step(r, own, deep, thin, att):
    f32 = jnp.float32
    blocks = r["blocks_in"][...].reshape(-1, r["blocks_in"].shape[2])
    main = dot(r["slab_rows"][...], blocks)
    pair = dot(r["pair_rows"][...], r["pair_in"][...].reshape(-1, r["pair_in"].shape[2]))
    tall = main.shape[0]
    r["ffn_slab"][...] = jnp.concatenate(
        [pair, main[:, :deep], main[:, deep : deep + thin], jnp.zeros((tall, 128 - thin), f32)], axis=1
    ).astype(LOW)
    att_slab = jnp.concatenate(
        [main[:, deep + thin :], jnp.zeros((tall, -att % 128), f32)], axis=1
    ).astype(LOW)
    early = dot(r["first_rows"][...], blocks[:, : r["early_all"].shape[-1]]).astype(LOW)
    return att_slab, early


def vectors_ready_step(r, parts, quarter):
    wide_in = r["nat_in"].shape[0]
    width = r["table"].shape[1]
    devices = r["vector_rows"].shape[0]
    early, half = r["early_all"], width // 2
    tall = 2 * parts * wide_in // devices
    both = [
        pick(r["nat_in"][...], early[k, :, :, :tall, :half].reshape(wide_in, half)) for k in range(2)
    ]
    both = jnp.concatenate(both, axis=1)
    for c in range(parts):
        r["proj"][c] = both[:, c * quarter : (c + 1) * quarter]
    lanes = early.shape[-1]
    cells = widen(early[0, :, :, tall:].reshape(-1, early.shape[-2] - tall, lanes))
    cells = cells[:, : 2 * parts].reshape(devices, lanes).astype(LOW)
    turned = dot(r["vector_rows"][...], cells).T.astype(LOW)
    spread = (dot(turned, r["owner"][...]) * widen(r["take"][...])).astype(LOW)
    table = dot(r["row_of"][...], spread)
    r["table"][...] = table
    for c in range(parts):
        r["quarters"][c] = table[:, c * quarter : (c + 1) * quarter]
    r["columns"][...] = jnp.concatenate([table, jnp.zeros((112, width), jnp.float32)], axis=0).T
    spread = (dot(turned, r["owner_in"][...]) * widen(r["take_in"][...])).astype(LOW)
    r["edges"][...] = dot(r["row_in"][...], spread)
    r["hid_bias"][...] = column_sum(dot(turned, r["owner_hid"][...]) * widen(r["take_hid"][...]))


def conv_ready_step(r, per, side):
    groups, rows, fold = r["conv"].shape
    for g in range(groups):
        taken = jnp.concatenate(
            [
                r["conv_all"][k, (g * per + n) // side, (g * per + n) % side]
                for k in range(2) for n in range(per)
            ],
            axis=0,
        )
        r["conv"][g] = dot(r["conv_order"][...], taken).astype(LOW)


def conv_turned_step(r):
    for g in range(r["conv"].shape[0]):
        r["conv_turned"][g] = widen(r["conv"][g]).T.astype(LOW)


def attend_ready_step(r):
    width = r["nat"].shape[0]
    both = [r["att_all"][k].reshape(width, -1) for k in range(2)]
    slab_cols = pick(jnp.concatenate(both, axis=1), r["place_att"][...])
    r["attend"][...] = pick(r["nat"][...], slab_cols)


def project_step(r, here, m, frames):
    parts, _, narrow = r["gathered"].shape
    groups, _, fold = r["conv"].shape
    inner = fold // FOLD
    half = (r["padded"].shape[2] - frames) // 2
    at = slice(m * frames, (m + 1) * frames)
    normal, _ = norm_blocks([widen(r["gathered"][c, at]) for c in range(parts)])
    low = []
    for c, block in enumerate(normal):
        lanes = slice(c * narrow, (c + 1) * narrow)
        low.append((block * r["edges"][0:1, lanes] + r["edges"][1:2, lanes]).astype(LOW))
    result = dot(jnp.concatenate(low, axis=1), r["proj"][here]) + r["quarters"][here, 0:1]
    live = lax.broadcasted_iota(jnp.int32, (frames, 1), 0) < r["spans"][m]
    turned = jnp.where(live, result, 0.0).T
    for g in range(groups):
        piece = turned[g * inner : (g + 1) * inner]
        r["plain"][m * groups + g] = piece
        edge = jnp.zeros((inner, half), LOW)
        r["padded"][m * groups + g] = jnp.concatenate([edge, piece.astype(LOW), edge], axis=1)


def conv_step(r, here, m, frames):
    groups, many, fold = r["conv"].shape
    inner = fold // FOLD
    blocks = many // inner
    span = r["padded"].shape[2]
    quarter = groups * inner

    def one(g, carry):
        index = m * groups + g
        fold_rows(r["padded"][index], r["folded"], inner)
        sums = dot(r["conv"][g], r["folded"][...])
        total = sums[:inner, :frames]
        for b in range(1, blocks):
            part = pltpu.roll(sums[b * inner : (b + 1) * inner], span - FOLD * b, 1)
            total = total + part[:, :frames]
        start = pl.multiple_of(here * quarter + g * inner, 16)
        before = total + r["columns"][pl.ds(start, inner), 1:2]
        r["before"][index] = before
        r["plain"][index] = r["plain"][index] + smooth(before)
        return carry

    lax.fori_loop(0, groups, one, 0)
    both = [r["plain"][m * groups + g] for g in range(groups)]
    r["summed"][here, m * frames : (m + 1) * frames] = jnp.concatenate(both, axis=0).T.astype(LOW)


def attention_step(r, here, m, frames):
    parts, _, quarter = r["summed"].shape
    heads = quarter // HEAD_DIM
    seg = frames // parts
    ratio = HEAD_DIM ** (-0.5)
    at = slice(m * frames, (m + 1) * frames)
    normal, _ = norm_blocks([widen(r["summed"][c, at]) for c in range(parts)])
    joint = jnp.zeros((frames, 3 * quarter), jnp.float32)
    for c in range(parts):
        low = (normal[c] * r["quarters"][c, 2:3] + r["quarters"][c, 3:4]).astype(LOW)
        r["low"][c, at] = low
        joint = joint + dot(low, r["attend"][c * quarter : (c + 1) * quarter])
    query = joint[:, :quarter] + r["quarters"][here, 4:5]
    keys = joint[:, quarter : 2 * quarter]
    value = joint[:, 2 * quarter :] + r["quarters"][here, 5:6]
    joint_low = [v.astype(LOW) for v in (query, keys, value)]
    for i in range(3):
        r["joint"][i, at] = joint_low[i]
    value_turned = value.T.astype(LOW)
    live = lax.broadcasted_iota(jnp.int32, (frames, 1), 0) < r["spans"][m]
    results = []
    for h in range(heads):
        cols = slice(h * HEAD_DIM, (h + 1) * HEAD_DIM)
        scores = dot_nt(joint_low[1][:, cols], joint_low[0][:, cols]) * ratio
        scores = jnp.where(live, scores, NEGATIVE)
        expo = jnp.exp(scores - jnp.max(scores, axis=0, keepdims=True))
        probs = (expo / jnp.sum(expo, axis=0, keepdims=True)).astype(LOW)
        r["probs"][m * heads + h] = probs
        results.append(dot(value_turned[cols], probs))
    context = jnp.concatenate(results, axis=0).T.astype(LOW)
    for d in range(parts):
        r["context"][d, m * seg : (m + 1) * seg] = context[d * seg : (d + 1) * seg]


def forward_start(values, sizes, ident, micros, frames, own, own_in, own_hid, own_ret, count):
    parts, squares, side = sizes["y"], sizes["x"] * sizes["z"], sizes["z"]
    devices = 2 * parts * squares
    rows, narrow = values["features"].shape
    _, inner, taps = values["conv_raw"].shape
    eight, blocks, fold = 2 * parts, taps // FOLD, inner * FOLD
    tall_block, tall_pair = own + own_in + 1, own_ret
    tall_block, tall_pair = tall_block + -tall_block % 16, tall_pair + -tall_pair % 16
    tall = eight * own
    width, wide_in, hidden = own * devices, own_in * devices, own_hid * devices
    quarter = width // parts
    half = width // 2
    groups = quarter // inner
    many = blocks * inner
    per = inner // own // 2
    heads = quarter // HEAD_DIM
    span = frames + blocks * FOLD
    seg = frames // parts
    mine = micros * seg
    deep, thin, att = hidden // eight, width // eight, 3 * quarter // 2
    wide = att + -att % 128
    lanes_a = half + deep + 128
    f32 = jnp.float32

    ones = {}
    j, s = np.divmod(np.arange(tall), own)
    ones["slab_rows"] = onehot(j * tall_block + s, np.arange(eight * tall_block))
    early_rows = eight * own_in + eight + -(eight * own_in + eight) % 16
    j, s = np.divmod(np.arange(eight * own_in), own_in)
    from_rows = np.full(early_rows, -1)
    from_rows[: eight * own_in] = j * tall_block + own + s
    from_rows[eight * own_in : eight * own_in + eight] = np.arange(eight) * tall_block + own + own_in
    ones["first_rows"] = onehot(from_rows, np.arange(eight * tall_block))
    j, s = np.divmod(np.arange(2 * own_ret), own_ret)
    ones["pair_rows"] = onehot(j * tall_pair + s, np.arange(2 * tall_pair))
    ones["nat_in"] = onehot(np.arange(wide_in), natural_of(wide_in, parts, squares))
    ones["nat"] = onehot(np.arange(width), natural_of(width, parts, squares))
    lanes = np.arange(2 * att)
    ones["place_att"] = onehot(np.arange(2 * wide), np.where(lanes < att, lanes, lanes - att + wide))
    slab = np.arange(many).reshape(2, per, own, blocks)
    ones["conv_order"] = onehot(
        [slab[(o // own) % 2, o // own // 2, o % own, b] for b in range(blocks) for o in range(inner)],
        np.arange(many),
    )
    vector_lanes = count * own + 2 * own_in + own_hid
    early_lanes = max(half, vector_lanes + -vector_lanes % 128)
    spots = np.arange(devices).reshape(squares, parts, 2).transpose(1, 0, 2).reshape(-1)
    ones["vector_rows"] = onehot(spots, np.arange(devices))
    lane = np.arange(early_lanes)
    ask = np.arange(width)
    edge = count * own
    ones["take"] = (lane[:, None] < edge) & (lane[:, None] % own == ask[None, :] % own)
    ones["row_of"] = onehot(np.arange(16), np.where(lane < edge, lane // own, -1))
    ones["owner"] = onehot(np.arange(devices), ask // own)
    ones["owner_in"] = onehot(np.arange(devices), np.arange(wide_in) // own_in)
    ends = (lane >= edge) & (lane < edge + 2 * own_in)
    ones["take_in"] = ends[:, None] & (
        (lane[:, None] - edge) % own_in == (np.arange(wide_in) % own_in)[None, :]
    )
    ones["row_in"] = onehot(np.arange(16), np.where(ends, (lane - edge) // own_in, -1))
    ones["owner_hid"] = onehot(np.arange(devices), np.arange(hidden) // own_hid)
    ones["take_hid"] = onehot(lane, edge + 2 * own_in + np.arange(hidden) % own_hid)

    all_axes, row_axes = ("y", "x", "z"), ("x", "z")
    cut_a = lanes_a // 256 * 128 + 128 * (lanes_a // 128 % 2)
    jobs = {
        "conv_all": {
            "axes": row_axes,
            "cuts": [(0, tall, 0, fold // 2), (0, tall, fold // 2, fold // 2)],
            "orders": [("z", "x"), ("x", "z")],
        },
        "early_all": {
            "axes": row_axes, "cuts": [(0, early_rows, 0, early_lanes)], "orders": [("p",)],
        },
        "att_all": {"axes": row_axes, "cuts": [(0, tall, 0, wide)], "orders": [("x", "z")]},
        "weights": {
            "axes": all_axes, "half": True,
            "cuts": [(0, tall, 0, cut_a), (0, tall, cut_a, lanes_a - cut_a)],
            "orders": [("y", "z", "x"), ("y", "x", "z")],
        },
    }
    copies = gather_copies(jobs, sizes) + eight + 6 * (1 + micros) + micros * (parts - 1)
    lead = (sizes["x"], sizes["z"])
    lanes_cut = deep + thin + att
    scratch = {
        "blocks": pltpu.VMEM((eight, tall_block, lanes_cut), LOW),
        "pair": pltpu.VMEM((2, tall_pair, half), LOW),
        "taps": pltpu.VMEM((own, 2 * taps, inner), f32),
        "blocks_in": pltpu.VMEM((eight, tall_block, lanes_cut), LOW),
        "pair_in": pltpu.VMEM((2, tall_pair, half), LOW),
        "ffn_slab": pltpu.VMEM((tall, lanes_a), LOW),
        "early_all": pltpu.VMEM((2,) + lead + (early_rows, early_lanes), LOW),
        "conv_all": pltpu.VMEM((2,) + lead + (tall, fold), LOW),
        "att_all": pltpu.VMEM((2,) + lead + (tall, wide), LOW),
        "quarters": pltpu.VMEM((parts, 16, quarter), f32),
        "columns": pltpu.VMEM((width, 128), f32),
        "conv": pltpu.VMEM((groups, many, fold), LOW),
        "plain": pltpu.VMEM((micros * groups, inner, frames), f32),
        "folded": pltpu.VMEM((fold, span), LOW),
        "context": pltpu.VMEM((parts, mine, quarter), LOW),
    }
    outs = {
        "weights": ((parts,) + lead + (tall, lanes_a), LOW),
        "gathered": ((parts, rows, narrow), LOW),
        "proj": ((parts, wide_in, quarter), LOW),
        "table": ((16, width), f32),
        "edges": ((16, wide_in), f32),
        "hid_bias": ((1, hidden), f32),
        "attend": ((width, 3 * quarter), LOW),
        "conv_turned": ((groups, fold, many), LOW),
        "padded": ((micros * groups, inner, span), LOW),
        "before": ((micros * groups, inner, frames), f32),
        "summed": ((parts, rows, quarter), LOW),
        "low": ((parts, rows, quarter), LOW),
        "joint": ((3, rows, quarter), LOW),
        "probs": ((micros * heads, frames, frames), LOW),
        "context_in": ((parts, mine, quarter), LOW),
    }
    ins = dict(values)
    ins.update({name: jnp.asarray(value, LOW) for name, value in ones.items()})
    kept = ("gathered", "proj", "table", "edges", "hid_bias", "attend", "conv_turned", "padded",
            "before", "summed", "low", "joint", "probs")

    def body(r, move, need, keep, copy_here):
        spot = place(side)
        here, core, rank = spot["y"], spot["k"], lax.axis_index("rows")
        base = rank - core
        gathers = Gathers({name: r[name] for name in jobs}, jobs, spot, sizes, move)
        ring = [peer(spot, "y", step, sizes)[1] for step in range(1, parts)]
        others = [(here + step) % parts for step in range(1, parts)]
        to_right, to_left = ring[0], ring[2]
        number = here * 2 + core
        eights = [(number + step) % eight for step in range(1, eight)]
        eight_at = [(other // 2, base + other % 2) for other in eights]
        friends = eight_at + [device for _, device in plane(spot, sizes)]
        call_out(friends)
        need("hidden_raw", "output_raw", "attend_raw", "proj_raw", "return_raw")
        shards_step(r, parts, own, own_in, deep, thin, att, quarter)
        need("features")
        r["gathered"][here] = r["features"][...]
        greet(friends)
        sent = [
            move(r["blocks"].at[other], r["blocks_in"].at[number], device)
            for other, device in zip(eights, eight_at)
        ]
        sent.append(move(r["pair"].at[1 - core], r["pair_in"].at[core], (here, base + 1 - core)))
        features = Ring(move, r["gathered"], 0, rows, here, to_right, to_left)
        r["blocks_in"][number] = r["blocks"][number]
        r["pair_in"][core] = r["pair"][core]
        need("conv_raw")
        fold_own_step(r, gathers.own("conv_all"))
        gathers.start("conv_all")
        need("slab_rows", "first_rows", "pair_rows")
        for copy in sent:
            copy.wait_recv()
        att_slab, early = slabs_step(r, own, deep, thin, att)
        gathers.own("early_all")[...] = early
        gathers.start("early_all")
        first = copy_here(r["ffn_slab"], gathers.own("weights"))
        gathers.own("att_all")[...] = att_slab
        gathers.start("att_all")
        gathers.pump("conv_all")
        first.wait()
        gathers.start("weights")
        features.relay()
        gathers.pump("early_all", "weights")
        gathers.pump("conv_all")
        gathers.drain("early_all")
        need("nat_in", "vector_rows", "owner", "take", "row_of", "owner_in", "take_in", "row_in",
             "owner_hid", "take_hid")
        vectors_ready_step(r, parts, quarter)
        gathers.pump("conv_all", "weights")
        features.finish()
        keep("gathered")
        project_step(r, here, 0, frames)
        gathers.pump("att_all")
        gathers.drain("conv_all")
        gathers.pump("weights")
        need("conv_order")
        conv_ready_step(r, per, side)
        rings = []
        for m in range(micros):
            if m > 0:
                project_step(r, here, m, frames)
            conv_step(r, here, m, frames)
            if m > 0:
                rings[m - 1].relay()
            rings.append(Ring(move, r["summed"], m * frames, frames, here, to_right, to_left))
            gathers.pump("att_all")
        for name in ("proj", "table", "edges", "hid_bias", "padded", "before"):
            keep(name)
        gathers.drain("att_all")
        need("nat", "place_att")
        attend_ready_step(r)
        keep("attend")
        rings[-1].relay()
        conv_turned_step(r)
        keep("conv_turned")
        swaps = []
        for m in range(micros):
            rings[m].finish()
            attention_step(r, here, m, frames)
            cells = pl.ds(m * seg, seg)
            swaps += [
                move(r["context"].at[other, cells], r["context_in"].at[here, cells], device)
                for other, device in zip(others, ring)
            ]
            r["context_in"][here, cells] = r["context"][here, cells]
            at = pl.ds(m * frames, frames)
            for name in ("low", "joint"):
                keep(name, (slice(None), at))
            keep("probs", pl.ds(m * heads, heads))
            if m == 0:
                gathers.pump("weights")
        keep("summed")
        gathers.drain("weights")
        for copy in swaps:
            copy.wait()
        for copy in sent:
            copy.wait_send()
        for item in rings + [features, gathers]:
            item.close()
        return [first]

    return staged_call(
        ident, ins, outs, scratch, copies, body,
        {"spans": pltpu.SMEM, "weights": pl.ANY, "small": pltpu.VMEM}, kept, 32,
    )


def stages_of(axes, order, sizes):
    left = list(axes)
    result = []
    for axis in order:
        if axis == "p":
            result.append((axis, 0, (), (), False))
            continue
        where = left.index(axis)
        left = left[:where] + left[where + 1 :]
        dims = tuple(sizes[a] for a in left)
        result.append((axis, where, tuple(left), dims, sizes[axis] == 4 and len(dims) > 0))
    return result


def sum_scratch(jobs, sizes):
    scratch, copies = {}, 0
    for name, job in jobs.items():
        for part, (cut, order) in enumerate(zip(job["cuts"], job["orders"])):
            block = (cut[1], cut[3])
            dims = tuple(sizes[a] for a in job["axes"])
            key = f"{name}{part}"
            scratch[key + "got"] = pltpu.VMEM(dims + block, LOW)
            if job["far"]:
                scratch[key + "own"] = pltpu.VMEM((2,) + dims[1:] + block, LOW)
            copies += 1
            for number, (axis, _, _, dims, ring) in enumerate(stages_of(job["axes"], order, sizes)):
                if ring:
                    half = (dims[0] // 2,) + dims[1:] + block
                    scratch[f"{key}got{number}"] = pltpu.VMEM((6,) + half, LOW)
                    copies += 6
                else:
                    others = sizes["x"] * sizes["z"] - 1 if axis == "p" else sizes[axis] - 1
                    scratch[f"{key}got{number}"] = pltpu.VMEM((max(others, 1),) + dims + block, LOW)
                    copies += others
                if dims:
                    scratch[f"{key}sum{number}"] = pltpu.VMEM(dims + block, LOW)
    return scratch, copies


class Sums:
    def __init__(self, refs, jobs, spot, sizes, sources, sinks, local):
        self.refs, self.jobs, self.spot, self.sizes = refs, jobs, spot, sizes
        self.sources, self.sinks, self.local = sources, sinks, local
        self.states, self.finished = {}, []

    def move(self, source, target, device):
        copy = self.refs["move"](source, target, device)
        self.finished.append(copy)
        return copy

    def start(self, name):
        job, core = self.jobs[name], self.spot["k"]
        sibling = peer(self.spot, "k", 1, self.sizes)[1]
        states = []
        for part, (cut, order) in enumerate(zip(job["cuts"], job["orders"])):
            key = f"{name}{part}"
            window_at = window(job["axes"], {}, cut)
            got = self.refs[key + "got"]
            copy = self.move(self.sources[name].at[(1 - core,) + window_at], got, sibling)
            near = None
            if job["far"]:

                def near(number, slot, window_at=window_at, key=key, part=part):
                    return pltpu.make_async_copy(
                        self.sources[name].at[(core, number) + window_at[1:]],
                        self.refs[key + "own"].at[slot], self.local.at[2 * part + slot],
                    )

                near(0, 0).start()
            states.append(
                {
                    "key": key, "cut": cut, "held": got, "left": job["axes"], "step": 0, "near": near,
                    "copies": [copy], "half": False,
                    "stages": stages_of(job["axes"], order, self.sizes),
                }
            )
        self.states[name] = states

    def pump(self, *names):
        for name in names:
            for state in self.states[name]:
                self.advance(name, state)

    def drain(self, *names):
        while any(s["step"] <= len(s["stages"]) for name in names for s in self.states[name]):
            self.pump(*names)

    def advance(self, name, state):
        step, stages = state["step"], state["stages"]
        if step > len(stages):
            return
        if step == 0:
            self.add_own(name, state)
        elif state["half"]:
            self.relay(state, stages[step - 1], step - 1)
            return
        else:
            self.add_stage(name, state, stages[step - 1], step - 1)
        if step < len(stages):
            self.send_stage(state, stages[step], step)
        state["step"] = step + 1

    def add_own(self, name, state):
        for copy in state["copies"]:
            copy.wait_recv()
        held, cut = state["held"], state["cut"]
        dims = tuple(self.sizes[a] for a in state["left"])
        if state["near"] is not None:
            near, own = state["near"], self.refs[state["key"] + "own"]
            for number in range(dims[0]):
                slot = number % 2
                if number + 1 < dims[0]:
                    near(number + 1, 1 - slot).start()
                near(number, slot).wait()

                def add(index, number=number, slot=slot):
                    held[(number,) + index] = held[(number,) + index] + own[(slot,) + index]

                loop_blocks(dims[1:], add)
            return
        else:
            source, core = self.sources[name], self.spot["k"]

            def add(index):
                rows, lanes = slice(cut[0], cut[0] + cut[1]), slice(cut[2], cut[2] + cut[3])
                held[index] = held[index] + source[(core,) + index + (rows, lanes)]

        loop_blocks(dims, add)

    def send_stage(self, state, stage, number):
        axis, _, left, dims, ring = stage
        held, got = state["held"], self.refs[f"{state['key']}got{number}"]
        before = state["left"]
        state["copies"] = []
        if axis == "p":
            for number, (moved, device) in enumerate(plane(self.spot, self.sizes)):
                source = held.at[moved["x"], moved["z"]]
                state["copies"].append(self.move(source, got.at[number], device))
        elif not ring:
            for step in range(1, self.sizes[axis]):
                moved, device = peer(self.spot, axis, step, self.sizes)
                at = tuple(moved[a] if a == axis else slice(None) for a in before)
                state["copies"].append(self.move(held.at[at], got.at[step - 1], device))
        else:
            size = dims[0] // 2
            near, far = pl.ds(0, size), pl.ds(size, size)

            def piece(step, half):
                moved = peer(self.spot, axis, step, self.sizes)[0]
                return held.at[
                    tuple(
                        moved[a] if a == axis else (half if a == left[0] else slice(None)) for a in before
                    )
                ]

            right = peer(self.spot, axis, 1, self.sizes)[1]
            back = peer(self.spot, axis, 3, self.sizes)[1]
            state["copies"] = [
                self.move(piece(2, near), got.at[0], right),
                self.move(piece(2, far), got.at[1], back),
                self.move(piece(1, far), got.at[2], right),
                self.move(piece(3, near), got.at[3], back),
            ]
            state["half"] = True

    def relay(self, state, stage, number):
        axis, where, left, dims, _ = stage
        held = state["held"]
        got = self.refs[f"{state['key']}got{number}"]
        size = dims[0] // 2
        ahead, right = peer(self.spot, axis, 1, self.sizes)
        behind, back = peer(self.spot, axis, 3, self.sizes)
        for slot, spot, offset in ((0, ahead, 0), (1, behind, size)):
            state["copies"][slot].wait_recv()

            def add(index, slot=slot, spot=spot, offset=offset):
                full = (index[0] + offset,) + index[1:]
                full = full[:where] + (spot[axis],) + full[where:]
                held[full] = held[full] + got[(slot,) + index]

            loop_blocks((size,) + dims[1:], add)
            at = tuple(
                spot[a] if a == axis else (pl.ds(offset, size) if a == left[0] else slice(None))
                for a in state["left"]
            )
            state["copies"].append(
                self.move(held.at[at], got.at[4 + slot], (right, back)[slot])
            )
        state["half"] = False

    def add_stage(self, name, state, stage, number):
        axis, where, left, dims, ring = stage
        held, cut = state["held"], state["cut"]
        got = self.refs[f"{state['key']}got{number}"]
        target = self.refs[f"{state['key']}sum{number}"] if dims else None
        mine = None if axis == "p" else self.spot[axis]
        for copy in state["copies"][2 if ring else 0 :]:
            copy.wait_recv()
        if ring:
            size = dims[0] // 2
            for offset, first, second in ((0, 4, 3), (size, 2, 5)):

                def add(index, offset=offset, first=first, second=second):
                    full = (index[0] + offset,) + index[1:]
                    own = full[:where] + (mine,) + full[where:]
                    result = widen(held[own]) + widen(got[(first,) + index]) + widen(got[(second,) + index])
                    target[full] = result.astype(LOW)

                loop_blocks((size,) + dims[1:], add)
        else:

            def add(index):
                index = index if dims else ()
                if axis == "p":
                    result = widen(held[self.spot["x"], self.spot["z"]])
                else:
                    result = widen(held[index[:where] + (mine,) + index[where:]])
                for step in range(len(state["copies"])):
                    result = result + widen(got[(step,) + index])
                if target is None:
                    rows, lanes = slice(cut[0], cut[0] + cut[1]), slice(cut[2], cut[2] + cut[3])
                    self.sinks[name][rows, lanes] = result
                else:
                    target[index] = result.astype(LOW)

            loop_blocks(dims if dims else (1,), add)
        state["held"], state["left"] = target, left

    def close(self):
        for copy in self.finished:
            copy.wait_send()


def attention_back_step(r, m, frames):
    parts, mine, quarter = r["gctx_in"].shape
    heads = quarter // HEAD_DIM
    seg = frames // parts
    ratio = HEAD_DIM ** (-0.5)
    at, cells = slice(m * frames, (m + 1) * frames), slice(m * seg, (m + 1) * seg)
    grad = jnp.concatenate([r["gctx_in"][d, cells] for d in range(parts)], axis=0)
    query, keys, value = r["joint"][0, at], r["joint"][1, at], r["joint"][2, at]
    keys_turned = widen(keys).T.astype(LOW)
    queries, key_parts, values = [], [], []
    for h in range(heads):
        cols = slice(h * HEAD_DIM, (h + 1) * HEAD_DIM)
        probs_low = r["probs"][m * heads + h]
        grad_probs = dot_nt(value[:, cols], grad[:, cols])
        weighted = widen(probs_low) * grad_probs
        centre = jnp.sum(weighted, axis=0, keepdims=True)
        slope = (weighted - widen(probs_low) * centre).astype(LOW)
        values.append(dot(probs_low, grad[:, cols]))
        key_parts.append(dot(slope, query[:, cols]) * ratio)
        queries.append(dot(keys_turned[cols], slope) * ratio)
    slopes = [
        jnp.concatenate(queries, axis=0).T.astype(LOW),
        jnp.concatenate(key_parts, axis=1).astype(LOW),
        jnp.concatenate(values, axis=1).astype(LOW),
    ]
    for i, source in enumerate((0, 2)):
        found = column_sum(widen(slopes[source]))
        r["att_sums"][i : i + 1] = found if m == 0 else r["att_sums"][i : i + 1] + found
    slope = jnp.concatenate(slopes, axis=1)
    size = slope.shape[1] // 2
    for k in range(2):
        r["slope_joint"][k, at, :size] = slope[:, k * size : (k + 1) * size]
        r["slope_joint"][k, at, size:] = jnp.zeros((frames, r["slope_joint"].shape[2] - size), LOW)
    terms = dot_nt(slope, r["attend"][...]).astype(LOW)
    for d in range(parts):
        r["terms"][d, cells] = terms[d * seg : (d + 1) * seg]


def attention_weight_step(r):
    parts = r["low"].shape[0]
    for k in range(2):
        pieces = [dot_tn(r["low"][c], r["slope_joint"][k]).astype(LOW) for c in range(parts)]
        grads = dot(r["back_att"][...], jnp.concatenate(pieces, axis=0)).astype(LOW)
        r["att_grad"][k] = grads.reshape(r["att_grad"].shape[1:])


def norm_back_step(r, m, seg):
    parts, _, quarter = r["gpos"].shape
    cells = slice(m * seg, (m + 1) * seg)
    normal, scale = r["normal"][cells], r["scale"][cells, 0:1]
    grad = r["grad_attn"][cells] + r["terms_sum"][...]
    result = norm_back(grad, normal, scale, r["table"][2:3]).astype(LOW)
    for c in range(parts):
        r["gpos"][c, cells] = result[:, c * quarter : (c + 1) * quarter]
    for i, found in enumerate((column_sum(grad * normal), column_sum(grad))):
        r["sums_own"][i : i + 1] = found if m == 0 else r["sums_own"][i : i + 1] + found


def owner_rows(vector, mask, spread, place):
    cells = dot((widen(mask) * vector).astype(LOW), spread)
    return cells if place == 0 else pltpu.roll(cells, place, 1)


def vectors_step(r, own):
    owned = r["owned"][...]
    for v in range(2):
        owned = owned + owner_rows(r["sums_own"][v : v + 1], r["mask"][...], r["spread"][...], v * own)
    r["full"][...] = dot(r["row_full"][...], owned.astype(LOW)).astype(LOW).reshape(r["full"].shape)


def conv_back_step(r, here, m, frames, tall, per):
    parts, mine, quarter = r["gpos"].shape
    groups, fold, many = r["conv_turned"].shape
    inner = fold // FOLD
    blocks = many // inner
    half = blocks * FOLD // 2
    span = frames + blocks * FOLD
    seg = frames // parts
    side = r["conv_grad"].shape[2]
    f32 = jnp.float32
    cells = slice(m * seg, (m + 1) * seg)
    grad = jnp.concatenate([widen(r["gpos_in"][d, cells]) for d in range(parts)], axis=0).T
    for g in range(groups):
        r["grads"][g] = grad[g * inner : (g + 1) * inner]
    live = lax.broadcasted_iota(jnp.int32, (1, frames), 1) < r["spans"][m]

    def one(g, carry):
        index = m * groups + g
        grad = r["grads"][g]
        slope = (grad * smooth_slope(r["before"][index])).astype(LOW)
        r["turn"][index, :, 0:1] = jnp.sum(widen(slope), axis=1, keepdims=True)
        wide = jnp.concatenate([slope, jnp.zeros((inner, span - frames), LOW)], axis=1)
        spread_blocks(wide, r["moved"], inner, blocks)
        fold_rows(r["padded"][index], r["folded"], inner)
        weight = dot_nt(r["moved"][...], r["folded"][...])
        back_sums = dot(r["conv_turned"][g], r["moved"][...])
        total = grad
        for j in range(FOLD):
            part = pltpu.roll(back_sums[j * inner : (j + 1) * inner], (span + j - half) % span, 1)
            total = total + part[:, :frames]
        total = jnp.where(live, total, 0.0).astype(LOW).astype(f32)
        r["turn"][index, :, 1:2] = jnp.sum(total, axis=1, keepdims=True)
        r["grads"][g] = total
        weight = dot(r["back_conv"][...], weight.astype(LOW)).reshape(2, per, tall, fold)
        for n in range(per):
            xz = g * per + n
            for k in range(2):
                piece = weight[k, n]
                if m > 0:
                    piece = piece + widen(r["conv_grad"][k, xz // side, xz % side])
                r["conv_grad"][k, xz // side, xz % side] = piece.astype(LOW)
        return carry

    lax.fori_loop(0, groups, one, 0)
    both = [r["grads"][g] for g in range(groups)]
    r["slopes_all"][here, m * frames : (m + 1) * frames] = jnp.concatenate(both, axis=0).T.astype(LOW)


def conv_sums_step(r, micros):
    groups = r["turn"].shape[0] // micros
    sums = jnp.concatenate(
        [sum(r["turn"][m * groups + g] for m in range(micros)) for g in range(groups)], axis=0
    ).T
    r["conv_sums"][...] = sums[:8]


def finish_step(r, here, m, frames):
    parts, _, narrow = r["gathered"].shape
    f32 = jnp.float32
    size = parts * narrow
    chunk = 256
    mine_at = pl.ds(pl.multiple_of(here * narrow, narrow), narrow)
    gain, shift = r["edges"][0:1, mine_at], r["edges"][1:2, mine_at]
    if m == 0:
        r["edge_sums"][...] = jnp.zeros_like(r["edge_sums"])
        r["proj_grad"][...] = jnp.zeros_like(r["proj_grad"])

    def one(number, carry):
        at = pl.ds(pl.multiple_of(m * frames + number * chunk, chunk), chunk)
        blocks = [widen(r["gathered"][c, at]) for c in range(parts)]
        slopes = [r["slopes_all"][b, at] for b in range(parts)]
        normal, scale = norm_blocks(blocks)
        first = jnp.zeros((chunk, 1), f32)
        second = jnp.zeros((chunk, 1), f32)
        for c in range(parts):
            lanes = slice(c * narrow, (c + 1) * narrow)
            grad = sum(dot_nt(slopes[b], r["proj"][b, lanes]) for b in range(parts))
            scaled = grad * r["edges"][0:1, lanes]
            first = first + jnp.sum(scaled, axis=1, keepdims=True)
            second = second + jnp.sum(scaled * normal[c], axis=1, keepdims=True)
        mean = sum(jnp.sum(block, axis=1, keepdims=True) for block in blocks) / size
        mine = (widen(r["gathered"][here, at]) - mean) * scale
        grad = sum(dot_nt(slopes[b], r["proj"][b, mine_at]) for b in range(parts))
        r["features_grad"][at] = scale * (grad * gain - first / size - mine * (second / size))
        low = (mine * gain + shift).astype(LOW)
        r["proj_grad"][...] = r["proj_grad"][...] + jnp.concatenate(
            [dot_tn(low, slopes[b]) for b in range(parts)], axis=1
        )
        r["edge_sums"][0:1] = r["edge_sums"][0:1] + column_sum(grad * mine)
        r["edge_sums"][1:2] = r["edge_sums"][1:2] + column_sum(grad)
        return carry

    lax.fori_loop(0, frames // chunk, one, 0)


def local_step(r, own, own_in):
    ranks, quarter = r["mask_ch"].shape
    width = r["proj_grad"].shape[1]
    f32 = jnp.float32
    vectors = [
        r["conv_sums"][1:2], r["conv_sums"][0:1], r["att_sums"][0:1], r["att_sums"][1:2],
    ]
    owned = 0.0
    for v in range(4):
        owned = owned + owner_rows(vectors[v], r["mask_ch"][...], r["spread_ch"][...], v * own)
    for v in range(2):
        owned = owned + owner_rows(
            r["edge_sums"][v : v + 1], r["mask_in"][...], r["spread_in"][...], 4 * own + v * own_in
        )
    lanes = owned.shape[1]
    owned = jnp.concatenate([owned, jnp.zeros((ranks, width - lanes), f32)], axis=1)
    result = dot(r["row_proj"][...], r["proj_grad"][...].astype(LOW))
    result = result + dot(r["row_vector"][...], owned.astype(LOW))
    r["local"][...] = result.astype(LOW).reshape(r["local"].shape)


def backward_rest(values, sizes, ident, micros, frames, own, own_in, own_hid, own_ret, thin):
    parts, squares, side = sizes["y"], sizes["x"] * sizes["z"], sizes["z"]
    devices, ranks = 2 * parts * squares, 2 * squares
    _, mine, quarter = values["gctx_in"].shape
    width = parts * quarter
    rows = micros * frames
    narrow = values["gathered"].shape[2]
    groups, fold, many = values["conv_turned"].shape
    inner = fold // FOLD
    blocks = many // inner
    span = frames + blocks * FOLD
    per = inner // own // 2
    tall, lanes_a = values["ffn"].shape[-2:]
    half, deep = width // 2, lanes_a - width // 2 - 128
    att = 3 * quarter // 2
    wide = att + -att % 128
    eight = 2 * parts
    seg = frames // parts
    f32 = jnp.float32

    ones = {}
    ones["back_att"] = onehot(natural_of(width, parts, squares), np.arange(width))
    slab = np.arange(many).reshape(2, per, own, blocks)
    ones["back_conv"] = onehot(
        np.arange(many),
        [slab[(o // own) % 2, o // own // 2, o % own, b] for b in range(blocks) for o in range(inner)],
    )
    count = 8 * own + own_hid
    lane = np.arange(count + -count % 128)
    ones["mask"] = onehot(np.arange(devices), np.arange(width) // own)
    ones["spread"] = onehot(np.arange(width) % own, lane)
    full_rows = np.full((devices, 16), -1)
    full_rows[:, 0] = np.arange(devices).reshape(parts, squares, 2).transpose(2, 0, 1).reshape(-1)
    ones["row_full"] = onehot(full_rows.reshape(-1), np.arange(devices))
    few = 4 * own + 2 * own_in
    few = np.arange(few + -few % 128)
    ones["mask_ch"] = onehot(np.arange(ranks), np.arange(quarter) // own)
    ones["spread_ch"] = onehot(np.arange(quarter) % own, few)
    ones["mask_in"] = onehot(np.arange(ranks), np.arange(narrow) // own_in)
    ones["spread_in"] = onehot(np.arange(narrow) % own_in, few)
    high = own_in + 1 + -(own_in + 1) % 16
    order = np.arange(ranks).reshape(squares, 2).T.reshape(-1)
    proj_rows = np.full((ranks, high), -1)
    proj_rows[:, :own_in] = order[:, None] * own_in + np.arange(own_in)[None, :]
    ones["row_proj"] = onehot(proj_rows.reshape(-1), np.arange(narrow))
    vector_rows = np.full((ranks, high), -1)
    vector_rows[:, own_in] = order
    ones["row_vector"] = onehot(vector_rows.reshape(-1), np.arange(ranks))

    cut_lanes = lanes_a // 256 * 128 + 128 * (lanes_a // 128 % 2)
    jobs = {
        "ffn": {
            "axes": ("y", "x", "z"), "far": True,
            "cuts": [(0, tall, 0, cut_lanes), (0, tall, cut_lanes, lanes_a - cut_lanes)],
            "orders": [("x", "z", "y"), ("z", "x", "y")],
        },
        "full": {
            "axes": ("y", "x", "z"), "far": False, "cuts": [(0, 16, 0, len(lane))],
            "orders": [("z", "x", "y")],
        },
        "att": {
            "axes": ("x", "z"), "far": False, "cuts": [(0, tall, 0, wide)], "orders": [("x", "z")],
        },
        "conv": {
            "axes": ("x", "z"), "far": False,
            "cuts": [(0, tall, 0, fold // 2), (0, tall, fold // 2, fold // 2)],
            "orders": [("x", "z"), ("z", "x")],
        },
        "local": {
            "axes": ("x", "z"), "far": False, "cuts": [(0, high, 0, width)], "orders": [("p",)],
        },
    }
    scratch, copies = sum_scratch(jobs, sizes)
    copies += micros * (parts - 1 + 12) + eight
    lead = {"y": parts, "x": sizes["x"], "z": sizes["z"]}
    low_rows = own + -own % 8
    block_lanes = deep + 128 + wide
    scratch.update(
        {
            "terms": pltpu.VMEM((parts, mine, width), LOW),
            "terms_held": pltpu.VMEM((micros, 6, seg // 2, width), LOW),
            "terms_sum": pltpu.VMEM((seg, width), f32),
            "slope_joint": pltpu.VMEM((2, rows, wide), LOW),
            "att_grad": pltpu.VMEM((2, sizes["x"], sizes["z"], tall, wide), LOW),
            "att_sums": pltpu.VMEM((8, quarter), f32),
            "gpos": pltpu.VMEM((parts, mine, quarter), LOW),
            "gpos_in": pltpu.VMEM((parts, mine, quarter), LOW),
            "sums_own": pltpu.VMEM((8, width), f32),
            "full": pltpu.VMEM((2, parts, sizes["x"], sizes["z"], 16, len(lane)), LOW),
            "grads": pltpu.VMEM((groups, inner, frames), f32),
            "turn": pltpu.VMEM((micros * groups, inner, 128), f32),
            "moved": pltpu.VMEM((many, span), LOW),
            "folded": pltpu.VMEM((fold, span), LOW),
            "slopes_all": pltpu.VMEM((parts, rows, quarter), LOW),
            "conv_sums": pltpu.VMEM((8, quarter), f32),
            "conv_grad": pltpu.VMEM((2, sizes["x"], sizes["z"], tall, fold), LOW),
            "proj_grad": pltpu.VMEM((narrow, width), f32),
            "edge_sums": pltpu.VMEM((8, narrow), f32),
            "local": pltpu.VMEM((2, sizes["x"], sizes["z"], high, width), LOW),
            "ffn_sum": pltpu.VMEM((tall, lanes_a), f32),
            "att_sum": pltpu.VMEM((tall, wide), f32),
            "block": pltpu.VMEM((eight, low_rows, block_lanes), f32),
            "pair": pltpu.VMEM((2, own_ret, half), f32),
        }
    )
    outs = {
        "features_grad": ((rows, narrow), f32),
        "full_sum": ((16, len(lane)), f32),
        "conv_sum": ((tall, fold), f32),
        "local_sum": ((high, width), f32),
        "block_in": ((eight, low_rows, block_lanes), f32),
        "pair_in": ((2, own_ret, half), f32),
    }
    ins = dict(values)
    ins.update({name: jnp.asarray(value, LOW) for name, value in ones.items()})

    def body(r, move, need, keep, copy_here):
        spot = place(side)
        here, core, rank = spot["y"], spot["k"], lax.axis_index("rows")
        base = rank - core
        local = r["local_sems"]
        r["move"] = move
        sources = {
            "ffn": r["ffn"], "full": r["full"], "att": r["att_grad"], "conv": r["conv_grad"],
            "local": r["local"],
        }
        sinks = {
            "ffn": r["ffn_sum"], "full": r["full_sum"], "att": r["att_sum"], "conv": r["conv_sum"],
            "local": r["local_sum"],
        }
        sums = Sums(r, jobs, spot, sizes, sources, sinks, local)
        ring = [peer(spot, "y", step, sizes)[1] for step in range(1, parts)]
        others = [(here + step) % parts for step in range(1, parts)]
        number = here * 2 + core
        eights = [(number + step) % eight for step in range(1, eight)]
        eight_at = [(other // 2, base + other % 2) for other in eights]
        friends = eight_at + [device for _, device in plane(spot, sizes)]
        call_out(friends)
        greet(friends)
        sent = []

        def swap(source, target, m):
            cells = pl.ds(m * seg, seg)
            copies = [
                move(source.at[other, cells], target.at[here, cells], device)
                for other, device in zip(others, ring)
            ]
            target[here, cells] = source[here, cells]
            sent.extend(copies)
            return copies

        def arrived(copies):
            for copy in copies:
                copy.wait_recv()

        to_right, to_left = ring[0], ring[2]
        right, across, left = [(here + step) % 4 for step in (1, 2, 3)]
        terms = r["terms"]

        def ring_add(m):
            held, size = r["terms_held"], seg // 2
            near, far = pl.ds(m * seg, size), pl.ds(m * seg + size, size)
            return [
                move(terms.at[across, near], held.at[m, 0], to_right),
                move(terms.at[across, far], held.at[m, 1], to_left),
                move(terms.at[right, far], held.at[m, 2], to_right),
                move(terms.at[left, near], held.at[m, 3], to_left),
            ]

        def ring_relay(m, copies):
            held, size = r["terms_held"], seg // 2
            near, far = pl.ds(m * seg, size), pl.ds(m * seg + size, size)
            copies[0].wait_recv()
            terms[right, near] = terms[right, near] + held[m, 0]
            copies.append(move(terms.at[right, near], held.at[m, 4], to_right))
            copies[1].wait_recv()
            terms[left, far] = terms[left, far] + held[m, 1]
            copies.append(move(terms.at[left, far], held.at[m, 5], to_left))

        def ring_end(m, copies):
            held, size = r["terms_held"], seg // 2
            near, far = pl.ds(m * seg, size), pl.ds(m * seg + size, size)
            arrived(copies[2:])
            sent.extend(copies)
            r["terms_sum"][:size] = widen(terms[here, near]) + widen(held[m, 4]) + widen(held[m, 3])
            r["terms_sum"][size:] = widen(terms[here, far]) + widen(held[m, 2]) + widen(held[m, 5])

        sums.start("ffn")
        need("joint", "probs", "attend")
        added = []
        for m in range(micros):
            attention_back_step(r, m, frames)
            added.append(ring_add(m))
            if m > 0:
                ring_relay(m - 1, added[m - 1])
        need("low", "back_att")
        attention_weight_step(r)
        ring_relay(micros - 1, added[-1])
        sums.start("att")
        sums.pump("ffn")
        swapped = []
        need("normal", "scale", "grad_attn", "table")
        for m in range(micros):
            ring_end(m, added[m])
            norm_back_step(r, m, seg)
            swapped.append(swap(r["gpos"], r["gpos_in"], m))
        need("owned", "mask", "spread", "row_full")
        vectors_step(r, own)
        sums.start("full")
        sums.pump("att")
        rings = []
        need("conv_turned", "before", "padded", "back_conv")
        for m in range(micros):
            arrived(swapped[m])
            conv_back_step(r, here, m, frames, tall, per)
            rings.append(Ring(move, r["slopes_all"], m * frames, frames, here, to_right, to_left))
            if m > 0:
                rings[m - 1].relay()
            sums.pump("ffn", "att", "full")
        sums.start("conv")
        rings[-1].relay()
        conv_sums_step(r, micros)
        sums.pump("ffn", "att", "full")
        need("gathered", "proj", "edges")
        for m in range(micros):
            rings[m].finish()
            finish_step(r, here, m, frames)
            sums.pump("conv", "ffn", "att", "full")
        need("mask_ch", "spread_ch", "mask_in", "spread_in", "row_proj", "row_vector")
        local_step(r, own, own_in)
        sums.start("local")
        sums.pump("conv", "ffn", "att", "full")
        sums.pump("local")
        sums.drain("ffn", "att")

        for j in range(eight):
            at = slice(j * own, (j + 1) * own)
            r["block"][j, :own, : deep + 128] = r["ffn_sum"][at, half:]
            r["block"][j, :own, deep + 128 :] = r["att_sum"][at]
        for k in range(2):
            r["pair"][k] = r["ffn_sum"][k * own_ret : (k + 1) * own_ret, :half]
        last = [
            move(r["block"].at[other], r["block_in"].at[number], device)
            for other, device in zip(eights, eight_at)
        ]
        last.append(move(r["pair"].at[1 - core], r["pair_in"].at[core], (here, base + 1 - core)))
        r["block_in"][number] = r["block"][number]
        r["pair_in"][core] = r["pair"][core]
        sums.drain("conv", "full", "local")
        for copy in last:
            copy.wait()
        for copy in sent:
            copy.wait_send()
        for item in rings + [sums]:
            item.close()
        return []

    scratch["local_sems"] = pltpu.SemaphoreType.DMA((4,))
    return staged_call(
        ident, ins, outs, scratch, copies, body,
        {"spans": pltpu.SMEM, "ffn": pl.ANY, "gctx_in": pltpu.VMEM},
    )


def owners(sums, own, own_in, own_hid, deep, thin, att, quarter, inner, taps, order):
    f32 = jnp.float32
    eight, _, lanes = sums["block_in"].shape
    parts, width, half = eight // 2, quarter * eight // 2, quarter * eight // 4
    blocks = taps // FOLD
    own_ret = sums["pair_in"].shape[1]
    names = list(sums)
    shapes = {
        "features_grad": sums["features_grad"].shape, "proj": (own_in, width),
        "conv": (own, inner, taps), "hidden": (own, eight * deep), "output": (own, width),
        "attend": (own, 3 * width), "return": (own_ret, width),
    }
    places = {}
    for name, source, begin, size in order:
        shapes[name] = (1, size)
        places[name] = (source, begin, size)

    def kernel(*refs):
        r = dict(zip(names, refs))
        o = dict(zip(shapes, refs[len(names) :]))
        folded = refs[-1]
        o["features_grad"][...] = r["features_grad"][...]
        for j in range(eight):
            o["hidden"][:, j * deep : (j + 1) * deep] = r["block_in"][j, :own, :deep]
        pieces = [r["block_in"][j, :own, deep : deep + thin] for j in range(eight)]
        o["output"][...] = jnp.concatenate(pieces, axis=1)
        for c in range(parts):
            both = [r["block_in"][2 * c + k, :own, deep + 128 : deep + 128 + att] for k in range(2)]
            both = jnp.concatenate(both, axis=1)
            for i in range(3):
                at = slice(i * width + c * quarter, i * width + (c + 1) * quarter)
                o["attend"][:, at] = both[:, i * quarter : (i + 1) * quarter]
        for k in range(2):
            o["return"][:, k * half : (k + 1) * half] = r["pair_in"][k]
        for i in range(own):
            rows = r["conv_sum"][i * blocks : (i + 1) * blocks]
            for j in range(FOLD):
                folded[pl.ds(j, blocks, stride=FOLD), :] = rows[:, j * inner : (j + 1) * inner]
            o["conv"][i] = folded[:taps].T
        o["proj"][...] = r["local_sum"][:own_in]
        rows = {"local": r["local_sum"][own_in : own_in + 1], "full": r["full_sum"][0:1]}
        for name, (source, begin, size) in places.items():
            o[name][...] = rows[source][:, begin : begin + size]

    results = local_call(
        kernel, [(shape, f32) for shape in shapes.values()], [pltpu.VMEM((2 * taps, inner), f32)],
        *sums.values(),
    )
    return dict(zip(shapes, results))


def per_device(
    features, lengths, input_gain, input_bias, proj_weight, proj_bias, conv_weight, conv_bias,
    encoder_gain, encoder_bias, attend_weight, query_bias, value_bias, output_weight, output_bias,
    attend_gain, attend_bias, hidden_weight, hidden_bias, return_weight, return_bias, final_gain,
    final_bias, out_grad,
):
    parts = lax.axis_size("ch")
    ranks = lax.axis_size("rows")
    side = math.isqrt(ranks // 2)
    sizes = {"y": parts, "x": side, "z": side, "k": 2}
    micros, _, frames, narrow = features.shape
    own = proj_bias.shape[0]
    width = proj_weight.shape[1]
    quarter = width // parts
    inner, taps = conv_weight.shape[1:]
    blocks = taps // FOLD
    hidden = hidden_weight.shape[1]
    own_in = input_gain.shape[0]
    own_hid = hidden_bias.shape[0]
    seg = out_grad.shape[2]
    eight = 2 * parts
    squares = side * side
    tall = eight * own
    deep, thin, att = hidden // eight, width // eight, 3 * quarter // 2
    half = width // 2
    rows = micros * frames
    mine = micros * seg
    fold = FOLD * inner
    spans = lengths.reshape(micros)

    small = (proj_bias, conv_bias, encoder_gain, encoder_bias, query_bias, value_bias, output_bias,
             attend_gain, attend_bias, return_bias, final_gain, final_bias)
    own_ret = return_weight.shape[0]
    f = forward_start(
        {
            "features": features.reshape(rows, narrow), "hidden_raw": hidden_weight,
            "output_raw": output_weight, "attend_raw": attend_weight, "proj_raw": proj_weight,
            "return_raw": return_weight, "conv_raw": conv_weight, "small": jnp.stack(small),
            "ends": jnp.stack([input_gain, input_bias]), "hid_own": hidden_bias.reshape(1, own_hid),
            "spans": spans,
        },
        sizes, 0, micros, frames, own, own_in, own_hid, own_ret, len(small),
    )
    output, grad_attn, grad_context, ffn, normal, scale, owned = feed_forward(
        f["context_in"], f["summed"], out_grad.reshape(mine, width), f["weights"], f["table"],
        f["hid_bias"], sizes, 1, micros, frames, thin, own, own_hid,
    )
    third = backward_rest(
        {
            "gctx_in": grad_context, "grad_attn": grad_attn, "normal": normal, "scale": scale,
            "owned": owned, "spans": spans,
            **{
                name: f[name]
                for name in ("low", "joint", "probs", "attend", "table", "before", "padded",
                             "conv_turned", "gathered", "proj", "edges")
            },
            "ffn": ffn.reshape(2, parts, side, side, tall, -1),
        },
        sizes, 9, micros, frames, own, own_in, own_hid, own_ret, thin,
    )

    full, local = ("full", "local")
    order = []
    for number, name in enumerate(("proj_bias", "conv_bias", "query_bias", "value_bias")):
        order.append((name, local, number * own, own))
    for number, name in enumerate(("input_gain", "input_bias")):
        order.append((name, local, 4 * own + number * own_in, own_in))
    names = ("encoder_gain", "encoder_bias", "output_bias", "attend_gain", "attend_bias",
             "return_bias", "final_gain", "final_bias")
    for number, name in enumerate(names):
        order.append((name, full, number * own, own))
    order.append(("hidden_bias", full, 8 * own, own_hid))
    o = owners(
        third, own, own_in, own_hid, deep, thin, att, quarter, inner, taps, order
    )
    for name, _, _, size in order:
        o[name] = o[name].reshape(size)
    return (
        output.reshape(out_grad.shape), o["features_grad"].reshape(features.shape),
        o["input_gain"], o["input_bias"], o["proj"], o["proj_bias"], o["conv"], o["conv_bias"],
        o["encoder_gain"], o["encoder_bias"], o["attend"], o["query_bias"], o["value_bias"],
        o["output"], o["output_bias"], o["attend_gain"], o["attend_bias"], o["hidden"],
        o["hidden_bias"], o["return"], o["return_bias"], o["final_gain"], o["final_bias"],
    )


def solution(mesh):
    vector, matrix, cube = P(ALL), P(ALL, None), P(ALL, None, None)
    weights = (
        vector, vector, matrix, vector, cube, vector, vector, vector, matrix, vector, vector,
        matrix, vector, vector, vector, matrix, vector, matrix, vector, vector, vector,
    )
    by_channel = P(None, "rows", None, "ch")
    by_frame = P(None, "rows", "ch", None)
    return jax.shard_map(
        per_device,
        mesh=mesh,
        in_specs=(by_channel, P(None, "rows")) + weights + (by_frame,),
        out_specs=(by_frame, by_channel) + weights,
        check_vma=False,
    )
```
